32 devices in a mesh: shard: 8 (over z, y), grp: 4 (over x, core).
Axes of the slice: x: 2, y: 2, z: 4, core: 2. Of those that a mesh axis runs over, the one named last changes fastest.
Arguments:
- entity_table: float32 [131072, 400], P(('shard', 'grp')), may hold values from -1.5 to 1.5
- rel_diag: float32 [64, 400], replicated, may hold values from 0.25 to 1.75
- src_ids: int32 [64000], P(('shard', 'grp')), may hold values from 0 to 131071, as said below
- dst_ids: int32 [64000], P(('shard', 'grp')), may hold values from 0 to 131071, as said below
- rel_ids: int32 [64000], P(('shard', 'grp')), may hold values from 0 to 63
- neg_ids: int32 [16, 1000], P('shard'), may hold values from 0 to 131071, as said below
Outputs:
- entity_grad: float32 [131072, 400], P(('shard', 'grp'))
The draws below stay inside these ranges and needn't reach their ends.
Inputs may be any that keep to these rules, and one draw needn't show every extreme that they name: `src_ids`: entity e is held by device e // 4096 of shard+grp. Among the sources and destinations of the 2000 edges of one device (aligned blocks of 2000 edges), at most 250 are held by any one device; in every draw one device holds exactly 250 of those of every block. `dst_ids`: drawn together with src_ids, under the bound stated there. `neg_ids`: for a shard index s and a column block g (columns g * 250 to (g + 1) * 250 - 1), the entries of rows s * 2 to (s + 1) * 2 - 1 in that block name at most 31 entities held by any one device; in every draw one device holds exactly 31 of those of every such block. A whole row set s thus names at most 124 of one device's entities, reached.
All inputs are finite; a program needn't handle non-finite values.
Results may differ from the reference program's by a relative error of at most 0.0037.
Values may be sent and summed in bfloat16 or wider, within the bound.
No kernel may reach another device: no remote copies, remote signals or barrier semaphores. Data moves between devices by JAX's collectives and lax.ppermute only.
A program may use at most 192 MiB of HBM per device.

```python
import jax
import jax.numpy as jnp
from jax import lax

D = 400
NREL = 64
NNEG = 1000
CH = 1000
SPANS_DEV = 2
ROW_DEV = 4096
SHARERS = 4
E_DEV = 2000
EDGES = 64000
NENT = 131072
LISTS = 16
NEG_W = 250
NEG_DEV = 500
CAP = 250
NCAP = 31


def block_owners(key, blocks, block_size, capacity, owning_shards):
    busiest = jax.random.randint(jax.random.fold_in(key, 7), (), 0, owning_shards)
    owner_pool = jnp.arange((owning_shards - 1) * capacity, dtype=jnp.int32) // capacity
    others = owner_pool + (owner_pool >= busiest).astype(jnp.int32)

    def single_block(block_key):
        first_key = jax.random.fold_in(block_key, 1)
        second_key = jax.random.fold_in(block_key, 2)
        chosen = jax.random.permutation(first_key, others)[:block_size - capacity]
        filled = jnp.concatenate([jnp.zeros((capacity,), jnp.int32) + busiest, chosen])
        return jax.random.permutation(second_key, filled)
    block_keys = jax.random.split(jax.random.fold_in(key, 11), blocks)
    return jax.vmap(single_block)(block_keys)


def edge_endpoints(key):
    devices = NENT // ROW_DEV
    owning_shards = block_owners(jax.random.fold_in(key, 101), EDGES // E_DEV, 2 * E_DEV, CAP, devices)
    local_rows = jax.random.randint(jax.random.fold_in(key, 102), owning_shards.shape, 0, ROW_DEV)
    return owning_shards * ROW_DEV + local_rows


def draw_src_ids(key, part):
    entity_ids = edge_endpoints(key)
    return entity_ids[:, :E_DEV].reshape(-1)


def draw_dst_ids(key, part):
    entity_ids = edge_endpoints(key)
    return entity_ids[:, E_DEV:].reshape(-1)


def draw_neg_ids(key, part):
    devices = NENT // ROW_DEV
    sharers = NNEG // NEG_W
    shards = devices // sharers
    owning_shards = block_owners(jax.random.fold_in(key, 201), devices, NEG_DEV, NCAP, devices)
    local_rows = jax.random.randint(jax.random.fold_in(key, 202), owning_shards.shape, 0, ROW_DEV)
    entity_ids = (owning_shards * ROW_DEV + local_rows).reshape(shards, sharers, SPANS_DEV, NEG_W)
    return entity_ids.transpose(0, 2, 1, 3).reshape(LISTS, NNEG)


def with_ends(entries, stream_key, low, largest):
    longest = entries.shape.index(max(entries.shape))
    spots = []
    for shift in (0, 1):
        where = [jax.random.randint(jax.random.fold_in(stream_key, axis), (), 0, length) for axis, length in enumerate(entries.shape)]
        where[longest] = (where[longest] + shift) % entries.shape[longest]
        spots.append(tuple(where))
    return entries.at[spots[0]].set(low).at[spots[1]].set(largest)


def level_of(key, extent, cuts, low, largest):
    level, own = 1.0, jax.random.fold_in(key, 6)
    for axis_at, blocks in cuts:
        heights = jnp.exp(jax.random.uniform(jax.random.fold_in(own, axis_at), (blocks,), jnp.float32, low / len(cuts), largest / len(cuts)))
        level = level * jnp.repeat(heights, extent[axis_at] // blocks).reshape([-1 if axis == axis_at else 1 for axis in range(len(extent))])
    return level


def centred(key, shape, width, bound, cuts=(), kind=jnp.bfloat16):
    drawn = width * jax.random.normal(key, shape, jnp.float32)
    if cuts:
        drawn = drawn * level_of(key, shape, cuts, -0.22, 0.18)
    return jnp.clip(drawn, -bound, bound).astype(kind)


def setup_inputs(seed: int = 0) -> dict:
    arg_keys = jax.random.split(jax.random.key(seed), 7)
    entity_table = centred(arg_keys[0], (NENT, D), 0.25, 1.5, ((0, 32),), jnp.float32)
    rel_diag = jnp.clip(1.0 + 0.15 * jax.random.normal(arg_keys[1], (NREL, D), jnp.float32), 0.25, 1.75)
    src_ids = draw_src_ids(jax.random.fold_in(arg_keys[6], 71), 0)
    dst_ids = draw_dst_ids(jax.random.fold_in(arg_keys[6], 71), 0)
    rel_ids = with_ends(jax.random.randint(arg_keys[4], (EDGES,), 0, NREL), jax.random.fold_in(arg_keys[4], 1), 0, NREL - 1).astype(jnp.int32)
    neg_ids = draw_neg_ids(jax.random.fold_in(arg_keys[6], 71), 0)
    return dict(entity_table=entity_table, rel_diag=rel_diag, src_ids=src_ids, dst_ids=dst_ids, rel_ids=rel_ids, neg_ids=neg_ids)


def reorder(values):
    shards = LISTS // SPANS_DEV
    return values.reshape(shards, SHARERS, SPANS_DEV, CH).transpose(0, 2, 1, 3).reshape(LISTS, SHARERS * CH)


def rounded(values):
    return lax.optimization_barrier(values.astype(jnp.bfloat16)).astype(jnp.float32)


def reference(entity_table, rel_diag, src_ids, dst_ids, rel_ids, neg_ids):
    highest = lax.Precision.HIGHEST

    def list_step(accum_grad, pieces):
        source_ids, target_ids, relation_ids, negative_ids = pieces
        source = rounded(entity_table[source_ids])
        target = rounded(entity_table[target_ids])
        negative_samples = rounded(entity_table[negative_ids])
        relation = rel_diag[relation_ids]
        positive = jnp.sum(source * relation * target, axis=-1)
        query_vector = rounded(source * relation)
        logit_scores = jnp.dot(query_vector, negative_samples.T, precision=highest)
        sample_weight = rounded(jax.nn.sigmoid(logit_scores))
        pos_weight = -jax.nn.sigmoid(-positive)
        source_grad = pos_weight[:, None] * relation * target + relation * jnp.dot(sample_weight, negative_samples, precision=highest)
        target_grad = pos_weight[:, None] * source * relation
        negative_grad = jnp.dot(sample_weight.T, query_vector, precision=highest)
        accum_grad = accum_grad.at[source_ids].add(source_grad)
        accum_grad = accum_grad.at[target_ids].add(target_grad)
        accum_grad = accum_grad.at[negative_ids].add(negative_grad)
        return accum_grad, None

    start_grad = jnp.zeros(entity_table.shape, jnp.float32)
    pieces = (reorder(src_ids), reorder(dst_ids), reorder(rel_ids), neg_ids)
    entity_grad, _ = lax.scan(list_step, start_grad, pieces)
    return entity_grad
```

```python
import functools

import jax
import jax.numpy as jnp
from jax import lax
from jax.experimental import pallas as pl
from jax.experimental.pallas import tpu as pltpu
from jax.sharding import PartitionSpec as P

LANES = 128
VMEM_BYTES = 56 << 20
F32 = jnp.float32
BF16 = jnp.bfloat16
NN = (((1,), (0,)), ((), ()))
NT = (((1,), (1,)), ((), ()))
TN = (((0,), (0,)), ((), ()))


def round_up(value, unit):
    return -(-value // unit) * unit


def dot(left, right, dims):
    return lax.dot_general(left, right, dims, preferred_element_type=F32)


def one_hot(rows, row, base=0):
    places = lax.broadcasted_iota(jnp.int32, (rows, row.shape[1]), 0) + base
    return jnp.where(places == row, 1.0, 0.0).astype(BF16)


def call(kernel, name, flops, nbytes, **kwargs):
    return pl.pallas_call(
        kernel,
        name=name,
        compiler_params=pltpu.CompilerParams(vmem_limit_bytes=VMEM_BYTES),
        cost_estimate=pl.CostEstimate(flops=flops, bytes_accessed=nbytes, transcendentals=0),
        **kwargs,
    )


def slots_kernel(ids_ref, req_ref, *slot_refs, rows_dev, devices):
    segments, width = ids_ref.shape
    chunks = len(slot_refs)
    upper = jnp.where(
        lax.broadcasted_iota(jnp.int32, (LANES, LANES), 0)
        < lax.broadcasted_iota(jnp.int32, (LANES, LANES), 1),
        1.0,
        0.0,
    ).astype(BF16)
    owners = lax.broadcasted_iota(jnp.int32, (devices, LANES), 0)
    taken = jnp.zeros((devices, 1), F32)
    sums = [[jnp.zeros((devices, LANES), F32) for _ in range(2)] for _ in range(chunks)]
    for segment in range(segments):
        for start in range(0, width, LANES):
            ids = ids_ref[segment : segment + 1, start : start + LANES]
            valid = ids >= 0
            owner = jnp.where(valid, ids // rows_dev, -1)
            code = jnp.where(valid, ids - owner * rows_dev + 1, 0)
            member = jnp.where(owners == owner, 1.0, 0.0)
            before = dot(member.astype(BF16), upper, NN) + taken
            taken = taken + jnp.sum(member, axis=1, keepdims=True)
            rank = jnp.sum(before * member, axis=0, keepdims=True).astype(jnp.int32)
            high = (member * (code // 64).astype(F32)).astype(BF16)
            low = (member * (code % 64).astype(F32)).astype(BF16)
            for chunk in range(chunks):
                place = rank - chunk * LANES
                inside = valid & (place >= 0) & (place < LANES)
                slot_refs[chunk][segment : segment + 1, start : start + LANES] = jnp.where(
                    inside, owner * LANES + place, -1
                )
                hot = one_hot(LANES, jnp.where(inside, place, -1))
                sums[chunk][0] += dot(high, hot, NT)
                sums[chunk][1] += dot(low, hot, NT)
    for chunk in range(chunks):
        value = 64.0 * sums[chunk][0] + sums[chunk][1]
        req_ref[:, chunk * LANES : (chunk + 1) * LANES] = value.astype(jnp.int32) - 1


def make_slots(ids, rows_dev, devices, chunks):
    shape = ids.shape
    return call(
        functools.partial(slots_kernel, rows_dev=rows_dev, devices=devices),
        "slots",
        4 * devices * LANES * ids.size,
        8 * ids.size,
        out_shape=[jax.ShapeDtypeStruct((devices, chunks * LANES), jnp.int32)]
        + [jax.ShapeDtypeStruct(shape, jnp.int32)] * chunks,
    )(ids)


def gather_kernel(table_ref, req_ref, out_ref, *, group):
    first = pl.program_id(0) * group
    row = jnp.concatenate([req_ref[pl.ds(first + i, 1), :] for i in range(group)], axis=1)
    rows = dot(table_ref[...], one_hot(table_ref.shape[1], row), NN).astype(BF16)
    for i in range(group):
        out_ref[i] = rows[:, i * LANES : (i + 1) * LANES]


def gather(table, requests):
    feature, rows_dev = table.shape
    devices = requests.shape[0]
    group = 4
    slots = devices * LANES
    return call(
        functools.partial(gather_kernel, group=group),
        "gather_rows",
        2 * feature * rows_dev * slots,
        2 * feature * (rows_dev + slots),
        grid=(devices // group,),
        in_specs=[
            pl.BlockSpec((feature, rows_dev), lambda i: (0, 0)),
            pl.BlockSpec((devices, LANES), lambda i: (0, 0)),
        ],
        out_specs=pl.BlockSpec((group, feature, LANES), lambda i: (i, 0, 0)),
        out_shape=jax.ShapeDtypeStruct((devices, feature, LANES), BF16),
    )(table, requests)


def gather_neg_kernel(table_ref, req_ref, out_ref, *, cap):
    devices = req_ref.shape[0]
    row = jnp.concatenate([req_ref[d : d + 1, :cap] for d in range(devices)], axis=1)
    rows = dot(table_ref[...], one_hot(table_ref.shape[1], row), NN)
    out_ref[...] = rows.T.astype(BF16)


def gather_neg(table, requests, cap):
    feature, rows_dev = table.shape
    slots = requests.shape[0] * cap
    return call(
        functools.partial(gather_neg_kernel, cap=cap),
        "gather_negatives",
        2 * feature * rows_dev * slots,
        2 * feature * (rows_dev + slots),
        out_shape=jax.ShapeDtypeStruct((slots, feature), BF16),
    )(table, requests)


def neg_slot_row(slot, cap):
    return jnp.where(slot >= 0, (slot // LANES) * cap + slot % LANES, -1)


def spread_neg_kernel(back_ref, slot_ref, out_ref, *, cap):
    parts, width = slot_ref.shape
    for part in range(parts):
        row = neg_slot_row(slot_ref[part : part + 1, :], cap)
        hot = one_hot(back_ref.shape[0], row)
        out_ref[part] = dot(hot, back_ref[...], TN).astype(BF16)


def spread_neg(back, slot, cap):
    parts, width = slot.shape
    return call(
        functools.partial(spread_neg_kernel, cap=cap),
        "spread_negatives",
        2 * back.size * slot.size,
        2 * back.size,
        out_shape=jax.ShapeDtypeStruct((parts, width, back.shape[1]), BF16),
    )(back, slot)


def collect_neg_kernel(grad_ref, slot_ref, out_ref, *, cap):
    parts, width = slot_ref.shape
    total = jnp.zeros(out_ref.shape, F32)
    for part in range(parts):
        value = grad_ref[0, part].astype(F32)
        for sharer in range(1, grad_ref.shape[0]):
            value = value + grad_ref[sharer, part].astype(F32)
        row = neg_slot_row(slot_ref[part : part + 1, :], cap)
        total = total + dot(one_hot(out_ref.shape[0], row), value.astype(BF16), NN)
    out_ref[...] = total.astype(BF16)


def collect_neg(grads, slot, cap, devices):
    feature = grads.shape[-1]
    return call(
        functools.partial(collect_neg_kernel, cap=cap),
        "collect_negatives",
        2 * devices * cap * feature * slot.size,
        4 * grads.size,
        out_shape=jax.ShapeDtypeStruct((devices * cap, feature), BF16),
    )(grads, slot)


def spread_kernel(*refs, first):
    if first:
        back_ref, slot_ref, out_ref, flat = refs
    else:
        back_ref, slot_ref, so_far_ref, out_ref, flat = refs

    @pl.when(pl.program_id(0) == 0)
    def _():
        for d in range(back_ref.shape[0]):
            flat[:, d * LANES : (d + 1) * LANES] = back_ref[d]

    row = slot_ref[...].reshape(1, slot_ref.shape[-1])
    rows = dot(flat[...], one_hot(flat.shape[1], row), NN)
    if not first:
        rows = rows + so_far_ref[...].astype(F32)
    out_ref[...] = rows.astype(BF16)


def spread(back, slot, so_far):
    devices, feature, _ = back.shape
    segments, width = slot.shape
    tile = 512 if devices * LANES <= 4096 else 128
    steps = width // tile
    slots = devices * LANES
    rows_spec = pl.BlockSpec((feature, tile), lambda i: (0, i))
    return call(
        functools.partial(spread_kernel, first=so_far is None),
        "spread_rows",
        2 * feature * slots * slot.size,
        2 * feature * (slots + slot.size),
        grid=(segments * steps,),
        in_specs=[
            pl.BlockSpec((devices, feature, LANES), lambda i: (0, 0, 0)),
            pl.BlockSpec((1, 1, tile), lambda i: (i // steps, 0, i % steps)),
        ]
        + ([] if so_far is None else [rows_spec]),
        out_specs=rows_spec,
        out_shape=jax.ShapeDtypeStruct((feature, slot.size), BF16),
        scratch_shapes=[pltpu.VMEM((feature, slots), BF16)],
    )(back, slot.reshape(segments, 1, width), *([] if so_far is None else [so_far]))


def edges_kernel(
    src_ref, dst_ref, rel_ids_ref, rel_ref, neg_ref, src_grad_ref, dst_grad_ref, neg_grad_ref, sums
):
    step = pl.program_id(1)
    parts, _, part, feature = neg_ref.shape
    negatives = neg_ref[...].reshape(parts * part, feature)
    nrel = rel_ref.shape[1]
    hot = one_hot(nrel, rel_ids_ref[...].reshape(1, rel_ids_ref.shape[-1]))
    table = rel_ref[...]
    relation = jnp.zeros(src_ref.shape, F32)
    for _ in range(3):
        piece = table.astype(BF16)
        relation = relation + dot(piece, hot, NN)
        table = table - piece.astype(F32)
    source = src_ref[...].astype(F32)
    target = dst_ref[...].astype(F32)
    product = source * relation
    positive = jnp.sum(product * target, axis=0, keepdims=True)
    pos_weight = -jax.nn.sigmoid(-positive)
    query = product.astype(BF16)
    weight = jax.nn.sigmoid(dot(negatives, query, NN)).astype(BF16)
    gathered = dot(negatives, weight, TN)
    src_grad_ref[...] = (relation * (pos_weight * target + gathered)).astype(BF16)
    dst_grad_ref[...] = (pos_weight * product).astype(BF16)
    neg_grad = dot(weight, query, NT)

    @pl.when(step == 0)
    def _():
        sums[...] = neg_grad

    @pl.when(step != 0)
    def _():
        sums[...] += neg_grad

    @pl.when(step == pl.num_programs(1) - 1)
    def _():
        neg_grad_ref[...] = sums[...].astype(BF16).reshape(neg_grad_ref.shape)


def edges(rows, rel_ids, relations, negatives):
    feature, endpoints = rows.shape
    parts, spans, part, _ = negatives.shape
    width = rel_ids.shape[1]
    tile = 512
    steps = width // tile
    blocks = spans * steps
    edge_spec = pl.BlockSpec((feature, tile), lambda b, i: (0, b * steps + i))
    flops = 6 * feature * parts * part * spans * width
    src_grad, dst_grad, neg_grad = call(
        edges_kernel,
        "edges",
        flops,
        2 * (2 * rows.size + 2 * negatives.size),
        grid=(spans, steps),
        in_specs=[
            edge_spec,
            pl.BlockSpec((feature, tile), lambda b, i: (0, blocks + b * steps + i)),
            pl.BlockSpec((1, 1, tile), lambda b, i: (b, 0, i)),
            pl.BlockSpec(relations.shape, lambda b, i: (0, 0)),
            pl.BlockSpec((parts, 1, part, feature), lambda b, i: (0, b, 0, 0)),
        ],
        out_specs=[
            edge_spec,
            edge_spec,
            pl.BlockSpec((parts, 1, part, feature), lambda b, i: (0, b, 0, 0)),
        ],
        out_shape=[
            jax.ShapeDtypeStruct((feature, endpoints // 2), BF16),
            jax.ShapeDtypeStruct((feature, endpoints // 2), BF16),
            jax.ShapeDtypeStruct(negatives.shape, BF16),
        ],
        scratch_shapes=[pltpu.VMEM((parts * part, feature), F32)],
    )(rows, rows, rel_ids.reshape(spans, 1, width), relations, negatives)
    return src_grad, dst_grad, neg_grad


def collect_kernel(src_ref, dst_ref, slot_ref, out_ref, *, group):
    segments, width = slot_ref.shape
    base = pl.program_id(0) * group * LANES
    total = jnp.zeros((src_ref.shape[0], group * LANES), F32)
    for segment in range(segments):
        grads = src_ref if segment < segments // 2 else dst_ref
        start = segment % (segments // 2) * width
        hot = one_hot(group * LANES, slot_ref[segment : segment + 1, :], base)
        total = total + dot(grads[:, start : start + width], hot, NT)
    total = total.astype(BF16)
    for i in range(group):
        out_ref[i] = total[:, i * LANES : (i + 1) * LANES]


def collect(src_grad, dst_grad, slot, devices):
    feature = src_grad.shape[0]
    group = 4
    slots = devices * LANES
    whole = pl.BlockSpec(src_grad.shape, lambda i: (0, 0))
    return call(
        functools.partial(collect_kernel, group=group),
        "collect_grads",
        2 * feature * slots * slot.size,
        2 * feature * (slots + slot.size),
        grid=(devices // group,),
        in_specs=[whole, whole, pl.BlockSpec(slot.shape, lambda i: (0, 0))],
        out_specs=pl.BlockSpec((group, feature, LANES), lambda i: (i, 0, 0)),
        out_shape=jax.ShapeDtypeStruct((devices, feature, LANES), BF16),
    )(src_grad, dst_grad, slot)


def add_kernel(*refs, rows, cap, with_neg, first):
    refs = list(refs)
    recv_ref, req_ref = refs[:2]
    refs = refs[2:]
    if with_neg:
        neg_ref, neg_req_ref = refs[:2]
        refs = refs[2:]
    if not first:
        so_far_ref = refs.pop(0)
    out_ref, flat = refs[:2]
    devices = recv_ref.shape[0]
    step = pl.program_id(0)

    @pl.when(step == 0)
    def _():
        for d in range(devices):
            flat[:, d * LANES : (d + 1) * LANES] = recv_ref[d]

    base = step * rows
    row = jnp.concatenate([req_ref[d : d + 1, :] for d in range(devices)], axis=1)
    total = dot(flat[...], one_hot(rows, row, base), NT)
    if with_neg:
        row = jnp.concatenate([neg_req_ref[d : d + 1, :cap] for d in range(devices)], axis=1)
        total = total + dot(neg_ref[...].astype(F32).T.astype(BF16), one_hot(rows, row, base), NT)
    if not first:
        total = total + so_far_ref[...]
    out_ref[...] = total


def add_rows(recv, requests, so_far, neg, neg_requests, cap, rows_dev):
    devices, feature, _ = recv.shape
    rows = 512 if devices * LANES <= 4096 else 128
    slots = devices * LANES
    with_neg = neg is not None
    whole_req = pl.BlockSpec((devices, LANES), lambda i: (0, 0))
    rows_spec = pl.BlockSpec((feature, rows), lambda i: (0, i))
    operands = [recv, requests]
    specs = [pl.BlockSpec((devices, feature, LANES), lambda i: (0, 0, 0)), whole_req]
    if with_neg:
        operands += [neg, neg_requests]
        specs += [pl.BlockSpec(neg.shape, lambda i: (0, 0)), whole_req]
    if so_far is not None:
        operands.append(so_far)
        specs.append(rows_spec)
    return call(
        functools.partial(
            add_kernel, rows=rows, cap=cap, with_neg=with_neg, first=so_far is None
        ),
        "add_grads",
        2 * feature * slots * rows_dev,
        2 * feature * slots + 8 * feature * rows_dev,
        grid=(rows_dev // rows,),
        in_specs=specs,
        out_specs=rows_spec,
        out_shape=jax.ShapeDtypeStruct((feature, rows_dev), F32),
        scratch_shapes=[pltpu.VMEM((feature, slots), BF16)],
    )(*operands)


def exchange(value, axes=("shard", "grp")):
    return lax.all_to_all(value, axes, split_axis=0, concat_axis=0, tiled=True)


def pad_lanes(value, width, fill):
    return jnp.pad(value, ((0, 0), (0, width - value.shape[1])), constant_values=fill)


def body(entity_table, rel_diag, src_ids, dst_ids, rel_ids, neg_ids):
    rows_dev, feature = entity_table.shape
    sharers = lax.axis_size("grp")
    devices = lax.axis_size("shard") * sharers
    spans, neg_count = neg_ids.shape
    edge_count = src_ids.shape[0]
    block_len = edge_count // spans
    edge_cap = 4 * edge_count // devices
    chunks = round_up(edge_cap, LANES) // LANES
    part_width = neg_count // sharers
    neg_cap = round_up(2 * spans * part_width // devices, 16)
    width = round_up(block_len, 512)
    part = round_up(part_width, LANES)

    table = entity_table.T.astype(BF16)
    own_ids = lax.dynamic_slice_in_dim(
        neg_ids, lax.axis_index("grp") * part_width, part_width, 1
    )
    ends = jnp.concatenate(
        [src_ids.reshape(spans, block_len), dst_ids.reshape(spans, block_len)]
    )
    edge_req, *edge_slots = make_slots(pad_lanes(ends, width, -1), rows_dev, devices, chunks)
    neg_req, neg_slot = make_slots(pad_lanes(own_ids, part, -1), rows_dev, devices, 1)
    rel_rows = pad_lanes(rel_ids.reshape(spans, block_len), width, -1)

    asked = exchange(jnp.concatenate([edge_req, neg_req], axis=1))
    edge_asked = [asked[:, c * LANES : (c + 1) * LANES] for c in range(chunks)]
    neg_asked = asked[:, chunks * LANES :]

    neg_rows = gather_neg(table, neg_asked, neg_cap)
    neg_back = exchange(neg_rows.reshape(devices, neg_cap, feature))
    edge_back = [exchange(gather(table, edge_asked[c])) for c in range(chunks)]

    own_neg = spread_neg(neg_back.reshape(devices * neg_cap, feature), neg_slot, neg_cap)
    negatives = lax.all_gather(own_neg, "grp", axis=0, tiled=False)
    rows = None
    for c in range(chunks):
        rows = spread(edge_back[c], edge_slots[c], rows)
    src_grad, dst_grad, neg_grad = edges(rows, rel_rows, rel_diag.T, negatives)

    edge_recv = [exchange(collect(src_grad, dst_grad, edge_slots[c], devices)) for c in range(chunks)]
    neg_parts = exchange(neg_grad, "grp")
    neg_out = collect_neg(neg_parts, neg_slot, neg_cap, devices)
    neg_recv = exchange(neg_out.reshape(devices, neg_cap, feature))
    grad = None
    for c in range(chunks):
        last = c == chunks - 1
        grad = add_rows(
            edge_recv[c],
            edge_asked[c],
            grad,
            neg_recv.reshape(devices * neg_cap, feature) if last else None,
            neg_asked if last else None,
            neg_cap,
            rows_dev,
        )
    return grad.T


def solution(mesh):
    placed = (
        P(("shard", "grp"), None),
        P(),
        P(("shard", "grp")),
        P(("shard", "grp")),
        P(("shard", "grp")),
        P("shard", None),
    )
    return jax.shard_map(
        body, mesh=mesh, in_specs=placed, out_specs=P(("shard", "grp"), None), check_vma=False
    )
```

```python
import functools

import jax
import jax.numpy as jnp
from jax import lax
from jax.experimental import pallas as pl
from jax.experimental.pallas import tpu as pltpu
from jax.sharding import PartitionSpec as P

LANES = 128
POOL = 48
VMEM_BYTES = 56 << 20
F32 = jnp.float32
BF16 = jnp.bfloat16
NN = (((1,), (0,)), ((), ()))
NT = (((1,), (1,)), ((), ()))
TN = (((0,), (0,)), ((), ()))


def round_up(value, unit):
    return -(-value // unit) * unit


def dot(left, right, dims):
    return lax.dot_general(left, right, dims, preferred_element_type=F32)


def one_hot(rows, row, base=0):
    places = lax.broadcasted_iota(jnp.int32, (rows, row.shape[1]), 0) + base
    return jnp.where(places == row, 1.0, 0.0).astype(BF16)


def call(kernel, name, flops, nbytes, **kwargs):
    return pl.pallas_call(
        kernel,
        name=name,
        compiler_params=pltpu.CompilerParams(vmem_limit_bytes=VMEM_BYTES),
        cost_estimate=pl.CostEstimate(flops=flops, bytes_accessed=nbytes, transcendentals=0),
        **kwargs,
    )


def ranks(members, mixer):
    groups = members[0].shape[0]
    both = dot(jnp.concatenate(members, axis=0).astype(BF16), mixer, NN)
    taken = jnp.zeros((groups, LANES), F32)
    found = []
    for i, member in enumerate(members):
        chunk = both[i * groups : (i + 1) * groups]
        found.append(jnp.sum((chunk[:, :LANES] + taken) * member, axis=0, keepdims=True))
        taken = taken + chunk[:, LANES:]
    return [rank.astype(jnp.int32) for rank in found], taken


def fill(members, codes, places, count):
    groups = members[0].shape[0]
    high = [m * (c // LANES).astype(F32) for m, c in zip(members, codes)]
    low = [m * (c % LANES).astype(F32) for m, c in zip(members, codes)]
    left = jnp.concatenate(
        [jnp.concatenate(high, axis=1), jnp.concatenate(low, axis=1)], axis=0
    ).astype(BF16)
    sums = dot(left, one_hot(count, jnp.concatenate(places, axis=1)), NT)
    return (LANES * sums[:groups] + sums[groups:]).astype(jnp.int32) - 1


def slots_kernel(ends_ref, own_ref, *refs, rows_dev, devices, sharers, chunks, neg_cap):
    msg_ref = refs[0]
    slot_refs = refs[1 : 1 + chunks]
    pool_ref = refs[1 + chunks] if chunks > 1 else None
    neg_ref = refs[-1]
    row = lax.broadcasted_iota(jnp.int32, (LANES, 2 * LANES), 0)
    lane = lax.broadcasted_iota(jnp.int32, (LANES, 2 * LANES), 1)
    mixer = jnp.where(row < lane, 1.0, 0.0).astype(BF16)
    owners = lax.broadcasted_iota(jnp.int32, (devices, LANES), 0)

    def prepare(ids_ref):
        where, holder, codes, members = [], [], [], []
        for segment in range(ids_ref.shape[0]):
            for start in range(0, ids_ref.shape[1], LANES):
                ids = ids_ref[segment : segment + 1, start : start + LANES]
                owner = jnp.where(ids >= 0, ids // rows_dev, -1)
                where.append((slice(segment, segment + 1), slice(start, start + LANES)))
                holder.append(owner)
                codes.append(jnp.where(ids >= 0, ids - owner * rows_dev + 1, 0))
                members.append(jnp.where(owners == owner, 1.0, 0.0))
        found, _ = ranks(members, mixer)
        return where, holder, codes, members, found

    where, holder, codes, members, found = prepare(ends_ref)
    for chunk in range(chunks):
        places = []
        for at, owner, rank in zip(where, holder, found):
            place = rank - chunk * LANES
            place = jnp.where((owner >= 0) & (place >= 0) & (place < LANES), place, -1)
            slot_refs[chunk][at] = jnp.where(place >= 0, owner * LANES + place, -1)
            places.append(place)
        msg_ref[:, chunk * LANES : (chunk + 1) * LANES] = fill(members, codes, places, LANES)
    offset = chunks * LANES
    flag = jnp.full((1, 1), -1, jnp.int32)
    if chunks > 1:
        shards = devices // sharers
        room = sharers * POOL
        shard_rows = lax.broadcasted_iota(jnp.int32, (shards, LANES), 0)
        spilled, spill_codes = [], []
        for owner, code, rank in zip(holder, codes, found):
            shard = jnp.where(rank >= LANES, owner // sharers, -1)
            spilled.append(jnp.where(shard_rows == shard, 1.0, 0.0))
            spill_codes.append(code + (owner % sharers) * rows_dev)
        pooled, taken = ranks(spilled, mixer)
        places = []
        for at, owner, rank, place in zip(where, holder, found, pooled):
            inside = (owner >= 0) & (rank >= LANES) & (place < room)
            pool_ref[at] = jnp.where(inside, owner // sharers * room + place, -1)
            places.append(jnp.where(inside, place, -1))
        listed = fill(spilled, spill_codes, places, 2 * LANES)
        for shard in range(shards):
            msg_ref[shard * sharers : (shard + 1) * sharers, offset : offset + 2 * LANES] = (
                jnp.broadcast_to(listed[shard : shard + 1], (sharers, 2 * LANES))
            )
        offset += 2 * LANES
        most = jnp.max(jnp.max(taken, axis=1, keepdims=True), axis=0, keepdims=True)
        flag = jnp.where(most > room, 1, -1)

    where, holder, codes, members, found = prepare(own_ref)
    for at, owner, rank in zip(where, holder, found):
        neg_ref[at] = jnp.where(owner >= 0, owner * neg_cap + rank, -1)
    places = [jnp.where(owner >= 0, rank, -1) for owner, rank in zip(holder, found)]
    listed = fill(members, codes, places, LANES)
    lanes = lax.broadcasted_iota(jnp.int32, listed.shape, 1)
    msg_ref[:, offset:] = jnp.where(lanes == LANES - 1, flag, listed)


def make_slots(ends, own, rows_dev, devices, sharers, chunks, neg_cap):
    pooled = chunks > 1
    width = (chunks + 1 + 2 * pooled) * LANES
    return call(
        functools.partial(
            slots_kernel,
            rows_dev=rows_dev,
            devices=devices,
            sharers=sharers,
            chunks=chunks,
            neg_cap=neg_cap,
        ),
        "slots",
        16 * devices * LANES * ends.size,
        8 * ends.size,
        out_shape=[jax.ShapeDtypeStruct((devices, width), jnp.int32)]
        + [jax.ShapeDtypeStruct(ends.shape, jnp.int32)] * (chunks + pooled)
        + [jax.ShapeDtypeStruct(own.shape, jnp.int32)],
    )(ends, own)


def pack(out_ref, at, start, rows):
    count, feature = rows.shape
    full = round_up(feature, LANES)
    rows = jnp.concatenate([rows, jnp.zeros((count, full - feature), rows.dtype)], axis=1)
    for piece in range(full // LANES):
        out_ref[at, start + piece * count : start + (piece + 1) * count, :] = rows[
            :, piece * LANES : (piece + 1) * LANES
        ].astype(out_ref.dtype)


def unpack(in_ref, at, start, count, flat_ref, to):
    for piece in range(flat_ref.shape[1] // LANES):
        flat_ref[to : to + count, piece * LANES : (piece + 1) * LANES] = in_ref[
            at, start + piece * count : start + (piece + 1) * count, :
        ]


def gather_kernel(table_ref, *refs, group, neg_cap):
    feature, rows_dev = table_ref.shape
    first = pl.program_id(0) * group
    req_ref, out_ref = refs[0], refs[-1]
    row = [req_ref[pl.ds(first + i, 1), :] for i in range(group)]
    if neg_cap:
        row += [refs[1][pl.ds(first + i, 1), :neg_cap] for i in range(group)]
    rows = dot(table_ref[...], one_hot(rows_dev, jnp.concatenate(row, axis=1)), NN)
    start = out_ref.shape[1] - feature
    for i in range(group):
        out_ref[i, start:] = rows[:, i * LANES : (i + 1) * LANES].astype(BF16)
    if neg_cap:
        neg = rows[:, group * LANES :].T
        for i in range(group):
            pack(out_ref, i, 0, neg[i * neg_cap : (i + 1) * neg_cap])


def gather(table, requests, neg_requests=None, neg_cap=0):
    feature, rows_dev = table.shape
    devices = requests.shape[0]
    group = 4
    height = feature + neg_cap * (round_up(feature, LANES) // LANES)
    slots = devices * (LANES + neg_cap)
    whole = pl.BlockSpec((devices, LANES), lambda i: (0, 0))
    return call(
        functools.partial(gather_kernel, group=group, neg_cap=neg_cap),
        "gather_rows",
        2 * feature * rows_dev * slots,
        2 * feature * (rows_dev + slots),
        grid=(devices // group,),
        in_specs=[pl.BlockSpec((feature, rows_dev), lambda i: (0, 0)), whole]
        + ([whole] if neg_cap else []),
        out_specs=pl.BlockSpec((group, height, LANES), lambda i: (i, 0, 0)),
        out_shape=jax.ShapeDtypeStruct((devices, height, LANES), BF16),
    )(table, requests, *([neg_requests] if neg_cap else []))


def gather_pool_kernel(table_ref, req_ref, out_ref, *, group):
    rows_dev = table_ref.shape[1]
    row = req_ref[...].reshape(1, group * POOL)
    rows = dot(table_ref[...], one_hot(rows_dev, row), NN).T
    for i in range(group):
        pack(out_ref, i, 0, rows[i * POOL : (i + 1) * POOL])


def gather_pool(table, requests, devices):
    feature, rows_dev = table.shape
    relays = requests.shape[0]
    group = 8
    steps = devices // group
    height = POOL * (round_up(feature, LANES) // LANES)
    return call(
        functools.partial(gather_pool_kernel, group=group),
        "gather_pool",
        2 * feature * rows_dev * requests.size,
        2 * feature * (rows_dev + requests.size),
        grid=(relays * steps,),
        in_specs=[
            pl.BlockSpec((feature, rows_dev), lambda i: (0, 0)),
            pl.BlockSpec((1, 1, group * POOL), lambda i: (i, 0, 0)),
        ],
        out_specs=pl.BlockSpec((group, height, LANES), lambda i: (i, 0, 0)),
        out_shape=jax.ShapeDtypeStruct((relays * devices, height, LANES), BF16),
    )(table, requests.reshape(relays * steps, 1, group * POOL))


def spread_neg_kernel(back_ref, slot_ref, out_ref, flat, *, cap):
    parts = slot_ref.shape[0]
    feature = out_ref.shape[-1]
    devices = back_ref.shape[0]
    for d in range(devices):
        unpack(back_ref, d, 0, cap, flat, d * cap)
    for part in range(parts):
        hot = one_hot(devices * cap, slot_ref[part : part + 1, :])
        out_ref[part] = dot(hot, flat[...], TN)[:, :feature].astype(BF16)


def spread_neg(back, slot, cap, feature):
    devices = back.shape[0]
    parts, width = slot.shape
    full = round_up(feature, LANES)
    height = cap * full // LANES
    return call(
        functools.partial(spread_neg_kernel, cap=cap),
        "spread_negatives",
        2 * devices * cap * full * slot.size,
        2 * devices * cap * full,
        grid=(1,),
        in_specs=[
            pl.BlockSpec((devices, height, LANES), lambda i: (0, 0, 0)),
            pl.BlockSpec(slot.shape, lambda i: (0, 0)),
        ],
        out_specs=pl.BlockSpec((parts, width, feature), lambda i: (0, 0, 0)),
        out_shape=jax.ShapeDtypeStruct((parts, width, feature), BF16),
        scratch_shapes=[pltpu.VMEM((devices * cap, full), BF16)],
    )(back, slot)


def spread_kernel(*refs, first, pooled):
    back_ref, slot_ref = refs[:2]
    so_far_ref = None if first else refs[2]
    out_ref, flat = refs[2 + (not first) :][:2]
    devices = back_ref.shape[0]
    feature = flat.shape[0]

    @pl.when(pl.program_id(0) == 0)
    def _():
        if pooled:
            for d in range(devices):
                unpack(back_ref, d, 0, POOL, refs[-1], d * POOL)
            flat[...] = refs[-1][...].astype(F32).T[:feature].astype(BF16)
        else:
            start = back_ref.shape[1] - feature
            for d in range(devices):
                flat[:, d * LANES : (d + 1) * LANES] = back_ref[d, start:]

    row = slot_ref[...].reshape(1, slot_ref.shape[-1])
    rows = dot(flat[...], one_hot(flat.shape[1], row), NN)
    if not first:
        rows = rows + so_far_ref[...].astype(F32)
    out_ref[...] = rows.astype(BF16)


def spread(back, slot, so_far, feature, pooled=False):
    devices = back.shape[0]
    segments, width = slot.shape
    slots = devices * (POOL if pooled else LANES)
    tile = 512 if slots <= 4096 else 128
    steps = width // tile
    rows_spec = pl.BlockSpec((feature, tile), lambda i: (0, i))
    extra = [] if so_far is None else [so_far]
    scratch = [pltpu.VMEM((feature, slots), BF16)]
    if pooled:
        scratch.append(pltpu.VMEM((slots, round_up(feature, LANES)), BF16))
    return call(
        functools.partial(spread_kernel, first=so_far is None, pooled=pooled),
        "spread_pool" if pooled else "spread_rows",
        2 * feature * slots * slot.size,
        2 * feature * (slots + slot.size),
        grid=(segments * steps,),
        in_specs=[
            pl.BlockSpec(back.shape, lambda i: (0, 0, 0)),
            pl.BlockSpec((1, 1, tile), lambda i: (i // steps, 0, i % steps)),
        ]
        + [rows_spec] * len(extra),
        out_specs=rows_spec,
        out_shape=jax.ShapeDtypeStruct((feature, slot.size), BF16),
        scratch_shapes=scratch,
    )(back, slot.reshape(segments, 1, width), *extra)


def edges_kernel(
    src_ref, dst_ref, rel_ids_ref, rel_ref, neg_ref, src_grad_ref, dst_grad_ref, neg_grad_ref, sums
):
    step = pl.program_id(1)
    parts, _, part, feature = neg_ref.shape
    negatives = neg_ref[...].reshape(parts * part, feature)
    nrel = rel_ref.shape[1]
    hot = one_hot(nrel, rel_ids_ref[...].reshape(1, rel_ids_ref.shape[-1]))
    table = rel_ref[...]
    relation = jnp.zeros(src_ref.shape, F32)
    for _ in range(3):
        piece = table.astype(BF16)
        relation = relation + dot(piece, hot, NN)
        table = table - piece.astype(F32)
    source = src_ref[...].astype(F32)
    target = dst_ref[...].astype(F32)
    product = source * relation
    positive = jnp.sum(product * target, axis=0, keepdims=True)
    pos_weight = -jax.nn.sigmoid(-positive)
    query = product.astype(BF16)
    weight = jax.nn.sigmoid(dot(negatives, query, NN)).astype(BF16)
    gathered = dot(negatives, weight, TN)
    src_grad_ref[...] = (relation * (pos_weight * target + gathered)).astype(BF16)
    dst_grad_ref[...] = (pos_weight * product).astype(BF16)
    neg_grad = dot(weight, query, NT)

    @pl.when(step == 0)
    def _():
        sums[...] = neg_grad

    @pl.when(step != 0)
    def _():
        sums[...] += neg_grad

    @pl.when(step == pl.num_programs(1) - 1)
    def _():
        neg_grad_ref[...] = sums[...].reshape(neg_grad_ref.shape)


def edges(rows, rel_ids, relations, negatives):
    feature, endpoints = rows.shape
    parts, spans, part, _ = negatives.shape
    width = rel_ids.shape[1]
    tile = 512
    steps = width // tile
    blocks = spans * steps
    edge_spec = pl.BlockSpec((feature, tile), lambda b, i: (0, b * steps + i))
    flops = 6 * feature * parts * part * spans * width
    src_grad, dst_grad, neg_grad = call(
        edges_kernel,
        "edges",
        flops,
        2 * (2 * rows.size + 2 * negatives.size),
        grid=(spans, steps),
        in_specs=[
            edge_spec,
            pl.BlockSpec((feature, tile), lambda b, i: (0, blocks + b * steps + i)),
            pl.BlockSpec((1, 1, tile), lambda b, i: (b, 0, i)),
            pl.BlockSpec(relations.shape, lambda b, i: (0, 0)),
            pl.BlockSpec((parts, 1, part, feature), lambda b, i: (0, b, 0, 0)),
        ],
        out_specs=[
            edge_spec,
            edge_spec,
            pl.BlockSpec((parts, 1, part, feature), lambda b, i: (0, b, 0, 0)),
        ],
        out_shape=[
            jax.ShapeDtypeStruct((feature, endpoints // 2), BF16),
            jax.ShapeDtypeStruct((feature, endpoints // 2), BF16),
            jax.ShapeDtypeStruct(negatives.shape, F32),
        ],
        scratch_shapes=[pltpu.VMEM((parts * part, feature), F32)],
    )(rows, rows, rel_ids.reshape(spans, 1, width), relations, negatives)
    return src_grad, dst_grad, neg_grad


def collect_kernel(src_ref, dst_ref, slot_ref, *refs, group, neg_cap):
    segments, width = slot_ref.shape
    feature = src_ref.shape[0]
    out_ref = refs[-1]
    step = pl.program_id(0)
    total = jnp.zeros((feature, group * LANES), F32)
    for segment in range(segments):
        grads = src_ref if segment < segments // 2 else dst_ref
        start = segment % (segments // 2) * width
        hot = one_hot(group * LANES, slot_ref[segment : segment + 1, :], step * group * LANES)
        total = total + dot(grads[:, start : start + width], hot, NT)
    total = total.astype(BF16)
    first = out_ref.shape[1] - feature
    for i in range(group):
        out_ref[i, first:] = total[:, i * LANES : (i + 1) * LANES]
    if neg_cap:
        neg_grad_ref, neg_slot_ref = refs[:2]
        rows = jnp.zeros((group * neg_cap, feature), F32)
        for part in range(neg_slot_ref.shape[0]):
            row = neg_slot_ref[part : part + 1, :]
            hot = one_hot(group * neg_cap, row, step * group * neg_cap)
            rows = rows + dot(hot, neg_grad_ref[part].astype(BF16), NN)
        for i in range(group):
            pack(out_ref, i, 0, rows[i * neg_cap : (i + 1) * neg_cap])


def collect(src_grad, dst_grad, slot, devices, neg_grad=None, neg_slot=None, neg_cap=0):
    feature = src_grad.shape[0]
    group = 4
    slots = devices * LANES
    height = feature + neg_cap * (round_up(feature, LANES) // LANES)
    whole = pl.BlockSpec(src_grad.shape, lambda i: (0, 0))
    operands = [src_grad, dst_grad, slot]
    specs = [whole, whole, pl.BlockSpec(slot.shape, lambda i: (0, 0))]
    if neg_cap:
        operands += [neg_grad, neg_slot]
        specs += [
            pl.BlockSpec(neg_grad.shape, lambda i: (0, 0, 0)),
            pl.BlockSpec(neg_slot.shape, lambda i: (0, 0)),
        ]
    return call(
        functools.partial(collect_kernel, group=group, neg_cap=neg_cap),
        "collect_grads",
        2 * feature * slots * slot.size,
        2 * feature * (slots + slot.size),
        grid=(devices // group,),
        in_specs=specs,
        out_specs=pl.BlockSpec((group, height, LANES), lambda i: (i, 0, 0)),
        out_shape=jax.ShapeDtypeStruct((devices, height, LANES), BF16),
    )(*operands)


def collect_pool_kernel(src_ref, dst_ref, slot_ref, out_ref, *, group):
    segments, width = slot_ref.shape
    count = group * POOL
    rows = jnp.zeros((count, src_ref.shape[0]), F32)
    for segment in range(segments):
        grads = src_ref if segment < segments // 2 else dst_ref
        start = segment % (segments // 2) * width
        hot = one_hot(count, slot_ref[segment : segment + 1, :], pl.program_id(0) * count)
        rows = rows + dot(hot, grads[:, start : start + width], NT)
    for i in range(group):
        pack(out_ref, i, 0, rows[i * POOL : (i + 1) * POOL])


def collect_pool(src_grad, dst_grad, slot, devices):
    feature = src_grad.shape[0]
    group = 8
    slots = devices * POOL
    height = POOL * (round_up(feature, LANES) // LANES)
    whole = pl.BlockSpec(src_grad.shape, lambda i: (0, 0))
    return call(
        functools.partial(collect_pool_kernel, group=group),
        "collect_pool",
        2 * feature * slots * slot.size,
        2 * feature * (slots + slot.size),
        grid=(devices // group,),
        in_specs=[whole, whole, pl.BlockSpec(slot.shape, lambda i: (0, 0))],
        out_specs=pl.BlockSpec((group, height, LANES), lambda i: (i, 0, 0)),
        out_shape=jax.ShapeDtypeStruct((devices, height, LANES), BF16),
    )(src_grad, dst_grad, slot)


def add_kernel(*refs, rows, neg_cap, first):
    refs = list(refs)
    recv_ref, req_ref = refs[:2]
    refs = refs[2:]
    if neg_cap:
        neg_req_ref = refs.pop(0)
        neg_rows, neg_flat = refs[-2:]
    if not first:
        so_far_ref = refs.pop(0)
    out_ref, flat = refs[:2]
    devices = recv_ref.shape[0]
    feature = flat.shape[0]
    step = pl.program_id(0)

    @pl.when(step == 0)
    def _():
        start = recv_ref.shape[1] - feature
        for d in range(devices):
            flat[:, d * LANES : (d + 1) * LANES] = recv_ref[d, start:]
        if neg_cap:
            for d in range(devices):
                unpack(recv_ref, d, 0, neg_cap, neg_rows, d * neg_cap)
            neg_flat[...] = neg_rows[...].astype(F32).T[:feature].astype(BF16)

    base = step * rows
    row = jnp.concatenate([req_ref[d : d + 1, :] for d in range(devices)], axis=1)
    total = dot(flat[...], one_hot(rows, row, base), NT)
    if neg_cap:
        row = jnp.concatenate([neg_req_ref[d : d + 1, :neg_cap] for d in range(devices)], axis=1)
        total = total + dot(neg_flat[...], one_hot(rows, row, base), NT)
    if not first:
        total = total + so_far_ref[...]
    out_ref[...] = total


def add_rows(recv, requests, so_far, feature, rows_dev, neg_requests=None, neg_cap=0):
    devices = recv.shape[0]
    rows = 512 if devices * LANES <= 4096 else 128
    slots = devices * LANES
    full = round_up(feature, LANES)
    whole_req = pl.BlockSpec((devices, LANES), lambda i: (0, 0))
    rows_spec = pl.BlockSpec((feature, rows), lambda i: (0, i))
    operands = [recv, requests]
    specs = [pl.BlockSpec(recv.shape, lambda i: (0, 0, 0)), whole_req]
    scratch = [pltpu.VMEM((feature, slots), BF16)]
    if neg_cap:
        operands.append(neg_requests)
        specs.append(whole_req)
        scratch += [
            pltpu.VMEM((devices * neg_cap, full), BF16),
            pltpu.VMEM((feature, devices * neg_cap), BF16),
        ]
    if so_far is not None:
        operands.append(so_far)
        specs.append(rows_spec)
    return call(
        functools.partial(add_kernel, rows=rows, neg_cap=neg_cap, first=so_far is None),
        "add_grads",
        2 * feature * slots * rows_dev,
        2 * feature * slots + 8 * feature * rows_dev,
        grid=(rows_dev // rows,),
        in_specs=specs,
        out_specs=rows_spec,
        out_shape=jax.ShapeDtypeStruct((feature, rows_dev), F32),
        scratch_shapes=scratch,
    )(*operands)


def add_pool_kernel(recv_ref, req_ref, out_ref, packed, flat, *, rows):
    feature = flat.shape[0]
    count = packed.shape[0]
    per_relay = count // POOL
    step = pl.program_id(0)

    @pl.when(step == 0)
    def _():
        for relay in range(recv_ref.shape[0] // per_relay):
            for d in range(per_relay):
                unpack(recv_ref, relay * per_relay + d, 0, POOL, packed, d * POOL)
            flat[:, relay * count : (relay + 1) * count] = (
                packed[...].astype(F32).T[:feature].astype(BF16)
            )

    out_ref[...] = dot(flat[...], one_hot(rows, req_ref[...], step * rows), NT)


def add_pool(recv, requests, devices, feature, rows_dev):
    rows = 512
    full = round_up(feature, LANES)
    return call(
        functools.partial(add_pool_kernel, rows=rows),
        "add_pool",
        2 * feature * requests.size * rows_dev,
        2 * feature * requests.size + 4 * feature * rows_dev,
        grid=(rows_dev // rows,),
        in_specs=[
            pl.BlockSpec(recv.shape, lambda i: (0, 0, 0)),
            pl.BlockSpec((1, requests.size), lambda i: (0, 0)),
        ],
        out_specs=pl.BlockSpec((feature, rows), lambda i: (0, i)),
        out_shape=jax.ShapeDtypeStruct((feature, rows_dev), F32),
        scratch_shapes=[
            pltpu.VMEM((devices * POOL, full), BF16),
            pltpu.VMEM((feature, requests.size), BF16),
        ],
    )(recv, requests.reshape(1, -1))


def exchange(value):
    return lax.all_to_all(value, ("shard", "grp"), split_axis=0, concat_axis=0, tiled=True)


def swap(value, bit):
    sharers = lax.axis_size("grp")
    return lax.ppermute(value, "grp", [(i, i ^ bit) for i in range(sharers)])


def sharer_order(sharers):
    order, bit = [0], sharers // 2
    while bit:
        order += [k ^ bit for k in order]
        bit //= 2
    return order


def share_out(value):
    bit = lax.axis_size("grp") // 2
    while bit:
        value = jnp.concatenate([value, swap(value, bit)])
        bit //= 2
    return value


def add_up(value, sent=None):
    sharers = lax.axis_size("grp")
    bit = 1
    while bit < sharers:
        half = value.shape[0] // 2
        away = value[half:]
        if bit > 1 and sent is not None:
            away = away.astype(sent)
        value = value[:half] + swap(away, bit).astype(value.dtype)
        bit *= 2
    return value


def pad_lanes(value, width, fill):
    return jnp.pad(value, ((0, 0), (0, width - value.shape[1])), constant_values=fill)


def body(entity_table, rel_diag, src_ids, dst_ids, rel_ids, neg_ids):
    rows_dev, feature = entity_table.shape
    sharers = lax.axis_size("grp")
    devices = lax.axis_size("shard") * sharers
    spans, neg_count = neg_ids.shape
    edge_count = src_ids.shape[0]
    block_len = edge_count // spans
    edge_cap = 4 * edge_count // devices
    chunks = round_up(edge_cap, LANES) // LANES
    part_width = neg_count // sharers
    neg_cap = round_up(2 * spans * part_width // devices, 16)
    width = round_up(block_len, 512)
    part = round_up(part_width, LANES)
    me = lax.axis_index("grp")

    table = entity_table.T.astype(BF16)
    relations = rel_diag.T
    own_ids = lax.dynamic_slice_in_dim(neg_ids, me * part_width, part_width, 1)
    ends = jnp.concatenate(
        [src_ids.reshape(spans, block_len), dst_ids.reshape(spans, block_len)]
    )
    message, *slots = make_slots(
        pad_lanes(ends, width, -1),
        pad_lanes(own_ids, part, -1),
        rows_dev,
        devices,
        sharers,
        chunks,
        neg_cap,
    )
    neg_slot = slots[-1]
    rel_rows = pad_lanes(rel_ids.reshape(spans, block_len), width, -1)
    asked = exchange(message)
    direct = [asked[:, c * LANES : (c + 1) * LANES] for c in range(chunks)]
    neg_asked = asked[:, -LANES:]

    def chunked():
        back = [exchange(gather(table, direct[0], neg_asked, neg_cap))]
        back += [exchange(gather(table, direct[c])) for c in range(1, chunks)]
        negatives = share_out(spread_neg(back[0], neg_slot, neg_cap, feature)[None])
        rows = None
        for c in range(chunks):
            rows = spread(back[c], slots[c], rows, feature)
        src_grad, dst_grad, neg_grad = edges(rows, rel_rows, relations, negatives)
        grad = None
        for c in range(1, chunks):
            sent = exchange(collect(src_grad, dst_grad, slots[c], devices))
            grad = add_rows(sent, direct[c], grad, feature, rows_dev)
        neg_sum = add_up(neg_grad, BF16)[0]
        sent = exchange(
            collect(src_grad, dst_grad, slots[0], devices, neg_sum, neg_slot, neg_cap)
        )
        return add_rows(sent, direct[0], grad, feature, rows_dev, neg_asked, neg_cap)

    def pooled():
        start = chunks * LANES
        listed = asked[:, start : start + sharers * POOL].reshape(devices, sharers, POOL)
        listed = listed.transpose(1, 0, 2).reshape(sharers, devices * POOL) - me * rows_dev
        listed = listed[me ^ jnp.array(sharer_order(sharers), jnp.int32)]
        back = exchange(gather(table, direct[0], neg_asked, neg_cap))
        held = gather_pool(table, listed, devices)
        relayed = add_up(held.reshape(sharers, devices, *held.shape[1:]))[0]
        negatives = share_out(spread_neg(back, neg_slot, neg_cap, feature)[None])
        rows = spread(back, slots[0], None, feature)
        rows = spread(exchange(relayed), slots[chunks], rows, feature, True)
        src_grad, dst_grad, neg_grad = edges(rows, rel_rows, relations, negatives)
        pool = share_out(exchange(collect_pool(src_grad, dst_grad, slots[chunks], devices)))
        neg_sum = add_up(neg_grad, BF16)[0]
        sent = exchange(
            collect(src_grad, dst_grad, slots[0], devices, neg_sum, neg_slot, neg_cap)
        )
        grad = add_pool(pool, listed, devices, feature, rows_dev)
        return add_rows(sent, direct[0], grad, feature, rows_dev, neg_asked, neg_cap)

    if chunks == 1:
        return chunked().T
    fits = jnp.max(neg_asked[:, -1]) < 0
    return lax.cond(fits, pooled, chunked).T


def solution(mesh):
    placed = (
        P(("shard", "grp"), None),
        P(),
        P(("shard", "grp")),
        P(("shard", "grp")),
        P(("shard", "grp")),
        P("shard", None),
    )
    return jax.shard_map(
        body, mesh=mesh, in_specs=placed, out_specs=P(("shard", "grp"), None), check_vma=False
    )
```

```python
import functools

import jax
import jax.numpy as jnp
from jax import lax
from jax.experimental import pallas as pl
from jax.experimental.pallas import tpu as pltpu
from jax.sharding import PartitionSpec as P

LANES = 128
POOL = 48
VMEM_BYTES = 56 << 20
F32 = jnp.float32
BF16 = jnp.bfloat16
NN = (((1,), (0,)), ((), ()))
NT = (((1,), (1,)), ((), ()))
TN = (((0,), (0,)), ((), ()))


def round_up(value, unit):
    return -(-value // unit) * unit


def dot(left, right, dims):
    return lax.dot_general(left, right, dims, preferred_element_type=F32)


def one_hot(rows, row, base=0):
    places = lax.broadcasted_iota(jnp.int32, (rows, row.shape[1]), 0) + base
    return jnp.where(places == row, 1.0, 0.0).astype(BF16)


def call(kernel, name, flops, nbytes, **kwargs):
    return pl.pallas_call(
        kernel,
        name=name,
        compiler_params=pltpu.CompilerParams(vmem_limit_bytes=VMEM_BYTES),
        cost_estimate=pl.CostEstimate(flops=flops, bytes_accessed=nbytes, transcendentals=0),
        **kwargs,
    )


def ranks(members, mixer):
    groups = members[0].shape[0]
    both = dot(jnp.concatenate(members, axis=0).astype(BF16), mixer, NN)
    taken = jnp.zeros((groups, LANES), F32)
    found = []
    for i, member in enumerate(members):
        chunk = both[i * groups : (i + 1) * groups]
        found.append(jnp.sum((chunk[:, :LANES] + taken) * member, axis=0, keepdims=True))
        taken = taken + chunk[:, LANES:]
    return [rank.astype(jnp.int32) for rank in found], taken


def fill(members, codes, places, count):
    groups = members[0].shape[0]
    high = [m * (c // LANES).astype(F32) for m, c in zip(members, codes)]
    low = [m * (c % LANES).astype(F32) for m, c in zip(members, codes)]
    left = jnp.concatenate(
        [jnp.concatenate(high, axis=1), jnp.concatenate(low, axis=1)], axis=0
    ).astype(BF16)
    sums = dot(left, one_hot(count, jnp.concatenate(places, axis=1)), NT)
    return (LANES * sums[:groups] + sums[groups:]).astype(jnp.int32) - 1


def slots_kernel(ends_ref, own_ref, *refs, rows_dev, devices, sharers, chunks, neg_cap):
    msg_ref = refs[0]
    slot_refs = refs[1 : 1 + chunks]
    pool_ref = refs[1 + chunks] if chunks > 1 else None
    neg_ref = refs[-1]
    row = lax.broadcasted_iota(jnp.int32, (LANES, 2 * LANES), 0)
    lane = lax.broadcasted_iota(jnp.int32, (LANES, 2 * LANES), 1)
    mixer = jnp.where(row < lane, 1.0, 0.0).astype(BF16)
    owners = lax.broadcasted_iota(jnp.int32, (devices, LANES), 0)

    def prepare(ids_ref):
        where, holder, codes, members = [], [], [], []
        for segment in range(ids_ref.shape[0]):
            for start in range(0, ids_ref.shape[1], LANES):
                ids = ids_ref[segment : segment + 1, start : start + LANES]
                owner = jnp.where(ids >= 0, ids // rows_dev, -1)
                where.append((slice(segment, segment + 1), slice(start, start + LANES)))
                holder.append(owner)
                codes.append(jnp.where(ids >= 0, ids - owner * rows_dev + 1, 0))
                members.append(jnp.where(owners == owner, 1.0, 0.0))
        found, _ = ranks(members, mixer)
        return where, holder, codes, members, found

    where, holder, codes, members, found = prepare(ends_ref)
    for chunk in range(chunks):
        places = []
        for at, owner, rank in zip(where, holder, found):
            place = rank - chunk * LANES
            place = jnp.where((owner >= 0) & (place >= 0) & (place < LANES), place, -1)
            slot_refs[chunk][at] = jnp.where(place >= 0, owner * LANES + place, -1)
            places.append(place)
        msg_ref[:, chunk * LANES : (chunk + 1) * LANES] = fill(members, codes, places, LANES)
    offset = chunks * LANES
    flag = jnp.full((1, 1), -1, jnp.int32)
    if chunks > 1:
        shards = devices // sharers
        room = sharers * POOL
        shard_rows = lax.broadcasted_iota(jnp.int32, (shards, LANES), 0)
        spilled, spill_codes = [], []
        for owner, code, rank in zip(holder, codes, found):
            shard = jnp.where(rank >= LANES, owner // sharers, -1)
            spilled.append(jnp.where(shard_rows == shard, 1.0, 0.0))
            spill_codes.append(code + (owner % sharers) * rows_dev)
        pooled, taken = ranks(spilled, mixer)
        places = []
        for at, owner, rank, place in zip(where, holder, found, pooled):
            inside = (owner >= 0) & (rank >= LANES) & (place < room)
            pool_ref[at] = jnp.where(inside, owner // sharers * room + place, -1)
            places.append(jnp.where(inside, place, -1))
        listed = fill(spilled, spill_codes, places, 2 * LANES)
        for shard in range(shards):
            msg_ref[shard * sharers : (shard + 1) * sharers, offset : offset + 2 * LANES] = (
                jnp.broadcast_to(listed[shard : shard + 1], (sharers, 2 * LANES))
            )
        offset += 2 * LANES
        most = jnp.max(jnp.max(taken, axis=1, keepdims=True), axis=0, keepdims=True)
        flag = jnp.where(most > room, 1, -1)

    where, holder, codes, members, found = prepare(own_ref)
    for at, owner, rank in zip(where, holder, found):
        neg_ref[at] = jnp.where(owner >= 0, owner * neg_cap + rank, -1)
    places = [jnp.where(owner >= 0, rank, -1) for owner, rank in zip(holder, found)]
    listed = fill(members, codes, places, LANES)
    lanes = lax.broadcasted_iota(jnp.int32, listed.shape, 1)
    msg_ref[:, offset:] = jnp.where(lanes == LANES - 1, flag, listed)


def make_slots(ends, own, rows_dev, devices, sharers, chunks, neg_cap):
    pooled = chunks > 1
    width = (chunks + 1 + 2 * pooled) * LANES
    return call(
        functools.partial(
            slots_kernel,
            rows_dev=rows_dev,
            devices=devices,
            sharers=sharers,
            chunks=chunks,
            neg_cap=neg_cap,
        ),
        "slots",
        16 * devices * LANES * ends.size,
        8 * ends.size,
        out_shape=[jax.ShapeDtypeStruct((devices, width), jnp.int32)]
        + [jax.ShapeDtypeStruct(ends.shape, jnp.int32)] * (chunks + pooled)
        + [jax.ShapeDtypeStruct(own.shape, jnp.int32)],
    )(ends, own)


def pack(out_ref, at, start, rows):
    count, feature = rows.shape
    full = round_up(feature, LANES)
    rows = jnp.concatenate([rows, jnp.zeros((count, full - feature), rows.dtype)], axis=1)
    for piece in range(full // LANES):
        out_ref[at, start + piece * count : start + (piece + 1) * count, :] = rows[
            :, piece * LANES : (piece + 1) * LANES
        ].astype(out_ref.dtype)


def unpack(in_ref, at, start, count, flat_ref, to):
    for piece in range(flat_ref.shape[1] // LANES):
        flat_ref[to : to + count, piece * LANES : (piece + 1) * LANES] = in_ref[
            at, start + piece * count : start + (piece + 1) * count, :
        ]


def gather_kernel(table_ref, *refs, group, neg_cap):
    feature, rows_dev = table_ref.shape
    first = pl.program_id(0) * group
    req_ref, out_ref = refs[0], refs[-1]
    row = [req_ref[pl.ds(first + i, 1), :] for i in range(group)]
    if neg_cap:
        row += [refs[1][pl.ds(first + i, 1), :neg_cap] for i in range(group)]
    rows = dot(table_ref[...], one_hot(rows_dev, jnp.concatenate(row, axis=1)), NN)
    start = out_ref.shape[1] - feature
    for i in range(group):
        out_ref[i, start:] = rows[:, i * LANES : (i + 1) * LANES].astype(BF16)
    if neg_cap:
        neg = rows[:, group * LANES :].T
        for i in range(group):
            pack(out_ref, i, 0, neg[i * neg_cap : (i + 1) * neg_cap])


def gather(table, requests, neg_requests=None, neg_cap=0):
    feature, rows_dev = table.shape
    devices = requests.shape[0]
    group = 4
    height = feature + neg_cap * (round_up(feature, LANES) // LANES)
    slots = devices * (LANES + neg_cap)
    whole = pl.BlockSpec((devices, LANES), lambda i: (0, 0))
    return call(
        functools.partial(gather_kernel, group=group, neg_cap=neg_cap),
        "gather_rows",
        2 * feature * rows_dev * slots,
        2 * feature * (rows_dev + slots),
        grid=(devices // group,),
        in_specs=[pl.BlockSpec((feature, rows_dev), lambda i: (0, 0)), whole]
        + ([whole] if neg_cap else []),
        out_specs=pl.BlockSpec((group, height, LANES), lambda i: (i, 0, 0)),
        out_shape=jax.ShapeDtypeStruct((devices, height, LANES), BF16),
    )(table, requests, *([neg_requests] if neg_cap else []))


def gather_pool_kernel(table_ref, req_ref, out_ref, *, group):
    rows_dev = table_ref.shape[1]
    row = req_ref[...].reshape(1, group * POOL)
    rows = dot(table_ref[...], one_hot(rows_dev, row), NN).T
    for i in range(group):
        pack(out_ref, i, 0, rows[i * POOL : (i + 1) * POOL])


def gather_pool(table, requests, devices):
    feature, rows_dev = table.shape
    group = 8
    steps = devices // group
    height = POOL * (round_up(feature, LANES) // LANES)
    return call(
        functools.partial(gather_pool_kernel, group=group),
        "gather_pool",
        2 * feature * rows_dev * requests.size,
        2 * feature * (rows_dev + requests.size),
        grid=(steps,),
        in_specs=[
            pl.BlockSpec((feature, rows_dev), lambda i: (0, 0)),
            pl.BlockSpec((1, 1, group * POOL), lambda i: (i, 0, 0)),
        ],
        out_specs=pl.BlockSpec((group, height, LANES), lambda i: (i, 0, 0)),
        out_shape=jax.ShapeDtypeStruct((devices, height, LANES), BF16),
    )(table, requests.reshape(steps, 1, group * POOL))


def spread_neg_kernel(back_ref, slot_ref, out_ref, flat, *, cap):
    parts = slot_ref.shape[0]
    feature = out_ref.shape[-1]
    devices = back_ref.shape[0]
    for d in range(devices):
        unpack(back_ref, d, 0, cap, flat, d * cap)
    for part in range(parts):
        hot = one_hot(devices * cap, slot_ref[part : part + 1, :])
        out_ref[part] = dot(hot, flat[...], TN)[:, :feature].astype(BF16)


def spread_neg(back, slot, cap, feature):
    devices = back.shape[0]
    parts, width = slot.shape
    full = round_up(feature, LANES)
    height = cap * full // LANES
    return call(
        functools.partial(spread_neg_kernel, cap=cap),
        "spread_negatives",
        2 * devices * cap * full * slot.size,
        2 * devices * cap * full,
        grid=(1,),
        in_specs=[
            pl.BlockSpec((devices, height, LANES), lambda i: (0, 0, 0)),
            pl.BlockSpec(slot.shape, lambda i: (0, 0)),
        ],
        out_specs=pl.BlockSpec((parts, width, feature), lambda i: (0, 0, 0)),
        out_shape=jax.ShapeDtypeStruct((parts, width, feature), BF16),
        scratch_shapes=[pltpu.VMEM((devices * cap, full), BF16)],
    )(back, slot)


def spread_kernel(*refs, first, pooled):
    back_ref, slot_ref = refs[:2]
    so_far_ref = None if first else refs[2]
    out_ref, flat = refs[2 + (not first) :][:2]
    devices = back_ref.shape[0]
    feature = flat.shape[0]

    @pl.when(pl.program_id(0) == 0)
    def _():
        if pooled:
            for d in range(devices):
                unpack(back_ref, d, 0, POOL, refs[-1], d * POOL)
            flat[...] = refs[-1][...].astype(F32).T[:feature].astype(BF16)
        else:
            start = back_ref.shape[1] - feature
            for d in range(devices):
                flat[:, d * LANES : (d + 1) * LANES] = back_ref[d, start:]

    row = slot_ref[...].reshape(1, slot_ref.shape[-1])
    rows = dot(flat[...], one_hot(flat.shape[1], row), NN)
    if not first:
        rows = rows + so_far_ref[...].astype(F32)
    out_ref[...] = rows.astype(BF16)


def spread(back, slot, so_far, feature, pooled=False):
    devices = back.shape[0]
    segments, width = slot.shape
    slots = devices * (POOL if pooled else LANES)
    tile = 512 if slots <= 4096 else 128
    steps = width // tile
    rows_spec = pl.BlockSpec((feature, tile), lambda i: (0, i))
    extra = [] if so_far is None else [so_far]
    scratch = [pltpu.VMEM((feature, slots), BF16)]
    if pooled:
        scratch.append(pltpu.VMEM((slots, round_up(feature, LANES)), BF16))
    return call(
        functools.partial(spread_kernel, first=so_far is None, pooled=pooled),
        "spread_pool" if pooled else "spread_rows",
        2 * feature * slots * slot.size,
        2 * feature * (slots + slot.size),
        grid=(segments * steps,),
        in_specs=[
            pl.BlockSpec(back.shape, lambda i: (0, 0, 0)),
            pl.BlockSpec((1, 1, tile), lambda i: (i // steps, 0, i % steps)),
        ]
        + [rows_spec] * len(extra),
        out_specs=rows_spec,
        out_shape=jax.ShapeDtypeStruct((feature, slot.size), BF16),
        scratch_shapes=scratch,
    )(back, slot.reshape(segments, 1, width), *extra)


def edges_kernel(*refs, parts):
    src_ref, dst_ref, rel_ids_ref, rel_ref = refs[:4]
    neg_refs = refs[4 : 4 + parts]
    src_grad_ref, dst_grad_ref = refs[4 + parts : 6 + parts]
    neg_grad_refs = refs[6 + parts : 6 + 2 * parts]
    negatives, turned, sums = refs[6 + 2 * parts :]
    step = pl.program_id(1)
    part = neg_refs[0].shape[1]

    @pl.when(step == 0)
    def _():
        for k in range(parts):
            negatives[k * part : (k + 1) * part] = neg_refs[k][0]
        turned[...] = negatives[...].astype(F32).T.astype(BF16)

    hot = one_hot(rel_ref.shape[1], rel_ids_ref[...].reshape(1, rel_ids_ref.shape[-1]))
    table = rel_ref[...]
    relation = jnp.zeros(src_ref.shape, F32)
    for _ in range(3):
        piece = table.astype(BF16)
        relation = relation + dot(piece, hot, NN)
        table = table - piece.astype(F32)
    source = src_ref[...].astype(F32)
    target = dst_ref[...].astype(F32)
    product = source * relation
    positive = jnp.sum(product * target, axis=0, keepdims=True)
    pos_weight = -jax.nn.sigmoid(-positive)
    query = product.astype(BF16)
    weight = jax.nn.sigmoid(dot(negatives[...], query, NN)).astype(BF16)
    gathered = dot(turned[...], weight, NN)
    src_grad_ref[...] = (relation * (pos_weight * target + gathered)).astype(BF16)
    dst_grad_ref[...] = (pos_weight * product).astype(BF16)
    neg_grad = dot(weight, query, NT)

    @pl.when(step == 0)
    def _():
        sums[...] = neg_grad

    @pl.when(step != 0)
    def _():
        sums[...] += neg_grad

    @pl.when(step == pl.num_programs(1) - 1)
    def _():
        for k in range(parts):
            neg_grad_refs[k][0] = sums[k * part : (k + 1) * part].astype(BF16)


def edges(rows, rel_ids, relations, negatives):
    feature, endpoints = rows.shape
    parts = len(negatives)
    spans, part, _ = negatives[0].shape
    width = rel_ids.shape[1]
    tile = 512
    steps = width // tile
    blocks = spans * steps
    edge_spec = pl.BlockSpec((feature, tile), lambda b, i: (0, b * steps + i))
    neg_spec = pl.BlockSpec((1, part, feature), lambda b, i: (b, 0, 0))
    src_grad, dst_grad, *neg_grads = call(
        functools.partial(edges_kernel, parts=parts),
        "edges",
        6 * feature * parts * part * spans * width,
        4 * (rows.size + parts * negatives[0].size),
        grid=(spans, steps),
        in_specs=[
            edge_spec,
            pl.BlockSpec((feature, tile), lambda b, i: (0, blocks + b * steps + i)),
            pl.BlockSpec((1, 1, tile), lambda b, i: (b, 0, i)),
            pl.BlockSpec(relations.shape, lambda b, i: (0, 0)),
        ]
        + [neg_spec] * parts,
        out_specs=[edge_spec, edge_spec] + [neg_spec] * parts,
        out_shape=[jax.ShapeDtypeStruct((feature, endpoints // 2), BF16)] * 2
        + [jax.ShapeDtypeStruct((spans, part, feature), BF16)] * parts,
        scratch_shapes=[
            pltpu.VMEM((parts * part, feature), BF16),
            pltpu.VMEM((feature, parts * part), BF16),
            pltpu.VMEM((parts * part, feature), F32),
        ],
    )(rows, rows, rel_ids.reshape(spans, 1, width), relations, *negatives)
    return src_grad, dst_grad, neg_grads


def collect_kernel(src_ref, dst_ref, slot_ref, out_ref, *, group):
    segments, width = slot_ref.shape
    feature = src_ref.shape[0]
    step = pl.program_id(0)
    total = jnp.zeros((feature, group * LANES), F32)
    for segment in range(segments):
        grads = src_ref if segment < segments // 2 else dst_ref
        start = segment % (segments // 2) * width
        hot = one_hot(group * LANES, slot_ref[segment : segment + 1, :], step * group * LANES)
        total = total + dot(grads[:, start : start + width], hot, NT)
    total = total.astype(BF16)
    first = out_ref.shape[1] - feature
    for i in range(group):
        out_ref[i, first:] = total[:, i * LANES : (i + 1) * LANES]


def collect(src_grad, dst_grad, slot, devices, neg_cap=0):
    feature = src_grad.shape[0]
    group = 4
    slots = devices * LANES
    height = feature + neg_cap * (round_up(feature, LANES) // LANES)
    whole = pl.BlockSpec(src_grad.shape, lambda i: (0, 0))
    return call(
        functools.partial(collect_kernel, group=group),
        "collect_grads",
        2 * feature * slots * slot.size,
        2 * feature * (slots + slot.size),
        grid=(devices // group,),
        in_specs=[whole, whole, pl.BlockSpec(slot.shape, lambda i: (0, 0))],
        out_specs=pl.BlockSpec((group, height, LANES), lambda i: (i, 0, 0)),
        out_shape=jax.ShapeDtypeStruct((devices, height, LANES), BF16),
    )(src_grad, dst_grad, slot)


def collect_neg_kernel(sent_ref, slot_ref, *refs, group, cap):
    grad_refs, out_ref, sums = refs[:-2], refs[-2], refs[-1]
    step = pl.program_id(0)

    @pl.when(step == 0)
    def _():
        total = grad_refs[0][...].astype(F32)
        for grad_ref in grad_refs[1:]:
            total = total + grad_ref[...].astype(F32)
        sums[...] = total.astype(BF16)

    rows = jnp.zeros((group * cap, sums.shape[-1]), F32)
    for part in range(slot_ref.shape[0]):
        hot = one_hot(group * cap, slot_ref[part : part + 1, :], step * group * cap)
        rows = rows + dot(hot, sums[part], NN)
    for i in range(group):
        pack(out_ref, i, 0, rows[i * cap : (i + 1) * cap])


def collect_neg(sent, slot, grads, cap):
    devices = sent.shape[0]
    feature = grads[0].shape[-1]
    group = 16
    height = cap * (round_up(feature, LANES) // LANES)
    return call(
        functools.partial(collect_neg_kernel, group=group, cap=cap),
        "collect_negatives",
        2 * devices * cap * feature * slot.size,
        4 * len(grads) * grads[0].size,
        grid=(devices // group,),
        in_specs=[
            pl.BlockSpec(memory_space=pl.ANY),
            pl.BlockSpec(slot.shape, lambda i: (0, 0)),
        ]
        + [pl.BlockSpec(grads[0].shape, lambda i: (0, 0, 0))] * len(grads),
        out_specs=pl.BlockSpec((group, height, LANES), lambda i: (i, 0, 0)),
        out_shape=jax.ShapeDtypeStruct(sent.shape, BF16),
        scratch_shapes=[pltpu.VMEM(grads[0].shape, BF16)],
        input_output_aliases={0: 0},
    )(sent, slot, *grads)


def collect_pool_kernel(src_ref, dst_ref, slot_ref, out_ref, *, group):
    segments, width = slot_ref.shape
    count = group * POOL
    rows = jnp.zeros((count, src_ref.shape[0]), F32)
    for segment in range(segments):
        grads = src_ref if segment < segments // 2 else dst_ref
        start = segment % (segments // 2) * width
        hot = one_hot(count, slot_ref[segment : segment + 1, :], pl.program_id(0) * count)
        rows = rows + dot(hot, grads[:, start : start + width], NT)
    for i in range(group):
        pack(out_ref, i, 0, rows[i * POOL : (i + 1) * POOL])


def collect_pool(src_grad, dst_grad, slot, devices):
    feature = src_grad.shape[0]
    group = 8
    slots = devices * POOL
    height = POOL * (round_up(feature, LANES) // LANES)
    whole = pl.BlockSpec(src_grad.shape, lambda i: (0, 0))
    return call(
        functools.partial(collect_pool_kernel, group=group),
        "collect_pool",
        2 * feature * slots * slot.size,
        2 * feature * (slots + slot.size),
        grid=(devices // group,),
        in_specs=[whole, whole, pl.BlockSpec(slot.shape, lambda i: (0, 0))],
        out_specs=pl.BlockSpec((group, height, LANES), lambda i: (i, 0, 0)),
        out_shape=jax.ShapeDtypeStruct((devices, height, LANES), BF16),
    )(src_grad, dst_grad, slot)


def add_kernel(*refs, rows, neg_cap, first):
    refs = list(refs)
    recv_ref, req_ref = refs[:2]
    refs = refs[2:]
    if neg_cap:
        neg_req_ref = refs.pop(0)
        neg_rows, neg_flat = refs[-2:]
    if not first:
        so_far_ref = refs.pop(0)
    out_ref, flat = refs[:2]
    devices = recv_ref.shape[0]
    feature = flat.shape[0]
    step = pl.program_id(0)

    @pl.when(step == 0)
    def _():
        start = recv_ref.shape[1] - feature
        for d in range(devices):
            flat[:, d * LANES : (d + 1) * LANES] = recv_ref[d, start:]
        if neg_cap:
            for d in range(devices):
                unpack(recv_ref, d, 0, neg_cap, neg_rows, d * neg_cap)
            neg_flat[...] = neg_rows[...].astype(F32).T[:feature].astype(BF16)

    base = step * rows
    row = jnp.concatenate([req_ref[d : d + 1, :] for d in range(devices)], axis=1)
    total = dot(flat[...], one_hot(rows, row, base), NT)
    if neg_cap:
        row = jnp.concatenate([neg_req_ref[d : d + 1, :neg_cap] for d in range(devices)], axis=1)
        total = total + dot(neg_flat[...], one_hot(rows, row, base), NT)
    if not first:
        total = total + so_far_ref[...]
    out_ref[...] = total


def add_rows(recv, requests, so_far, feature, rows_dev, neg_requests=None, neg_cap=0):
    devices = recv.shape[0]
    rows = 512 if devices * LANES <= 4096 else 128
    slots = devices * LANES
    full = round_up(feature, LANES)
    whole_req = pl.BlockSpec((devices, LANES), lambda i: (0, 0))
    rows_spec = pl.BlockSpec((feature, rows), lambda i: (0, i))
    operands = [recv, requests]
    specs = [pl.BlockSpec(recv.shape, lambda i: (0, 0, 0)), whole_req]
    scratch = [pltpu.VMEM((feature, slots), BF16)]
    if neg_cap:
        operands.append(neg_requests)
        specs.append(whole_req)
        scratch += [
            pltpu.VMEM((devices * neg_cap, full), BF16),
            pltpu.VMEM((feature, devices * neg_cap), BF16),
        ]
    if so_far is not None:
        operands.append(so_far)
        specs.append(rows_spec)
    return call(
        functools.partial(add_kernel, rows=rows, neg_cap=neg_cap, first=so_far is None),
        "add_grads",
        2 * feature * slots * rows_dev,
        2 * feature * slots + 8 * feature * rows_dev,
        grid=(rows_dev // rows,),
        in_specs=specs,
        out_specs=rows_spec,
        out_shape=jax.ShapeDtypeStruct((feature, rows_dev), F32),
        scratch_shapes=scratch,
    )(*operands)


def add_pool_kernel(*refs, rows, relays):
    recv_refs = refs[:relays]
    req_ref = refs[relays]
    so_far_ref = refs[relays + 1] if len(refs) == relays + 5 else None
    out_ref, packed, flat = refs[-3:]
    feature = flat.shape[0]
    count = packed.shape[0]
    step = pl.program_id(0)

    @pl.when(step == 0)
    def _():
        for relay in range(relays):
            for d in range(count // POOL):
                unpack(recv_refs[relay], d, 0, POOL, packed, d * POOL)
            flat[:, relay * count : (relay + 1) * count] = (
                packed[...].astype(F32).T[:feature].astype(BF16)
            )

    total = dot(flat[...], one_hot(rows, req_ref[...], step * rows), NT)
    if so_far_ref is not None:
        total = total + so_far_ref[...]
    out_ref[...] = total


def add_pool(recv, requests, so_far, feature, rows_dev):
    rows = 512
    devices, height, _ = recv[0].shape
    slots = len(recv) * devices * POOL
    rows_spec = pl.BlockSpec((feature, rows), lambda i: (0, i))
    extra = [] if so_far is None else [so_far]
    return call(
        functools.partial(add_pool_kernel, rows=rows, relays=len(recv)),
        "add_pool",
        2 * feature * slots * rows_dev,
        2 * feature * slots + 4 * feature * rows_dev,
        grid=(rows_dev // rows,),
        in_specs=[pl.BlockSpec(recv[0].shape, lambda i: (0, 0, 0))] * len(recv)
        + [pl.BlockSpec((1, slots), lambda i: (0, 0))]
        + [rows_spec] * len(extra),
        out_specs=rows_spec,
        out_shape=jax.ShapeDtypeStruct((feature, rows_dev), F32),
        scratch_shapes=[
            pltpu.VMEM((devices * POOL, round_up(feature, LANES)), BF16),
            pltpu.VMEM((feature, slots), BF16),
        ],
    )(*recv, requests.reshape(1, slots), *extra)


def exchange(value):
    return lax.all_to_all(value, ("shard", "grp"), split_axis=0, concat_axis=0, tiled=True)


def swap(value, bit):
    sharers = lax.axis_size("grp")
    return lax.ppermute(value, "grp", [(i, i ^ bit) for i in range(sharers)])


def share_out(value):
    return [value] + [swap(value, k) for k in range(1, lax.axis_size("grp"))]


def trade(blocks):
    return blocks[:1] + [swap(block, k) for k, block in enumerate(blocks) if k]


def pad_lanes(value, width, fill):
    return jnp.pad(value, ((0, 0), (0, width - value.shape[1])), constant_values=fill)


def body(entity_table, rel_diag, src_ids, dst_ids, rel_ids, neg_ids):
    rows_dev, feature = entity_table.shape
    sharers = lax.axis_size("grp")
    devices = lax.axis_size("shard") * sharers
    spans, neg_count = neg_ids.shape
    edge_count = src_ids.shape[0]
    block_len = edge_count // spans
    edge_cap = 4 * edge_count // devices
    chunks = round_up(edge_cap, LANES) // LANES
    part_width = neg_count // sharers
    neg_cap = round_up(2 * spans * part_width // devices, 16)
    width = round_up(block_len, 512)
    part = round_up(part_width, LANES)
    me = lax.axis_index("grp")

    table = entity_table.T.astype(BF16)
    relations = rel_diag.T
    own_ids = lax.dynamic_slice_in_dim(neg_ids, me * part_width, part_width, 1)
    ends = jnp.concatenate(
        [src_ids.reshape(spans, block_len), dst_ids.reshape(spans, block_len)]
    )
    message, *slots = make_slots(
        pad_lanes(ends, width, -1),
        pad_lanes(own_ids, part, -1),
        rows_dev,
        devices,
        sharers,
        chunks,
        neg_cap,
    )
    neg_slot = slots[-1]
    rel_rows = pad_lanes(rel_ids.reshape(spans, block_len), width, -1)
    asked = exchange(message)
    direct = [asked[:, c * LANES : (c + 1) * LANES] for c in range(chunks)]
    neg_asked = asked[:, -LANES:]

    def negatives_of(back):
        return share_out(spread_neg(back, neg_slot, neg_cap, feature))

    def direct_sent(src_grad, dst_grad, neg_grads):
        sent = collect(src_grad, dst_grad, slots[0], devices, neg_cap)
        return exchange(collect_neg(sent, neg_slot, trade(neg_grads), neg_cap))

    def chunked():
        back = [exchange(gather(table, direct[0], neg_asked, neg_cap))]
        back += [exchange(gather(table, direct[c])) for c in range(1, chunks)]
        negatives = negatives_of(back[0])
        rows = None
        for c in range(chunks):
            rows = spread(back[c], slots[c], rows, feature)
        src_grad, dst_grad, neg_grads = edges(rows, rel_rows, relations, negatives)
        grad = None
        for c in range(1, chunks):
            sent = exchange(collect(src_grad, dst_grad, slots[c], devices))
            grad = add_rows(sent, direct[c], grad, feature, rows_dev)
        sent = direct_sent(src_grad, dst_grad, neg_grads)
        return add_rows(sent, direct[0], grad, feature, rows_dev, neg_asked, neg_cap)

    def pooled():
        start = chunks * LANES
        listed = asked[:, start : start + sharers * POOL].reshape(devices, sharers, POOL)
        listed = listed.transpose(1, 0, 2).reshape(sharers, devices * POOL) - me * rows_dev
        listed = listed[me ^ jnp.arange(sharers, dtype=jnp.int32)]
        back = exchange(gather(table, direct[0], neg_asked, neg_cap))
        far = gather_pool(table, listed[2], devices) + swap(
            gather_pool(table, listed[3], devices), 1
        )
        far = swap(far, 2)
        near = gather_pool(table, listed[0], devices) + swap(
            gather_pool(table, listed[1], devices), 1
        )
        negatives = negatives_of(back)
        rows = spread(back, slots[0], None, feature)
        rows = spread(exchange(near + far), slots[chunks], rows, feature, True)
        src_grad, dst_grad, neg_grads = edges(rows, rel_rows, relations, negatives)
        near = exchange(collect_pool(src_grad, dst_grad, slots[chunks], devices))
        far = swap(near, 2)
        sent = direct_sent(src_grad, dst_grad, neg_grads)
        grad = add_pool([near, swap(near, 1)], listed[:2], None, feature, rows_dev)
        grad = add_pool([far, swap(far, 1)], listed[2:], grad, feature, rows_dev)
        return add_rows(sent, direct[0], grad, feature, rows_dev, neg_asked, neg_cap)

    if chunks == 1 or sharers != 4:
        return chunked().T
    fits = jnp.max(neg_asked[:, -1]) < 0
    return lax.cond(fits, pooled, chunked).T


def solution(mesh):
    placed = (
        P(("shard", "grp"), None),
        P(),
        P(("shard", "grp")),
        P(("shard", "grp")),
        P(("shard", "grp")),
        P("shard", None),
    )
    return jax.shard_map(
        body, mesh=mesh, in_specs=placed, out_specs=P(("shard", "grp"), None), check_vma=False
    )
```

```python
import functools

import jax
import jax.numpy as jnp
from jax import lax
from jax.experimental import pallas as pl
from jax.experimental.pallas import tpu as pltpu
from jax.sharding import PartitionSpec as P

LANES = 128
POOL = 80
RELAYS = 2
VMEM_BYTES = 56 << 20
F32 = jnp.float32
BF16 = jnp.bfloat16
NN = (((1,), (0,)), ((), ()))
NT = (((1,), (1,)), ((), ()))
TN = (((0,), (0,)), ((), ()))


def round_up(value, unit):
    return -(-value // unit) * unit


def dot(left, right, dims):
    return lax.dot_general(left, right, dims, preferred_element_type=F32)


def one_hot(rows, row, base=0):
    places = lax.broadcasted_iota(jnp.int32, (rows, row.shape[1]), 0) + base
    return jnp.where(places == row, 1.0, 0.0).astype(BF16)


def call(kernel, name, flops, nbytes, **kwargs):
    return pl.pallas_call(
        kernel,
        name=name,
        compiler_params=pltpu.CompilerParams(vmem_limit_bytes=VMEM_BYTES),
        cost_estimate=pl.CostEstimate(flops=flops, bytes_accessed=nbytes, transcendentals=0),
        **kwargs,
    )


def ranks(members, mixer):
    groups = members[0].shape[0]
    both = dot(jnp.concatenate(members, axis=0).astype(BF16), mixer, NN)
    taken = jnp.zeros((groups, LANES), F32)
    found = []
    for i, member in enumerate(members):
        chunk = both[i * groups : (i + 1) * groups]
        found.append(jnp.sum((chunk[:, :LANES] + taken) * member, axis=0, keepdims=True))
        taken = taken + chunk[:, LANES:]
    return [rank.astype(jnp.int32) for rank in found], taken


def fill(members, codes, places, count):
    groups = members[0].shape[0]
    high = [m * (c // LANES).astype(F32) for m, c in zip(members, codes)]
    low = [m * (c % LANES).astype(F32) for m, c in zip(members, codes)]
    left = jnp.concatenate(
        [jnp.concatenate(high, axis=1), jnp.concatenate(low, axis=1)], axis=0
    ).astype(BF16)
    sums = dot(left, one_hot(count, jnp.concatenate(places, axis=1)), NT)
    return (LANES * sums[:groups] + sums[groups:]).astype(jnp.int32) - 1


def slots_kernel(ends_ref, own_ref, *refs, rows_dev, devices, chunks, neg_cap):
    msg_ref = refs[0]
    slot_refs = refs[1 : 1 + chunks]
    pool_ref = refs[1 + chunks] if chunks > 1 else None
    neg_ref = refs[-1]
    row = lax.broadcasted_iota(jnp.int32, (LANES, 2 * LANES), 0)
    lane = lax.broadcasted_iota(jnp.int32, (LANES, 2 * LANES), 1)
    mixer = jnp.where(row < lane, 1.0, 0.0).astype(BF16)
    owners = lax.broadcasted_iota(jnp.int32, (devices, LANES), 0)

    def prepare(ids_ref):
        where, holder, codes, members = [], [], [], []
        for segment in range(ids_ref.shape[0]):
            for start in range(0, ids_ref.shape[1], LANES):
                ids = ids_ref[segment : segment + 1, start : start + LANES]
                owner = jnp.where(ids >= 0, ids // rows_dev, -1)
                where.append((slice(segment, segment + 1), slice(start, start + LANES)))
                holder.append(owner)
                codes.append(jnp.where(ids >= 0, ids - owner * rows_dev + 1, 0))
                members.append(jnp.where(owners == owner, 1.0, 0.0))
        found, _ = ranks(members, mixer)
        return where, holder, codes, members, found

    where, holder, codes, members, found = prepare(ends_ref)
    for chunk in range(chunks):
        places = []
        for at, owner, rank in zip(where, holder, found):
            place = rank - chunk * LANES
            place = jnp.where((owner >= 0) & (place >= 0) & (place < LANES), place, -1)
            slot_refs[chunk][at] = jnp.where(place >= 0, owner * LANES + place, -1)
            places.append(place)
        msg_ref[:, chunk * LANES : (chunk + 1) * LANES] = fill(members, codes, places, LANES)
    offset = chunks * LANES
    flag = jnp.full((1, 1), -1, jnp.int32)
    if chunks > 1:
        chips = devices // RELAYS
        room = RELAYS * POOL
        chip_rows = lax.broadcasted_iota(jnp.int32, (chips, LANES), 0)
        spilled, spill_codes = [], []
        for owner, code, rank in zip(holder, codes, found):
            chip = jnp.where(rank >= LANES, owner // RELAYS, -1)
            spilled.append(jnp.where(chip_rows == chip, 1.0, 0.0))
            spill_codes.append(code + (owner % RELAYS) * rows_dev)
        pooled, taken = ranks(spilled, mixer)
        places = []
        for at, owner, rank, place in zip(where, holder, found, pooled):
            inside = (owner >= 0) & (rank >= LANES) & (place < room)
            pool_ref[at] = jnp.where(inside, owner // RELAYS * room + place, -1)
            places.append(jnp.where(inside, place, -1))
        listed = fill(spilled, spill_codes, places, 2 * LANES)
        for chip in range(chips):
            msg_ref[chip * RELAYS : (chip + 1) * RELAYS, offset : offset + 2 * LANES] = (
                jnp.broadcast_to(listed[chip : chip + 1], (RELAYS, 2 * LANES))
            )
        offset += 2 * LANES
        most = jnp.max(jnp.max(taken, axis=1, keepdims=True), axis=0, keepdims=True)
        flag = jnp.where(most > room, 1, -1)

    where, holder, codes, members, found = prepare(own_ref)
    for at, owner, rank in zip(where, holder, found):
        neg_ref[at] = jnp.where(owner >= 0, owner * neg_cap + rank, -1)
    places = [jnp.where(owner >= 0, rank, -1) for owner, rank in zip(holder, found)]
    listed = fill(members, codes, places, LANES)
    lanes = lax.broadcasted_iota(jnp.int32, listed.shape, 1)
    msg_ref[:, offset:] = jnp.where(lanes == LANES - 1, flag, listed)


def make_slots(ends, own, rows_dev, devices, chunks, neg_cap):
    pooled = chunks > 1
    width = (chunks + 1 + 2 * pooled) * LANES
    return call(
        functools.partial(
            slots_kernel,
            rows_dev=rows_dev,
            devices=devices,
            chunks=chunks,
            neg_cap=neg_cap,
        ),
        "slots",
        16 * devices * LANES * ends.size,
        8 * ends.size,
        out_shape=[jax.ShapeDtypeStruct((devices, width), jnp.int32)]
        + [jax.ShapeDtypeStruct(ends.shape, jnp.int32)] * (chunks + pooled)
        + [jax.ShapeDtypeStruct(own.shape, jnp.int32)],
    )(ends, own)


def packed_height(count, feature):
    return feature // LANES * count + feature % LANES


def pack(out_ref, at, start, rows, tail):
    count, feature = rows.shape
    for piece in range(feature // LANES):
        out_ref[at, start + piece * count : start + (piece + 1) * count, :] = rows[
            :, piece * LANES : (piece + 1) * LANES
        ].astype(out_ref.dtype)
    tail = jnp.concatenate([tail, jnp.zeros((tail.shape[0], LANES - count), tail.dtype)], axis=1)
    end = start + packed_height(count, feature)
    out_ref[at, end - tail.shape[0] : end, :] = tail.astype(out_ref.dtype)


def pack_all(out_ref, start, count, rows, turned):
    feature = rows.shape[1]
    first = feature // LANES * LANES
    for i in range(out_ref.shape[0]):
        at = slice(i * count, (i + 1) * count)
        pack(out_ref, i, start, rows[at], turned[first:, at])


def unpack_all(in_ref, start, count, rows_ref, flat_ref):
    feature = flat_ref.shape[0]
    pieces = feature // LANES
    end = start + packed_height(count, feature)
    devices = in_ref.shape[0]
    for d in range(devices):
        for piece in range(pieces):
            rows_ref[d * count : (d + 1) * count, piece * LANES : (piece + 1) * LANES] = in_ref[
                d, start + piece * count : start + (piece + 1) * count, :
            ]
    tails = [
        in_ref[d, end - feature % LANES : end, :].astype(F32)[:, :count] for d in range(devices)
    ]
    flat_ref[: pieces * LANES] = rows_ref[...].astype(F32).T.astype(BF16)
    flat_ref[pieces * LANES :] = jnp.concatenate(tails, axis=1).astype(BF16)


def unpack_scratch(devices, count, feature):
    return [
        pltpu.VMEM((devices * count, feature // LANES * LANES), BF16),
        pltpu.VMEM((feature, devices * count), BF16),
    ]


def gather_kernel(table_ref, *refs, group, neg_cap):
    feature, rows_dev = table_ref.shape
    first = pl.program_id(0) * group
    req_ref, out_ref = refs[0], refs[-1]
    row = [req_ref[pl.ds(first + i, 1), :] for i in range(group)]
    if neg_cap:
        row += [refs[1][pl.ds(first + i, 1), :neg_cap] for i in range(group)]
    rows = dot(table_ref[...], one_hot(rows_dev, jnp.concatenate(row, axis=1)), NN)
    start = out_ref.shape[1] - feature
    for i in range(group):
        out_ref[i, start:] = rows[:, i * LANES : (i + 1) * LANES].astype(BF16)
    if neg_cap:
        neg = rows[:, group * LANES :]
        pack_all(out_ref, 0, neg_cap, neg.T, neg)


def gather(table, requests, neg_requests=None, neg_cap=0):
    feature, rows_dev = table.shape
    devices = requests.shape[0]
    group = 4
    height = feature + (packed_height(neg_cap, feature) if neg_cap else 0)
    slots = devices * (LANES + neg_cap)
    whole = pl.BlockSpec((devices, LANES), lambda i: (0, 0))
    return call(
        functools.partial(gather_kernel, group=group, neg_cap=neg_cap),
        "gather_rows",
        2 * feature * rows_dev * slots,
        2 * feature * (rows_dev + slots),
        grid=(devices // group,),
        in_specs=[pl.BlockSpec((feature, rows_dev), lambda i: (0, 0)), whole]
        + ([whole] if neg_cap else []),
        out_specs=pl.BlockSpec((group, height, LANES), lambda i: (i, 0, 0)),
        out_shape=jax.ShapeDtypeStruct((devices, height, LANES), BF16),
    )(table, requests, *([neg_requests] if neg_cap else []))


def gather_pool_kernel(table_ref, req_ref, out_ref, *, group):
    rows_dev = table_ref.shape[1]
    row = req_ref[...].reshape(1, group * POOL)
    rows = dot(table_ref[...], one_hot(rows_dev, row), NN)
    pack_all(out_ref, 0, POOL, rows.T, rows)


def gather_pool(table, requests, devices):
    feature, rows_dev = table.shape
    group = 8
    steps = devices // group
    height = packed_height(POOL, feature)
    return call(
        functools.partial(gather_pool_kernel, group=group),
        "gather_pool",
        2 * feature * rows_dev * requests.size,
        2 * feature * (rows_dev + requests.size),
        grid=(steps,),
        in_specs=[
            pl.BlockSpec((feature, rows_dev), lambda i: (0, 0)),
            pl.BlockSpec((1, 1, group * POOL), lambda i: (i, 0, 0)),
        ],
        out_specs=pl.BlockSpec((group, height, LANES), lambda i: (i, 0, 0)),
        out_shape=jax.ShapeDtypeStruct((devices, height, LANES), BF16),
    )(table, requests.reshape(steps, 1, group * POOL))


def spread_neg_kernel(back_ref, slot_ref, out_ref, rows, flat, *, cap):
    unpack_all(back_ref, 0, cap, rows, flat)
    for part in range(slot_ref.shape[0]):
        hot = one_hot(flat.shape[1], slot_ref[part : part + 1, :])
        out_ref[part] = dot(flat[...], hot, NN).T.astype(BF16)


def spread_neg(back, slot, cap, feature):
    devices = back.shape[0]
    parts, width = slot.shape
    height = packed_height(cap, feature)
    return call(
        functools.partial(spread_neg_kernel, cap=cap),
        "spread_negatives",
        2 * devices * cap * feature * slot.size,
        2 * devices * cap * feature,
        grid=(1,),
        in_specs=[
            pl.BlockSpec((devices, height, LANES), lambda i: (0, 0, 0)),
            pl.BlockSpec(slot.shape, lambda i: (0, 0)),
        ],
        out_specs=pl.BlockSpec((parts, width, feature), lambda i: (0, 0, 0)),
        out_shape=jax.ShapeDtypeStruct((parts, width, feature), BF16),
        scratch_shapes=unpack_scratch(devices, cap, feature),
    )(back, slot)


def spread_kernel(*refs, first, pooled):
    back_ref, slot_ref = refs[:2]
    so_far_ref = None if first else refs[2]
    out_ref, flat = refs[2 + (not first)], refs[-1]
    devices = back_ref.shape[0]
    feature = flat.shape[0]

    @pl.when(pl.program_id(0) == 0)
    def _():
        if pooled:
            unpack_all(back_ref, 0, POOL, refs[-2], flat)
        else:
            start = back_ref.shape[1] - feature
            for d in range(devices):
                flat[:, d * LANES : (d + 1) * LANES] = back_ref[d, start:]

    row = slot_ref[...].reshape(1, slot_ref.shape[-1])
    rows = dot(flat[...], one_hot(flat.shape[1], row), NN)
    if not first:
        rows = rows + so_far_ref[...].astype(F32)
    out_ref[...] = rows.astype(BF16)


def spread(back, slot, so_far, feature, pooled=False):
    devices = back.shape[0]
    segments, width = slot.shape
    slots = devices * (POOL if pooled else LANES)
    tile = 512 if slots <= 4096 else 128
    steps = width // tile
    rows_spec = pl.BlockSpec((feature, tile), lambda i: (0, i))
    extra = [] if so_far is None else [so_far]
    if pooled:
        scratch = unpack_scratch(devices, POOL, feature)
    else:
        scratch = [pltpu.VMEM((feature, slots), BF16)]
    return call(
        functools.partial(spread_kernel, first=so_far is None, pooled=pooled),
        "spread_pool" if pooled else "spread_rows",
        2 * feature * slots * slot.size,
        2 * feature * (slots + slot.size),
        grid=(segments * steps,),
        in_specs=[
            pl.BlockSpec(back.shape, lambda i: (0, 0, 0)),
            pl.BlockSpec((1, 1, tile), lambda i: (i // steps, 0, i % steps)),
        ]
        + [rows_spec] * len(extra),
        out_specs=rows_spec,
        out_shape=jax.ShapeDtypeStruct((feature, slot.size), BF16),
        scratch_shapes=scratch,
    )(back, slot.reshape(segments, 1, width), *extra)


def edges_kernel(*refs, parts):
    src_ref, dst_ref, rel_ids_ref, rel_ref = refs[:4]
    neg_refs = refs[4 : 4 + parts]
    src_grad_ref, dst_grad_ref = refs[4 + parts : 6 + parts]
    neg_grad_refs = refs[6 + parts : 6 + 2 * parts]
    negatives, turned, sums = refs[6 + 2 * parts :]
    step = pl.program_id(1)
    part = neg_refs[0].shape[1]

    @pl.when(step == 0)
    def _():
        for k in range(parts):
            negatives[k * part : (k + 1) * part] = neg_refs[k][0]
        turned[...] = negatives[...].astype(F32).T.astype(BF16)

    hot = one_hot(rel_ref.shape[1], rel_ids_ref[...].reshape(1, rel_ids_ref.shape[-1]))
    table = rel_ref[...]
    relation = jnp.zeros(src_ref.shape, F32)
    for _ in range(3):
        piece = table.astype(BF16)
        relation = relation + dot(piece, hot, NN)
        table = table - piece.astype(F32)
    source = src_ref[...].astype(F32)
    target = dst_ref[...].astype(F32)
    product = source * relation
    positive = jnp.sum(product * target, axis=0, keepdims=True)
    pos_weight = -jax.nn.sigmoid(-positive)
    query = product.astype(BF16)
    weight = jax.nn.sigmoid(dot(negatives[...], query, NN)).astype(BF16)
    gathered = dot(turned[...], weight, NN)
    src_grad_ref[...] = (relation * (pos_weight * target + gathered)).astype(BF16)
    dst_grad_ref[...] = (pos_weight * product).astype(BF16)
    neg_grad = dot(weight, query, NT)

    @pl.when(step == 0)
    def _():
        sums[...] = neg_grad

    @pl.when(step != 0)
    def _():
        sums[...] += neg_grad

    @pl.when(step == pl.num_programs(1) - 1)
    def _():
        for k in range(parts):
            neg_grad_refs[k][0] = sums[k * part : (k + 1) * part].astype(BF16)


def edges(rows, rel_ids, relations, negatives):
    feature, endpoints = rows.shape
    parts = len(negatives)
    spans, part, _ = negatives[0].shape
    width = rel_ids.shape[1]
    tile = 512
    steps = width // tile
    blocks = spans * steps
    edge_spec = pl.BlockSpec((feature, tile), lambda b, i: (0, b * steps + i))
    neg_spec = pl.BlockSpec((1, part, feature), lambda b, i: (b, 0, 0))
    src_grad, dst_grad, *neg_grads = call(
        functools.partial(edges_kernel, parts=parts),
        "edges",
        6 * feature * parts * part * spans * width,
        4 * (rows.size + parts * negatives[0].size),
        grid=(spans, steps),
        in_specs=[
            edge_spec,
            pl.BlockSpec((feature, tile), lambda b, i: (0, blocks + b * steps + i)),
            pl.BlockSpec((1, 1, tile), lambda b, i: (b, 0, i)),
            pl.BlockSpec(relations.shape, lambda b, i: (0, 0)),
        ]
        + [neg_spec] * parts,
        out_specs=[edge_spec, edge_spec] + [neg_spec] * parts,
        out_shape=[jax.ShapeDtypeStruct((feature, endpoints // 2), BF16)] * 2
        + [jax.ShapeDtypeStruct((spans, part, feature), BF16)] * parts,
        scratch_shapes=[
            pltpu.VMEM((parts * part, feature), BF16),
            pltpu.VMEM((feature, parts * part), BF16),
            pltpu.VMEM((parts * part, feature), F32),
        ],
    )(rows, rows, rel_ids.reshape(spans, 1, width), relations, *negatives)
    return src_grad, dst_grad, neg_grads


def collect_kernel(src_ref, dst_ref, slot_ref, out_ref, *, group):
    segments, width = slot_ref.shape
    feature = src_ref.shape[0]
    step = pl.program_id(0)
    total = jnp.zeros((feature, group * LANES), F32)
    for segment in range(segments):
        grads = src_ref if segment < segments // 2 else dst_ref
        start = segment % (segments // 2) * width
        hot = one_hot(group * LANES, slot_ref[segment : segment + 1, :], step * group * LANES)
        total = total + dot(grads[:, start : start + width], hot, NT)
    total = total.astype(BF16)
    first = out_ref.shape[1] - feature
    for i in range(group):
        out_ref[i, first:] = total[:, i * LANES : (i + 1) * LANES]


def collect(src_grad, dst_grad, slot, devices, neg_cap=0):
    feature = src_grad.shape[0]
    group = 4
    slots = devices * LANES
    height = feature + (packed_height(neg_cap, feature) if neg_cap else 0)
    whole = pl.BlockSpec(src_grad.shape, lambda i: (0, 0))
    return call(
        functools.partial(collect_kernel, group=group),
        "collect_grads",
        2 * feature * slots * slot.size,
        2 * feature * (slots + slot.size),
        grid=(devices // group,),
        in_specs=[whole, whole, pl.BlockSpec(slot.shape, lambda i: (0, 0))],
        out_specs=pl.BlockSpec((group, height, LANES), lambda i: (i, 0, 0)),
        out_shape=jax.ShapeDtypeStruct((devices, height, LANES), BF16),
    )(src_grad, dst_grad, slot)


def collect_neg_kernel(sent_ref, slot_ref, *refs, group, cap):
    grad_refs, out_ref, sums = refs[:-2], refs[-2], refs[-1]
    step = pl.program_id(0)

    @pl.when(step == 0)
    def _():
        total = grad_refs[0][...].astype(F32)
        for grad_ref in grad_refs[1:]:
            total = total + grad_ref[...].astype(F32)
        sums[...] = total.astype(BF16)

    rows = jnp.zeros((group * cap, sums.shape[-1]), F32)
    for part in range(slot_ref.shape[0]):
        hot = one_hot(group * cap, slot_ref[part : part + 1, :], step * group * cap)
        rows = rows + dot(hot, sums[part], NN)
    pack_all(out_ref, 0, cap, rows, rows.T)


def collect_neg(sent, slot, grads, cap):
    devices = sent.shape[0]
    feature = grads[0].shape[-1]
    group = 16
    height = packed_height(cap, feature)
    return call(
        functools.partial(collect_neg_kernel, group=group, cap=cap),
        "collect_negatives",
        2 * devices * cap * feature * slot.size,
        4 * len(grads) * grads[0].size,
        grid=(devices // group,),
        in_specs=[
            pl.BlockSpec(memory_space=pl.ANY),
            pl.BlockSpec(slot.shape, lambda i: (0, 0)),
        ]
        + [pl.BlockSpec(grads[0].shape, lambda i: (0, 0, 0))] * len(grads),
        out_specs=pl.BlockSpec((group, height, LANES), lambda i: (i, 0, 0)),
        out_shape=jax.ShapeDtypeStruct(sent.shape, BF16),
        scratch_shapes=[pltpu.VMEM(grads[0].shape, BF16)],
        input_output_aliases={0: 0},
    )(sent, slot, *grads)


def collect_pool_kernel(src_ref, dst_ref, slot_ref, out_ref, *, group):
    segments, width = slot_ref.shape
    count = group * POOL
    rows = jnp.zeros((count, src_ref.shape[0]), F32)
    for segment in range(segments):
        grads = src_ref if segment < segments // 2 else dst_ref
        start = segment % (segments // 2) * width
        hot = one_hot(count, slot_ref[segment : segment + 1, :], pl.program_id(0) * count)
        rows = rows + dot(hot, grads[:, start : start + width], NT)
    pack_all(out_ref, 0, POOL, rows, rows.T)


def collect_pool(src_grad, dst_grad, slot, devices):
    feature = src_grad.shape[0]
    group = 8
    slots = devices * POOL
    height = packed_height(POOL, feature)
    whole = pl.BlockSpec(src_grad.shape, lambda i: (0, 0))
    return call(
        functools.partial(collect_pool_kernel, group=group),
        "collect_pool",
        2 * feature * slots * slot.size,
        2 * feature * (slots + slot.size),
        grid=(devices // group,),
        in_specs=[whole, whole, pl.BlockSpec(slot.shape, lambda i: (0, 0))],
        out_specs=pl.BlockSpec((group, height, LANES), lambda i: (i, 0, 0)),
        out_shape=jax.ShapeDtypeStruct((devices, height, LANES), BF16),
    )(src_grad, dst_grad, slot)


def add_kernel(*refs, rows, neg_cap, first):
    refs = list(refs)
    recv_ref, req_ref = refs[:2]
    refs = refs[2:]
    if neg_cap:
        neg_req_ref = refs.pop(0)
        neg_rows, neg_flat = refs[-2:]
    if not first:
        so_far_ref = refs.pop(0)
    out_ref, flat = refs[:2]
    devices = recv_ref.shape[0]
    feature = flat.shape[0]
    step = pl.program_id(0)

    @pl.when(step == 0)
    def _():
        start = recv_ref.shape[1] - feature
        for d in range(devices):
            flat[:, d * LANES : (d + 1) * LANES] = recv_ref[d, start:]
        if neg_cap:
            unpack_all(recv_ref, 0, neg_cap, neg_rows, neg_flat)

    base = step * rows
    row = jnp.concatenate([req_ref[d : d + 1, :] for d in range(devices)], axis=1)
    total = dot(flat[...], one_hot(rows, row, base), NT)
    if neg_cap:
        row = jnp.concatenate([neg_req_ref[d : d + 1, :neg_cap] for d in range(devices)], axis=1)
        total = total + dot(neg_flat[...], one_hot(rows, row, base), NT)
    if not first:
        total = total + so_far_ref[...]
    out_ref[...] = total


def add_rows(recv, requests, so_far, feature, rows_dev, neg_requests=None, neg_cap=0):
    devices = recv.shape[0]
    rows = 512 if devices * LANES <= 4096 else 128
    slots = devices * LANES
    whole_req = pl.BlockSpec((devices, LANES), lambda i: (0, 0))
    rows_spec = pl.BlockSpec((feature, rows), lambda i: (0, i))
    operands = [recv, requests]
    specs = [pl.BlockSpec(recv.shape, lambda i: (0, 0, 0)), whole_req]
    scratch = [pltpu.VMEM((feature, slots), BF16)]
    if neg_cap:
        operands.append(neg_requests)
        specs.append(whole_req)
        scratch += unpack_scratch(devices, neg_cap, feature)
    if so_far is not None:
        operands.append(so_far)
        specs.append(rows_spec)
    return call(
        functools.partial(add_kernel, rows=rows, neg_cap=neg_cap, first=so_far is None),
        "add_grads",
        2 * feature * slots * rows_dev,
        2 * feature * slots + 8 * feature * rows_dev,
        grid=(rows_dev // rows,),
        in_specs=specs,
        out_specs=rows_spec,
        out_shape=jax.ShapeDtypeStruct((feature, rows_dev), F32),
        scratch_shapes=scratch,
    )(*operands)


def add_pool_kernel(near_ref, far_ref, near_req_ref, far_req_ref, out_ref, packed, *flats, rows):
    step = pl.program_id(0)

    @pl.when(step == 0)
    def _():
        for recv_ref, flat in zip((near_ref, far_ref), flats):
            unpack_all(recv_ref, 0, POOL, packed, flat)

    total = dot(flats[0][...], one_hot(rows, near_req_ref[...], step * rows), NT)
    out_ref[...] = total + dot(flats[1][...], one_hot(rows, far_req_ref[...], step * rows), NT)


def add_pool(near, far, requests, feature, rows_dev):
    rows = 512
    devices = near.shape[0]
    slots = devices * POOL
    recv_spec = pl.BlockSpec(near.shape, lambda i: (0, 0, 0))
    req_spec = pl.BlockSpec((1, slots), lambda i: (0, 0))
    packed, flat = unpack_scratch(devices, POOL, feature)
    return call(
        functools.partial(add_pool_kernel, rows=rows),
        "add_pool",
        4 * feature * slots * rows_dev,
        4 * feature * slots + 4 * feature * rows_dev,
        grid=(rows_dev // rows,),
        in_specs=[recv_spec, recv_spec, req_spec, req_spec],
        out_specs=pl.BlockSpec((feature, rows), lambda i: (0, i)),
        out_shape=jax.ShapeDtypeStruct((feature, rows_dev), F32),
        scratch_shapes=[packed, flat, flat],
    )(near, far, requests[0][None], requests[1][None])


def exchange(value):
    return lax.all_to_all(value, ("shard", "grp"), split_axis=0, concat_axis=0, tiled=True)


def swap(value, bit):
    sharers = lax.axis_size("grp")
    return lax.ppermute(value, "grp", [(i, i ^ bit) for i in range(sharers)])


def share_out(value):
    return [value] + [swap(value, k) for k in range(1, lax.axis_size("grp"))]


def trade(blocks):
    return blocks[:1] + [swap(block, k) for k, block in enumerate(blocks) if k]


def pad_lanes(value, width, fill):
    return jnp.pad(value, ((0, 0), (0, width - value.shape[1])), constant_values=fill)


def body(entity_table, rel_diag, src_ids, dst_ids, rel_ids, neg_ids):
    rows_dev, feature = entity_table.shape
    sharers = lax.axis_size("grp")
    devices = lax.axis_size("shard") * sharers
    spans, neg_count = neg_ids.shape
    edge_count = src_ids.shape[0]
    block_len = edge_count // spans
    edge_cap = 4 * edge_count // devices
    chunks = round_up(edge_cap, LANES) // LANES
    part_width = neg_count // sharers
    neg_cap = round_up(2 * spans * part_width // devices, 16)
    width = round_up(block_len, 512)
    part = round_up(part_width, LANES)
    me = lax.axis_index("grp")

    table = entity_table.T.astype(BF16)
    relations = rel_diag.T
    own_ids = lax.dynamic_slice_in_dim(neg_ids, me * part_width, part_width, 1)
    ends = jnp.concatenate(
        [src_ids.reshape(spans, block_len), dst_ids.reshape(spans, block_len)]
    )
    message, *slots = make_slots(
        pad_lanes(ends, width, -1),
        pad_lanes(own_ids, part, -1),
        rows_dev,
        devices,
        chunks,
        neg_cap,
    )
    neg_slot = slots[-1]
    rel_rows = pad_lanes(rel_ids.reshape(spans, block_len), width, -1)
    asked = exchange(message)
    direct = [asked[:, c * LANES : (c + 1) * LANES] for c in range(chunks)]
    neg_asked = asked[:, -LANES:]

    def negatives_of(back):
        return share_out(spread_neg(back, neg_slot, neg_cap, feature))

    def direct_sent(src_grad, dst_grad, neg_grads):
        sent = collect(src_grad, dst_grad, slots[0], devices, neg_cap)
        return exchange(collect_neg(sent, neg_slot, trade(neg_grads), neg_cap))

    def chunked():
        back = [exchange(gather(table, direct[0], neg_asked, neg_cap))]
        back += [exchange(gather(table, direct[c])) for c in range(1, chunks)]
        negatives = negatives_of(back[0])
        rows = None
        for c in range(chunks):
            rows = spread(back[c], slots[c], rows, feature)
        src_grad, dst_grad, neg_grads = edges(rows, rel_rows, relations, negatives)
        grad = None
        for c in range(1, chunks):
            sent = exchange(collect(src_grad, dst_grad, slots[c], devices))
            grad = add_rows(sent, direct[c], grad, feature, rows_dev)
        sent = direct_sent(src_grad, dst_grad, neg_grads)
        return add_rows(sent, direct[0], grad, feature, rows_dev, neg_asked, neg_cap)

    def pooled():
        start = chunks * LANES
        core = me % RELAYS
        listed = asked[:, start : start + RELAYS * POOL].reshape(devices, RELAYS, POOL)
        listed = listed.transpose(1, 0, 2).reshape(RELAYS, devices * POOL) - core * rows_dev
        listed = [jnp.where(core == k, listed[0], listed[1]) for k in range(RELAYS)]
        back = exchange(gather(table, direct[0], neg_asked, neg_cap))
        far = swap(gather_pool(table, listed[1], devices), 1)
        relayed = gather_pool(table, listed[0], devices) + far
        negatives = negatives_of(back)
        rows = spread(back, slots[0], None, feature)
        rows = spread(exchange(relayed), slots[chunks], rows, feature, True)
        src_grad, dst_grad, neg_grads = edges(rows, rel_rows, relations, negatives)
        near = exchange(collect_pool(src_grad, dst_grad, slots[chunks], devices))
        sent = direct_sent(src_grad, dst_grad, neg_grads)
        grad = add_pool(near, swap(near, 1), listed, feature, rows_dev)
        return add_rows(sent, direct[0], grad, feature, rows_dev, neg_asked, neg_cap)

    if chunks == 1 or sharers % RELAYS:
        return chunked().T
    fits = jnp.max(neg_asked[:, -1]) < 0
    return lax.cond(fits, pooled, chunked).T


def solution(mesh):
    placed = (
        P(("shard", "grp"), None),
        P(),
        P(("shard", "grp")),
        P(("shard", "grp")),
        P(("shard", "grp")),
        P("shard", None),
    )
    return jax.shard_map(
        body, mesh=mesh, in_specs=placed, out_specs=P(("shard", "grp"), None), check_vma=False
    )
```

```python
import functools

import jax
import jax.numpy as jnp
from jax import lax
from jax.experimental import pallas as pl
from jax.experimental.pallas import tpu as pltpu
from jax.sharding import PartitionSpec as P

LANES = 128
POOL = 80
RELAYS = 2
VMEM_BYTES = 56 << 20
F32 = jnp.float32
BF16 = jnp.bfloat16
NN = (((1,), (0,)), ((), ()))
NT = (((1,), (1,)), ((), ()))
TN = (((0,), (0,)), ((), ()))


def round_up(value, unit):
    return -(-value // unit) * unit


def dot(left, right, dims):
    return lax.dot_general(left, right, dims, preferred_element_type=F32)


def one_hot(rows, row, base=0):
    places = lax.broadcasted_iota(jnp.int32, (rows, row.shape[1]), 0) + base
    return jnp.where(places == row, 1.0, 0.0).astype(BF16)


def call(kernel, name, flops, nbytes, **kwargs):
    return pl.pallas_call(
        kernel,
        name=name,
        compiler_params=pltpu.CompilerParams(vmem_limit_bytes=VMEM_BYTES),
        cost_estimate=pl.CostEstimate(flops=flops, bytes_accessed=nbytes, transcendentals=0),
        **kwargs,
    )


def ranks(members, mixer):
    groups = members[0].shape[0]
    both = dot(jnp.concatenate(members, axis=0).astype(BF16), mixer, NN)
    taken = jnp.zeros((groups, LANES), F32)
    found = []
    for i, member in enumerate(members):
        chunk = both[i * groups : (i + 1) * groups]
        found.append(jnp.sum((chunk[:, :LANES] + taken) * member, axis=0, keepdims=True))
        taken = taken + chunk[:, LANES:]
    return [rank.astype(jnp.int32) for rank in found], taken


def fill(members, codes, places, count):
    groups = members[0].shape[0]
    high = [m * (c // LANES).astype(F32) for m, c in zip(members, codes)]
    low = [m * (c % LANES).astype(F32) for m, c in zip(members, codes)]
    left = jnp.concatenate(
        [jnp.concatenate(high, axis=1), jnp.concatenate(low, axis=1)], axis=0
    ).astype(BF16)
    sums = dot(left, one_hot(count, jnp.concatenate(places, axis=1)), NT)
    return (LANES * sums[:groups] + sums[groups:]).astype(jnp.int32) - 1


def slots_kernel(me_ref, ends_ref, own_ref, *refs, rows_dev, devices, chunks, neg_cap):
    me = me_ref[0, 0]

    def position(device):
        offset = device ^ me
        return offset % (devices // 2) * 2 + offset // (devices // 2)

    msg_ref = refs[0]
    slot_refs = refs[1 : 1 + chunks]
    pool_ref = refs[1 + chunks] if chunks > 1 else None
    neg_ref = refs[-1]
    row = lax.broadcasted_iota(jnp.int32, (LANES, 2 * LANES), 0)
    lane = lax.broadcasted_iota(jnp.int32, (LANES, 2 * LANES), 1)
    mixer = jnp.where(row < lane, 1.0, 0.0).astype(BF16)
    owners = lax.broadcasted_iota(jnp.int32, (devices, LANES), 0)

    def prepare(ids_ref):
        where, holder, codes, members = [], [], [], []
        for segment in range(ids_ref.shape[0]):
            for start in range(0, ids_ref.shape[1], LANES):
                ids = ids_ref[segment : segment + 1, start : start + LANES]
                owner = jnp.where(ids >= 0, ids // rows_dev, -1)
                where.append((slice(segment, segment + 1), slice(start, start + LANES)))
                holder.append(owner)
                codes.append(jnp.where(ids >= 0, ids - owner * rows_dev + 1, 0))
                members.append(jnp.where(owners == owner, 1.0, 0.0))
        found, _ = ranks(members, mixer)
        return where, holder, codes, members, found

    where, holder, codes, members, found = prepare(ends_ref)
    for chunk in range(chunks):
        places = []
        for at, owner, rank in zip(where, holder, found):
            place = rank - chunk * LANES
            place = jnp.where((owner >= 0) & (place >= 0) & (place < LANES), place, -1)
            slot_refs[chunk][at] = jnp.where(
                place >= 0, position(owner) * LANES + place, -1
            )
            places.append(place)
        msg_ref[:, chunk * LANES : (chunk + 1) * LANES] = fill(members, codes, places, LANES)
    offset = chunks * LANES
    flag = jnp.full((1, 1), -1, jnp.int32)
    if chunks > 1:
        chips = devices // RELAYS
        room = RELAYS * POOL
        chip_rows = lax.broadcasted_iota(jnp.int32, (chips, LANES), 0)
        spilled, spill_codes = [], []
        for owner, code, rank in zip(holder, codes, found):
            chip = jnp.where(rank >= LANES, owner // RELAYS, -1)
            spilled.append(jnp.where(chip_rows == chip, 1.0, 0.0))
            spill_codes.append(code + (owner % RELAYS) * rows_dev)
        pooled, taken = ranks(spilled, mixer)
        places = []
        for at, owner, rank, place in zip(where, holder, found, pooled):
            inside = (owner >= 0) & (rank >= LANES) & (place < room)
            relay = owner // RELAYS * RELAYS + place // POOL
            pool_ref[at] = jnp.where(inside, position(relay) * POOL + place % POOL, -1)
            places.append(jnp.where(inside, place, -1))
        listed = fill(spilled, spill_codes, places, 2 * LANES)
        for chip in range(chips):
            msg_ref[chip * RELAYS : (chip + 1) * RELAYS, offset : offset + 2 * LANES] = (
                jnp.broadcast_to(listed[chip : chip + 1], (RELAYS, 2 * LANES))
            )
        offset += 2 * LANES
        most = jnp.max(jnp.max(taken, axis=1, keepdims=True), axis=0, keepdims=True)
        flag = jnp.where(most > room, 1, -1)

    where, holder, codes, members, found = prepare(own_ref)
    for at, owner, rank in zip(where, holder, found):
        neg_ref[at] = jnp.where(owner >= 0, position(owner) * neg_cap + rank, -1)
    places = [jnp.where(owner >= 0, rank, -1) for owner, rank in zip(holder, found)]
    listed = fill(members, codes, places, LANES)
    lanes = lax.broadcasted_iota(jnp.int32, listed.shape, 1)
    msg_ref[:, offset:] = jnp.where(lanes == LANES - 1, flag, listed)


def make_slots(me, ends, own, rows_dev, devices, chunks, neg_cap):
    pooled = chunks > 1
    width = (chunks + 1 + 2 * pooled) * LANES
    return call(
        functools.partial(
            slots_kernel,
            rows_dev=rows_dev,
            devices=devices,
            chunks=chunks,
            neg_cap=neg_cap,
        ),
        "slots",
        16 * devices * LANES * ends.size,
        8 * ends.size,
        in_specs=[
            pl.BlockSpec(memory_space=pltpu.SMEM),
            pl.BlockSpec(ends.shape, lambda: (0, 0)),
            pl.BlockSpec(own.shape, lambda: (0, 0)),
        ],
        out_shape=[jax.ShapeDtypeStruct((devices, width), jnp.int32)]
        + [jax.ShapeDtypeStruct(ends.shape, jnp.int32)] * (chunks + pooled)
        + [jax.ShapeDtypeStruct(own.shape, jnp.int32)],
    )(me.reshape(1, 1), ends, own)


def packed_height(count, feature):
    return feature // LANES * count + feature % LANES


def pack(out_ref, start, rows, tail):
    count, feature = rows.shape
    for piece in range(feature // LANES):
        out_ref[start + piece * count : start + (piece + 1) * count, :] = rows[
            :, piece * LANES : (piece + 1) * LANES
        ].astype(out_ref.dtype)
    tail = jnp.concatenate([tail, jnp.zeros((tail.shape[0], LANES - count), tail.dtype)], axis=1)
    end = start + packed_height(count, feature)
    out_ref[end - tail.shape[0] : end, :] = tail.astype(out_ref.dtype)


def blocks_of(ref):
    return [ref.at[i] for i in range(ref.shape[0])]


def pack_all(out_refs, start, count, rows, turned):
    feature = rows.shape[1]
    first = feature // LANES * LANES
    for i, out_ref in enumerate(out_refs):
        at = slice(i * count, (i + 1) * count)
        pack(out_ref, start, rows[at], turned[first:, at])


def unpack_all(in_refs, start, count, rows_ref, flat_ref):
    feature = flat_ref.shape[0]
    pieces = feature // LANES
    end = start + packed_height(count, feature)
    for d, in_ref in enumerate(in_refs):
        for piece in range(pieces):
            rows_ref[d * count : (d + 1) * count, piece * LANES : (piece + 1) * LANES] = in_ref[
                start + piece * count : start + (piece + 1) * count, :
            ]
    tails = [
        in_ref[end - feature % LANES : end, :].astype(F32)[:, :count] for in_ref in in_refs
    ]
    flat_ref[: pieces * LANES] = rows_ref[...].astype(F32).T.astype(BF16)
    flat_ref[pieces * LANES :] = jnp.concatenate(tails, axis=1).astype(BF16)


def unpack_scratch(devices, count, feature):
    return [
        pltpu.VMEM((devices * count, feature // LANES * LANES), BF16),
        pltpu.VMEM((feature, devices * count), BF16),
    ]


def gather_kernel(table_ref, *refs, group, neg_cap):
    feature, rows_dev = table_ref.shape
    first = pl.program_id(0) * group
    req_ref, out_ref = refs[0], refs[-1]
    row = [req_ref[pl.ds(first + i, 1), :] for i in range(group)]
    if neg_cap:
        row += [refs[1][pl.ds(first + i, 1), :neg_cap] for i in range(group)]
    rows = dot(table_ref[...], one_hot(rows_dev, jnp.concatenate(row, axis=1)), NN)
    start = out_ref.shape[1] - feature
    for i in range(group):
        out_ref[i, start:] = rows[:, i * LANES : (i + 1) * LANES].astype(BF16)
    if neg_cap:
        neg = rows[:, group * LANES :]
        pack_all(blocks_of(out_ref), 0, neg_cap, neg.T, neg)


def gather(table, requests, neg_requests=None, neg_cap=0):
    feature, rows_dev = table.shape
    devices = requests.shape[0]
    group = 4
    height = feature + (packed_height(neg_cap, feature) if neg_cap else 0)
    slots = devices * (LANES + neg_cap)
    whole = pl.BlockSpec((devices, LANES), lambda i: (0, 0))
    return call(
        functools.partial(gather_kernel, group=group, neg_cap=neg_cap),
        "gather_rows",
        2 * feature * rows_dev * slots,
        2 * feature * (rows_dev + slots),
        grid=(devices // group,),
        in_specs=[pl.BlockSpec((feature, rows_dev), lambda i: (0, 0)), whole]
        + ([whole] if neg_cap else []),
        out_specs=pl.BlockSpec((group, height, LANES), lambda i: (i, 0, 0)),
        out_shape=jax.ShapeDtypeStruct((devices, height, LANES), BF16),
    )(table, requests, *([neg_requests] if neg_cap else []))


def gather_pool_kernel(table_ref, req_ref, out_ref, *, group):
    rows_dev = table_ref.shape[1]
    row = req_ref[...].reshape(1, group * POOL)
    rows = dot(table_ref[...], one_hot(rows_dev, row), NN)
    pack_all(blocks_of(out_ref), 0, POOL, rows.T, rows)


def gather_pool(table, requests, devices):
    feature, rows_dev = table.shape
    group = 8
    steps = devices // group
    height = packed_height(POOL, feature)
    return call(
        functools.partial(gather_pool_kernel, group=group),
        "gather_pool",
        2 * feature * rows_dev * requests.size,
        2 * feature * (rows_dev + requests.size),
        grid=(steps,),
        in_specs=[
            pl.BlockSpec((feature, rows_dev), lambda i: (0, 0)),
            pl.BlockSpec((1, 1, group * POOL), lambda i: (i, 0, 0)),
        ],
        out_specs=pl.BlockSpec((group, height, LANES), lambda i: (i, 0, 0)),
        out_shape=jax.ShapeDtypeStruct((devices, height, LANES), BF16),
    )(table, requests.reshape(steps, 1, group * POOL))


def spread_neg_kernel(back_ref, slot_ref, out_ref, rows, flat, *, cap):
    unpack_all(blocks_of(back_ref), 0, cap, rows, flat)
    for part in range(slot_ref.shape[0]):
        hot = one_hot(flat.shape[1], slot_ref[part : part + 1, :])
        out_ref[part] = dot(flat[...], hot, NN).T.astype(BF16)


def spread_neg(back, slot, cap, feature):
    devices = back.shape[0]
    parts, width = slot.shape
    height = packed_height(cap, feature)
    return call(
        functools.partial(spread_neg_kernel, cap=cap),
        "spread_negatives",
        2 * devices * cap * feature * slot.size,
        2 * devices * cap * feature,
        grid=(1,),
        in_specs=[
            pl.BlockSpec((devices, height, LANES), lambda i: (0, 0, 0)),
            pl.BlockSpec(slot.shape, lambda i: (0, 0)),
        ],
        out_specs=pl.BlockSpec((parts, width, feature), lambda i: (0, 0, 0)),
        out_shape=jax.ShapeDtypeStruct((parts, width, feature), BF16),
        scratch_shapes=unpack_scratch(devices, cap, feature),
    )(back, slot)


def spread_kernel(*refs, first):
    back_ref, slot_ref = refs[:2]
    so_far_ref = None if first else refs[2]
    out_ref, flat = refs[2 + (not first)], refs[-1]
    devices = back_ref.shape[0]
    feature = flat.shape[0]

    @pl.when(pl.program_id(0) == 0)
    def _():
        start = back_ref.shape[1] - feature
        for d in range(devices):
            flat[:, d * LANES : (d + 1) * LANES] = back_ref[d, start:]

    row = slot_ref[...].reshape(1, slot_ref.shape[-1])
    rows = dot(flat[...], one_hot(flat.shape[1], row), NN)
    if not first:
        rows = rows + so_far_ref[...].astype(F32)
    out_ref[...] = rows.astype(BF16)


def spread(back, slot, so_far, feature):
    devices = back.shape[0]
    segments, width = slot.shape
    slots = devices * LANES
    tile = 512 if slots <= 4096 else 128
    steps = width // tile
    rows_spec = pl.BlockSpec((feature, tile), lambda i: (0, i))
    extra = [] if so_far is None else [so_far]
    return call(
        functools.partial(spread_kernel, first=so_far is None),
        "spread_rows",
        2 * feature * slots * slot.size,
        2 * feature * (slots + slot.size),
        grid=(segments * steps,),
        in_specs=[
            pl.BlockSpec(back.shape, lambda i: (0, 0, 0)),
            pl.BlockSpec((1, 1, tile), lambda i: (i // steps, 0, i % steps)),
        ]
        + [rows_spec] * len(extra),
        out_specs=rows_spec,
        out_shape=jax.ShapeDtypeStruct((feature, slot.size), BF16),
        scratch_shapes=[pltpu.VMEM((feature, slots), BF16)],
    )(back, slot.reshape(segments, 1, width), *extra)


def gather_blocks_kernel(table_ref, req_ref, neg_req_ref, *out_refs, first, neg_cap):
    feature, rows_dev = table_ref.shape
    group = len(out_refs)
    row = [req_ref[first + i : first + i + 1, :] for i in range(group)]
    row += [neg_req_ref[first + i : first + i + 1, :neg_cap] for i in range(group)]
    rows = dot(table_ref[...], one_hot(rows_dev, jnp.concatenate(row, axis=1)), NN)
    for i, out_ref in enumerate(out_refs):
        out_ref[out_ref.shape[0] - feature :] = rows[:, i * LANES : (i + 1) * LANES].astype(BF16)
    neg = rows[:, group * LANES :]
    pack_all(out_refs, 0, neg_cap, neg.T, neg)


def gather_blocks(table, requests, neg_requests, first, group, neg_cap):
    feature, rows_dev = table.shape
    slots = group * (LANES + neg_cap)
    block = jax.ShapeDtypeStruct((packed_height(neg_cap, feature) + feature, LANES), BF16)
    return call(
        functools.partial(gather_blocks_kernel, first=first, neg_cap=neg_cap),
        "gather_blocks",
        2 * feature * rows_dev * slots,
        2 * feature * (rows_dev + slots),
        out_shape=[block] * group,
    )(table, requests, neg_requests)


def relay_blocks_kernel(table_ref, req_ref, far_ref, *out_refs):
    row = req_ref[...].reshape(1, req_ref.shape[-1])
    rows = dot(table_ref[...], one_hot(table_ref.shape[1], row), NN)
    pack_all(out_refs, 0, POOL, rows.T, rows)
    for i, out_ref in enumerate(out_refs):
        out_ref[...] = out_ref[...] + far_ref[i]


def relay_blocks(table, requests, far, first, group):
    feature, rows_dev = table.shape
    devices, height, _ = far.shape
    step = first // group
    slots = group * POOL
    return call(
        relay_blocks_kernel,
        "relay_blocks",
        2 * feature * rows_dev * slots,
        2 * feature * (rows_dev + 2 * slots),
        grid=(1,),
        in_specs=[
            pl.BlockSpec((feature, rows_dev), lambda i: (0, 0)),
            pl.BlockSpec((1, 1, slots), lambda i: (step, 0, 0)),
            pl.BlockSpec((group, height, LANES), lambda i: (step, 0, 0)),
        ],
        out_specs=[pl.BlockSpec((height, LANES), lambda i: (0, 0))] * group,
        out_shape=[jax.ShapeDtypeStruct((height, LANES), BF16)] * group,
    )(table, requests.reshape(devices // group, 1, slots), far)


def spread_neg_blocks_kernel(*refs, blocks, cap):
    slot_ref, out_ref, rows, flat = refs[blocks:]
    unpack_all(refs[:blocks], 0, cap, rows, flat)
    for part in range(slot_ref.shape[0]):
        hot = one_hot(flat.shape[1], slot_ref[part : part + 1, :])
        out_ref[part] = dot(flat[...], hot, NN).T.astype(BF16)


def spread_neg_blocks(back, slot, cap, feature):
    devices = len(back)
    parts, width = slot.shape
    height = packed_height(cap, feature)
    return call(
        functools.partial(spread_neg_blocks_kernel, blocks=devices, cap=cap),
        "spread_negatives",
        2 * devices * cap * feature * slot.size,
        2 * devices * cap * feature,
        grid=(1,),
        in_specs=[pl.BlockSpec((height, LANES), lambda i: (0, 0))] * devices
        + [pl.BlockSpec(slot.shape, lambda i: (0, 0))],
        out_specs=pl.BlockSpec((parts, width, feature), lambda i: (0, 0, 0)),
        out_shape=jax.ShapeDtypeStruct((parts, width, feature), BF16),
        scratch_shapes=unpack_scratch(devices, cap, feature),
    )(*back, slot)


def spread_blocks_kernel(*refs, blocks, base, pooled, first):
    back_refs, slot_ref = refs[:blocks], refs[blocks]
    out_ref, flat = refs[blocks + 1 + (not first)], refs[-1]
    feature = flat.shape[0]

    @pl.when(pl.program_id(0) == 0)
    def _():
        if pooled:
            unpack_all(back_refs, 0, POOL, refs[-2], flat)
        else:
            for d, back_ref in enumerate(back_refs):
                flat[:, d * LANES : (d + 1) * LANES] = back_ref[back_ref.shape[0] - feature :]

    row = slot_ref[...].reshape(1, slot_ref.shape[-1])
    rows = dot(flat[...], one_hot(flat.shape[1], row, base), NN)
    if not first:
        rows = rows + refs[blocks + 1][...].astype(F32)
    out_ref[...] = rows.astype(BF16)


def spread_blocks(back, slot, so_far, feature, first, pooled=False):
    blocks = len(back)
    segments, width = slot.shape
    each = POOL if pooled else LANES
    tile = width
    steps = width // tile
    rows_spec = pl.BlockSpec((feature, tile), lambda i: (0, i))
    extra = [] if so_far is None else [so_far]
    if pooled:
        scratch = unpack_scratch(blocks, POOL, feature)
    else:
        scratch = [pltpu.VMEM((feature, blocks * each), BF16)]
    return call(
        functools.partial(
            spread_blocks_kernel,
            blocks=blocks,
            base=first * each,
            pooled=pooled,
            first=so_far is None,
        ),
        "spread_pool" if pooled else "spread_blocks",
        2 * feature * blocks * each * slot.size,
        4 * feature * slot.size,
        grid=(segments * steps,),
        in_specs=[pl.BlockSpec(back[0].shape, lambda i: (0, 0))] * blocks
        + [pl.BlockSpec((1, 1, tile), lambda i: (i // steps, 0, i % steps))]
        + [rows_spec] * len(extra),
        out_specs=rows_spec,
        out_shape=jax.ShapeDtypeStruct((feature, slot.size), BF16),
        scratch_shapes=scratch,
    )(*back, slot.reshape(segments, 1, width), *extra)


def edges_kernel(*refs, parts):
    src_ref, dst_ref, rel_ids_ref, rel_ref = refs[:4]
    neg_refs = refs[4 : 4 + parts]
    src_grad_ref, dst_grad_ref = refs[4 + parts : 6 + parts]
    neg_grad_refs = refs[6 + parts : 6 + 2 * parts]
    negatives, turned, sums = refs[6 + 2 * parts :]
    step = pl.program_id(1)
    part = neg_refs[0].shape[1]

    @pl.when(step == 0)
    def _():
        for k in range(parts):
            negatives[k * part : (k + 1) * part] = neg_refs[k][0]
        turned[...] = negatives[...].astype(F32).T.astype(BF16)

    hot = one_hot(rel_ref.shape[1], rel_ids_ref[...].reshape(1, rel_ids_ref.shape[-1]))
    table = rel_ref[...]
    relation = jnp.zeros(src_ref.shape, F32)
    for _ in range(3):
        piece = table.astype(BF16)
        relation = relation + dot(piece, hot, NN)
        table = table - piece.astype(F32)
    source = src_ref[...].astype(F32)
    target = dst_ref[...].astype(F32)
    product = source * relation
    positive = jnp.sum(product * target, axis=0, keepdims=True)
    pos_weight = -jax.nn.sigmoid(-positive)
    query = product.astype(BF16)
    weight = jax.nn.sigmoid(dot(negatives[...], query, NN)).astype(BF16)
    gathered = dot(turned[...], weight, NN)
    src_grad_ref[...] = (relation * (pos_weight * target + gathered)).astype(BF16)
    dst_grad_ref[...] = (pos_weight * product).astype(BF16)
    neg_grad = dot(weight, query, NT)

    @pl.when(step == 0)
    def _():
        sums[...] = neg_grad

    @pl.when(step != 0)
    def _():
        sums[...] += neg_grad

    @pl.when(step == pl.num_programs(1) - 1)
    def _():
        for k in range(parts):
            neg_grad_refs[k][0] = sums[k * part : (k + 1) * part].astype(BF16)


def edges(rows, rel_ids, relations, negatives):
    feature, endpoints = rows.shape
    parts = len(negatives)
    spans, part, _ = negatives[0].shape
    width = rel_ids.shape[1]
    tile = 512
    steps = width // tile
    blocks = spans * steps
    edge_spec = pl.BlockSpec((feature, tile), lambda b, i: (0, b * steps + i))
    neg_spec = pl.BlockSpec((1, part, feature), lambda b, i: (b, 0, 0))
    src_grad, dst_grad, *neg_grads = call(
        functools.partial(edges_kernel, parts=parts),
        "edges",
        6 * feature * parts * part * spans * width,
        4 * (rows.size + parts * negatives[0].size),
        grid=(spans, steps),
        in_specs=[
            edge_spec,
            pl.BlockSpec((feature, tile), lambda b, i: (0, blocks + b * steps + i)),
            pl.BlockSpec((1, 1, tile), lambda b, i: (b, 0, i)),
            pl.BlockSpec(relations.shape, lambda b, i: (0, 0)),
        ]
        + [neg_spec] * parts,
        out_specs=[edge_spec, edge_spec] + [neg_spec] * parts,
        out_shape=[jax.ShapeDtypeStruct((feature, endpoints // 2), BF16)] * 2
        + [jax.ShapeDtypeStruct((spans, part, feature), BF16)] * parts,
        scratch_shapes=[
            pltpu.VMEM((parts * part, feature), BF16),
            pltpu.VMEM((feature, parts * part), BF16),
            pltpu.VMEM((parts * part, feature), F32),
        ],
    )(rows, rows, rel_ids.reshape(spans, 1, width), relations, *negatives)
    return src_grad, dst_grad, neg_grads


def collect_kernel(src_ref, dst_ref, slot_ref, out_ref, *, group):
    segments, width = slot_ref.shape
    feature = src_ref.shape[0]
    step = pl.program_id(0)
    total = jnp.zeros((feature, group * LANES), F32)
    for segment in range(segments):
        grads = src_ref if segment < segments // 2 else dst_ref
        start = segment % (segments // 2) * width
        hot = one_hot(group * LANES, slot_ref[segment : segment + 1, :], step * group * LANES)
        total = total + dot(grads[:, start : start + width], hot, NT)
    total = total.astype(BF16)
    first = out_ref.shape[1] - feature
    for i in range(group):
        out_ref[i, first:] = total[:, i * LANES : (i + 1) * LANES]


def collect(src_grad, dst_grad, slot, devices, neg_cap=0):
    feature = src_grad.shape[0]
    group = 4
    slots = devices * LANES
    height = feature + (packed_height(neg_cap, feature) if neg_cap else 0)
    whole = pl.BlockSpec(src_grad.shape, lambda i: (0, 0))
    return call(
        functools.partial(collect_kernel, group=group),
        "collect_grads",
        2 * feature * slots * slot.size,
        2 * feature * (slots + slot.size),
        grid=(devices // group,),
        in_specs=[whole, whole, pl.BlockSpec(slot.shape, lambda i: (0, 0))],
        out_specs=pl.BlockSpec((group, height, LANES), lambda i: (i, 0, 0)),
        out_shape=jax.ShapeDtypeStruct((devices, height, LANES), BF16),
    )(src_grad, dst_grad, slot)


def collect_neg_kernel(sent_ref, slot_ref, *refs, group, cap):
    grad_refs, out_ref, sums = refs[:-2], refs[-2], refs[-1]
    step = pl.program_id(0)

    @pl.when(step == 0)
    def _():
        total = grad_refs[0][...].astype(F32)
        for grad_ref in grad_refs[1:]:
            total = total + grad_ref[...].astype(F32)
        sums[...] = total.astype(BF16)

    rows = jnp.zeros((group * cap, sums.shape[-1]), F32)
    for part in range(slot_ref.shape[0]):
        hot = one_hot(group * cap, slot_ref[part : part + 1, :], step * group * cap)
        rows = rows + dot(hot, sums[part], NN)
    pack_all(blocks_of(out_ref), 0, cap, rows, rows.T)


def collect_neg(sent, slot, grads, cap):
    devices = sent.shape[0]
    feature = grads[0].shape[-1]
    group = 16
    height = packed_height(cap, feature)
    return call(
        functools.partial(collect_neg_kernel, group=group, cap=cap),
        "collect_negatives",
        2 * devices * cap * feature * slot.size,
        4 * len(grads) * grads[0].size,
        grid=(devices // group,),
        in_specs=[
            pl.BlockSpec(memory_space=pl.ANY),
            pl.BlockSpec(slot.shape, lambda i: (0, 0)),
        ]
        + [pl.BlockSpec(grads[0].shape, lambda i: (0, 0, 0))] * len(grads),
        out_specs=pl.BlockSpec((group, height, LANES), lambda i: (i, 0, 0)),
        out_shape=jax.ShapeDtypeStruct(sent.shape, BF16),
        scratch_shapes=[pltpu.VMEM(grads[0].shape, BF16)],
        input_output_aliases={0: 0},
    )(sent, slot, *grads)


def collect_blocks_kernel(src_ref, dst_ref, slot_ref, neg_slot_ref, *refs, first, neg_cap, group):
    segments, width = slot_ref.shape
    feature = src_ref.shape[0]
    grad_refs, out_refs = refs[:-group], refs[-group:]
    total = jnp.zeros((feature, group * LANES), F32)
    for segment in range(segments):
        grads = src_ref if segment < segments // 2 else dst_ref
        start = segment % (segments // 2) * width
        hot = one_hot(group * LANES, slot_ref[segment : segment + 1, :], first * LANES)
        total = total + dot(grads[:, start : start + width], hot, NT)
    total = total.astype(BF16)
    for i, out_ref in enumerate(out_refs):
        out_ref[out_ref.shape[0] - feature :] = total[:, i * LANES : (i + 1) * LANES]
    rows = jnp.zeros((group * neg_cap, feature), F32)
    for part in range(neg_slot_ref.shape[0]):
        value = grad_refs[0][part].astype(F32)
        for grad_ref in grad_refs[1:]:
            value = value + grad_ref[part].astype(F32)
        hot = one_hot(group * neg_cap, neg_slot_ref[part : part + 1, :], first * neg_cap)
        rows = rows + dot(hot, value.astype(BF16), NN)
    pack_all(out_refs, 0, neg_cap, rows, rows.T)


def collect_blocks(src_grad, dst_grad, slot, neg_slot, neg_grads, first, group, neg_cap):
    feature = src_grad.shape[0]
    block = jax.ShapeDtypeStruct((packed_height(neg_cap, feature) + feature, LANES), BF16)
    return call(
        functools.partial(collect_blocks_kernel, first=first, neg_cap=neg_cap, group=group),
        "collect_blocks",
        2 * feature * group * LANES * slot.size,
        2 * feature * slot.size,
        out_shape=[block] * group,
    )(src_grad, dst_grad, slot, neg_slot, *neg_grads)


def collect_pool_kernel(src_ref, dst_ref, slot_ref, *out_refs, first):
    segments, width = slot_ref.shape
    count = len(out_refs) * POOL
    rows = jnp.zeros((count, src_ref.shape[0]), F32)
    for segment in range(segments):
        grads = src_ref if segment < segments // 2 else dst_ref
        start = segment % (segments // 2) * width
        hot = one_hot(count, slot_ref[segment : segment + 1, :], first * POOL)
        rows = rows + dot(hot, grads[:, start : start + width], NT)
    pack_all(out_refs, 0, POOL, rows, rows.T)


def collect_pool(src_grad, dst_grad, slot, first, group):
    feature = src_grad.shape[0]
    block = jax.ShapeDtypeStruct((packed_height(POOL, feature), LANES), BF16)
    return call(
        functools.partial(collect_pool_kernel, first=first),
        "collect_pool",
        2 * feature * group * POOL * slot.size,
        2 * feature * slot.size,
        out_shape=[block] * group,
    )(src_grad, dst_grad, slot)


def add_blocks_kernel(*refs, blocks, first, neg_cap, rows):
    recv_refs = refs[:blocks]
    req_ref, neg_req_ref, so_far_ref, out_ref, flat, neg_rows, neg_flat = refs[blocks:]
    feature = flat.shape[0]
    step = pl.program_id(0)

    @pl.when(step == 0)
    def _():
        for d, recv_ref in enumerate(recv_refs):
            flat[:, d * LANES : (d + 1) * LANES] = recv_ref[recv_ref.shape[0] - feature :]
        unpack_all(recv_refs, 0, neg_cap, neg_rows, neg_flat)

    base = step * rows
    row = jnp.concatenate([req_ref[first + d : first + d + 1, :] for d in range(blocks)], axis=1)
    total = dot(flat[...], one_hot(rows, row, base), NT)
    row = jnp.concatenate(
        [neg_req_ref[first + d : first + d + 1, :neg_cap] for d in range(blocks)], axis=1
    )
    total = total + dot(neg_flat[...], one_hot(rows, row, base), NT)
    out_ref[...] = total + so_far_ref[...]


def add_blocks(recv, requests, neg_requests, so_far, first, neg_cap):
    feature, rows_dev = so_far.shape
    blocks = len(recv)
    rows = 1024
    slots = blocks * LANES
    req_spec = pl.BlockSpec(requests.shape, lambda i: (0, 0))
    rows_spec = pl.BlockSpec((feature, rows), lambda i: (0, i))
    return call(
        functools.partial(
            add_blocks_kernel, blocks=blocks, first=first, neg_cap=neg_cap, rows=rows
        ),
        "add_blocks",
        2 * feature * slots * rows_dev,
        8 * feature * rows_dev,
        grid=(rows_dev // rows,),
        in_specs=[pl.BlockSpec(recv[0].shape, lambda i: (0, 0))] * blocks
        + [req_spec, req_spec, rows_spec],
        out_specs=rows_spec,
        out_shape=jax.ShapeDtypeStruct((feature, rows_dev), F32),
        scratch_shapes=[pltpu.VMEM((feature, slots), BF16)]
        + unpack_scratch(blocks, neg_cap, feature),
    )(*recv, requests, neg_requests, so_far)


def add_kernel(*refs, rows, neg_cap, first):
    refs = list(refs)
    recv_ref, req_ref = refs[:2]
    refs = refs[2:]
    if neg_cap:
        neg_req_ref = refs.pop(0)
        neg_rows, neg_flat = refs[-2:]
    if not first:
        so_far_ref = refs.pop(0)
    out_ref, flat = refs[:2]
    devices = recv_ref.shape[0]
    feature = flat.shape[0]
    step = pl.program_id(0)

    @pl.when(step == 0)
    def _():
        start = recv_ref.shape[1] - feature
        for d in range(devices):
            flat[:, d * LANES : (d + 1) * LANES] = recv_ref[d, start:]
        if neg_cap:
            unpack_all(blocks_of(recv_ref), 0, neg_cap, neg_rows, neg_flat)

    base = step * rows
    row = jnp.concatenate([req_ref[d : d + 1, :] for d in range(devices)], axis=1)
    total = dot(flat[...], one_hot(rows, row, base), NT)
    if neg_cap:
        row = jnp.concatenate([neg_req_ref[d : d + 1, :neg_cap] for d in range(devices)], axis=1)
        total = total + dot(neg_flat[...], one_hot(rows, row, base), NT)
    if not first:
        total = total + so_far_ref[...]
    out_ref[...] = total


def add_rows(recv, requests, so_far, feature, rows_dev, neg_requests=None, neg_cap=0):
    devices = recv.shape[0]
    rows = 512 if devices * LANES <= 4096 else 128
    slots = devices * LANES
    whole_req = pl.BlockSpec((devices, LANES), lambda i: (0, 0))
    rows_spec = pl.BlockSpec((feature, rows), lambda i: (0, i))
    operands = [recv, requests]
    specs = [pl.BlockSpec(recv.shape, lambda i: (0, 0, 0)), whole_req]
    scratch = [pltpu.VMEM((feature, slots), BF16)]
    if neg_cap:
        operands.append(neg_requests)
        specs.append(whole_req)
        scratch += unpack_scratch(devices, neg_cap, feature)
    if so_far is not None:
        operands.append(so_far)
        specs.append(rows_spec)
    return call(
        functools.partial(add_kernel, rows=rows, neg_cap=neg_cap, first=so_far is None),
        "add_grads",
        2 * feature * slots * rows_dev,
        2 * feature * slots + 8 * feature * rows_dev,
        grid=(rows_dev // rows,),
        in_specs=specs,
        out_specs=rows_spec,
        out_shape=jax.ShapeDtypeStruct((feature, rows_dev), F32),
        scratch_shapes=scratch,
    )(*operands)


def add_pool_kernel(near_ref, far_ref, near_req_ref, far_req_ref, out_ref, packed, *flats, rows):
    step = pl.program_id(0)

    @pl.when(step == 0)
    def _():
        for recv_ref, flat in zip((near_ref, far_ref), flats):
            unpack_all(blocks_of(recv_ref), 0, POOL, packed, flat)

    total = dot(flats[0][...], one_hot(rows, near_req_ref[...], step * rows), NT)
    out_ref[...] = total + dot(flats[1][...], one_hot(rows, far_req_ref[...], step * rows), NT)


def add_pool(near, far, requests, feature, rows_dev):
    rows = 512
    devices = near.shape[0]
    slots = devices * POOL
    recv_spec = pl.BlockSpec(near.shape, lambda i: (0, 0, 0))
    req_spec = pl.BlockSpec((1, slots), lambda i: (0, 0))
    packed, flat = unpack_scratch(devices, POOL, feature)
    return call(
        functools.partial(add_pool_kernel, rows=rows),
        "add_pool",
        4 * feature * slots * rows_dev,
        4 * feature * slots + 4 * feature * rows_dev,
        grid=(rows_dev // rows,),
        in_specs=[recv_spec, recv_spec, req_spec, req_spec],
        out_specs=pl.BlockSpec((feature, rows), lambda i: (0, i)),
        out_shape=jax.ShapeDtypeStruct((feature, rows_dev), F32),
        scratch_shapes=[packed, flat, flat],
    )(near, far, requests[0][None], requests[1][None])


def mixed(devices):
    return [p // 2 + p % 2 * (devices // 2) for p in range(devices)]


def exchange(value):
    axes = ("shard", "grp")
    devices = value.shape[0]
    me = lax.axis_index(axes)
    offsets = me ^ jnp.arange(devices, dtype=jnp.int32)
    value = value[offsets % (devices // 2) * 2 + offsets // (devices // 2)]
    value = lax.all_to_all(value, axes, split_axis=0, concat_axis=0, tiled=True)
    return value[me ^ jnp.array(mixed(devices), jnp.int32)]


def trade_blocks(blocks, first, devices):
    offsets = mixed(devices)[first : first + len(blocks)]
    return [
        lax.ppermute(block, ("shard", "grp"), [(i, i ^ k) for i in range(devices)]) if k else block
        for k, block in zip(offsets, blocks)
    ]


def swap(value, bit):
    sharers = lax.axis_size("grp")
    return lax.ppermute(value, "grp", [(i, i ^ bit) for i in range(sharers)])


def share_out(value):
    return [value] + [swap(value, k) for k in range(1, lax.axis_size("grp"))]


def trade(blocks):
    return blocks[:1] + [swap(block, k) for k, block in enumerate(blocks) if k]


def pad_lanes(value, width, fill):
    return jnp.pad(value, ((0, 0), (0, width - value.shape[1])), constant_values=fill)


def body(entity_table, rel_diag, src_ids, dst_ids, rel_ids, neg_ids):
    rows_dev, feature = entity_table.shape
    sharers = lax.axis_size("grp")
    devices = lax.axis_size("shard") * sharers
    spans, neg_count = neg_ids.shape
    edge_count = src_ids.shape[0]
    block_len = edge_count // spans
    edge_cap = 4 * edge_count // devices
    chunks = round_up(edge_cap, LANES) // LANES
    part_width = neg_count // sharers
    neg_cap = round_up(2 * spans * part_width // devices, 16)
    width = round_up(block_len, 512)
    part = round_up(part_width, LANES)
    me = lax.axis_index("grp")
    device = lax.axis_index(("shard", "grp"))

    table = entity_table.T.astype(BF16)
    relations = rel_diag.T
    own_ids = lax.dynamic_slice_in_dim(neg_ids, me * part_width, part_width, 1)
    ends = jnp.concatenate(
        [src_ids.reshape(spans, block_len), dst_ids.reshape(spans, block_len)]
    )
    message, *slots = make_slots(
        device,
        pad_lanes(ends, width, -1),
        pad_lanes(own_ids, part, -1),
        rows_dev,
        devices,
        chunks,
        neg_cap,
    )
    neg_slot = slots[-1]
    rel_rows = pad_lanes(rel_ids.reshape(spans, block_len), width, -1)
    asked = lax.all_to_all(message, ("shard", "grp"), split_axis=0, concat_axis=0, tiled=True)
    asked = asked[device ^ jnp.array(mixed(devices), jnp.int32)]
    direct = [asked[:, c * LANES : (c + 1) * LANES] for c in range(chunks)]
    neg_asked = asked[:, -LANES:]

    def negatives_of(back):
        return share_out(spread_neg(back, neg_slot, neg_cap, feature))

    def direct_sent(src_grad, dst_grad, neg_grads):
        sent = collect(src_grad, dst_grad, slots[0], devices, neg_cap)
        return exchange(collect_neg(sent, neg_slot, trade(neg_grads), neg_cap))

    def chunked():
        back = [exchange(gather(table, direct[0], neg_asked, neg_cap))]
        back += [exchange(gather(table, direct[c])) for c in range(1, chunks)]
        negatives = negatives_of(back[0])
        rows = None
        for c in range(chunks):
            rows = spread(back[c], slots[c], rows, feature)
        src_grad, dst_grad, neg_grads = edges(rows, rel_rows, relations, negatives)
        grad = None
        for c in range(1, chunks):
            sent = exchange(collect(src_grad, dst_grad, slots[c], devices))
            grad = add_rows(sent, direct[c], grad, feature, rows_dev)
        sent = direct_sent(src_grad, dst_grad, neg_grads)
        return add_rows(sent, direct[0], grad, feature, rows_dev, neg_asked, neg_cap)

    def pooled():
        start = chunks * LANES
        core = me % RELAYS
        listed = asked[:, start : start + RELAYS * POOL].reshape(devices, RELAYS, POOL)
        listed = listed.transpose(1, 0, 2) - core * rows_dev
        near_list = jnp.where(core == 0, listed[0], listed[1])
        far_list = jnp.where(core == 0, listed[1], listed[0])
        far_list = far_list.reshape(-1, 2, 2, POOL)[:, ::-1]
        near_list, far_list = near_list.reshape(1, -1), far_list.reshape(1, -1)
        small, large = 4, 8
        back = []
        for p in range(0, devices, small):
            sent = gather_blocks(table, direct[0], neg_asked, p, small, neg_cap)
            back += trade_blocks(sent, p, devices)
        far = swap(gather_pool(table, far_list, devices), 1)
        pool = []
        for p in range(0, devices, large):
            pool += trade_blocks(relay_blocks(table, near_list, far, p, large), p, devices)
        rows = None
        for p in range(0, devices, large):
            rows = spread_blocks(back[p : p + large], slots[0], rows, feature, p)
        negatives = share_out(spread_neg_blocks(back, neg_slot, neg_cap, feature))
        for p in range(0, devices, large):
            rows = spread_blocks(pool[p : p + large], slots[chunks], rows, feature, p, True)
        src_grad, dst_grad, neg_grads = edges(rows, rel_rows, relations, negatives)
        neg_grads = trade(neg_grads)
        near = []
        for p in range(0, devices, large):
            sent = collect_pool(src_grad, dst_grad, slots[chunks], p, large)
            near += trade_blocks(sent, p, devices)
        recv = []
        for p in range(0, devices, small):
            sent = collect_blocks(
                src_grad, dst_grad, slots[0], neg_slot, neg_grads, p, small, neg_cap
            )
            recv += trade_blocks(sent, p, devices)
        near = jnp.stack(near)
        grad = add_pool(near, swap(near, 1), [near_list[0], far_list[0]], feature, rows_dev)
        for p in range(0, devices, large):
            grad = add_blocks(recv[p : p + large], direct[0], neg_asked, grad, p, neg_cap)
        return grad

    if chunks == 1 or sharers % RELAYS:
        return chunked().T
    fits = jnp.max(neg_asked[:, -1]) < 0
    return lax.cond(fits, pooled, chunked).T


def solution(mesh):
    placed = (
        P(("shard", "grp"), None),
        P(),
        P(("shard", "grp")),
        P(("shard", "grp")),
        P(("shard", "grp")),
        P("shard", None),
    )
    return jax.shard_map(
        body, mesh=mesh, in_specs=placed, out_specs=P(("shard", "grp"), None), check_vma=False
    )
```

```python
import functools

import jax
import jax.numpy as jnp
from jax import lax
from jax.experimental import pallas as pl
from jax.experimental.pallas import tpu as pltpu
from jax.sharding import PartitionSpec as P

LANES = 128
POOL = 48
RELAYS = 4
SMALL = 32
VMEM_BYTES = 56 << 20
F32 = jnp.float32
BF16 = jnp.bfloat16
NN = (((1,), (0,)), ((), ()))
NT = (((1,), (1,)), ((), ()))
TN = (((0,), (0,)), ((), ()))


def round_up(value, unit):
    return -(-value // unit) * unit


def dot(left, right, dims):
    return lax.dot_general(left, right, dims, preferred_element_type=F32)


def one_hot(rows, row, base=0):
    places = lax.broadcasted_iota(jnp.int32, (rows, row.shape[1]), 0) + base
    return jnp.where(places == row, 1.0, 0.0).astype(BF16)


def call(kernel, name, flops, nbytes, **kwargs):
    return pl.pallas_call(
        kernel,
        name=name,
        compiler_params=pltpu.CompilerParams(vmem_limit_bytes=VMEM_BYTES),
        cost_estimate=pl.CostEstimate(flops=flops, bytes_accessed=nbytes, transcendentals=0),
        **kwargs,
    )


def ranks(members, mixer):
    groups = members[0].shape[0]
    both = dot(jnp.concatenate(members, axis=0).astype(BF16), mixer, NN)
    taken = jnp.zeros((groups, LANES), F32)
    found = []
    for i, member in enumerate(members):
        chunk = both[i * groups : (i + 1) * groups]
        found.append(jnp.sum((chunk[:, :LANES] + taken) * member, axis=0, keepdims=True))
        taken = taken + chunk[:, LANES:]
    return [rank.astype(jnp.int32) for rank in found], taken


def fill(members, codes, places, count):
    groups = members[0].shape[0]
    high = [m * (c // LANES).astype(F32) for m, c in zip(members, codes)]
    low = [m * (c % LANES).astype(F32) for m, c in zip(members, codes)]
    left = jnp.concatenate(
        [jnp.concatenate(high, axis=1), jnp.concatenate(low, axis=1)], axis=0
    ).astype(BF16)
    sums = dot(left, one_hot(count, jnp.concatenate(places, axis=1)), NT)
    return (LANES * sums[:groups] + sums[groups:]).astype(jnp.int32) - 1


def slots_kernel(ends_ref, own_ref, *refs, rows_dev, devices, chunks, neg_cap):
    msg_ref = refs[0]
    slot_refs = refs[1 : 1 + chunks]
    pool_ref, busy_ref = refs[1 + chunks : 3 + chunks] if chunks > 1 else (None, None)
    neg_ref = refs[-1]
    row = lax.broadcasted_iota(jnp.int32, (LANES, 2 * LANES), 0)
    lane = lax.broadcasted_iota(jnp.int32, (LANES, 2 * LANES), 1)
    mixer = jnp.where(row < lane, 1.0, 0.0).astype(BF16)
    owners = lax.broadcasted_iota(jnp.int32, (devices, LANES), 0)

    def prepare(ids_ref):
        where, holder, codes, members = [], [], [], []
        for segment in range(ids_ref.shape[0]):
            for start in range(0, ids_ref.shape[1], LANES):
                ids = ids_ref[segment : segment + 1, start : start + LANES]
                owner = jnp.where(ids >= 0, ids // rows_dev, -1)
                where.append((slice(segment, segment + 1), slice(start, start + LANES)))
                holder.append(owner)
                codes.append(jnp.where(ids >= 0, ids - owner * rows_dev + 1, 0))
                members.append(jnp.where(owners == owner, 1.0, 0.0))
        found, _ = ranks(members, mixer)
        return where, holder, codes, members, found

    where, holder, codes, members, found = prepare(ends_ref)
    for chunk in range(chunks):
        places = []
        for at, owner, rank in zip(where, holder, found):
            place = rank - chunk * LANES
            place = jnp.where((owner >= 0) & (place >= 0) & (place < LANES), place, -1)
            slot_refs[chunk][at] = jnp.where(place >= 0, owner * LANES + place, -1)
            places.append(place)
        msg_ref[:, chunk * LANES : (chunk + 1) * LANES] = fill(members, codes, places, LANES)
    offset = chunks * LANES
    flag = jnp.full((1, 1), -1, jnp.int32)
    if chunks > 1:
        shards = devices // RELAYS
        room = RELAYS * POOL
        shard_rows = lax.broadcasted_iota(jnp.int32, (shards, LANES), 0)
        spilled, spill_codes = [], []
        for owner, code, rank in zip(holder, codes, found):
            shard = jnp.where(rank >= LANES, owner // RELAYS, -1)
            spilled.append(jnp.where(shard_rows == shard, 1.0, 0.0))
            spill_codes.append(code + (owner % RELAYS) * rows_dev)
        pooled, taken = ranks(spilled, mixer)
        places = []
        for at, owner, rank, place in zip(where, holder, found, pooled):
            inside = (owner >= 0) & (rank >= LANES) & (place < room)
            compact = jnp.where(
                place < SMALL, owner // RELAYS * SMALL + place, (shards - 1) * SMALL + place
            )
            pool_ref[at] = jnp.where(inside, compact, -1)
            places.append(jnp.where(inside, place, -1))
        listed = fill(spilled, spill_codes, places, 2 * LANES)
        for shard in range(shards):
            msg_ref[shard * RELAYS : (shard + 1) * RELAYS, offset : offset + 2 * LANES] = (
                jnp.broadcast_to(listed[shard : shard + 1], (RELAYS, 2 * LANES))
            )
        offset += 2 * LANES
        most = jnp.max(taken, axis=0, keepdims=True)
        busy = jnp.where(taken > SMALL, 1.0, 0.0)
        crowded = jnp.sum(busy, axis=0, keepdims=True) > 1.0
        flag = jnp.where((most > room) | crowded, 1, -1)[:, :1]
        busy_ref[...] = jnp.sum(busy * shard_rows.astype(F32), axis=0, keepdims=True).astype(
            jnp.int32
        )[:, :1]

    where, holder, codes, members, found = prepare(own_ref)
    for at, owner, rank in zip(where, holder, found):
        neg_ref[at] = jnp.where(owner >= 0, owner * neg_cap + rank, -1)
    places = [jnp.where(owner >= 0, rank, -1) for owner, rank in zip(holder, found)]
    listed = fill(members, codes, places, LANES)
    lanes = lax.broadcasted_iota(jnp.int32, listed.shape, 1)
    msg_ref[:, offset:] = jnp.where(lanes == LANES - 1, flag, listed)


def make_slots(ends, own, rows_dev, devices, chunks, neg_cap):
    pooled = chunks > 1
    width = (chunks + 1 + 2 * pooled) * LANES
    return call(
        functools.partial(
            slots_kernel,
            rows_dev=rows_dev,
            devices=devices,
            chunks=chunks,
            neg_cap=neg_cap,
        ),
        "slots",
        16 * devices * LANES * ends.size,
        8 * ends.size,
        out_shape=[jax.ShapeDtypeStruct((devices, width), jnp.int32)]
        + [jax.ShapeDtypeStruct(ends.shape, jnp.int32)] * (chunks + pooled)
        + [jax.ShapeDtypeStruct((1, 1), jnp.int32)] * pooled
        + [jax.ShapeDtypeStruct(own.shape, jnp.int32)],
    )(ends, own)


def packed_height(count, feature):
    return feature // LANES * count + feature % LANES


def pack(out_ref, at, start, rows, tail):
    count, feature = rows.shape
    for piece in range(feature // LANES):
        out_ref[at, start + piece * count : start + (piece + 1) * count, :] = rows[
            :, piece * LANES : (piece + 1) * LANES
        ].astype(out_ref.dtype)
    tail = jnp.concatenate([tail, jnp.zeros((tail.shape[0], LANES - count), tail.dtype)], axis=1)
    end = start + packed_height(count, feature)
    out_ref[at, end - tail.shape[0] : end, :] = tail.astype(out_ref.dtype)


def pack_all(out_ref, start, count, rows, turned):
    feature = rows.shape[1]
    first = feature // LANES * LANES
    for i in range(out_ref.shape[0]):
        at = slice(i * count, (i + 1) * count)
        pack(out_ref, i, start, rows[at], turned[first:, at])


def unpack_all(in_ref, start, count, rows_ref, flat_ref):
    feature = flat_ref.shape[0]
    pieces = feature // LANES
    end = start + packed_height(count, feature)
    devices = in_ref.shape[0]
    for d in range(devices):
        for piece in range(pieces):
            rows_ref[d * count : (d + 1) * count, piece * LANES : (piece + 1) * LANES] = in_ref[
                d, start + piece * count : start + (piece + 1) * count, :
            ]
    tails = [
        in_ref[d, end - feature % LANES : end, :].astype(F32)[:, :count] for d in range(devices)
    ]
    flat_ref[: pieces * LANES] = rows_ref[...].astype(F32).T.astype(BF16)
    flat_ref[pieces * LANES :] = jnp.concatenate(tails, axis=1).astype(BF16)


def unpack_scratch(devices, count, feature):
    return [
        pltpu.VMEM((devices * count, feature // LANES * LANES), BF16),
        pltpu.VMEM((feature, devices * count), BF16),
    ]


def gather_kernel(table_ref, *refs, group, neg_cap):
    feature, rows_dev = table_ref.shape
    first = pl.program_id(0) * group
    req_ref, out_ref = refs[0], refs[-1]
    row = [req_ref[pl.ds(first + i, 1), :] for i in range(group)]
    if neg_cap:
        row += [refs[1][pl.ds(first + i, 1), :neg_cap] for i in range(group)]
    rows = dot(table_ref[...], one_hot(rows_dev, jnp.concatenate(row, axis=1)), NN)
    start = out_ref.shape[1] - feature
    for i in range(group):
        out_ref[i, start:] = rows[:, i * LANES : (i + 1) * LANES].astype(BF16)
    if neg_cap:
        neg = rows[:, group * LANES :]
        pack_all(out_ref, 0, neg_cap, neg.T, neg)


def gather(table, requests, neg_requests=None, neg_cap=0):
    feature, rows_dev = table.shape
    devices = requests.shape[0]
    group = 4
    height = feature + (packed_height(neg_cap, feature) if neg_cap else 0)
    slots = devices * (LANES + neg_cap)
    whole = pl.BlockSpec((devices, LANES), lambda i: (0, 0))
    return call(
        functools.partial(gather_kernel, group=group, neg_cap=neg_cap),
        "gather_rows",
        2 * feature * rows_dev * slots,
        2 * feature * (rows_dev + slots),
        grid=(devices // group,),
        in_specs=[pl.BlockSpec((feature, rows_dev), lambda i: (0, 0)), whole]
        + ([whole] if neg_cap else []),
        out_specs=pl.BlockSpec((group, height, LANES), lambda i: (i, 0, 0)),
        out_shape=jax.ShapeDtypeStruct((devices, height, LANES), BF16),
    )(table, requests, *([neg_requests] if neg_cap else []))


def gather_pool_kernel(table_ref, req_ref, out_ref, *, group):
    rows_dev = table_ref.shape[1]
    row = req_ref[...].reshape(1, group * POOL)
    rows = dot(table_ref[...], one_hot(rows_dev, row), NN)
    pack_all(out_ref, 0, POOL, rows.T, rows)


def gather_pool(table, requests, devices):
    feature, rows_dev = table.shape
    group = 8
    steps = devices // group
    height = packed_height(POOL, feature)
    return call(
        functools.partial(gather_pool_kernel, group=group),
        "gather_pool",
        2 * feature * rows_dev * requests.size,
        2 * feature * (rows_dev + requests.size),
        grid=(steps,),
        in_specs=[
            pl.BlockSpec((feature, rows_dev), lambda i: (0, 0)),
            pl.BlockSpec((1, 1, group * POOL), lambda i: (i, 0, 0)),
        ],
        out_specs=pl.BlockSpec((group, height, LANES), lambda i: (i, 0, 0)),
        out_shape=jax.ShapeDtypeStruct((devices, height, LANES), BF16),
    )(table, requests.reshape(steps, 1, group * POOL))


def spread_neg_kernel(back_ref, slot_ref, out_ref, rows, flat, *, cap):
    unpack_all(back_ref, 0, cap, rows, flat)
    for part in range(slot_ref.shape[0]):
        hot = one_hot(flat.shape[1], slot_ref[part : part + 1, :])
        out_ref[part] = dot(flat[...], hot, NN).T.astype(BF16)


def spread_neg(back, slot, cap, feature):
    devices = back.shape[0]
    parts, width = slot.shape
    height = packed_height(cap, feature)
    return call(
        functools.partial(spread_neg_kernel, cap=cap),
        "spread_negatives",
        2 * devices * cap * feature * slot.size,
        2 * devices * cap * feature,
        grid=(1,),
        in_specs=[
            pl.BlockSpec((devices, height, LANES), lambda i: (0, 0, 0)),
            pl.BlockSpec(slot.shape, lambda i: (0, 0)),
        ],
        out_specs=pl.BlockSpec((parts, width, feature), lambda i: (0, 0, 0)),
        out_shape=jax.ShapeDtypeStruct((parts, width, feature), BF16),
        scratch_shapes=unpack_scratch(devices, cap, feature),
    )(back, slot)


def spread_kernel(*refs, first):
    back_ref, slot_ref = refs[:2]
    so_far_ref = None if first else refs[2]
    out_ref, flat = refs[2 + (not first)], refs[-1]
    devices = back_ref.shape[0]
    feature = flat.shape[0]

    @pl.when(pl.program_id(0) == 0)
    def _():
        start = back_ref.shape[1] - feature
        for d in range(devices):
            flat[:, d * LANES : (d + 1) * LANES] = back_ref[d, start:]

    row = slot_ref[...].reshape(1, slot_ref.shape[-1])
    rows = dot(flat[...], one_hot(flat.shape[1], row), NN)
    if not first:
        rows = rows + so_far_ref[...].astype(F32)
    out_ref[...] = rows.astype(BF16)


def spread(back, slot, so_far, feature):
    devices = back.shape[0]
    segments, width = slot.shape
    slots = devices * LANES
    tile = 512 if slots <= 4096 else 128
    steps = width // tile
    rows_spec = pl.BlockSpec((feature, tile), lambda i: (0, i))
    extra = [] if so_far is None else [so_far]
    return call(
        functools.partial(spread_kernel, first=so_far is None),
        "spread_rows",
        2 * feature * slots * slot.size,
        2 * feature * (slots + slot.size),
        grid=(segments * steps,),
        in_specs=[
            pl.BlockSpec(back.shape, lambda i: (0, 0, 0)),
            pl.BlockSpec((1, 1, tile), lambda i: (i // steps, 0, i % steps)),
        ]
        + [rows_spec] * len(extra),
        out_specs=rows_spec,
        out_shape=jax.ShapeDtypeStruct((feature, slot.size), BF16),
        scratch_shapes=[pltpu.VMEM((feature, slots), BF16)],
    )(back, slot.reshape(segments, 1, width), *extra)


def compact_places(shards):
    places = [(shard, 0, 0, SMALL, shard * SMALL) for shard in range(shards)]
    to = shards * SMALL
    for relay in range(RELAYS):
        first = 0 if relay else SMALL
        places.append((None, relay, first, POOL - first, to))
        to += POOL - first
    return places


def compact_size(shards):
    return shards * SMALL + RELAYS * POOL - SMALL


def compact_pool(back_ref, busy, rows_ref, flat_ref):
    feature = flat_ref.shape[0]
    pieces = feature // LANES
    tails = []
    for shard, relay, first, count, to in compact_places(back_ref.shape[0] // RELAYS):
        at = (busy if shard is None else shard) * RELAYS + relay
        for piece in range(pieces):
            start = piece * POOL + first
            rows_ref[to : to + count, piece * LANES : (piece + 1) * LANES] = back_ref[
                at, start : start + count, :
            ]
        tail = back_ref[at, pieces * POOL :, :].astype(F32)
        tails.append(tail[:, first : first + count])
    flat_ref[: pieces * LANES] = rows_ref[...].astype(F32).T.astype(BF16)
    flat_ref[pieces * LANES :] = jnp.concatenate(tails, axis=1).astype(BF16)


def expand_pool(rows, busy, out_ref):
    feature = rows.shape[1]
    pieces = feature // LANES
    turned = rows.T
    out_ref[...] = jnp.zeros(out_ref.shape, out_ref.dtype)
    shards = out_ref.shape[0] // RELAYS
    for shard, relay, first, count, to in compact_places(shards):
        at = (busy if shard is None else shard) * RELAYS + relay
        for piece in range(pieces):
            start = piece * POOL + first
            out_ref[at, start : start + count, :] = rows[
                to : to + count, piece * LANES : (piece + 1) * LANES
            ].astype(BF16)
        if shard is not None:
            tail = turned[pieces * LANES :, to : to + count]
        else:
            small = turned[pieces * LANES :, : shards * SMALL]
            tail = turned[pieces * LANES :, to : to + count]
            if first:
                kept = jnp.zeros((feature % LANES, first), F32)
                for other in range(shards):
                    part = small[:, other * SMALL : (other + 1) * SMALL]
                    kept = jnp.where(busy == other, part, kept)
                tail = jnp.concatenate([kept, tail], axis=1)
        blank = jnp.zeros((tail.shape[0], LANES - tail.shape[1]), F32)
        out_ref[at, pieces * POOL :, :] = jnp.concatenate([tail, blank], axis=1).astype(BF16)


def edges_kernel(*refs, parts, pooled):
    refs = list(refs)
    src_ref, dst_ref, rel_ids_ref, rel_ref = refs[:4]
    neg_refs = refs[4 : 4 + parts]
    refs = refs[4 + parts :]
    if pooled:
        back_ref, src_slot_ref, dst_slot_ref, busy_ref = refs[:4]
        refs = refs[4:]
        pool_out_ref = refs.pop(2 + parts)
        pool_rows, pool_flat, pool_sums = refs[-3:]
    src_grad_ref, dst_grad_ref = refs[:2]
    neg_grad_refs = refs[2 : 2 + parts]
    negatives, turned, sums = refs[2 + parts : 5 + parts]
    block, step = pl.program_id(0), pl.program_id(1)
    last = step == pl.num_programs(1) - 1
    part = neg_refs[0].shape[1]

    if pooled:

        @pl.when((block == 0) & (step == 0))
        def _():
            compact_pool(back_ref, busy_ref[0, 0], pool_rows, pool_flat)
            pool_sums[...] = jnp.zeros(pool_sums.shape, F32)

    @pl.when(step == 0)
    def _():
        for k in range(parts):
            negatives[k * part : (k + 1) * part] = neg_refs[k][0]
        turned[...] = negatives[...].astype(F32).T.astype(BF16)

    hot = one_hot(rel_ref.shape[1], rel_ids_ref[...].reshape(1, rel_ids_ref.shape[-1]))
    table = rel_ref[...]
    relation = jnp.zeros(src_ref.shape, F32)
    for _ in range(3):
        piece = table.astype(BF16)
        relation = relation + dot(piece, hot, NN)
        table = table - piece.astype(F32)
    source = src_ref[...].astype(F32)
    target = dst_ref[...].astype(F32)
    if pooled:
        count = pool_flat.shape[1]
        src_hot = one_hot(count, src_slot_ref[...].reshape(1, src_slot_ref.shape[-1]))
        dst_hot = one_hot(count, dst_slot_ref[...].reshape(1, dst_slot_ref.shape[-1]))
        source = source + dot(pool_flat[...], src_hot, NN)
        target = target + dot(pool_flat[...], dst_hot, NN)
    product = source * relation
    positive = jnp.sum(product * target, axis=0, keepdims=True)
    pos_weight = -jax.nn.sigmoid(-positive)
    query = product.astype(BF16)
    weight = jax.nn.sigmoid(dot(negatives[...], query, NN)).astype(BF16)
    gathered = dot(turned[...], weight, NN)
    src_grad = (relation * (pos_weight * target + gathered)).astype(BF16)
    dst_grad = (pos_weight * product).astype(BF16)
    src_grad_ref[...] = src_grad
    dst_grad_ref[...] = dst_grad
    neg_grad = dot(weight, query, NT)
    if pooled:
        pool_sums[...] += dot(src_hot, src_grad, NT) + dot(dst_hot, dst_grad, NT)

    @pl.when(step == 0)
    def _():
        sums[...] = neg_grad

    @pl.when(step != 0)
    def _():
        sums[...] += neg_grad

    @pl.when(last)
    def _():
        for k in range(parts):
            neg_grad_refs[k][0] = sums[k * part : (k + 1) * part].astype(BF16)

    if pooled:

        @pl.when(last & (block == pl.num_programs(0) - 1))
        def _():
            expand_pool(pool_sums[...], busy_ref[0, 0], pool_out_ref)


def edges(rows, rel_ids, relations, negatives, pool=None, pool_slot=None, busy=None):
    feature, endpoints = rows.shape
    parts = len(negatives)
    spans, part, _ = negatives[0].shape
    width = rel_ids.shape[1]
    tile = 512
    steps = width // tile
    blocks = spans * steps
    edge_spec = pl.BlockSpec((feature, tile), lambda b, i: (0, b * steps + i))
    neg_spec = pl.BlockSpec((1, part, feature), lambda b, i: (b, 0, 0))
    operands = [rows, rows, rel_ids.reshape(spans, 1, width), relations, *negatives]
    specs = [
        edge_spec,
        pl.BlockSpec((feature, tile), lambda b, i: (0, blocks + b * steps + i)),
        pl.BlockSpec((1, 1, tile), lambda b, i: (b, 0, i)),
        pl.BlockSpec(relations.shape, lambda b, i: (0, 0)),
    ] + [neg_spec] * parts
    out_specs = [edge_spec, edge_spec] + [neg_spec] * parts
    out_shape = [jax.ShapeDtypeStruct((feature, endpoints // 2), BF16)] * 2
    out_shape += [jax.ShapeDtypeStruct((spans, part, feature), BF16)] * parts
    scratch = [
        pltpu.VMEM((parts * part, feature), BF16),
        pltpu.VMEM((feature, parts * part), BF16),
        pltpu.VMEM((parts * part, feature), F32),
    ]
    if pool is not None:
        slot = pool_slot.reshape(2 * spans, 1, width)
        pool_spec = pl.BlockSpec(pool.shape, lambda b, i: (0, 0, 0))
        operands += [pool, slot, slot, busy]
        specs += [
            pool_spec,
            pl.BlockSpec((1, 1, tile), lambda b, i: (b, 0, i)),
            pl.BlockSpec((1, 1, tile), lambda b, i: (spans + b, 0, i)),
            pl.BlockSpec(memory_space=pltpu.SMEM),
        ]
        out_specs.append(pool_spec)
        out_shape.append(jax.ShapeDtypeStruct(pool.shape, BF16))
        count = compact_size(pool.shape[0] // RELAYS)
        scratch += [
            pltpu.VMEM((count, feature // LANES * LANES), BF16),
            pltpu.VMEM((feature, count), BF16),
            pltpu.VMEM((count, feature), F32),
        ]
    src_grad, dst_grad, *rest = call(
        functools.partial(edges_kernel, parts=parts, pooled=pool is not None),
        "edges",
        6 * feature * parts * part * spans * width,
        4 * (rows.size + parts * negatives[0].size),
        grid=(spans, steps),
        in_specs=specs,
        out_specs=out_specs,
        out_shape=out_shape,
        scratch_shapes=scratch,
    )(*operands)
    return src_grad, dst_grad, rest


def collect_kernel(src_ref, dst_ref, slot_ref, out_ref, *, group):
    segments, width = slot_ref.shape
    feature = src_ref.shape[0]
    step = pl.program_id(0)
    total = jnp.zeros((feature, group * LANES), F32)
    for segment in range(segments):
        grads = src_ref if segment < segments // 2 else dst_ref
        start = segment % (segments // 2) * width
        hot = one_hot(group * LANES, slot_ref[segment : segment + 1, :], step * group * LANES)
        total = total + dot(grads[:, start : start + width], hot, NT)
    total = total.astype(BF16)
    first = out_ref.shape[1] - feature
    for i in range(group):
        out_ref[i, first:] = total[:, i * LANES : (i + 1) * LANES]


def collect(src_grad, dst_grad, slot, devices, neg_cap=0):
    feature = src_grad.shape[0]
    group = 4
    slots = devices * LANES
    height = feature + (packed_height(neg_cap, feature) if neg_cap else 0)
    whole = pl.BlockSpec(src_grad.shape, lambda i: (0, 0))
    return call(
        functools.partial(collect_kernel, group=group),
        "collect_grads",
        2 * feature * slots * slot.size,
        2 * feature * (slots + slot.size),
        grid=(devices // group,),
        in_specs=[whole, whole, pl.BlockSpec(slot.shape, lambda i: (0, 0))],
        out_specs=pl.BlockSpec((group, height, LANES), lambda i: (i, 0, 0)),
        out_shape=jax.ShapeDtypeStruct((devices, height, LANES), BF16),
    )(src_grad, dst_grad, slot)


def collect_neg_kernel(sent_ref, slot_ref, *refs, group, cap):
    grad_refs, out_ref, sums = refs[:-2], refs[-2], refs[-1]
    step = pl.program_id(0)

    @pl.when(step == 0)
    def _():
        total = grad_refs[0][...].astype(F32)
        for grad_ref in grad_refs[1:]:
            total = total + grad_ref[...].astype(F32)
        sums[...] = total.astype(BF16)

    rows = jnp.zeros((group * cap, sums.shape[-1]), F32)
    for part in range(slot_ref.shape[0]):
        hot = one_hot(group * cap, slot_ref[part : part + 1, :], step * group * cap)
        rows = rows + dot(hot, sums[part], NN)
    pack_all(out_ref, 0, cap, rows, rows.T)


def collect_neg(sent, slot, grads, cap):
    devices = sent.shape[0]
    feature = grads[0].shape[-1]
    group = 16
    height = packed_height(cap, feature)
    return call(
        functools.partial(collect_neg_kernel, group=group, cap=cap),
        "collect_negatives",
        2 * devices * cap * feature * slot.size,
        4 * len(grads) * grads[0].size,
        grid=(devices // group,),
        in_specs=[
            pl.BlockSpec(memory_space=pl.ANY),
            pl.BlockSpec(slot.shape, lambda i: (0, 0)),
        ]
        + [pl.BlockSpec(grads[0].shape, lambda i: (0, 0, 0))] * len(grads),
        out_specs=pl.BlockSpec((group, height, LANES), lambda i: (i, 0, 0)),
        out_shape=jax.ShapeDtypeStruct(sent.shape, BF16),
        scratch_shapes=[pltpu.VMEM(grads[0].shape, BF16)],
        input_output_aliases={0: 0},
    )(sent, slot, *grads)


def add_kernel(*refs, rows, neg_cap, first):
    refs = list(refs)
    recv_ref, req_ref = refs[:2]
    refs = refs[2:]
    if neg_cap:
        neg_req_ref = refs.pop(0)
        neg_rows, neg_flat = refs[-2:]
    if not first:
        so_far_ref = refs.pop(0)
    out_ref, flat = refs[:2]
    devices = recv_ref.shape[0]
    feature = flat.shape[0]
    step = pl.program_id(0)

    @pl.when(step == 0)
    def _():
        start = recv_ref.shape[1] - feature
        for d in range(devices):
            flat[:, d * LANES : (d + 1) * LANES] = recv_ref[d, start:]
        if neg_cap:
            unpack_all(recv_ref, 0, neg_cap, neg_rows, neg_flat)

    base = step * rows
    row = jnp.concatenate([req_ref[d : d + 1, :] for d in range(devices)], axis=1)
    total = dot(flat[...], one_hot(rows, row, base), NT)
    if neg_cap:
        row = jnp.concatenate([neg_req_ref[d : d + 1, :neg_cap] for d in range(devices)], axis=1)
        total = total + dot(neg_flat[...], one_hot(rows, row, base), NT)
    if not first:
        total = total + so_far_ref[...]
    out_ref[...] = total


def add_rows(recv, requests, so_far, feature, rows_dev, neg_requests=None, neg_cap=0):
    devices = recv.shape[0]
    rows = 512 if devices * LANES <= 4096 else 128
    slots = devices * LANES
    whole_req = pl.BlockSpec((devices, LANES), lambda i: (0, 0))
    rows_spec = pl.BlockSpec((feature, rows), lambda i: (0, i))
    operands = [recv, requests]
    specs = [pl.BlockSpec(recv.shape, lambda i: (0, 0, 0)), whole_req]
    scratch = [pltpu.VMEM((feature, slots), BF16)]
    if neg_cap:
        operands.append(neg_requests)
        specs.append(whole_req)
        scratch += unpack_scratch(devices, neg_cap, feature)
    if so_far is not None:
        operands.append(so_far)
        specs.append(rows_spec)
    return call(
        functools.partial(add_kernel, rows=rows, neg_cap=neg_cap, first=so_far is None),
        "add_grads",
        2 * feature * slots * rows_dev,
        2 * feature * slots + 8 * feature * rows_dev,
        grid=(rows_dev // rows,),
        in_specs=specs,
        out_specs=rows_spec,
        out_shape=jax.ShapeDtypeStruct((feature, rows_dev), F32),
        scratch_shapes=scratch,
    )(*operands)


def add_pool_kernel(*refs, rows, first):
    one_ref, two_ref, one_req_ref, two_req_ref = refs[:4]
    out_ref, packed, *flats = refs[4 + (not first) :]
    step = pl.program_id(0)

    @pl.when(step == 0)
    def _():
        for recv_ref, flat in zip((one_ref, two_ref), flats):
            unpack_all(recv_ref, 0, POOL, packed, flat)

    total = dot(flats[0][...], one_hot(rows, one_req_ref[...], step * rows), NT)
    total = total + dot(flats[1][...], one_hot(rows, two_req_ref[...], step * rows), NT)
    if not first:
        total = total + refs[4][...]
    out_ref[...] = total


def add_pool(one, two, requests, so_far, feature, rows_dev):
    rows = 512
    devices = one.shape[0]
    slots = devices * POOL
    recv_spec = pl.BlockSpec(one.shape, lambda i: (0, 0, 0))
    req_spec = pl.BlockSpec((1, slots), lambda i: (0, 0))
    rows_spec = pl.BlockSpec((feature, rows), lambda i: (0, i))
    packed, flat = unpack_scratch(devices, POOL, feature)
    extra = [] if so_far is None else [so_far]
    return call(
        functools.partial(add_pool_kernel, rows=rows, first=so_far is None),
        "add_pool",
        4 * feature * slots * rows_dev,
        4 * feature * slots + 4 * feature * rows_dev,
        grid=(rows_dev // rows,),
        in_specs=[recv_spec, recv_spec, req_spec, req_spec] + [rows_spec] * len(extra),
        out_specs=rows_spec,
        out_shape=jax.ShapeDtypeStruct((feature, rows_dev), F32),
        scratch_shapes=[packed, flat, flat],
    )(one, two, requests[0][None], requests[1][None], *extra)


def after(value, other):
    anywhere = pl.BlockSpec(memory_space=pl.ANY)
    return call(
        lambda value_ref, other_ref, out_ref: None,
        "after",
        0,
        0,
        in_specs=[anywhere, anywhere],
        out_specs=anywhere,
        out_shape=jax.ShapeDtypeStruct(value.shape, value.dtype),
        input_output_aliases={0: 0},
    )(value, other)


def exchange(value):
    return lax.all_to_all(value, ("shard", "grp"), split_axis=0, concat_axis=0, tiled=True)


def swap(value, bit):
    sharers = lax.axis_size("grp")
    return lax.ppermute(value, "grp", [(i, i ^ bit) for i in range(sharers)])


def share_out(value):
    return [value] + [swap(value, k) for k in range(1, lax.axis_size("grp"))]


def trade(blocks):
    return blocks[:1] + [swap(block, k) for k, block in enumerate(blocks) if k]


def pad_lanes(value, width, fill):
    return jnp.pad(value, ((0, 0), (0, width - value.shape[1])), constant_values=fill)


def body(entity_table, rel_diag, src_ids, dst_ids, rel_ids, neg_ids):
    rows_dev, feature = entity_table.shape
    sharers = lax.axis_size("grp")
    devices = lax.axis_size("shard") * sharers
    spans, neg_count = neg_ids.shape
    edge_count = src_ids.shape[0]
    block_len = edge_count // spans
    edge_cap = 4 * edge_count // devices
    chunks = round_up(edge_cap, LANES) // LANES
    part_width = neg_count // sharers
    neg_cap = round_up(2 * spans * part_width // devices, 16)
    width = round_up(block_len, 512)
    part = round_up(part_width, LANES)
    me = lax.axis_index("grp")

    table = entity_table.T.astype(BF16)
    relations = rel_diag.T
    own_ids = lax.dynamic_slice_in_dim(neg_ids, me * part_width, part_width, 1)
    ends = jnp.concatenate(
        [src_ids.reshape(spans, block_len), dst_ids.reshape(spans, block_len)]
    )
    message, *slots = make_slots(
        pad_lanes(ends, width, -1),
        pad_lanes(own_ids, part, -1),
        rows_dev,
        devices,
        chunks,
        neg_cap,
    )
    neg_slot = slots[-1]
    busy = slots[-2]
    rel_rows = pad_lanes(rel_ids.reshape(spans, block_len), width, -1)
    asked = exchange(message)
    direct = [asked[:, c * LANES : (c + 1) * LANES] for c in range(chunks)]
    neg_asked = asked[:, -LANES:]

    def negatives_of(back):
        return share_out(spread_neg(back, neg_slot, neg_cap, feature))

    def direct_sent(src_grad, dst_grad, neg_grads):
        sent = collect(src_grad, dst_grad, slots[0], devices, neg_cap)
        return exchange(collect_neg(sent, neg_slot, trade(neg_grads), neg_cap))

    def chunked():
        back = [exchange(gather(table, direct[0], neg_asked, neg_cap))]
        back += [exchange(gather(table, direct[c])) for c in range(1, chunks)]
        negatives = negatives_of(back[0])
        rows = None
        for c in range(chunks):
            rows = spread(back[c], slots[c], rows, feature)
        src_grad, dst_grad, neg_grads = edges(rows, rel_rows, relations, negatives)
        grad = None
        for c in range(1, chunks):
            sent = exchange(collect(src_grad, dst_grad, slots[c], devices))
            grad = add_rows(sent, direct[c], grad, feature, rows_dev)
        sent = direct_sent(src_grad, dst_grad, neg_grads)
        return add_rows(sent, direct[0], grad, feature, rows_dev, neg_asked, neg_cap)

    def pooled():
        start = chunks * LANES
        listed = asked[:, start : start + RELAYS * POOL].reshape(devices, RELAYS, POOL)
        listed = listed.transpose(1, 0, 2).reshape(RELAYS, devices * POOL) - me * rows_dev
        listed = listed[me ^ jnp.arange(RELAYS, dtype=jnp.int32)]
        back = exchange(gather(table, direct[0], neg_asked, neg_cap))
        far = swap(gather_pool(table, listed[3], devices), 1)
        far = swap(gather_pool(table, listed[2], devices) + far, 2)
        near = swap(gather_pool(table, listed[1], devices), 1)
        near = gather_pool(table, listed[0], devices) + near
        negatives = negatives_of(back)
        rows = spread(back, slots[0], None, feature)
        src_grad, dst_grad, rest = edges(
            rows, rel_rows, relations, negatives, exchange(near + far), slots[chunks], busy
        )
        neg_grads, pool = rest[:-1], rest[-1]
        near = exchange(pool)
        far = swap(near, 2)
        sent = direct_sent(src_grad, dst_grad, neg_grads)
        grad = add_pool(near, swap(near, 1), listed[:2], None, feature, rows_dev)
        far = after(far, grad)
        grad = add_pool(far, swap(far, 1), listed[2:], grad, feature, rows_dev)
        return add_rows(sent, direct[0], grad, feature, rows_dev, neg_asked, neg_cap)

    if chunks == 1 or sharers != RELAYS:
        return chunked().T
    fits = jnp.max(neg_asked[:, -1]) < 0
    return lax.cond(fits, pooled, chunked).T


def solution(mesh):
    placed = (
        P(("shard", "grp"), None),
        P(),
        P(("shard", "grp")),
        P(("shard", "grp")),
        P(("shard", "grp")),
        P("shard", None),
    )
    return jax.shard_map(
        body, mesh=mesh, in_specs=placed, out_specs=P(("shard", "grp"), None), check_vma=False
    )
```

```python
import functools

import jax
import jax.numpy as jnp
from jax import lax
from jax.experimental import pallas as pl
from jax.experimental.pallas import tpu as pltpu
from jax.sharding import PartitionSpec as P

LANES = 128
POOL = 48
RELAYS = 4
SMALL = 32
VMEM_BYTES = 56 << 20
F32 = jnp.float32
BF16 = jnp.bfloat16
NN = (((1,), (0,)), ((), ()))
NT = (((1,), (1,)), ((), ()))
TN = (((0,), (0,)), ((), ()))


def round_up(value, unit):
    return -(-value // unit) * unit


def dot(left, right, dims):
    return lax.dot_general(left, right, dims, preferred_element_type=F32)


def one_hot(rows, row, base=0):
    places = lax.broadcasted_iota(jnp.int32, (rows, row.shape[1]), 0) + base
    return jnp.where(places == row, 1.0, 0.0).astype(BF16)


def call(kernel, name, flops, nbytes, **kwargs):
    return pl.pallas_call(
        kernel,
        name=name,
        compiler_params=pltpu.CompilerParams(vmem_limit_bytes=VMEM_BYTES),
        cost_estimate=pl.CostEstimate(flops=flops, bytes_accessed=nbytes, transcendentals=0),
        **kwargs,
    )


def ranks(members, mixer):
    groups = members[0].shape[0]
    both = dot(jnp.concatenate(members, axis=0).astype(BF16), mixer, NN)
    taken = jnp.zeros((groups, LANES), F32)
    found = []
    for i, member in enumerate(members):
        chunk = both[i * groups : (i + 1) * groups]
        found.append(jnp.sum((chunk[:, :LANES] + taken) * member, axis=0, keepdims=True))
        taken = taken + chunk[:, LANES:]
    return [rank.astype(jnp.int32) for rank in found], taken


def fill(members, codes, places, count):
    groups = members[0].shape[0]
    high = [m * (c // LANES).astype(F32) for m, c in zip(members, codes)]
    low = [m * (c % LANES).astype(F32) for m, c in zip(members, codes)]
    left = jnp.concatenate(
        [jnp.concatenate(high, axis=1), jnp.concatenate(low, axis=1)], axis=0
    ).astype(BF16)
    sums = dot(left, one_hot(count, jnp.concatenate(places, axis=1)), NT)
    return (LANES * sums[:groups] + sums[groups:]).astype(jnp.int32) - 1


def slots_kernel(ends_ref, own_ref, *refs, rows_dev, devices, chunks, neg_cap):
    msg_ref = refs[0]
    slot_refs = refs[1 : 1 + chunks]
    pool_ref, busy_ref = refs[1 + chunks : 3 + chunks] if chunks > 1 else (None, None)
    neg_ref = refs[-1]
    row = lax.broadcasted_iota(jnp.int32, (LANES, 2 * LANES), 0)
    lane = lax.broadcasted_iota(jnp.int32, (LANES, 2 * LANES), 1)
    mixer = jnp.where(row < lane, 1.0, 0.0).astype(BF16)
    owners = lax.broadcasted_iota(jnp.int32, (devices, LANES), 0)

    def prepare(ids_ref):
        where, holder, codes, members = [], [], [], []
        for segment in range(ids_ref.shape[0]):
            for start in range(0, ids_ref.shape[1], LANES):
                ids = ids_ref[segment : segment + 1, start : start + LANES]
                owner = jnp.where(ids >= 0, ids // rows_dev, -1)
                where.append((slice(segment, segment + 1), slice(start, start + LANES)))
                holder.append(owner)
                codes.append(jnp.where(ids >= 0, ids - owner * rows_dev + 1, 0))
                members.append(jnp.where(owners == owner, 1.0, 0.0))
        found, _ = ranks(members, mixer)
        return where, holder, codes, members, found

    where, holder, codes, members, found = prepare(ends_ref)
    for chunk in range(chunks):
        places = []
        for at, owner, rank in zip(where, holder, found):
            place = rank - chunk * LANES
            place = jnp.where((owner >= 0) & (place >= 0) & (place < LANES), place, -1)
            slot_refs[chunk][at] = jnp.where(place >= 0, owner * LANES + place, -1)
            places.append(place)
        msg_ref[:, chunk * LANES : (chunk + 1) * LANES] = fill(members, codes, places, LANES)
    offset = chunks * LANES
    flag = jnp.full((1, 1), -1, jnp.int32)
    if chunks > 1:
        shards = devices // RELAYS
        room = RELAYS * POOL
        shard_rows = lax.broadcasted_iota(jnp.int32, (shards, LANES), 0)
        spilled, spill_codes = [], []
        for owner, code, rank in zip(holder, codes, found):
            shard = jnp.where(rank >= LANES, owner // RELAYS, -1)
            spilled.append(jnp.where(shard_rows == shard, 1.0, 0.0))
            spill_codes.append(code + (owner % RELAYS) * rows_dev)
        pooled, taken = ranks(spilled, mixer)
        places = []
        for at, owner, rank, place in zip(where, holder, found, pooled):
            inside = (owner >= 0) & (rank >= LANES) & (place < room)
            compact = jnp.where(
                place < SMALL, owner // RELAYS * SMALL + place, (shards - 1) * SMALL + place
            )
            pool_ref[at] = jnp.where(inside, compact, -1)
            places.append(jnp.where(inside, place, -1))
        listed = fill(spilled, spill_codes, places, 2 * LANES)
        for shard in range(shards):
            msg_ref[shard * RELAYS : (shard + 1) * RELAYS, offset : offset + 2 * LANES] = (
                jnp.broadcast_to(listed[shard : shard + 1], (RELAYS, 2 * LANES))
            )
        offset += 2 * LANES
        most = jnp.max(taken, axis=0, keepdims=True)
        busy = jnp.where(taken > SMALL, 1.0, 0.0)
        crowded = jnp.sum(busy, axis=0, keepdims=True) > 1.0
        flag = jnp.where((most > room) | crowded, 1, -1)[:, :1]
        busy_ref[...] = jnp.sum(busy * shard_rows.astype(F32), axis=0, keepdims=True).astype(
            jnp.int32
        )[:, :1]

    where, holder, codes, members, found = prepare(own_ref)
    for at, owner, rank in zip(where, holder, found):
        neg_ref[at] = jnp.where(owner >= 0, owner * neg_cap + rank, -1)
    places = [jnp.where(owner >= 0, rank, -1) for owner, rank in zip(holder, found)]
    listed = fill(members, codes, places, LANES)
    lanes = lax.broadcasted_iota(jnp.int32, listed.shape, 1)
    msg_ref[:, offset:] = jnp.where(lanes == LANES - 1, flag, listed)


def make_slots(ends, own, rows_dev, devices, chunks, neg_cap):
    pooled = chunks > 1
    width = (chunks + 1 + 2 * pooled) * LANES
    return call(
        functools.partial(
            slots_kernel,
            rows_dev=rows_dev,
            devices=devices,
            chunks=chunks,
            neg_cap=neg_cap,
        ),
        "slots",
        16 * devices * LANES * ends.size,
        8 * ends.size,
        out_shape=[jax.ShapeDtypeStruct((devices, width), jnp.int32)]
        + [jax.ShapeDtypeStruct(ends.shape, jnp.int32)] * (chunks + pooled)
        + [jax.ShapeDtypeStruct((1, 1), jnp.int32)] * pooled
        + [jax.ShapeDtypeStruct(own.shape, jnp.int32)],
    )(ends, own)


def packed_height(count, feature):
    return feature // LANES * count + feature % LANES


def pack(out_ref, at, start, rows, tail):
    count, feature = rows.shape
    for piece in range(feature // LANES):
        out_ref[at, start + piece * count : start + (piece + 1) * count, :] = rows[
            :, piece * LANES : (piece + 1) * LANES
        ].astype(out_ref.dtype)
    tail = jnp.concatenate([tail, jnp.zeros((tail.shape[0], LANES - count), tail.dtype)], axis=1)
    end = start + packed_height(count, feature)
    out_ref[at, end - tail.shape[0] : end, :] = tail.astype(out_ref.dtype)


def pack_all(out_ref, start, count, rows, turned):
    feature = rows.shape[1]
    first = feature // LANES * LANES
    for i in range(out_ref.shape[0]):
        at = slice(i * count, (i + 1) * count)
        pack(out_ref, i, start, rows[at], turned[first:, at])


def unpack_all(in_ref, start, count, rows_ref, flat_ref):
    feature = flat_ref.shape[0]
    pieces = feature // LANES
    end = start + packed_height(count, feature)
    devices = in_ref.shape[0]
    for d in range(devices):
        for piece in range(pieces):
            rows_ref[d * count : (d + 1) * count, piece * LANES : (piece + 1) * LANES] = in_ref[
                d, start + piece * count : start + (piece + 1) * count, :
            ]
    tails = [
        in_ref[d, end - feature % LANES : end, :].astype(F32)[:, :count] for d in range(devices)
    ]
    flat_ref[: pieces * LANES] = rows_ref[...].astype(F32).T.astype(BF16)
    flat_ref[pieces * LANES :] = jnp.concatenate(tails, axis=1).astype(BF16)


def unpack_scratch(devices, count, feature):
    return [
        pltpu.VMEM((devices * count, feature // LANES * LANES), BF16),
        pltpu.VMEM((feature, devices * count), BF16),
    ]


def gather_kernel(table_ref, *refs, group, neg_cap):
    feature, rows_dev = table_ref.shape
    first = pl.program_id(0) * group
    req_ref, out_ref = refs[0], refs[-1]
    row = [req_ref[pl.ds(first + i, 1), :] for i in range(group)]
    if neg_cap:
        row += [refs[1][pl.ds(first + i, 1), :neg_cap] for i in range(group)]
    rows = dot(table_ref[...], one_hot(rows_dev, jnp.concatenate(row, axis=1)), NN)
    start = out_ref.shape[1] - feature
    for i in range(group):
        out_ref[i, start:] = rows[:, i * LANES : (i + 1) * LANES].astype(BF16)
    if neg_cap:
        neg = rows[:, group * LANES :]
        pack_all(out_ref, 0, neg_cap, neg.T, neg)


def gather(table, requests, neg_requests=None, neg_cap=0):
    feature, rows_dev = table.shape
    devices = requests.shape[0]
    group = 4
    height = feature + (packed_height(neg_cap, feature) if neg_cap else 0)
    slots = devices * (LANES + neg_cap)
    whole = pl.BlockSpec((devices, LANES), lambda i: (0, 0))
    return call(
        functools.partial(gather_kernel, group=group, neg_cap=neg_cap),
        "gather_rows",
        2 * feature * rows_dev * slots,
        2 * feature * (rows_dev + slots),
        grid=(devices // group,),
        in_specs=[pl.BlockSpec((feature, rows_dev), lambda i: (0, 0)), whole]
        + ([whole] if neg_cap else []),
        out_specs=pl.BlockSpec((group, height, LANES), lambda i: (i, 0, 0)),
        out_shape=jax.ShapeDtypeStruct((devices, height, LANES), BF16),
    )(table, requests, *([neg_requests] if neg_cap else []))


def gather_pool_kernel(table_ref, req_ref, out_ref, *, group):
    rows_dev = table_ref.shape[1]
    row = req_ref[...].reshape(1, group * POOL)
    rows = dot(table_ref[...], one_hot(rows_dev, row), NN)
    pack_all(out_ref, 0, POOL, rows.T, rows)


def gather_pool(table, requests, devices):
    feature, rows_dev = table.shape
    group = 8
    steps = devices // group
    height = packed_height(POOL, feature)
    return call(
        functools.partial(gather_pool_kernel, group=group),
        "gather_pool",
        2 * feature * rows_dev * requests.size,
        2 * feature * (rows_dev + requests.size),
        grid=(steps,),
        in_specs=[
            pl.BlockSpec((feature, rows_dev), lambda i: (0, 0)),
            pl.BlockSpec((1, 1, group * POOL), lambda i: (i, 0, 0)),
        ],
        out_specs=pl.BlockSpec((group, height, LANES), lambda i: (i, 0, 0)),
        out_shape=jax.ShapeDtypeStruct((devices, height, LANES), BF16),
    )(table, requests.reshape(steps, 1, group * POOL))


def spread_neg_kernel(back_ref, slot_ref, out_ref, rows, flat, *, cap):
    unpack_all(back_ref, 0, cap, rows, flat)
    for part in range(slot_ref.shape[0]):
        hot = one_hot(flat.shape[1], slot_ref[part : part + 1, :])
        out_ref[part] = dot(flat[...], hot, NN).T.astype(BF16)


def spread_neg(back, slot, cap, feature):
    devices = back.shape[0]
    parts, width = slot.shape
    height = packed_height(cap, feature)
    return call(
        functools.partial(spread_neg_kernel, cap=cap),
        "spread_negatives",
        2 * devices * cap * feature * slot.size,
        2 * devices * cap * feature,
        grid=(1,),
        in_specs=[
            pl.BlockSpec((devices, height, LANES), lambda i: (0, 0, 0)),
            pl.BlockSpec(slot.shape, lambda i: (0, 0)),
        ],
        out_specs=pl.BlockSpec((parts, width, feature), lambda i: (0, 0, 0)),
        out_shape=jax.ShapeDtypeStruct((parts, width, feature), BF16),
        scratch_shapes=unpack_scratch(devices, cap, feature),
    )(back, slot)


def spread_kernel(*refs, first):
    back_ref, slot_ref = refs[:2]
    so_far_ref = None if first else refs[2]
    out_ref, flat = refs[2 + (not first)], refs[-1]
    devices = back_ref.shape[0]
    feature = flat.shape[0]

    @pl.when(pl.program_id(0) == 0)
    def _():
        start = back_ref.shape[1] - feature
        for d in range(devices):
            flat[:, d * LANES : (d + 1) * LANES] = back_ref[d, start:]

    row = slot_ref[...].reshape(1, slot_ref.shape[-1])
    rows = dot(flat[...], one_hot(flat.shape[1], row), NN)
    if not first:
        rows = rows + so_far_ref[...].astype(F32)
    out_ref[...] = rows.astype(BF16)


def spread(back, slot, so_far, feature):
    devices = back.shape[0]
    segments, width = slot.shape
    slots = devices * LANES
    tile = 512 if slots <= 4096 else 128
    steps = width // tile
    rows_spec = pl.BlockSpec((feature, tile), lambda i: (0, i))
    extra = [] if so_far is None else [so_far]
    return call(
        functools.partial(spread_kernel, first=so_far is None),
        "spread_rows",
        2 * feature * slots * slot.size,
        2 * feature * (slots + slot.size),
        grid=(segments * steps,),
        in_specs=[
            pl.BlockSpec(back.shape, lambda i: (0, 0, 0)),
            pl.BlockSpec((1, 1, tile), lambda i: (i // steps, 0, i % steps)),
        ]
        + [rows_spec] * len(extra),
        out_specs=rows_spec,
        out_shape=jax.ShapeDtypeStruct((feature, slot.size), BF16),
        scratch_shapes=[pltpu.VMEM((feature, slots), BF16)],
    )(back, slot.reshape(segments, 1, width), *extra)


def compact_places(shards):
    places = [(shard, 0, 0, SMALL, shard * SMALL) for shard in range(shards)]
    to = shards * SMALL
    for relay in range(RELAYS):
        first = 0 if relay else SMALL
        places.append((None, relay, first, POOL - first, to))
        to += POOL - first
    return places


def compact_size(shards):
    return shards * SMALL + RELAYS * POOL - SMALL


def compact_pool(back_ref, busy, rows_ref, flat_ref):
    feature = flat_ref.shape[0]
    pieces = feature // LANES
    tails = []
    for shard, relay, first, count, to in compact_places(back_ref.shape[0] // RELAYS):
        at = (busy if shard is None else shard) * RELAYS + relay
        for piece in range(pieces):
            start = piece * POOL + first
            rows_ref[to : to + count, piece * LANES : (piece + 1) * LANES] = back_ref[
                at, start : start + count, :
            ]
        tail = back_ref[at, pieces * POOL :, :].astype(F32)
        tails.append(tail[:, first : first + count])
    flat_ref[: pieces * LANES] = rows_ref[...].astype(F32).T.astype(BF16)
    flat_ref[pieces * LANES :] = jnp.concatenate(tails, axis=1).astype(BF16)


def expand_pool(rows, busy, out_ref):
    feature = rows.shape[1]
    pieces = feature // LANES
    turned = rows.T
    out_ref[...] = jnp.zeros(out_ref.shape, out_ref.dtype)
    shards = out_ref.shape[0] // RELAYS
    for shard, relay, first, count, to in compact_places(shards):
        at = (busy if shard is None else shard) * RELAYS + relay
        for piece in range(pieces):
            start = piece * POOL + first
            out_ref[at, start : start + count, :] = rows[
                to : to + count, piece * LANES : (piece + 1) * LANES
            ].astype(BF16)
        if shard is not None:
            tail = turned[pieces * LANES :, to : to + count]
        else:
            small = turned[pieces * LANES :, : shards * SMALL]
            tail = turned[pieces * LANES :, to : to + count]
            if first:
                kept = jnp.zeros((feature % LANES, first), F32)
                for other in range(shards):
                    part = small[:, other * SMALL : (other + 1) * SMALL]
                    kept = jnp.where(busy == other, part, kept)
                tail = jnp.concatenate([kept, tail], axis=1)
        blank = jnp.zeros((tail.shape[0], LANES - tail.shape[1]), F32)
        out_ref[at, pieces * POOL :, :] = jnp.concatenate([tail, blank], axis=1).astype(BF16)


def edges_kernel(*refs, parts, pooled):
    refs = list(refs)
    src_ref, dst_ref, rel_ids_ref, rel_ref = refs[:4]
    neg_refs = refs[4 : 4 + parts]
    refs = refs[4 + parts :]
    if pooled:
        back_ref, src_slot_ref, dst_slot_ref, busy_ref = refs[:4]
        refs = refs[4:]
        pool_out_ref = refs.pop(2 + parts)
        pool_rows, pool_flat, pool_sums = refs[-3:]
    src_grad_ref, dst_grad_ref = refs[:2]
    neg_grad_refs = refs[2 : 2 + parts]
    negatives, turned, sums = refs[2 + parts : 5 + parts]
    block, step = pl.program_id(0), pl.program_id(1)
    last = step == pl.num_programs(1) - 1
    part = neg_refs[0].shape[1]

    if pooled:

        @pl.when((block == 0) & (step == 0))
        def _():
            compact_pool(back_ref, busy_ref[0, 0], pool_rows, pool_flat)
            pool_sums[...] = jnp.zeros(pool_sums.shape, F32)

    @pl.when(step == 0)
    def _():
        for k in range(parts):
            negatives[k * part : (k + 1) * part] = neg_refs[k][0]
        turned[...] = negatives[...].astype(F32).T.astype(BF16)

    hot = one_hot(rel_ref.shape[1], rel_ids_ref[...].reshape(1, rel_ids_ref.shape[-1]))
    table = rel_ref[...]
    relation = jnp.zeros(src_ref.shape, F32)
    for _ in range(3):
        piece = table.astype(BF16)
        relation = relation + dot(piece, hot, NN)
        table = table - piece.astype(F32)
    source = src_ref[...].astype(F32)
    target = dst_ref[...].astype(F32)
    if pooled:
        count = pool_flat.shape[1]
        src_hot = one_hot(count, src_slot_ref[...].reshape(1, src_slot_ref.shape[-1]))
        dst_hot = one_hot(count, dst_slot_ref[...].reshape(1, dst_slot_ref.shape[-1]))
        source = source + dot(pool_flat[...], src_hot, NN)
        target = target + dot(pool_flat[...], dst_hot, NN)
    product = source * relation
    positive = jnp.sum(product * target, axis=0, keepdims=True)
    pos_weight = -jax.nn.sigmoid(-positive)
    query = product.astype(BF16)
    weight = jax.nn.sigmoid(dot(negatives[...], query, NN)).astype(BF16)
    gathered = dot(turned[...], weight, NN)
    src_grad = (relation * (pos_weight * target + gathered)).astype(BF16)
    dst_grad = (pos_weight * product).astype(BF16)
    src_grad_ref[...] = src_grad
    dst_grad_ref[...] = dst_grad
    neg_grad = dot(weight, query, NT)
    if pooled:
        pool_sums[...] += dot(src_hot, src_grad, NT) + dot(dst_hot, dst_grad, NT)

    @pl.when(step == 0)
    def _():
        sums[...] = neg_grad

    @pl.when(step != 0)
    def _():
        sums[...] += neg_grad

    @pl.when(last)
    def _():
        for k in range(parts):
            neg_grad_refs[k][0] = sums[k * part : (k + 1) * part].astype(BF16)

    if pooled:

        @pl.when(last & (block == pl.num_programs(0) - 1))
        def _():
            expand_pool(pool_sums[...], busy_ref[0, 0], pool_out_ref)


def edges(rows, rel_ids, relations, negatives, pool=None, pool_slot=None, busy=None):
    feature, endpoints = rows.shape
    parts = len(negatives)
    spans, part, _ = negatives[0].shape
    width = rel_ids.shape[1]
    tile = 512
    steps = width // tile
    blocks = spans * steps
    edge_spec = pl.BlockSpec((feature, tile), lambda b, i: (0, b * steps + i))
    neg_spec = pl.BlockSpec((1, part, feature), lambda b, i: (b, 0, 0))
    operands = [rows, rows, rel_ids.reshape(spans, 1, width), relations, *negatives]
    specs = [
        edge_spec,
        pl.BlockSpec((feature, tile), lambda b, i: (0, blocks + b * steps + i)),
        pl.BlockSpec((1, 1, tile), lambda b, i: (b, 0, i)),
        pl.BlockSpec(relations.shape, lambda b, i: (0, 0)),
    ] + [neg_spec] * parts
    out_specs = [edge_spec, edge_spec] + [neg_spec] * parts
    out_shape = [jax.ShapeDtypeStruct((feature, endpoints // 2), BF16)] * 2
    out_shape += [jax.ShapeDtypeStruct((spans, part, feature), BF16)] * parts
    scratch = [
        pltpu.VMEM((parts * part, feature), BF16),
        pltpu.VMEM((feature, parts * part), BF16),
        pltpu.VMEM((parts * part, feature), F32),
    ]
    if pool is not None:
        slot = pool_slot.reshape(2 * spans, 1, width)
        pool_spec = pl.BlockSpec(pool.shape, lambda b, i: (0, 0, 0))
        operands += [pool, slot, slot, busy]
        specs += [
            pool_spec,
            pl.BlockSpec((1, 1, tile), lambda b, i: (b, 0, i)),
            pl.BlockSpec((1, 1, tile), lambda b, i: (spans + b, 0, i)),
            pl.BlockSpec(memory_space=pltpu.SMEM),
        ]
        out_specs.append(pool_spec)
        out_shape.append(jax.ShapeDtypeStruct(pool.shape, BF16))
        count = compact_size(pool.shape[0] // RELAYS)
        scratch += [
            pltpu.VMEM((count, feature // LANES * LANES), BF16),
            pltpu.VMEM((feature, count), BF16),
            pltpu.VMEM((count, feature), F32),
        ]
    src_grad, dst_grad, *rest = call(
        functools.partial(edges_kernel, parts=parts, pooled=pool is not None),
        "edges",
        6 * feature * parts * part * spans * width,
        4 * (rows.size + parts * negatives[0].size),
        grid=(spans, steps),
        in_specs=specs,
        out_specs=out_specs,
        out_shape=out_shape,
        scratch_shapes=scratch,
    )(*operands)
    return src_grad, dst_grad, rest


def collect_kernel(src_ref, dst_ref, slot_ref, out_ref, *, group):
    segments, width = slot_ref.shape
    feature = src_ref.shape[0]
    step = pl.program_id(0)
    total = jnp.zeros((feature, group * LANES), F32)
    for segment in range(segments):
        grads = src_ref if segment < segments // 2 else dst_ref
        start = segment % (segments // 2) * width
        hot = one_hot(group * LANES, slot_ref[segment : segment + 1, :], step * group * LANES)
        total = total + dot(grads[:, start : start + width], hot, NT)
    total = total.astype(BF16)
    first = out_ref.shape[1] - feature
    for i in range(group):
        out_ref[i, first:] = total[:, i * LANES : (i + 1) * LANES]


def collect(src_grad, dst_grad, slot, devices, neg_cap=0):
    feature = src_grad.shape[0]
    group = 4
    slots = devices * LANES
    height = feature + (packed_height(neg_cap, feature) if neg_cap else 0)
    whole = pl.BlockSpec(src_grad.shape, lambda i: (0, 0))
    return call(
        functools.partial(collect_kernel, group=group),
        "collect_grads",
        2 * feature * slots * slot.size,
        2 * feature * (slots + slot.size),
        grid=(devices // group,),
        in_specs=[whole, whole, pl.BlockSpec(slot.shape, lambda i: (0, 0))],
        out_specs=pl.BlockSpec((group, height, LANES), lambda i: (i, 0, 0)),
        out_shape=jax.ShapeDtypeStruct((devices, height, LANES), BF16),
    )(src_grad, dst_grad, slot)


def collect_neg_kernel(sent_ref, slot_ref, *refs, group, cap):
    grad_refs, out_ref, sums = refs[:-2], refs[-2], refs[-1]
    step = pl.program_id(0)

    @pl.when(step == 0)
    def _():
        total = grad_refs[0][...].astype(F32)
        for grad_ref in grad_refs[1:]:
            total = total + grad_ref[...].astype(F32)
        sums[...] = total.astype(BF16)

    rows = jnp.zeros((group * cap, sums.shape[-1]), F32)
    for part in range(slot_ref.shape[0]):
        hot = one_hot(group * cap, slot_ref[part : part + 1, :], step * group * cap)
        rows = rows + dot(hot, sums[part], NN)
    pack_all(out_ref, 0, cap, rows, rows.T)


def collect_neg(sent, slot, grads, cap):
    devices = sent.shape[0]
    feature = grads[0].shape[-1]
    group = 16
    height = packed_height(cap, feature)
    return call(
        functools.partial(collect_neg_kernel, group=group, cap=cap),
        "collect_negatives",
        2 * devices * cap * feature * slot.size,
        4 * len(grads) * grads[0].size,
        grid=(devices // group,),
        in_specs=[
            pl.BlockSpec(memory_space=pl.ANY),
            pl.BlockSpec(slot.shape, lambda i: (0, 0)),
        ]
        + [pl.BlockSpec(grads[0].shape, lambda i: (0, 0, 0))] * len(grads),
        out_specs=pl.BlockSpec((group, height, LANES), lambda i: (i, 0, 0)),
        out_shape=jax.ShapeDtypeStruct(sent.shape, BF16),
        scratch_shapes=[pltpu.VMEM(grads[0].shape, BF16)],
        input_output_aliases={0: 0},
    )(sent, slot, *grads)


def add_kernel(*refs, rows, neg_cap, first):
    refs = list(refs)
    recv_ref, req_ref = refs[:2]
    refs = refs[2:]
    if neg_cap:
        neg_req_ref = refs.pop(0)
        neg_rows, neg_flat = refs[-2:]
    if not first:
        so_far_ref = refs.pop(0)
    out_ref, flat = refs[:2]
    devices = recv_ref.shape[0]
    feature = flat.shape[0]
    step = pl.program_id(0)

    @pl.when(step == 0)
    def _():
        start = recv_ref.shape[1] - feature
        for d in range(devices):
            flat[:, d * LANES : (d + 1) * LANES] = recv_ref[d, start:]
        if neg_cap:
            unpack_all(recv_ref, 0, neg_cap, neg_rows, neg_flat)

    base = step * rows
    row = jnp.concatenate([req_ref[d : d + 1, :] for d in range(devices)], axis=1)
    total = dot(flat[...], one_hot(rows, row, base), NT)
    if neg_cap:
        row = jnp.concatenate([neg_req_ref[d : d + 1, :neg_cap] for d in range(devices)], axis=1)
        total = total + dot(neg_flat[...], one_hot(rows, row, base), NT)
    if not first:
        total = total + so_far_ref[...]
    out_ref[...] = total


def add_rows(recv, requests, so_far, feature, rows_dev, neg_requests=None, neg_cap=0):
    devices = recv.shape[0]
    rows = 512 if devices * LANES <= 4096 else 128
    slots = devices * LANES
    whole_req = pl.BlockSpec((devices, LANES), lambda i: (0, 0))
    rows_spec = pl.BlockSpec((feature, rows), lambda i: (0, i))
    operands = [recv, requests]
    specs = [pl.BlockSpec(recv.shape, lambda i: (0, 0, 0)), whole_req]
    scratch = [pltpu.VMEM((feature, slots), BF16)]
    if neg_cap:
        operands.append(neg_requests)
        specs.append(whole_req)
        scratch += unpack_scratch(devices, neg_cap, feature)
    if so_far is not None:
        operands.append(so_far)
        specs.append(rows_spec)
    return call(
        functools.partial(add_kernel, rows=rows, neg_cap=neg_cap, first=so_far is None),
        "add_grads",
        2 * feature * slots * rows_dev,
        2 * feature * slots + 8 * feature * rows_dev,
        grid=(rows_dev // rows,),
        in_specs=specs,
        out_specs=rows_spec,
        out_shape=jax.ShapeDtypeStruct((feature, rows_dev), F32),
        scratch_shapes=scratch,
    )(*operands)


def add_pool_kernel(*refs, rows, first):
    one_ref, two_ref, one_req_ref, two_req_ref = refs[:4]
    out_ref, packed, *flats = refs[4 + (not first) :]
    step = pl.program_id(0)

    @pl.when(step == 0)
    def _():
        for recv_ref, flat in zip((one_ref, two_ref), flats):
            unpack_all(recv_ref, 0, POOL, packed, flat)

    total = dot(flats[0][...], one_hot(rows, one_req_ref[...], step * rows), NT)
    total = total + dot(flats[1][...], one_hot(rows, two_req_ref[...], step * rows), NT)
    if not first:
        total = total + refs[4][...]
    out_ref[...] = total


def add_pool(one, two, requests, so_far, feature, rows_dev):
    rows = 512
    devices = one.shape[0]
    slots = devices * POOL
    recv_spec = pl.BlockSpec(one.shape, lambda i: (0, 0, 0))
    req_spec = pl.BlockSpec((1, slots), lambda i: (0, 0))
    rows_spec = pl.BlockSpec((feature, rows), lambda i: (0, i))
    packed, flat = unpack_scratch(devices, POOL, feature)
    extra = [] if so_far is None else [so_far]
    return call(
        functools.partial(add_pool_kernel, rows=rows, first=so_far is None),
        "add_pool",
        4 * feature * slots * rows_dev,
        4 * feature * slots + 4 * feature * rows_dev,
        grid=(rows_dev // rows,),
        in_specs=[recv_spec, recv_spec, req_spec, req_spec] + [rows_spec] * len(extra),
        out_specs=rows_spec,
        out_shape=jax.ShapeDtypeStruct((feature, rows_dev), F32),
        scratch_shapes=[packed, flat, flat],
    )(one, two, requests[0][None], requests[1][None], *extra)


def after(value, other):
    anywhere = pl.BlockSpec(memory_space=pl.ANY)
    return call(
        lambda value_ref, other_ref, out_ref: None,
        "after",
        0,
        0,
        in_specs=[anywhere, anywhere],
        out_specs=anywhere,
        out_shape=jax.ShapeDtypeStruct(value.shape, value.dtype),
        input_output_aliases={0: 0},
    )(value, other)


def exchange(value):
    return lax.all_to_all(value, ("shard", "grp"), split_axis=0, concat_axis=0, tiled=True)


def swap(value, bit):
    sharers = lax.axis_size("grp")
    return lax.ppermute(value, "grp", [(i, i ^ bit) for i in range(sharers)])


def share_out(value):
    sharers = lax.axis_size("grp")
    blocks = {0: value}
    bit = sharers // 2
    while bit:
        for k in list(blocks):
            blocks[k ^ bit] = swap(blocks[k], bit)
        bit //= 2
    return [blocks[k] for k in range(sharers)]


def trade(blocks):
    sharers = len(blocks)
    terms = [[block] for block in blocks]
    bit = 1
    while bit < sharers:
        for k in range(0, sharers, 2 * bit):
            total = terms[k ^ bit][0].astype(F32)
            for term in terms[k ^ bit][1:]:
                total = total + term.astype(F32)
            terms[k].append(swap(total.astype(BF16), bit))
        bit *= 2
    return terms[0]


def pad_lanes(value, width, fill):
    return jnp.pad(value, ((0, 0), (0, width - value.shape[1])), constant_values=fill)


def body(entity_table, rel_diag, src_ids, dst_ids, rel_ids, neg_ids):
    rows_dev, feature = entity_table.shape
    sharers = lax.axis_size("grp")
    devices = lax.axis_size("shard") * sharers
    spans, neg_count = neg_ids.shape
    edge_count = src_ids.shape[0]
    block_len = edge_count // spans
    edge_cap = 4 * edge_count // devices
    chunks = round_up(edge_cap, LANES) // LANES
    part_width = neg_count // sharers
    neg_cap = round_up(2 * spans * part_width // devices, 16)
    width = round_up(block_len, 512)
    part = round_up(part_width, LANES)
    me = lax.axis_index("grp")

    table = entity_table.T.astype(BF16)
    relations = rel_diag.T
    own_ids = lax.dynamic_slice_in_dim(neg_ids, me * part_width, part_width, 1)
    ends = jnp.concatenate(
        [src_ids.reshape(spans, block_len), dst_ids.reshape(spans, block_len)]
    )
    message, *slots = make_slots(
        pad_lanes(ends, width, -1),
        pad_lanes(own_ids, part, -1),
        rows_dev,
        devices,
        chunks,
        neg_cap,
    )
    neg_slot = slots[-1]
    busy = slots[-2]
    rel_rows = pad_lanes(rel_ids.reshape(spans, block_len), width, -1)
    asked = exchange(message)
    direct = [asked[:, c * LANES : (c + 1) * LANES] for c in range(chunks)]
    neg_asked = asked[:, -LANES:]

    sent_rows = gather(table, direct[0], neg_asked, neg_cap)

    def negatives_of(back):
        return share_out(spread_neg(back, neg_slot, neg_cap, feature))

    def direct_sent(src_grad, dst_grad, neg_grads):
        sent = collect(src_grad, dst_grad, slots[0], devices, neg_cap)
        return exchange(collect_neg(sent, neg_slot, trade(neg_grads), neg_cap))

    def chunked():
        back = [exchange(sent_rows)]
        back += [exchange(gather(table, direct[c])) for c in range(1, chunks)]
        negatives = negatives_of(back[0])
        rows = None
        for c in range(chunks):
            rows = spread(back[c], slots[c], rows, feature)
        src_grad, dst_grad, neg_grads = edges(rows, rel_rows, relations, negatives)
        grad = None
        for c in range(1, chunks):
            sent = exchange(collect(src_grad, dst_grad, slots[c], devices))
            grad = add_rows(sent, direct[c], grad, feature, rows_dev)
        sent = direct_sent(src_grad, dst_grad, neg_grads)
        return add_rows(sent, direct[0], grad, feature, rows_dev, neg_asked, neg_cap)

    def pooled():
        start = chunks * LANES
        listed = asked[:, start : start + RELAYS * POOL].reshape(devices, RELAYS, POOL)
        listed = listed.transpose(1, 0, 2).reshape(RELAYS, devices * POOL) - me * rows_dev
        listed = listed[me ^ jnp.arange(RELAYS, dtype=jnp.int32)]
        back = exchange(sent_rows)
        far = swap(gather_pool(table, listed[3], devices), 1)
        far = swap(gather_pool(table, listed[2], devices) + far, 2)
        near = swap(gather_pool(table, listed[1], devices), 1)
        near = gather_pool(table, listed[0], devices) + near
        negatives = negatives_of(back)
        rows = spread(back, slots[0], None, feature)
        src_grad, dst_grad, rest = edges(
            rows, rel_rows, relations, negatives, exchange(near + far), slots[chunks], busy
        )
        neg_grads, pool = rest[:-1], rest[-1]
        near = exchange(pool)
        far = swap(near, 2)
        sent = direct_sent(src_grad, dst_grad, neg_grads)
        grad = add_pool(near, swap(near, 1), listed[:2], None, feature, rows_dev)
        far = after(far, grad)
        grad = add_pool(far, swap(far, 1), listed[2:], grad, feature, rows_dev)
        return add_rows(sent, direct[0], grad, feature, rows_dev, neg_asked, neg_cap)

    if chunks == 1 or sharers != RELAYS:
        return chunked().T
    fits = jnp.max(neg_asked[:, -1]) < 0
    return lax.cond(fits, pooled, chunked).T


def solution(mesh):
    placed = (
        P(("shard", "grp"), None),
        P(),
        P(("shard", "grp")),
        P(("shard", "grp")),
        P(("shard", "grp")),
        P("shard", None),
    )
    return jax.shard_map(
        body, mesh=mesh, in_specs=placed, out_specs=P(("shard", "grp"), None), check_vma=False
    )
```

```python
import functools

import jax
import jax.numpy as jnp
from jax import lax
from jax.experimental import pallas as pl
from jax.experimental.pallas import tpu as pltpu
from jax.sharding import PartitionSpec as P

LANES = 128
POOL = 48
RELAYS = 4
SMALL = 32
VMEM_BYTES = 56 << 20
F32 = jnp.float32
BF16 = jnp.bfloat16
NN = (((1,), (0,)), ((), ()))
NT = (((1,), (1,)), ((), ()))
TN = (((0,), (0,)), ((), ()))


def round_up(value, unit):
    return -(-value // unit) * unit


def dot(left, right, dims):
    return lax.dot_general(left, right, dims, preferred_element_type=F32)


def one_hot(rows, row, base=0):
    places = lax.broadcasted_iota(jnp.int32, (rows, row.shape[1]), 0) + base
    return jnp.where(places == row, 1.0, 0.0).astype(BF16)


def call(kernel, name, flops, nbytes, **kwargs):
    return pl.pallas_call(
        kernel,
        name=name,
        compiler_params=pltpu.CompilerParams(vmem_limit_bytes=VMEM_BYTES),
        cost_estimate=pl.CostEstimate(flops=flops, bytes_accessed=nbytes, transcendentals=0),
        **kwargs,
    )


def ranks(members, mixer):
    groups = members[0].shape[0]
    both = dot(jnp.concatenate(members, axis=0).astype(BF16), mixer, NN)
    taken = jnp.zeros((groups, LANES), F32)
    found = []
    for i, member in enumerate(members):
        chunk = both[i * groups : (i + 1) * groups]
        found.append(jnp.sum((chunk[:, :LANES] + taken) * member, axis=0, keepdims=True))
        taken = taken + chunk[:, LANES:]
    return [rank.astype(jnp.int32) for rank in found], taken


def fill(members, codes, places, count):
    groups = members[0].shape[0]
    high = [m * (c // LANES).astype(F32) for m, c in zip(members, codes)]
    low = [m * (c % LANES).astype(F32) for m, c in zip(members, codes)]
    left = jnp.concatenate(
        [jnp.concatenate(high, axis=1), jnp.concatenate(low, axis=1)], axis=0
    ).astype(BF16)
    sums = dot(left, one_hot(count, jnp.concatenate(places, axis=1)), NT)
    return (LANES * sums[:groups] + sums[groups:]).astype(jnp.int32) - 1


def slots_kernel(ends_ref, own_ref, *refs, rows_dev, devices, chunks, neg_cap):
    msg_ref = refs[0]
    slot_refs = refs[1 : 1 + chunks]
    pool_ref, busy_ref = refs[1 + chunks : 3 + chunks] if chunks > 1 else (None, None)
    neg_ref = refs[-1]
    row = lax.broadcasted_iota(jnp.int32, (LANES, 2 * LANES), 0)
    lane = lax.broadcasted_iota(jnp.int32, (LANES, 2 * LANES), 1)
    mixer = jnp.where(row < lane, 1.0, 0.0).astype(BF16)
    owners = lax.broadcasted_iota(jnp.int32, (devices, LANES), 0)

    def prepare(ids_ref):
        where, holder, codes, members = [], [], [], []
        for segment in range(ids_ref.shape[0]):
            for start in range(0, ids_ref.shape[1], LANES):
                ids = ids_ref[segment : segment + 1, start : start + LANES]
                owner = jnp.where(ids >= 0, ids // rows_dev, -1)
                where.append((slice(segment, segment + 1), slice(start, start + LANES)))
                holder.append(owner)
                codes.append(jnp.where(ids >= 0, ids - owner * rows_dev + 1, 0))
                members.append(jnp.where(owners == owner, 1.0, 0.0))
        found, _ = ranks(members, mixer)
        return where, holder, codes, members, found

    where, holder, codes, members, found = prepare(ends_ref)
    for chunk in range(chunks):
        places = []
        for at, owner, rank in zip(where, holder, found):
            place = rank - chunk * LANES
            place = jnp.where((owner >= 0) & (place >= 0) & (place < LANES), place, -1)
            slot_refs[chunk][at] = jnp.where(place >= 0, owner * LANES + place, -1)
            places.append(place)
        msg_ref[:, chunk * LANES : (chunk + 1) * LANES] = fill(members, codes, places, LANES)
    offset = chunks * LANES
    flag = jnp.full((1, 1), -1, jnp.int32)
    if chunks > 1:
        shards = devices // RELAYS
        room = RELAYS * POOL
        shard_rows = lax.broadcasted_iota(jnp.int32, (shards, LANES), 0)
        spilled, spill_codes = [], []
        for owner, code, rank in zip(holder, codes, found):
            shard = jnp.where(rank >= LANES, owner // RELAYS, -1)
            spilled.append(jnp.where(shard_rows == shard, 1.0, 0.0))
            spill_codes.append(code + (owner % RELAYS) * rows_dev)
        pooled, taken = ranks(spilled, mixer)
        places = []
        for at, owner, rank, place in zip(where, holder, found, pooled):
            inside = (owner >= 0) & (rank >= LANES) & (place < room)
            compact = jnp.where(
                place < SMALL, owner // RELAYS * SMALL + place, (shards - 1) * SMALL + place
            )
            pool_ref[at] = jnp.where(inside, compact, -1)
            places.append(jnp.where(inside, place, -1))
        listed = fill(spilled, spill_codes, places, 2 * LANES)
        for shard in range(shards):
            msg_ref[shard * RELAYS : (shard + 1) * RELAYS, offset : offset + 2 * LANES] = (
                jnp.broadcast_to(listed[shard : shard + 1], (RELAYS, 2 * LANES))
            )
        offset += 2 * LANES
        most = jnp.max(taken, axis=0, keepdims=True)
        busy = jnp.where(taken > SMALL, 1.0, 0.0)
        crowded = jnp.sum(busy, axis=0, keepdims=True) > 1.0
        flag = jnp.where((most > room) | crowded, 1, -1)[:, :1]
        place = jnp.sum(busy * shard_rows.astype(F32), axis=0, keepdims=True).astype(jnp.int32)
        busy_ref[...] = jnp.minimum(place, shards - 1)[:, :1]

    where, holder, codes, members, found = prepare(own_ref)
    for at, owner, rank in zip(where, holder, found):
        neg_ref[at] = jnp.where(owner >= 0, owner * neg_cap + rank, -1)
    places = [jnp.where(owner >= 0, rank, -1) for owner, rank in zip(holder, found)]
    listed = fill(members, codes, places, LANES)
    lanes = lax.broadcasted_iota(jnp.int32, listed.shape, 1)
    msg_ref[:, offset:] = jnp.where(lanes == LANES - 1, flag, listed)


def make_slots(ends, own, rows_dev, devices, chunks, neg_cap):
    pooled = chunks > 1
    width = (chunks + 1 + 2 * pooled) * LANES
    return call(
        functools.partial(
            slots_kernel,
            rows_dev=rows_dev,
            devices=devices,
            chunks=chunks,
            neg_cap=neg_cap,
        ),
        "slots",
        16 * devices * LANES * ends.size,
        8 * ends.size,
        out_shape=[jax.ShapeDtypeStruct((devices, width), jnp.int32)]
        + [jax.ShapeDtypeStruct(ends.shape, jnp.int32)] * (chunks + pooled)
        + [jax.ShapeDtypeStruct((1, 1), jnp.int32)] * pooled
        + [jax.ShapeDtypeStruct(own.shape, jnp.int32)],
    )(ends, own)


def packed_height(count, feature):
    return feature // LANES * count + feature % LANES


def pack(out_ref, at, start, rows, tail):
    count, feature = rows.shape
    for piece in range(feature // LANES):
        out_ref[at, start + piece * count : start + (piece + 1) * count, :] = rows[
            :, piece * LANES : (piece + 1) * LANES
        ].astype(out_ref.dtype)
    tail = jnp.concatenate([tail, jnp.zeros((tail.shape[0], LANES - count), tail.dtype)], axis=1)
    end = start + packed_height(count, feature)
    out_ref[at, end - tail.shape[0] : end, :] = tail.astype(out_ref.dtype)


def pack_all(out_ref, start, count, rows, turned):
    feature = rows.shape[1]
    first = feature // LANES * LANES
    for i in range(out_ref.shape[0]):
        at = slice(i * count, (i + 1) * count)
        pack(out_ref, i, start, rows[at], turned[first:, at])


def unpack_all(in_ref, start, count, rows_ref, flat_ref):
    feature = flat_ref.shape[0]
    pieces = feature // LANES
    end = start + packed_height(count, feature)
    devices = in_ref.shape[0]
    for d in range(devices):
        for piece in range(pieces):
            rows_ref[d * count : (d + 1) * count, piece * LANES : (piece + 1) * LANES] = in_ref[
                d, start + piece * count : start + (piece + 1) * count, :
            ]
    tails = [
        in_ref[d, end - feature % LANES : end, :].astype(F32)[:, :count] for d in range(devices)
    ]
    flat_ref[: pieces * LANES] = rows_ref[...].astype(F32).T.astype(BF16)
    flat_ref[pieces * LANES :] = jnp.concatenate(tails, axis=1).astype(BF16)


def unpack_scratch(devices, count, feature):
    return [
        pltpu.VMEM((devices * count, feature // LANES * LANES), BF16),
        pltpu.VMEM((feature, devices * count), BF16),
    ]


def gather_kernel(table_ref, *refs, group, neg_cap):
    feature, rows_dev = table_ref.shape
    first = pl.program_id(0) * group
    req_ref, out_ref = refs[0], refs[-1]
    row = [req_ref[pl.ds(first + i, 1), :] for i in range(group)]
    if neg_cap:
        row += [refs[1][pl.ds(first + i, 1), :neg_cap] for i in range(group)]
    rows = dot(table_ref[...], one_hot(rows_dev, jnp.concatenate(row, axis=1)), NN)
    start = out_ref.shape[1] - feature
    for i in range(group):
        out_ref[i, start:] = rows[:, i * LANES : (i + 1) * LANES].astype(BF16)
    if neg_cap:
        neg = rows[:, group * LANES :]
        pack_all(out_ref, 0, neg_cap, neg.T, neg)


def gather(table, requests, neg_requests=None, neg_cap=0):
    feature, rows_dev = table.shape
    devices = requests.shape[0]
    group = 4
    height = feature + (packed_height(neg_cap, feature) if neg_cap else 0)
    slots = devices * (LANES + neg_cap)
    whole = pl.BlockSpec((devices, LANES), lambda i: (0, 0))
    return call(
        functools.partial(gather_kernel, group=group, neg_cap=neg_cap),
        "gather_rows",
        2 * feature * rows_dev * slots,
        2 * feature * (rows_dev + slots),
        grid=(devices // group,),
        in_specs=[pl.BlockSpec((feature, rows_dev), lambda i: (0, 0)), whole]
        + ([whole] if neg_cap else []),
        out_specs=pl.BlockSpec((group, height, LANES), lambda i: (i, 0, 0)),
        out_shape=jax.ShapeDtypeStruct((devices, height, LANES), BF16),
    )(table, requests, *([neg_requests] if neg_cap else []))


def gather_pool_kernel(table_ref, req_ref, out_ref, *, group):
    rows_dev = table_ref.shape[1]
    row = req_ref[...].reshape(1, group * POOL)
    rows = dot(table_ref[...], one_hot(rows_dev, row), NN)
    pack_all(out_ref, 0, POOL, rows.T, rows)


def gather_pool(table, requests, devices):
    feature, rows_dev = table.shape
    group = 8
    steps = devices // group
    height = packed_height(POOL, feature)
    return call(
        functools.partial(gather_pool_kernel, group=group),
        "gather_pool",
        2 * feature * rows_dev * requests.size,
        2 * feature * (rows_dev + requests.size),
        grid=(steps,),
        in_specs=[
            pl.BlockSpec((feature, rows_dev), lambda i: (0, 0)),
            pl.BlockSpec((1, 1, group * POOL), lambda i: (i, 0, 0)),
        ],
        out_specs=pl.BlockSpec((group, height, LANES), lambda i: (i, 0, 0)),
        out_shape=jax.ShapeDtypeStruct((devices, height, LANES), BF16),
    )(table, requests.reshape(steps, 1, group * POOL))


def spread_neg_kernel(back_ref, slot_ref, out_ref, rows, flat, *, cap):
    unpack_all(back_ref, 0, cap, rows, flat)
    for part in range(slot_ref.shape[0]):
        hot = one_hot(flat.shape[1], slot_ref[part : part + 1, :])
        out_ref[part] = dot(flat[...], hot, NN).T.astype(BF16)


def spread_neg(back, slot, cap, feature):
    devices = back.shape[0]
    parts, width = slot.shape
    height = packed_height(cap, feature)
    return call(
        functools.partial(spread_neg_kernel, cap=cap),
        "spread_negatives",
        2 * devices * cap * feature * slot.size,
        2 * devices * cap * feature,
        grid=(1,),
        in_specs=[
            pl.BlockSpec((devices, height, LANES), lambda i: (0, 0, 0)),
            pl.BlockSpec(slot.shape, lambda i: (0, 0)),
        ],
        out_specs=pl.BlockSpec((parts, width, feature), lambda i: (0, 0, 0)),
        out_shape=jax.ShapeDtypeStruct((parts, width, feature), BF16),
        scratch_shapes=unpack_scratch(devices, cap, feature),
    )(back, slot)


def spread_kernel(*refs, first):
    back_ref, slot_ref = refs[:2]
    so_far_ref = None if first else refs[2]
    out_ref, flat = refs[2 + (not first)], refs[-1]
    devices = back_ref.shape[0]
    feature = flat.shape[0]

    @pl.when(pl.program_id(0) == 0)
    def _():
        start = back_ref.shape[1] - feature
        for d in range(devices):
            flat[:, d * LANES : (d + 1) * LANES] = back_ref[d, start:]

    row = slot_ref[...].reshape(1, slot_ref.shape[-1])
    rows = dot(flat[...], one_hot(flat.shape[1], row), NN)
    if not first:
        rows = rows + so_far_ref[...].astype(F32)
    out_ref[...] = rows.astype(BF16)


def spread(back, slot, so_far, feature):
    devices = back.shape[0]
    segments, width = slot.shape
    slots = devices * LANES
    tile = 512 if slots <= 4096 else 128
    steps = width // tile
    rows_spec = pl.BlockSpec((feature, tile), lambda i: (0, i))
    extra = [] if so_far is None else [so_far]
    return call(
        functools.partial(spread_kernel, first=so_far is None),
        "spread_rows",
        2 * feature * slots * slot.size,
        2 * feature * (slots + slot.size),
        grid=(segments * steps,),
        in_specs=[
            pl.BlockSpec(back.shape, lambda i: (0, 0, 0)),
            pl.BlockSpec((1, 1, tile), lambda i: (i // steps, 0, i % steps)),
        ]
        + [rows_spec] * len(extra),
        out_specs=rows_spec,
        out_shape=jax.ShapeDtypeStruct((feature, slot.size), BF16),
        scratch_shapes=[pltpu.VMEM((feature, slots), BF16)],
    )(back, slot.reshape(segments, 1, width), *extra)


def compact_places(shards):
    places = [(shard, 0, 0, SMALL, shard * SMALL) for shard in range(shards)]
    to = shards * SMALL
    for relay in range(RELAYS):
        first = 0 if relay else SMALL
        places.append((None, relay, first, POOL - first, to))
        to += POOL - first
    return places


def compact_size(shards):
    return shards * SMALL + RELAYS * POOL - SMALL


def compact_pool(back_ref, busy, rows_ref, flat_ref):
    feature = flat_ref.shape[0]
    pieces = feature // LANES
    tails = []
    for shard, relay, first, count, to in compact_places(back_ref.shape[0] // RELAYS):
        at = (busy if shard is None else shard) * RELAYS + relay
        for piece in range(pieces):
            start = piece * POOL + first
            rows_ref[to : to + count, piece * LANES : (piece + 1) * LANES] = back_ref[
                at, start : start + count, :
            ]
        tail = back_ref[at, pieces * POOL :, :].astype(F32)
        tails.append(tail[:, first : first + count])
    flat_ref[: pieces * LANES] = rows_ref[...].astype(F32).T.astype(BF16)
    flat_ref[pieces * LANES :] = jnp.concatenate(tails, axis=1).astype(BF16)


def expand_pool(rows, busy, out_ref):
    feature = rows.shape[1]
    pieces = feature // LANES
    turned = rows.T
    out_ref[...] = jnp.zeros(out_ref.shape, out_ref.dtype)
    shards = out_ref.shape[0] // RELAYS
    for shard, relay, first, count, to in compact_places(shards):
        at = (busy if shard is None else shard) * RELAYS + relay
        for piece in range(pieces):
            start = piece * POOL + first
            out_ref[at, start : start + count, :] = rows[
                to : to + count, piece * LANES : (piece + 1) * LANES
            ].astype(BF16)
        if shard is not None:
            tail = turned[pieces * LANES :, to : to + count]
        else:
            small = turned[pieces * LANES :, : shards * SMALL]
            tail = turned[pieces * LANES :, to : to + count]
            if first:
                kept = jnp.zeros((feature % LANES, first), F32)
                for other in range(shards):
                    part = small[:, other * SMALL : (other + 1) * SMALL]
                    kept = jnp.where(busy == other, part, kept)
                tail = jnp.concatenate([kept, tail], axis=1)
        blank = jnp.zeros((tail.shape[0], LANES - tail.shape[1]), F32)
        out_ref[at, pieces * POOL :, :] = jnp.concatenate([tail, blank], axis=1).astype(BF16)


def edges_kernel(*refs, parts, pooled):
    refs = list(refs)
    src_ref, dst_ref, rel_ids_ref, rel_ref = refs[:4]
    neg_refs = refs[4 : 4 + parts]
    refs = refs[4 + parts :]
    if pooled:
        back_ref, src_slot_ref, dst_slot_ref, busy_ref = refs[:4]
        refs = refs[4:]
        pool_out_ref = refs.pop(2 + parts)
        pool_rows, pool_flat, pool_sums = refs[-3:]
    src_grad_ref, dst_grad_ref = refs[:2]
    neg_grad_refs = refs[2 : 2 + parts]
    negatives, turned, sums = refs[2 + parts : 5 + parts]
    block, step = pl.program_id(0), pl.program_id(1)
    last = step == pl.num_programs(1) - 1
    part = neg_refs[0].shape[1]

    if pooled:

        @pl.when((block == 0) & (step == 0))
        def _():
            compact_pool(back_ref, busy_ref[0, 0], pool_rows, pool_flat)
            pool_sums[...] = jnp.zeros(pool_sums.shape, F32)

    @pl.when(step == 0)
    def _():
        for k in range(parts):
            negatives[k * part : (k + 1) * part] = neg_refs[k][0]
        turned[...] = negatives[...].astype(F32).T.astype(BF16)

    hot = one_hot(rel_ref.shape[1], rel_ids_ref[...].reshape(1, rel_ids_ref.shape[-1]))
    table = rel_ref[...]
    relation = jnp.zeros(src_ref.shape, F32)
    for _ in range(3):
        piece = table.astype(BF16)
        relation = relation + dot(piece, hot, NN)
        table = table - piece.astype(F32)
    source = src_ref[...].astype(F32)
    target = dst_ref[...].astype(F32)
    if pooled:
        count = pool_flat.shape[1]
        src_hot = one_hot(count, src_slot_ref[...].reshape(1, src_slot_ref.shape[-1]))
        dst_hot = one_hot(count, dst_slot_ref[...].reshape(1, dst_slot_ref.shape[-1]))
        source = source + dot(pool_flat[...], src_hot, NN)
        target = target + dot(pool_flat[...], dst_hot, NN)
    product = source * relation
    positive = jnp.sum(product * target, axis=0, keepdims=True)
    pos_weight = -jax.nn.sigmoid(-positive)
    query = product.astype(BF16)
    weight = jax.nn.sigmoid(dot(negatives[...], query, NN)).astype(BF16)
    gathered = dot(turned[...], weight, NN)
    src_grad = (relation * (pos_weight * target + gathered)).astype(BF16)
    dst_grad = (pos_weight * product).astype(BF16)
    src_grad_ref[...] = src_grad
    dst_grad_ref[...] = dst_grad
    neg_grad = dot(weight, query, NT)
    if pooled:
        pool_sums[...] += dot(src_hot, src_grad, NT) + dot(dst_hot, dst_grad, NT)

    @pl.when(step == 0)
    def _():
        sums[...] = neg_grad

    @pl.when(step != 0)
    def _():
        sums[...] += neg_grad

    @pl.when(last)
    def _():
        for k in range(parts):
            neg_grad_refs[k][0] = sums[k * part : (k + 1) * part].astype(BF16)

    if pooled:

        @pl.when(last & (block == pl.num_programs(0) - 1))
        def _():
            expand_pool(pool_sums[...], busy_ref[0, 0], pool_out_ref)


def edges(rows, rel_ids, relations, negatives, pool=None, pool_slot=None, busy=None):
    feature, endpoints = rows.shape
    parts = len(negatives)
    spans, part, _ = negatives[0].shape
    width = rel_ids.shape[1]
    tile = 512
    steps = width // tile
    blocks = spans * steps
    edge_spec = pl.BlockSpec((feature, tile), lambda b, i: (0, b * steps + i))
    neg_spec = pl.BlockSpec((1, part, feature), lambda b, i: (b, 0, 0))
    operands = [rows, rows, rel_ids.reshape(spans, 1, width), relations, *negatives]
    specs = [
        edge_spec,
        pl.BlockSpec((feature, tile), lambda b, i: (0, blocks + b * steps + i)),
        pl.BlockSpec((1, 1, tile), lambda b, i: (b, 0, i)),
        pl.BlockSpec(relations.shape, lambda b, i: (0, 0)),
    ] + [neg_spec] * parts
    out_specs = [edge_spec, edge_spec] + [neg_spec] * parts
    out_shape = [jax.ShapeDtypeStruct((feature, endpoints // 2), BF16)] * 2
    out_shape += [jax.ShapeDtypeStruct((spans, part, feature), BF16)] * parts
    scratch = [
        pltpu.VMEM((parts * part, feature), BF16),
        pltpu.VMEM((feature, parts * part), BF16),
        pltpu.VMEM((parts * part, feature), F32),
    ]
    if pool is not None:
        slot = pool_slot.reshape(2 * spans, 1, width)
        pool_spec = pl.BlockSpec(pool.shape, lambda b, i: (0, 0, 0))
        operands += [pool, slot, slot, busy]
        specs += [
            pool_spec,
            pl.BlockSpec((1, 1, tile), lambda b, i: (b, 0, i)),
            pl.BlockSpec((1, 1, tile), lambda b, i: (spans + b, 0, i)),
            pl.BlockSpec(memory_space=pltpu.SMEM),
        ]
        out_specs.append(pool_spec)
        out_shape.append(jax.ShapeDtypeStruct(pool.shape, BF16))
        count = compact_size(pool.shape[0] // RELAYS)
        scratch += [
            pltpu.VMEM((count, feature // LANES * LANES), BF16),
            pltpu.VMEM((feature, count), BF16),
            pltpu.VMEM((count, feature), F32),
        ]
    src_grad, dst_grad, *rest = call(
        functools.partial(edges_kernel, parts=parts, pooled=pool is not None),
        "edges",
        6 * feature * parts * part * spans * width,
        4 * (rows.size + parts * negatives[0].size),
        grid=(spans, steps),
        in_specs=specs,
        out_specs=out_specs,
        out_shape=out_shape,
        scratch_shapes=scratch,
    )(*operands)
    return src_grad, dst_grad, rest


def collect_kernel(src_ref, dst_ref, slot_ref, out_ref, *, group):
    segments, width = slot_ref.shape
    feature = src_ref.shape[0]
    step = pl.program_id(0)
    total = jnp.zeros((feature, group * LANES), F32)
    for segment in range(segments):
        grads = src_ref if segment < segments // 2 else dst_ref
        start = segment % (segments // 2) * width
        hot = one_hot(group * LANES, slot_ref[segment : segment + 1, :], step * group * LANES)
        total = total + dot(grads[:, start : start + width], hot, NT)
    total = total.astype(BF16)
    first = out_ref.shape[1] - feature
    for i in range(group):
        out_ref[i, first:] = total[:, i * LANES : (i + 1) * LANES]


def collect(src_grad, dst_grad, slot, devices, neg_cap=0):
    feature = src_grad.shape[0]
    group = 4
    slots = devices * LANES
    height = feature + (packed_height(neg_cap, feature) if neg_cap else 0)
    whole = pl.BlockSpec(src_grad.shape, lambda i: (0, 0))
    return call(
        functools.partial(collect_kernel, group=group),
        "collect_grads",
        2 * feature * slots * slot.size,
        2 * feature * (slots + slot.size),
        grid=(devices // group,),
        in_specs=[whole, whole, pl.BlockSpec(slot.shape, lambda i: (0, 0))],
        out_specs=pl.BlockSpec((group, height, LANES), lambda i: (i, 0, 0)),
        out_shape=jax.ShapeDtypeStruct((devices, height, LANES), BF16),
    )(src_grad, dst_grad, slot)


def collect_neg_kernel(sent_ref, slot_ref, *refs, group, cap):
    grad_refs, out_ref, sums = refs[:-2], refs[-2], refs[-1]
    step = pl.program_id(0)

    @pl.when(step == 0)
    def _():
        total = grad_refs[0][...].astype(F32)
        for grad_ref in grad_refs[1:]:
            total = total + grad_ref[...].astype(F32)
        sums[...] = total.astype(BF16)

    rows = jnp.zeros((group * cap, sums.shape[-1]), F32)
    for part in range(slot_ref.shape[0]):
        hot = one_hot(group * cap, slot_ref[part : part + 1, :], step * group * cap)
        rows = rows + dot(hot, sums[part], NN)
    pack_all(out_ref, 0, cap, rows, rows.T)


def collect_neg(sent, slot, grads, cap):
    devices = sent.shape[0]
    feature = grads[0].shape[-1]
    group = 16
    height = packed_height(cap, feature)
    return call(
        functools.partial(collect_neg_kernel, group=group, cap=cap),
        "collect_negatives",
        2 * devices * cap * feature * slot.size,
        4 * len(grads) * grads[0].size,
        grid=(devices // group,),
        in_specs=[
            pl.BlockSpec(memory_space=pl.ANY),
            pl.BlockSpec(slot.shape, lambda i: (0, 0)),
        ]
        + [pl.BlockSpec(grads[0].shape, lambda i: (0, 0, 0))] * len(grads),
        out_specs=pl.BlockSpec((group, height, LANES), lambda i: (i, 0, 0)),
        out_shape=jax.ShapeDtypeStruct(sent.shape, BF16),
        scratch_shapes=[pltpu.VMEM(grads[0].shape, BF16)],
        input_output_aliases={0: 0},
    )(sent, slot, *grads)


def add_kernel(*refs, rows, neg_cap, first):
    refs = list(refs)
    recv_ref, req_ref = refs[:2]
    refs = refs[2:]
    if neg_cap:
        neg_req_ref = refs.pop(0)
        neg_rows, neg_flat = refs[-2:]
    if not first:
        so_far_ref = refs.pop(0)
    out_ref, flat = refs[:2]
    devices = recv_ref.shape[0]
    feature = flat.shape[0]
    step = pl.program_id(0)

    @pl.when(step == 0)
    def _():
        start = recv_ref.shape[1] - feature
        for d in range(devices):
            flat[:, d * LANES : (d + 1) * LANES] = recv_ref[d, start:]
        if neg_cap:
            unpack_all(recv_ref, 0, neg_cap, neg_rows, neg_flat)

    base = step * rows
    row = jnp.concatenate([req_ref[d : d + 1, :] for d in range(devices)], axis=1)
    total = dot(flat[...], one_hot(rows, row, base), NT)
    if neg_cap:
        row = jnp.concatenate([neg_req_ref[d : d + 1, :neg_cap] for d in range(devices)], axis=1)
        total = total + dot(neg_flat[...], one_hot(rows, row, base), NT)
    if not first:
        total = total + so_far_ref[...]
    out_ref[...] = total


def add_rows(recv, requests, so_far, feature, rows_dev, neg_requests=None, neg_cap=0):
    devices = recv.shape[0]
    rows = 512 if devices * LANES <= 4096 else 128
    slots = devices * LANES
    whole_req = pl.BlockSpec((devices, LANES), lambda i: (0, 0))
    rows_spec = pl.BlockSpec((feature, rows), lambda i: (0, i))
    operands = [recv, requests]
    specs = [pl.BlockSpec(recv.shape, lambda i: (0, 0, 0)), whole_req]
    scratch = [pltpu.VMEM((feature, slots), BF16)]
    if neg_cap:
        operands.append(neg_requests)
        specs.append(whole_req)
        scratch += unpack_scratch(devices, neg_cap, feature)
    if so_far is not None:
        operands.append(so_far)
        specs.append(rows_spec)
    return call(
        functools.partial(add_kernel, rows=rows, neg_cap=neg_cap, first=so_far is None),
        "add_grads",
        2 * feature * slots * rows_dev,
        2 * feature * slots + 8 * feature * rows_dev,
        grid=(rows_dev // rows,),
        in_specs=specs,
        out_specs=rows_spec,
        out_shape=jax.ShapeDtypeStruct((feature, rows_dev), F32),
        scratch_shapes=scratch,
    )(*operands)


def add_pool_kernel(*refs, rows, first):
    one_ref, two_ref, one_req_ref, two_req_ref = refs[:4]
    out_ref, packed, *flats = refs[4 + (not first) :]
    step = pl.program_id(0)

    @pl.when(step == 0)
    def _():
        for recv_ref, flat in zip((one_ref, two_ref), flats):
            unpack_all(recv_ref, 0, POOL, packed, flat)

    total = dot(flats[0][...], one_hot(rows, one_req_ref[...], step * rows), NT)
    total = total + dot(flats[1][...], one_hot(rows, two_req_ref[...], step * rows), NT)
    if not first:
        total = total + refs[4][...]
    out_ref[...] = total


def add_pool(one, two, requests, so_far, feature, rows_dev):
    rows = 512
    devices = one.shape[0]
    slots = devices * POOL
    recv_spec = pl.BlockSpec(one.shape, lambda i: (0, 0, 0))
    req_spec = pl.BlockSpec((1, slots), lambda i: (0, 0))
    rows_spec = pl.BlockSpec((feature, rows), lambda i: (0, i))
    packed, flat = unpack_scratch(devices, POOL, feature)
    extra = [] if so_far is None else [so_far]
    return call(
        functools.partial(add_pool_kernel, rows=rows, first=so_far is None),
        "add_pool",
        4 * feature * slots * rows_dev,
        4 * feature * slots + 4 * feature * rows_dev,
        grid=(rows_dev // rows,),
        in_specs=[recv_spec, recv_spec, req_spec, req_spec] + [rows_spec] * len(extra),
        out_specs=rows_spec,
        out_shape=jax.ShapeDtypeStruct((feature, rows_dev), F32),
        scratch_shapes=[packed, flat, flat],
    )(one, two, requests[0][None], requests[1][None], *extra)


def after(value, other):
    anywhere = pl.BlockSpec(memory_space=pl.ANY)
    return call(
        lambda value_ref, other_ref, out_ref: None,
        "after",
        0,
        0,
        in_specs=[anywhere, anywhere],
        out_specs=anywhere,
        out_shape=jax.ShapeDtypeStruct(value.shape, value.dtype),
        input_output_aliases={0: 0},
    )(value, other)


def exchange(value):
    return lax.all_to_all(value, ("shard", "grp"), split_axis=0, concat_axis=0, tiled=True)


def swap(value, bit):
    sharers = lax.axis_size("grp")
    return lax.ppermute(value, "grp", [(i, i ^ bit) for i in range(sharers)])


def share_out(value, wait=lambda block: block):
    sharers = lax.axis_size("grp")
    blocks = {0: value}
    bit = sharers // 2
    while bit:
        for k in list(blocks):
            blocks[k ^ bit] = swap(wait(blocks[k]) if k else blocks[k], bit)
        bit //= 2
    return [blocks[k] for k in range(sharers)]


def trade(blocks):
    sharers = len(blocks)
    terms = [[block] for block in blocks]
    bit = 1
    while bit < sharers:
        for k in range(0, sharers, 2 * bit):
            total = terms[k ^ bit][0].astype(F32)
            for term in terms[k ^ bit][1:]:
                total = total + term.astype(F32)
            terms[k].append(swap(total.astype(BF16), bit))
        bit *= 2
    return terms[0]


def pad_lanes(value, width, fill):
    return jnp.pad(value, ((0, 0), (0, width - value.shape[1])), constant_values=fill)


def body(entity_table, rel_diag, src_ids, dst_ids, rel_ids, neg_ids):
    rows_dev, feature = entity_table.shape
    sharers = lax.axis_size("grp")
    devices = lax.axis_size("shard") * sharers
    spans, neg_count = neg_ids.shape
    edge_count = src_ids.shape[0]
    block_len = edge_count // spans
    edge_cap = 4 * edge_count // devices
    chunks = round_up(edge_cap, LANES) // LANES
    part_width = neg_count // sharers
    neg_cap = round_up(2 * spans * part_width // devices, 16)
    width = round_up(block_len, 512)
    part = round_up(part_width, LANES)
    me = lax.axis_index("grp")

    table = entity_table.T.astype(BF16)
    relations = rel_diag.T
    own_ids = lax.dynamic_slice_in_dim(neg_ids, me * part_width, part_width, 1)
    ends = jnp.concatenate(
        [src_ids.reshape(spans, block_len), dst_ids.reshape(spans, block_len)]
    )
    message, *slots = make_slots(
        pad_lanes(ends, width, -1),
        pad_lanes(own_ids, part, -1),
        rows_dev,
        devices,
        chunks,
        neg_cap,
    )
    neg_slot = slots[-1]
    busy = slots[-2]
    rel_rows = pad_lanes(rel_ids.reshape(spans, block_len), width, -1)
    asked = exchange(message)
    direct = [asked[:, c * LANES : (c + 1) * LANES] for c in range(chunks)]
    neg_asked = asked[:, -LANES:]

    sent_rows = gather(table, direct[0], neg_asked, neg_cap)

    def negatives_of(back, *wait):
        return share_out(spread_neg(back, neg_slot, neg_cap, feature), *wait)

    def direct_sent(src_grad, dst_grad, neg_grads):
        sent = collect(src_grad, dst_grad, slots[0], devices, neg_cap)
        return exchange(collect_neg(sent, neg_slot, trade(neg_grads), neg_cap))

    def chunked(zero=0):
        back = [exchange(sent_rows)]
        back += [exchange(gather(table, direct[c] + zero)) for c in range(1, chunks)]
        negatives = negatives_of(back[0])
        rows = None
        for c in range(chunks):
            rows = spread(back[c], slots[c], rows, feature)
        src_grad, dst_grad, neg_grads = edges(rows, rel_rows, relations, negatives)
        grad = None
        for c in range(1, chunks):
            sent = exchange(collect(src_grad, dst_grad, slots[c], devices))
            grad = add_rows(sent, direct[c], grad, feature, rows_dev)
        sent = direct_sent(src_grad, dst_grad, neg_grads)
        return add_rows(sent, direct[0], grad, feature, rows_dev, neg_asked, neg_cap)

    def pooled():
        start = chunks * LANES
        listed = asked[:, start : start + RELAYS * POOL].reshape(devices, RELAYS, POOL)
        listed = listed.transpose(1, 0, 2).reshape(RELAYS, devices * POOL) - me * rows_dev
        listed = listed[me ^ jnp.arange(RELAYS, dtype=jnp.int32)]
        back = exchange(sent_rows)
        far = swap(gather_pool(table, listed[3], devices), 1)
        far = swap(gather_pool(table, listed[2], devices) + far, 2)
        near = swap(gather_pool(table, listed[1], devices), 1)
        near = gather_pool(table, listed[0], devices) + near
        rows = spread(back, slots[0], None, feature)
        negatives = negatives_of(back, lambda block: after(block, rows))
        src_grad, dst_grad, rest = edges(
            rows, rel_rows, relations, negatives, exchange(near + far), slots[chunks], busy
        )
        neg_grads, pool = rest[:-1], rest[-1]
        near = exchange(pool)
        far = swap(near, 2)
        sent = direct_sent(src_grad, dst_grad, neg_grads)
        grad = add_pool(near, swap(near, 1), listed[:2], None, feature, rows_dev)
        far = after(far, grad)
        grad = add_pool(far, swap(far, 1), listed[2:], grad, feature, rows_dev)
        return add_rows(sent, direct[0], grad, feature, rows_dev, neg_asked, neg_cap)

    if chunks == 1 or sharers != RELAYS:
        return chunked().T
    flag = jnp.max(neg_asked[:, -1])
    return lax.while_loop(
        lambda state: state[1] > 0,
        lambda state: (chunked(jnp.minimum(state[1], 0)), -state[1]),
        (pooled(), flag),
    )[0].T


def solution(mesh):
    placed = (
        P(("shard", "grp"), None),
        P(),
        P(("shard", "grp")),
        P(("shard", "grp")),
        P(("shard", "grp")),
        P("shard", None),
    )
    return jax.shard_map(
        body, mesh=mesh, in_specs=placed, out_specs=P(("shard", "grp"), None), check_vma=False
    )
```

```python
import functools

import jax
import jax.numpy as jnp
from jax import lax
from jax.experimental import pallas as pl
from jax.experimental.pallas import tpu as pltpu
from jax.sharding import PartitionSpec as P

LANES = 128
POOL = 48
RELAYS = 4
SMALL = 64
HALF = LANES // 2
VMEM_BYTES = 56 << 20
F32 = jnp.float32
BF16 = jnp.bfloat16
NN = (((1,), (0,)), ((), ()))
NT = (((1,), (1,)), ((), ()))
TN = (((0,), (0,)), ((), ()))


def round_up(value, unit):
    return -(-value // unit) * unit


def dot(left, right, dims):
    return lax.dot_general(left, right, dims, preferred_element_type=F32)


def one_hot(rows, row, base=0):
    places = lax.broadcasted_iota(jnp.int32, (rows, row.shape[1]), 0) + base
    return jnp.where(places == row, 1.0, 0.0).astype(BF16)


def call(kernel, name, flops, nbytes, **kwargs):
    return pl.pallas_call(
        kernel,
        name=name,
        compiler_params=pltpu.CompilerParams(vmem_limit_bytes=VMEM_BYTES),
        cost_estimate=pl.CostEstimate(flops=flops, bytes_accessed=nbytes, transcendentals=0),
        **kwargs,
    )


def ranks(members, mixer):
    groups = members[0].shape[0]
    both = dot(jnp.concatenate(members, axis=0).astype(BF16), mixer, NN)
    taken = jnp.zeros((groups, LANES), F32)
    found = []
    for i, member in enumerate(members):
        chunk = both[i * groups : (i + 1) * groups]
        found.append(jnp.sum((chunk[:, :LANES] + taken) * member, axis=0, keepdims=True))
        taken = taken + chunk[:, LANES:]
    return [rank.astype(jnp.int32) for rank in found], taken


def fill(members, codes, places, count):
    groups = members[0].shape[0]
    high = [m * (c // LANES).astype(F32) for m, c in zip(members, codes)]
    low = [m * (c % LANES).astype(F32) for m, c in zip(members, codes)]
    left = jnp.concatenate(
        [jnp.concatenate(high, axis=1), jnp.concatenate(low, axis=1)], axis=0
    ).astype(BF16)
    sums = dot(left, one_hot(count, jnp.concatenate(places, axis=1)), NT)
    return (LANES * sums[:groups] + sums[groups:]).astype(jnp.int32) - 1


def slots_kernel(me_ref, ends_ref, own_ref, *refs, rows_dev, devices, chunks, neg_cap):
    pooled = chunks == 0
    msg_ref, neg_ref = refs[0], refs[-1]
    slot_refs = refs[1:-1]
    row = lax.broadcasted_iota(jnp.int32, (LANES, 2 * LANES), 0)
    lane = lax.broadcasted_iota(jnp.int32, (LANES, 2 * LANES), 1)
    mixer = jnp.where(row < lane, 1.0, 0.0).astype(BF16)
    owners = lax.broadcasted_iota(jnp.int32, (devices, LANES), 0)

    def prepare(ids_ref):
        where, holder, codes, members = [], [], [], []
        for segment in range(ids_ref.shape[0]):
            for start in range(0, ids_ref.shape[1], LANES):
                ids = ids_ref[segment : segment + 1, start : start + LANES]
                owner = jnp.where(ids >= 0, ids // rows_dev, -1)
                where.append((slice(segment, segment + 1), slice(start, start + LANES)))
                holder.append(owner)
                codes.append(jnp.where(ids >= 0, ids - owner * rows_dev + 1, 0))
                members.append(jnp.where(owners == owner, 1.0, 0.0))
        return where, holder, codes, members

    where, holder, codes, members = prepare(ends_ref)
    flag = jnp.full((1, 1), -1, jnp.int32)
    if pooled:
        parity = me_ref[0, 0] % 2
        upper = [jnp.where(code > rows_dev // 2, 1, 0) for code in codes]
        halves = [
            jnp.concatenate([member * (1.0 - u), member * u], axis=0)
            for member, u in zip(members, [u.astype(F32) for u in upper])
        ]
        found, _ = ranks(halves, mixer)
        places = []
        for at, owner, rank, u in zip(where, holder, found, upper):
            inside = (owner >= 0) & (rank < HALF)
            place = (u ^ parity) * HALF + rank
            slot_refs[0][at] = jnp.where(inside, owner * LANES + place, -1)
            places.append(jnp.where(inside, place, -1))
        msg_ref[:, :LANES] = fill(members, codes, places, LANES)
        offset = LANES

        pool_ref, busy_ref = slot_refs[1:]
        shards = devices // RELAYS
        room = RELAYS * POOL
        shard_rows = lax.broadcasted_iota(jnp.int32, (shards, LANES), 0)
        spilled, spill_codes = [], []
        for owner, code, rank in zip(holder, codes, found):
            shard = jnp.where(rank >= HALF, owner // RELAYS, -1)
            spilled.append(jnp.where(shard_rows == shard, 1.0, 0.0))
            spill_codes.append(code + (owner % RELAYS) * rows_dev)
        listed, taken = ranks(spilled, mixer)
        places = []
        for at, owner, rank, place in zip(where, holder, found, listed):
            inside = (owner >= 0) & (rank >= HALF) & (place < room)
            compact = jnp.where(
                place < SMALL, owner // RELAYS * SMALL + place, (shards - 1) * SMALL + place
            )
            pool_ref[at] = jnp.where(inside, compact, -1)
            places.append(jnp.where(inside, place, -1))
        listed = fill(spilled, spill_codes, places, 2 * LANES)
        for shard in range(shards):
            msg_ref[shard * RELAYS : (shard + 1) * RELAYS, offset : offset + 2 * LANES] = (
                jnp.broadcast_to(listed[shard : shard + 1], (RELAYS, 2 * LANES))
            )
        offset += 2 * LANES
        most = jnp.max(taken, axis=0, keepdims=True)
        busy = jnp.where(taken > SMALL, 1.0, 0.0)
        crowded = jnp.sum(busy, axis=0, keepdims=True) > 1.0
        flag = jnp.where((most > room) | crowded, 1, -1)[:, :1]
        place = jnp.sum(busy * shard_rows.astype(F32), axis=0, keepdims=True).astype(jnp.int32)
        busy_ref[...] = jnp.minimum(place, shards - 1)[:, :1]
    else:
        found, _ = ranks(members, mixer)
        for chunk in range(chunks):
            places = []
            for at, owner, rank in zip(where, holder, found):
                place = rank - chunk * LANES
                place = jnp.where((owner >= 0) & (place >= 0) & (place < LANES), place, -1)
                slot_refs[chunk][at] = jnp.where(place >= 0, owner * LANES + place, -1)
                places.append(place)
            msg_ref[:, chunk * LANES : (chunk + 1) * LANES] = fill(members, codes, places, LANES)
        offset = chunks * LANES

    where, holder, codes, members = prepare(own_ref)
    found, _ = ranks(members, mixer)
    for at, owner, rank in zip(where, holder, found):
        neg_ref[at] = jnp.where(owner >= 0, owner * neg_cap + rank, -1)
    places = [jnp.where(owner >= 0, rank, -1) for owner, rank in zip(holder, found)]
    listed = fill(members, codes, places, LANES)
    lanes = lax.broadcasted_iota(jnp.int32, listed.shape, 1)
    msg_ref[:, offset:] = jnp.where(lanes == LANES - 1, flag, listed)


def make_slots(me, ends, own, rows_dev, devices, chunks, neg_cap):
    width = (chunks + 1 if chunks else 4) * LANES
    ends_shape = jax.ShapeDtypeStruct(ends.shape, jnp.int32)
    if chunks:
        slots = [ends_shape] * chunks
    else:
        slots = [ends_shape, ends_shape, jax.ShapeDtypeStruct((1, 1), jnp.int32)]
    return call(
        functools.partial(
            slots_kernel,
            rows_dev=rows_dev,
            devices=devices,
            chunks=chunks,
            neg_cap=neg_cap,
        ),
        "slots",
        16 * devices * LANES * ends.size,
        8 * ends.size,
        in_specs=[
            pl.BlockSpec(memory_space=pltpu.SMEM),
            pl.BlockSpec(ends.shape, lambda: (0, 0)),
            pl.BlockSpec(own.shape, lambda: (0, 0)),
        ],
        out_shape=[jax.ShapeDtypeStruct((devices, width), jnp.int32)]
        + slots
        + [jax.ShapeDtypeStruct(own.shape, jnp.int32)],
    )(me.reshape(1, 1), ends, own)


def packed_height(count, feature):
    return feature // LANES * count + feature % LANES


def pack(out_ref, at, start, rows, tail):
    count, feature = rows.shape
    for piece in range(feature // LANES):
        out_ref[at, start + piece * count : start + (piece + 1) * count, :] = rows[
            :, piece * LANES : (piece + 1) * LANES
        ].astype(out_ref.dtype)
    tail = jnp.concatenate([tail, jnp.zeros((tail.shape[0], LANES - count), tail.dtype)], axis=1)
    end = start + packed_height(count, feature)
    out_ref[at, end - tail.shape[0] : end, :] = tail.astype(out_ref.dtype)


def pack_all(out_ref, start, count, rows, turned):
    feature = rows.shape[1]
    first = feature // LANES * LANES
    for i in range(out_ref.shape[0]):
        at = slice(i * count, (i + 1) * count)
        pack(out_ref, i, start, rows[at], turned[first:, at])


def unpack_all(in_ref, start, count, rows_ref, flat_ref):
    feature = flat_ref.shape[0]
    pieces = feature // LANES
    end = start + packed_height(count, feature)
    devices = in_ref.shape[0]
    for d in range(devices):
        for piece in range(pieces):
            rows_ref[d * count : (d + 1) * count, piece * LANES : (piece + 1) * LANES] = in_ref[
                d, start + piece * count : start + (piece + 1) * count, :
            ]
    tails = [
        in_ref[d, end - feature % LANES : end, :].astype(F32)[:, :count] for d in range(devices)
    ]
    flat_ref[: pieces * LANES] = rows_ref[...].astype(F32).T.astype(BF16)
    flat_ref[pieces * LANES :] = jnp.concatenate(tails, axis=1).astype(BF16)


def unpack_scratch(devices, count, feature):
    return [
        pltpu.VMEM((devices * count, feature // LANES * LANES), BF16),
        pltpu.VMEM((feature, devices * count), BF16),
    ]


def gather_kernel(table_ref, *refs, group, neg_cap):
    feature, rows_dev = table_ref.shape
    first = pl.program_id(0) * group
    req_ref, out_ref = refs[0], refs[-1]
    row = [req_ref[pl.ds(first + i, 1), :] for i in range(group)]
    if neg_cap:
        row += [refs[1][pl.ds(first + i, 1), :neg_cap] for i in range(group)]
    rows = dot(table_ref[...], one_hot(rows_dev, jnp.concatenate(row, axis=1)), NN)
    start = out_ref.shape[1] - feature
    for i in range(group):
        out_ref[i, start:] = rows[:, i * LANES : (i + 1) * LANES].astype(BF16)
    if neg_cap:
        neg = rows[:, group * LANES :]
        pack_all(out_ref, 0, neg_cap, neg.T, neg)


def gather(table, requests, neg_requests=None, neg_cap=0):
    feature, rows_dev = table.shape
    devices = requests.shape[0]
    group = 4
    height = feature + (packed_height(neg_cap, feature) if neg_cap else 0)
    slots = devices * (LANES + neg_cap)
    whole = pl.BlockSpec((devices, LANES), lambda i: (0, 0))
    return call(
        functools.partial(gather_kernel, group=group, neg_cap=neg_cap),
        "gather_rows",
        2 * feature * rows_dev * slots,
        2 * feature * (rows_dev + slots),
        grid=(devices // group,),
        in_specs=[pl.BlockSpec((feature, rows_dev), lambda i: (0, 0)), whole]
        + ([whole] if neg_cap else []),
        out_specs=pl.BlockSpec((group, height, LANES), lambda i: (i, 0, 0)),
        out_shape=jax.ShapeDtypeStruct((devices, height, LANES), BF16),
    )(table, requests, *([neg_requests] if neg_cap else []))


def gather_halves_kernel(table_ref, req_ref, neg_req_ref, out_ref, *, neg_cap):
    feature, rows_dev = table_ref.shape
    group = out_ref.shape[0]
    half = rows_dev // 2
    first = pl.program_id(0) * group
    ids = [req_ref[pl.ds(first + i, 1), :] for i in range(group)]
    left = lax.broadcasted_iota(jnp.int32, (1, LANES), 1) < HALF
    pairs = range(0, group, 2)
    low = jnp.concatenate([jnp.where(left, ids[i], ids[i + 1]) for i in pairs], axis=1)
    high = jnp.concatenate([jnp.where(left, ids[i + 1], ids[i]) for i in pairs], axis=1)
    low = dot(table_ref[:, :half], one_hot(half, low), NN)
    high = dot(table_ref[:, half:], one_hot(half, high, half), NN)
    start = out_ref.shape[1] - feature
    left = lax.broadcasted_iota(jnp.int32, (feature, LANES), 1) < HALF
    for i in pairs:
        at = slice(i // 2 * LANES, (i // 2 + 1) * LANES)
        out_ref[i, start:] = jnp.where(left, low[:, at], high[:, at]).astype(BF16)
        out_ref[i + 1, start:] = jnp.where(left, high[:, at], low[:, at]).astype(BF16)
    row = [neg_req_ref[pl.ds(first + i, 1), :neg_cap] for i in range(group)]
    neg = dot(table_ref[...], one_hot(rows_dev, jnp.concatenate(row, axis=1)), NN)
    pack_all(out_ref, 0, neg_cap, neg.T, neg)


def gather_halves(table, requests, neg_requests, neg_cap):
    feature, rows_dev = table.shape
    devices = requests.shape[0]
    group = 8
    height = feature + packed_height(neg_cap, feature)
    whole = pl.BlockSpec((devices, LANES), lambda i: (0, 0))
    return call(
        functools.partial(gather_halves_kernel, neg_cap=neg_cap),
        "gather_halves",
        feature * rows_dev * devices * (LANES + 2 * neg_cap),
        2 * feature * (rows_dev + devices * (LANES + neg_cap)),
        grid=(devices // group,),
        in_specs=[pl.BlockSpec((feature, rows_dev), lambda i: (0, 0)), whole, whole],
        out_specs=pl.BlockSpec((group, height, LANES), lambda i: (i, 0, 0)),
        out_shape=jax.ShapeDtypeStruct((devices, height, LANES), BF16),
    )(table, requests, neg_requests)


def gather_pool_kernel(table_ref, req_ref, out_ref, *, group):
    rows_dev = table_ref.shape[1]
    row = req_ref[...].reshape(1, group * POOL)
    rows = dot(table_ref[...], one_hot(rows_dev, row), NN)
    pack_all(out_ref, 0, POOL, rows.T, rows)


def gather_pool(table, requests, devices):
    feature, rows_dev = table.shape
    group = 8
    steps = devices // group
    height = packed_height(POOL, feature)
    return call(
        functools.partial(gather_pool_kernel, group=group),
        "gather_pool",
        2 * feature * rows_dev * requests.size,
        2 * feature * (rows_dev + requests.size),
        grid=(steps,),
        in_specs=[
            pl.BlockSpec((feature, rows_dev), lambda i: (0, 0)),
            pl.BlockSpec((1, 1, group * POOL), lambda i: (i, 0, 0)),
        ],
        out_specs=pl.BlockSpec((group, height, LANES), lambda i: (i, 0, 0)),
        out_shape=jax.ShapeDtypeStruct((devices, height, LANES), BF16),
    )(table, requests.reshape(steps, 1, group * POOL))


def spread_neg_kernel(back_ref, slot_ref, out_ref, rows, flat, *, cap):
    unpack_all(back_ref, 0, cap, rows, flat)
    for part in range(slot_ref.shape[0]):
        hot = one_hot(flat.shape[1], slot_ref[part : part + 1, :])
        out_ref[part] = dot(flat[...], hot, NN).T.astype(BF16)


def spread_neg(back, slot, cap, feature):
    devices = back.shape[0]
    parts, width = slot.shape
    height = packed_height(cap, feature)
    return call(
        functools.partial(spread_neg_kernel, cap=cap),
        "spread_negatives",
        2 * devices * cap * feature * slot.size,
        2 * devices * cap * feature,
        grid=(1,),
        in_specs=[
            pl.BlockSpec((devices, height, LANES), lambda i: (0, 0, 0)),
            pl.BlockSpec(slot.shape, lambda i: (0, 0)),
        ],
        out_specs=pl.BlockSpec((parts, width, feature), lambda i: (0, 0, 0)),
        out_shape=jax.ShapeDtypeStruct((parts, width, feature), BF16),
        scratch_shapes=unpack_scratch(devices, cap, feature),
    )(back, slot)


def spread_kernel(*refs, first):
    back_ref, slot_ref = refs[:2]
    so_far_ref = None if first else refs[2]
    out_ref, flat = refs[2 + (not first)], refs[-1]
    devices = back_ref.shape[0]
    feature = flat.shape[0]

    @pl.when(pl.program_id(0) == 0)
    def _():
        start = back_ref.shape[1] - feature
        for d in range(devices):
            flat[:, d * LANES : (d + 1) * LANES] = back_ref[d, start:]

    row = slot_ref[...].reshape(1, slot_ref.shape[-1])
    rows = dot(flat[...], one_hot(flat.shape[1], row), NN)
    if not first:
        rows = rows + so_far_ref[...].astype(F32)
    out_ref[...] = rows.astype(BF16)


def spread(back, slot, so_far, feature):
    devices = back.shape[0]
    segments, width = slot.shape
    slots = devices * LANES
    tile = 512 if slots <= 4096 else 128
    steps = width // tile
    rows_spec = pl.BlockSpec((feature, tile), lambda i: (0, i))
    extra = [] if so_far is None else [so_far]
    return call(
        functools.partial(spread_kernel, first=so_far is None),
        "spread_rows",
        2 * feature * slots * slot.size,
        2 * feature * (slots + slot.size),
        grid=(segments * steps,),
        in_specs=[
            pl.BlockSpec(back.shape, lambda i: (0, 0, 0)),
            pl.BlockSpec((1, 1, tile), lambda i: (i // steps, 0, i % steps)),
        ]
        + [rows_spec] * len(extra),
        out_specs=rows_spec,
        out_shape=jax.ShapeDtypeStruct((feature, slot.size), BF16),
        scratch_shapes=[pltpu.VMEM((feature, slots), BF16)],
    )(back, slot.reshape(segments, 1, width), *extra)


def compact_places(shards):
    places = []
    for start, end, whose in ((0, SMALL, range(shards)), (SMALL, RELAYS * POOL, [None])):
        for shard in whose:
            place = start
            while place < end:
                relay, first = place // POOL, place % POOL
                count = min(POOL - first, end - place)
                to = (shards - 1 if shard is None else shard) * SMALL + place
                places.append((shard, relay, first, count, to))
                place += count
    return places


def compact_size(shards):
    return shards * SMALL + RELAYS * POOL - SMALL


def compact_pool(back_ref, busy, rows_ref, flat_ref):
    feature = flat_ref.shape[0]
    pieces = feature // LANES
    tails = []
    for shard, relay, first, count, to in compact_places(back_ref.shape[0] // RELAYS):
        at = (busy if shard is None else shard) * RELAYS + relay
        for piece in range(pieces):
            start = piece * POOL + first
            rows_ref[to : to + count, piece * LANES : (piece + 1) * LANES] = back_ref[
                at, start : start + count, :
            ]
        tail = back_ref[at, pieces * POOL :, :].astype(F32)
        tails.append(tail[:, first : first + count])
    flat_ref[: pieces * LANES] = rows_ref[...].astype(F32).T.astype(BF16)
    flat_ref[pieces * LANES :] = jnp.concatenate(tails, axis=1).astype(BF16)


def expand_pool(rows, busy, out_ref):
    feature = rows.shape[1]
    pieces = feature // LANES
    turned = rows.T
    out_ref[...] = jnp.zeros(out_ref.shape, out_ref.dtype)
    shards = out_ref.shape[0] // RELAYS
    for shard, relay, first, count, to in compact_places(shards):
        at = (busy if shard is None else shard) * RELAYS + relay
        for piece in range(pieces):
            start = piece * POOL + first
            out_ref[at, start : start + count, :] = rows[
                to : to + count, piece * LANES : (piece + 1) * LANES
            ].astype(BF16)
        if shard is not None:
            tail = turned[pieces * LANES :, to : to + count]
        else:
            tail = turned[pieces * LANES :, to : to + count]
            if first:
                kept = jnp.zeros((feature % LANES, first), F32)
                for other in range(shards):
                    start = other * SMALL + relay * POOL
                    part = turned[pieces * LANES :, start : start + first]
                    kept = jnp.where(busy == other, part, kept)
                tail = jnp.concatenate([kept, tail], axis=1)
        blank = jnp.zeros((tail.shape[0], LANES - tail.shape[1]), F32)
        out_ref[at, pieces * POOL :, :] = jnp.concatenate([tail, blank], axis=1).astype(BF16)


def edges_kernel(*refs, parts, pooled):
    refs = list(refs)
    src_ref, dst_ref, rel_ids_ref, rel_ref = refs[:4]
    neg_refs = refs[4 : 4 + parts]
    refs = refs[4 + parts :]
    if pooled:
        back_ref, src_slot_ref, dst_slot_ref, busy_ref = refs[:4]
        refs = refs[4:]
        pool_out_ref = refs.pop(2 + parts)
        pool_rows, pool_flat, pool_sums = refs[-3:]
    src_grad_ref, dst_grad_ref = refs[:2]
    neg_grad_refs = refs[2 : 2 + parts]
    negatives, rel_flat = refs[2 + parts : 4 + parts]
    block = pl.program_id(0)
    part = neg_refs[0].shape[1]

    @pl.when(block == 0)
    def _():
        table, pieces = rel_ref[...], []
        for _ in range(3):
            pieces.append(table.astype(BF16).astype(F32))
            table = table - pieces[-1]
        rel_flat[...] = jnp.concatenate(pieces, axis=0).T.astype(BF16)
        if pooled:
            compact_pool(back_ref, busy_ref[0, 0], pool_rows, pool_flat)
            pool_sums[...] = jnp.zeros(pool_sums.shape, F32)

    for k in range(parts):
        negatives[k * part : (k + 1) * part] = neg_refs[k][0]
    turned = negatives[...].astype(F32).T.astype(BF16)
    hot = one_hot(rel_ref.shape[0], rel_ids_ref[...].reshape(1, rel_ids_ref.shape[-1]))
    relation = dot(rel_flat[...], jnp.concatenate([hot] * 3, axis=0), NN)
    source = src_ref[...].astype(F32)
    target = dst_ref[...].astype(F32)
    if pooled:
        count = pool_flat.shape[1]
        src_hot = one_hot(count, src_slot_ref[...].reshape(1, src_slot_ref.shape[-1]))
        dst_hot = one_hot(count, dst_slot_ref[...].reshape(1, dst_slot_ref.shape[-1]))
        source = source + dot(pool_flat[...], src_hot, NN)
        target = target + dot(pool_flat[...], dst_hot, NN)
    product = source * relation
    positive = jnp.sum(product * target, axis=0, keepdims=True)
    pos_weight = -jax.nn.sigmoid(-positive)
    query = product.astype(BF16)
    weight = jax.nn.sigmoid(dot(negatives[...], query, NN)).astype(BF16)
    gathered = dot(turned, weight, NN)
    src_grad = (relation * (pos_weight * target + gathered)).astype(BF16)
    dst_grad = (pos_weight * product).astype(BF16)
    src_grad_ref[...] = src_grad
    dst_grad_ref[...] = dst_grad
    neg_grad = dot(weight, query, NT)
    if pooled:
        pool_sums[...] += dot(src_hot, src_grad, NT) + dot(dst_hot, dst_grad, NT)

    for k in range(parts):
        neg_grad_refs[k][0] = neg_grad[k * part : (k + 1) * part].astype(BF16)
    if pooled:

        @pl.when(block == pl.num_programs(0) - 1)
        def _():
            expand_pool(pool_sums[...], busy_ref[0, 0], pool_out_ref)


def edges(rows, rel_ids, relations, negatives, pool=None, pool_slot=None, busy=None):
    feature, endpoints = rows.shape
    parts = len(negatives)
    spans, part, _ = negatives[0].shape
    width = rel_ids.shape[1]
    edge_spec = pl.BlockSpec((feature, width), lambda b: (0, b))
    neg_spec = pl.BlockSpec((1, part, feature), lambda b: (b, 0, 0))
    operands = [rows, rows, rel_ids.reshape(spans, 1, width), relations, *negatives]
    specs = [
        edge_spec,
        pl.BlockSpec((feature, width), lambda b: (0, spans + b)),
        pl.BlockSpec((1, 1, width), lambda b: (b, 0, 0)),
        pl.BlockSpec(relations.shape, lambda b: (0, 0)),
    ] + [neg_spec] * parts
    out_specs = [edge_spec, edge_spec] + [neg_spec] * parts
    out_shape = [jax.ShapeDtypeStruct((feature, endpoints // 2), BF16)] * 2
    out_shape += [jax.ShapeDtypeStruct((spans, part, feature), BF16)] * parts
    scratch = [
        pltpu.VMEM((parts * part, feature), BF16),
        pltpu.VMEM((feature, 3 * relations.shape[0]), BF16),
    ]
    if pool is not None:
        slot = pool_slot.reshape(2 * spans, 1, width)
        pool_spec = pl.BlockSpec(pool.shape, lambda b: (0, 0, 0))
        operands += [pool, slot, slot, busy]
        specs += [
            pool_spec,
            pl.BlockSpec((1, 1, width), lambda b: (b, 0, 0)),
            pl.BlockSpec((1, 1, width), lambda b: (spans + b, 0, 0)),
            pl.BlockSpec(memory_space=pltpu.SMEM),
        ]
        out_specs.append(pool_spec)
        out_shape.append(jax.ShapeDtypeStruct(pool.shape, BF16))
        count = compact_size(pool.shape[0] // RELAYS)
        scratch += [
            pltpu.VMEM((count, feature // LANES * LANES), BF16),
            pltpu.VMEM((feature, count), BF16),
            pltpu.VMEM((count, feature), F32),
        ]
    src_grad, dst_grad, *rest = call(
        functools.partial(edges_kernel, parts=parts, pooled=pool is not None),
        "edges",
        6 * feature * parts * part * spans * width,
        4 * (rows.size + parts * negatives[0].size),
        grid=(spans,),
        in_specs=specs,
        out_specs=out_specs,
        out_shape=out_shape,
        scratch_shapes=scratch,
    )(*operands)
    return src_grad, dst_grad, rest


def collect_kernel(src_ref, dst_ref, slot_ref, out_ref, *, group):
    segments, width = slot_ref.shape
    feature = src_ref.shape[0]
    step = pl.program_id(0)
    total = jnp.zeros((feature, group * LANES), F32)
    for segment in range(segments):
        grads = src_ref if segment < segments // 2 else dst_ref
        start = segment % (segments // 2) * width
        hot = one_hot(group * LANES, slot_ref[segment : segment + 1, :], step * group * LANES)
        total = total + dot(grads[:, start : start + width], hot, NT)
    total = total.astype(BF16)
    first = out_ref.shape[1] - feature
    for i in range(group):
        out_ref[i, first:] = total[:, i * LANES : (i + 1) * LANES]


def collect(src_grad, dst_grad, slot, devices, neg_cap=0):
    feature = src_grad.shape[0]
    group = 4
    slots = devices * LANES
    height = feature + (packed_height(neg_cap, feature) if neg_cap else 0)
    whole = pl.BlockSpec(src_grad.shape, lambda i: (0, 0))
    return call(
        functools.partial(collect_kernel, group=group),
        "collect_grads",
        2 * feature * slots * slot.size,
        2 * feature * (slots + slot.size),
        grid=(devices // group,),
        in_specs=[whole, whole, pl.BlockSpec(slot.shape, lambda i: (0, 0))],
        out_specs=pl.BlockSpec((group, height, LANES), lambda i: (i, 0, 0)),
        out_shape=jax.ShapeDtypeStruct((devices, height, LANES), BF16),
    )(src_grad, dst_grad, slot)


def collect_neg_kernel(sent_ref, slot_ref, *refs, group, cap):
    grad_refs, out_ref, sums = refs[:-2], refs[-2], refs[-1]
    step = pl.program_id(0)

    @pl.when(step == 0)
    def _():
        total = grad_refs[0][...].astype(F32)
        for grad_ref in grad_refs[1:]:
            total = total + grad_ref[...].astype(F32)
        sums[...] = total.astype(BF16)

    rows = jnp.zeros((group * cap, sums.shape[-1]), F32)
    for part in range(slot_ref.shape[0]):
        hot = one_hot(group * cap, slot_ref[part : part + 1, :], step * group * cap)
        rows = rows + dot(hot, sums[part], NN)
    pack_all(out_ref, 0, cap, rows, rows.T)


def collect_neg(sent, slot, grads, cap):
    devices = sent.shape[0]
    feature = grads[0].shape[-1]
    group = 16
    height = packed_height(cap, feature)
    return call(
        functools.partial(collect_neg_kernel, group=group, cap=cap),
        "collect_negatives",
        2 * devices * cap * feature * slot.size,
        4 * len(grads) * grads[0].size,
        grid=(devices // group,),
        in_specs=[
            pl.BlockSpec(memory_space=pl.ANY),
            pl.BlockSpec(slot.shape, lambda i: (0, 0)),
        ]
        + [pl.BlockSpec(grads[0].shape, lambda i: (0, 0, 0))] * len(grads),
        out_specs=pl.BlockSpec((group, height, LANES), lambda i: (i, 0, 0)),
        out_shape=jax.ShapeDtypeStruct(sent.shape, BF16),
        scratch_shapes=[pltpu.VMEM(grads[0].shape, BF16)],
        input_output_aliases={0: 0},
    )(sent, slot, *grads)


def add_kernel(*refs, rows, neg_cap, first):
    refs = list(refs)
    recv_ref, req_ref = refs[:2]
    refs = refs[2:]
    if neg_cap:
        neg_req_ref = refs.pop(0)
        neg_rows, neg_flat = refs[-2:]
    if not first:
        so_far_ref = refs.pop(0)
    out_ref, flat = refs[:2]
    devices = recv_ref.shape[0]
    feature = flat.shape[0]
    step = pl.program_id(0)

    @pl.when(step == 0)
    def _():
        start = recv_ref.shape[1] - feature
        for d in range(devices):
            flat[:, d * LANES : (d + 1) * LANES] = recv_ref[d, start:]
        if neg_cap:
            unpack_all(recv_ref, 0, neg_cap, neg_rows, neg_flat)

    base = step * rows
    row = jnp.concatenate([req_ref[d : d + 1, :] for d in range(devices)], axis=1)
    total = dot(flat[...], one_hot(rows, row, base), NT)
    if neg_cap:
        row = jnp.concatenate([neg_req_ref[d : d + 1, :neg_cap] for d in range(devices)], axis=1)
        total = total + dot(neg_flat[...], one_hot(rows, row, base), NT)
    if not first:
        total = total + so_far_ref[...]
    out_ref[...] = total


def add_rows(recv, requests, so_far, feature, rows_dev, neg_requests=None, neg_cap=0):
    devices = recv.shape[0]
    rows = 512 if devices * LANES <= 4096 else 128
    slots = devices * LANES
    whole_req = pl.BlockSpec((devices, LANES), lambda i: (0, 0))
    rows_spec = pl.BlockSpec((feature, rows), lambda i: (0, i))
    operands = [recv, requests]
    specs = [pl.BlockSpec(recv.shape, lambda i: (0, 0, 0)), whole_req]
    scratch = [pltpu.VMEM((feature, slots), BF16)]
    if neg_cap:
        operands.append(neg_requests)
        specs.append(whole_req)
        scratch += unpack_scratch(devices, neg_cap, feature)
    if so_far is not None:
        operands.append(so_far)
        specs.append(rows_spec)
    return call(
        functools.partial(add_kernel, rows=rows, neg_cap=neg_cap, first=so_far is None),
        "add_grads",
        2 * feature * slots * rows_dev,
        2 * feature * slots + 8 * feature * rows_dev,
        grid=(rows_dev // rows,),
        in_specs=specs,
        out_specs=rows_spec,
        out_shape=jax.ShapeDtypeStruct((feature, rows_dev), F32),
        scratch_shapes=scratch,
    )(*operands)


def add_halves_kernel(
    recv_ref, req_ref, neg_req_ref, so_far_ref, out_ref, flat, neg_rows, neg_flat, *, neg_cap
):
    devices = recv_ref.shape[0]
    feature, rows = out_ref.shape
    step = pl.program_id(0)
    pairs = range(0, devices, 2)

    @pl.when(step == 0)
    def _():
        start = recv_ref.shape[1] - feature
        for i in pairs:
            to = i // 2 * LANES
            for half in range(2):
                flat[half, :, to : to + HALF] = recv_ref[i + half, start:, :HALF]
                flat[half, :, to + HALF : to + LANES] = recv_ref[i + 1 - half, start:, HALF:]
        unpack_all(recv_ref, 0, neg_cap, neg_rows, neg_flat)

    base = step * rows
    upper = 2 * step // pl.num_programs(0)
    ids = [req_ref[d : d + 1, :] for d in range(devices)]
    left = (lax.broadcasted_iota(jnp.int32, (1, LANES), 1) < HALF) ^ (upper == 1)
    row = jnp.concatenate([jnp.where(left, ids[i], ids[i + 1]) for i in pairs], axis=1)
    total = dot(flat[upper], one_hot(rows, row, base), NT)
    row = jnp.concatenate([neg_req_ref[d : d + 1, :neg_cap] for d in range(devices)], axis=1)
    out_ref[...] = total + dot(neg_flat[...], one_hot(rows, row, base), NT) + so_far_ref[...]


def add_halves(recv, requests, neg_requests, so_far, neg_cap):
    feature, rows_dev = so_far.shape
    devices = recv.shape[0]
    rows = 1024
    slots = devices * LANES
    whole_req = pl.BlockSpec((devices, LANES), lambda i: (0, 0))
    rows_spec = pl.BlockSpec((feature, rows), lambda i: (0, i))
    return call(
        functools.partial(add_halves_kernel, neg_cap=neg_cap),
        "add_halves",
        feature * (slots + 2 * devices * neg_cap) * rows_dev,
        2 * feature * slots + 8 * feature * rows_dev,
        grid=(rows_dev // rows,),
        in_specs=[pl.BlockSpec(recv.shape, lambda i: (0, 0, 0)), whole_req, whole_req, rows_spec],
        out_specs=rows_spec,
        out_shape=jax.ShapeDtypeStruct((feature, rows_dev), F32),
        scratch_shapes=[pltpu.VMEM((2, feature, slots // 2), BF16)]
        + unpack_scratch(devices, neg_cap, feature),
    )(recv, requests, neg_requests, so_far)


def add_pool_kernel(*refs, rows, first):
    one_ref, two_ref, one_req_ref, two_req_ref = refs[:4]
    out_ref, packed, *flats = refs[4 + (not first) :]
    step = pl.program_id(0)

    @pl.when(step == 0)
    def _():
        for recv_ref, flat in zip((one_ref, two_ref), flats):
            unpack_all(recv_ref, 0, POOL, packed, flat)

    total = dot(flats[0][...], one_hot(rows, one_req_ref[...], step * rows), NT)
    total = total + dot(flats[1][...], one_hot(rows, two_req_ref[...], step * rows), NT)
    if not first:
        total = total + refs[4][...]
    out_ref[...] = total


def add_pool(one, two, requests, so_far, feature, rows_dev):
    rows = 512
    devices = one.shape[0]
    slots = devices * POOL
    recv_spec = pl.BlockSpec(one.shape, lambda i: (0, 0, 0))
    req_spec = pl.BlockSpec((1, slots), lambda i: (0, 0))
    rows_spec = pl.BlockSpec((feature, rows), lambda i: (0, i))
    packed, flat = unpack_scratch(devices, POOL, feature)
    extra = [] if so_far is None else [so_far]
    return call(
        functools.partial(add_pool_kernel, rows=rows, first=so_far is None),
        "add_pool",
        4 * feature * slots * rows_dev,
        4 * feature * slots + 4 * feature * rows_dev,
        grid=(rows_dev // rows,),
        in_specs=[recv_spec, recv_spec, req_spec, req_spec] + [rows_spec] * len(extra),
        out_specs=rows_spec,
        out_shape=jax.ShapeDtypeStruct((feature, rows_dev), F32),
        scratch_shapes=[packed, flat, flat],
    )(one, two, requests[0][None], requests[1][None], *extra)


def after(value, other):
    anywhere = pl.BlockSpec(memory_space=pl.ANY)
    return call(
        lambda value_ref, other_ref, out_ref: None,
        "after",
        0,
        0,
        in_specs=[anywhere, anywhere],
        out_specs=anywhere,
        out_shape=jax.ShapeDtypeStruct(value.shape, value.dtype),
        input_output_aliases={0: 0},
    )(value, other)


def exchange(value):
    return lax.all_to_all(value, ("shard", "grp"), split_axis=0, concat_axis=0, tiled=True)


def swap(value, bit):
    sharers = lax.axis_size("grp")
    return lax.ppermute(value, "grp", [(i, i ^ bit) for i in range(sharers)])


def share_out(value, wait=lambda block: block):
    sharers = lax.axis_size("grp")
    blocks = {0: value}
    bit = sharers // 2
    while bit:
        for k in list(blocks):
            blocks[k ^ bit] = swap(wait(blocks[k]) if k else blocks[k], bit)
        bit //= 2
    return [blocks[k] for k in range(sharers)]


def trade(blocks):
    sharers = len(blocks)
    terms = [[block] for block in blocks]
    bit = 1
    while bit < sharers:
        for k in range(0, sharers, 2 * bit):
            total = terms[k ^ bit][0].astype(F32)
            for term in terms[k ^ bit][1:]:
                total = total + term.astype(F32)
            terms[k].append(swap(total.astype(BF16), bit))
        bit *= 2
    return terms[0]


def pad_lanes(value, width, fill):
    return jnp.pad(value, ((0, 0), (0, width - value.shape[1])), constant_values=fill)


def body(entity_table, rel_diag, src_ids, dst_ids, rel_ids, neg_ids):
    rows_dev, feature = entity_table.shape
    sharers = lax.axis_size("grp")
    devices = lax.axis_size("shard") * sharers
    spans, neg_count = neg_ids.shape
    edge_count = src_ids.shape[0]
    block_len = edge_count // spans
    edge_cap = 4 * edge_count // devices
    chunks = round_up(edge_cap, LANES) // LANES
    part_width = neg_count // sharers
    neg_cap = round_up(2 * spans * part_width // devices, 16)
    width = round_up(block_len, 512)
    part = round_up(part_width, LANES)
    me = lax.axis_index("grp")

    table = entity_table.T.astype(BF16)
    own_ids = lax.dynamic_slice_in_dim(neg_ids, me * part_width, part_width, 1)
    ends = jnp.concatenate(
        [src_ids.reshape(spans, block_len), dst_ids.reshape(spans, block_len)]
    )
    ends = pad_lanes(ends, width, -1)
    own_ids = pad_lanes(own_ids, part, -1)
    rel_rows = pad_lanes(rel_ids.reshape(spans, block_len), width, -1)

    def ask(ends, chunks):
        message, *slots = make_slots(
            lax.axis_index(("shard", "grp")), ends, own_ids, rows_dev, devices, chunks, neg_cap
        )
        asked = exchange(message)
        return asked, asked[:, -LANES:], slots, slots[-1]

    def chunked(ends):
        asked, neg_asked, slots, neg_slot = ask(ends, chunks)
        direct = [asked[:, c * LANES : (c + 1) * LANES] for c in range(chunks)]
        back = [exchange(gather(table, direct[0], neg_asked, neg_cap))]
        back += [exchange(gather(table, direct[c])) for c in range(1, chunks)]
        negatives = share_out(spread_neg(back[0], neg_slot, neg_cap, feature))
        rows = None
        for c in range(chunks):
            rows = spread(back[c], slots[c], rows, feature)
        src_grad, dst_grad, neg_grads = edges(rows, rel_rows, rel_diag, negatives)
        grad = None
        for c in range(1, chunks):
            sent = exchange(collect(src_grad, dst_grad, slots[c], devices))
            grad = add_rows(sent, direct[c], grad, feature, rows_dev)
        sent = collect(src_grad, dst_grad, slots[0], devices, neg_cap)
        sent = exchange(collect_neg(sent, neg_slot, trade(neg_grads), neg_cap))
        return add_rows(sent, direct[0], grad, feature, rows_dev, neg_asked, neg_cap)

    def pooled():
        asked, neg_asked, (slot, pool_slot, busy, _), neg_slot = ask(ends, 0)
        direct = asked[:, :LANES]
        listed = asked[:, LANES : LANES + RELAYS * POOL].reshape(devices, RELAYS, POOL)
        listed = listed.transpose(1, 0, 2).reshape(RELAYS, devices * POOL) - me * rows_dev
        listed = listed[me ^ jnp.arange(RELAYS, dtype=jnp.int32)]
        back = exchange(gather_halves(table, direct, neg_asked, neg_cap))
        far = swap(gather_pool(table, listed[3], devices), 1)
        far = swap(gather_pool(table, listed[2], devices) + far, 2)
        near = swap(gather_pool(table, listed[1], devices), 1)
        near = gather_pool(table, listed[0], devices) + near
        rows = spread(back, slot, None, feature)
        negatives = share_out(
            spread_neg(back, neg_slot, neg_cap, feature), lambda block: after(block, rows)
        )
        src_grad, dst_grad, rest = edges(
            rows, rel_rows, rel_diag, negatives, exchange(near + far), pool_slot, busy
        )
        neg_grads, pool = rest[:-1], rest[-1]
        near = exchange(pool)
        far = swap(near, 2)
        sent = collect(src_grad, dst_grad, slot, devices, neg_cap)
        sent = exchange(collect_neg(sent, neg_slot, trade(neg_grads), neg_cap))
        grad = add_pool(near, swap(near, 1), listed[:2], None, feature, rows_dev)
        far = after(far, grad)
        grad = add_pool(far, swap(far, 1), listed[2:], grad, feature, rows_dev)
        return add_halves(sent, direct, neg_asked, grad, neg_cap), jnp.max(neg_asked[:, -1])

    if chunks == 1 or sharers != RELAYS:
        return chunked(ends).T
    return lax.while_loop(
        lambda state: state[1] > 0,
        lambda state: (chunked(ends + jnp.minimum(state[1], 0)), -state[1]),
        pooled(),
    )[0].T


def solution(mesh):
    placed = (
        P(("shard", "grp"), None),
        P(),
        P(("shard", "grp")),
        P(("shard", "grp")),
        P(("shard", "grp")),
        P("shard", None),
    )
    return jax.shard_map(
        body, mesh=mesh, in_specs=placed, out_specs=P(("shard", "grp"), None), check_vma=False
    )
```

```python
import functools

import jax
import jax.numpy as jnp
from jax import lax
from jax.experimental import pallas as pl
from jax.experimental.pallas import tpu as pltpu
from jax.sharding import PartitionSpec as P

LANES = 128
POOL = 48
RELAYS = 4
SMALL = 80
PARTS = 4
SHARE = LANES // PARTS
VMEM_BYTES = 56 << 20
F32 = jnp.float32
BF16 = jnp.bfloat16
NN = (((1,), (0,)), ((), ()))
NT = (((1,), (1,)), ((), ()))
TN = (((0,), (0,)), ((), ()))


def round_up(value, unit):
    return -(-value // unit) * unit


def dot(left, right, dims):
    return lax.dot_general(left, right, dims, preferred_element_type=F32)


def one_hot(rows, row, base=0):
    places = lax.broadcasted_iota(jnp.int32, (rows, row.shape[1]), 0) + base
    return jnp.where(places == row, 1.0, 0.0).astype(BF16)


def call(kernel, name, flops, nbytes, **kwargs):
    return pl.pallas_call(
        kernel,
        name=name,
        compiler_params=pltpu.CompilerParams(vmem_limit_bytes=VMEM_BYTES),
        cost_estimate=pl.CostEstimate(flops=flops, bytes_accessed=nbytes, transcendentals=0),
        **kwargs,
    )


def ranks(members, mixer):
    groups = members[0].shape[0]
    both = dot(jnp.concatenate(members, axis=0).astype(BF16), mixer, NN)
    taken = jnp.zeros((groups, LANES), F32)
    found = []
    for i, member in enumerate(members):
        chunk = both[i * groups : (i + 1) * groups]
        found.append(jnp.sum((chunk[:, :LANES] + taken) * member, axis=0, keepdims=True))
        taken = taken + chunk[:, LANES:]
    return [rank.astype(jnp.int32) for rank in found], taken


def fill(members, codes, places, count):
    groups = members[0].shape[0]
    high = [m * (c // LANES).astype(F32) for m, c in zip(members, codes)]
    low = [m * (c % LANES).astype(F32) for m, c in zip(members, codes)]
    left = jnp.concatenate(
        [jnp.concatenate(high, axis=1), jnp.concatenate(low, axis=1)], axis=0
    ).astype(BF16)
    sums = dot(left, one_hot(count, jnp.concatenate(places, axis=1)), NT)
    return (LANES * sums[:groups] + sums[groups:]).astype(jnp.int32) - 1


def slots_kernel(
    me_ref, src_ref, dst_ref, own_ref, *refs, rows_dev, devices, chunks, neg_cap, spans, part
):
    pooled = chunks == 0
    msg_ref, neg_ref = refs[0], refs[-1]
    slot_refs = refs[1:-1]
    row = lax.broadcasted_iota(jnp.int32, (LANES, 2 * LANES), 0)
    lane = lax.broadcasted_iota(jnp.int32, (LANES, 2 * LANES), 1)
    mixer = jnp.where(row < lane, 1.0, 0.0).astype(BF16)
    owners = lax.broadcasted_iota(jnp.int32, (devices, LANES), 0)

    def prepare(rows, width):
        where, holder, codes, members = [], [], [], []
        for segment, ids_row in enumerate(rows):
            blank = jnp.full((1, width - ids_row.shape[1]), -1, jnp.int32)
            ids_row = jnp.concatenate([ids_row, blank], axis=1)
            for start in range(0, width, LANES):
                ids = ids_row[:, start : start + LANES]
                owner = jnp.where(ids >= 0, ids // rows_dev, -1)
                where.append((slice(segment, segment + 1), slice(start, start + LANES)))
                holder.append(owner)
                codes.append(jnp.where(ids >= 0, ids - owner * rows_dev + 1, 0))
                members.append(jnp.where(owners == owner, 1.0, 0.0))
        return where, holder, codes, members

    ends = []
    for ids_ref in (src_ref, dst_ref):
        ids = ids_ref[...].reshape(1, ids_ref.shape[0])
        length = ids.shape[1] // spans
        ends += [ids[:, b * length : (b + 1) * length] for b in range(spans)]
    where, holder, codes, members = prepare(ends, slot_refs[0].shape[1])
    flag = jnp.full((1, 1), -1, jnp.int32)
    if pooled:
        turn = me_ref[0, 0] % PARTS
        quarters = [jnp.maximum(code - 1, 0) // (rows_dev // PARTS) for code in codes]
        split = [
            jnp.concatenate([jnp.where(q == k, member, 0.0) for k in range(PARTS)], axis=0)
            for member, q in zip(members, quarters)
        ]
        found, _ = ranks(split, mixer)
        places = []
        for at, owner, rank, q in zip(where, holder, found, quarters):
            inside = (owner >= 0) & (rank < SHARE)
            place = (q ^ turn) * SHARE + rank
            slot_refs[0][at] = jnp.where(inside, owner * LANES + place, -1)
            places.append(jnp.where(inside, place, -1))
        msg_ref[:, :LANES] = fill(members, codes, places, LANES)
        offset = LANES

        pool_ref, busy_ref = slot_refs[1:]
        shards = devices // RELAYS
        room = RELAYS * POOL
        shard_rows = lax.broadcasted_iota(jnp.int32, (shards, LANES), 0)
        spilled, spill_codes = [], []
        for owner, code, rank in zip(holder, codes, found):
            shard = jnp.where(rank >= SHARE, owner // RELAYS, -1)
            spilled.append(jnp.where(shard_rows == shard, 1.0, 0.0))
            spill_codes.append(code + (owner % RELAYS) * rows_dev)
        listed, taken = ranks(spilled, mixer)
        places = []
        for at, owner, rank, place in zip(where, holder, found, listed):
            inside = (owner >= 0) & (rank >= SHARE) & (place < room)
            compact = jnp.where(
                place < SMALL, owner // RELAYS * SMALL + place, (shards - 1) * SMALL + place
            )
            pool_ref[at] = jnp.where(inside, compact, -1)
            places.append(jnp.where(inside, place, -1))
        listed = fill(spilled, spill_codes, places, 2 * LANES)
        for shard in range(shards):
            msg_ref[shard * RELAYS : (shard + 1) * RELAYS, offset : offset + 2 * LANES] = (
                jnp.broadcast_to(listed[shard : shard + 1], (RELAYS, 2 * LANES))
            )
        offset += 2 * LANES
        most = jnp.max(taken, axis=0, keepdims=True)
        busy = jnp.where(taken > SMALL, 1.0, 0.0)
        crowded = jnp.sum(busy, axis=0, keepdims=True) > 1.0
        flag = jnp.where((most > room) | crowded, 1, -1)[:, :1]
        place = jnp.sum(busy * shard_rows.astype(F32), axis=0, keepdims=True).astype(jnp.int32)
        busy_ref[...] = jnp.minimum(place, shards - 1)[:, :1]
    else:
        found, _ = ranks(members, mixer)
        for chunk in range(chunks):
            places = []
            for at, owner, rank in zip(where, holder, found):
                place = rank - chunk * LANES
                place = jnp.where((owner >= 0) & (place >= 0) & (place < LANES), place, -1)
                slot_refs[chunk][at] = jnp.where(place >= 0, owner * LANES + place, -1)
                places.append(place)
            msg_ref[:, chunk * LANES : (chunk + 1) * LANES] = fill(members, codes, places, LANES)
        offset = chunks * LANES

    where, holder, codes, members = prepare([own_ref[b : b + 1, :] for b in range(spans)], part)
    found, _ = ranks(members, mixer)
    for at, owner, rank in zip(where, holder, found):
        neg_ref[at] = jnp.where(owner >= 0, owner * neg_cap + rank, -1)
    places = [jnp.where(owner >= 0, rank, -1) for owner, rank in zip(holder, found)]
    listed = fill(members, codes, places, LANES)
    lanes = lax.broadcasted_iota(jnp.int32, listed.shape, 1)
    msg_ref[:, offset:] = jnp.where(lanes == LANES - 1, flag, listed)


def make_slots(me, src_ids, dst_ids, own, rows_dev, devices, chunks, neg_cap, width, part):
    lanes = (chunks + 1 if chunks else 4) * LANES
    spans = own.shape[0]
    ends_shape = jax.ShapeDtypeStruct((2 * spans, width), jnp.int32)
    if chunks:
        slots = [ends_shape] * chunks
    else:
        slots = [ends_shape, ends_shape, jax.ShapeDtypeStruct((1, 1), jnp.int32)]
    return call(
        functools.partial(
            slots_kernel,
            rows_dev=rows_dev,
            devices=devices,
            chunks=chunks,
            neg_cap=neg_cap,
            spans=spans,
            part=part,
        ),
        "slots",
        32 * devices * LANES * spans * width,
        16 * spans * width,
        in_specs=[
            pl.BlockSpec(memory_space=pltpu.SMEM),
            pl.BlockSpec(src_ids.shape, lambda: (0,)),
            pl.BlockSpec(dst_ids.shape, lambda: (0,)),
            pl.BlockSpec(own.shape, lambda: (0, 0)),
        ],
        out_shape=[jax.ShapeDtypeStruct((devices, lanes), jnp.int32)]
        + slots
        + [jax.ShapeDtypeStruct((spans, part), jnp.int32)],
    )(me.reshape(1, 1), src_ids, dst_ids, own)


def packed_height(count, feature):
    return feature // LANES * count + feature % LANES


def pack(out_ref, at, start, rows, tail):
    count, feature = rows.shape
    for piece in range(feature // LANES):
        out_ref[at, start + piece * count : start + (piece + 1) * count, :] = rows[
            :, piece * LANES : (piece + 1) * LANES
        ].astype(out_ref.dtype)
    tail = jnp.concatenate([tail, jnp.zeros((tail.shape[0], LANES - count), tail.dtype)], axis=1)
    end = start + packed_height(count, feature)
    out_ref[at, end - tail.shape[0] : end, :] = tail.astype(out_ref.dtype)


def pack_all(out_ref, start, count, rows, turned):
    feature = rows.shape[1]
    first = feature // LANES * LANES
    for i in range(out_ref.shape[0]):
        at = slice(i * count, (i + 1) * count)
        pack(out_ref, i, start, rows[at], turned[first:, at])


def unpack_all(in_ref, start, count, rows_ref, flat_ref):
    feature = flat_ref.shape[0]
    pieces = feature // LANES
    end = start + packed_height(count, feature)
    devices = in_ref.shape[0]
    for d in range(devices):
        for piece in range(pieces):
            rows_ref[d * count : (d + 1) * count, piece * LANES : (piece + 1) * LANES] = in_ref[
                d, start + piece * count : start + (piece + 1) * count, :
            ]
    tails = [
        in_ref[d, end - feature % LANES : end, :].astype(F32)[:, :count] for d in range(devices)
    ]
    flat_ref[: pieces * LANES] = rows_ref[...].astype(F32).T.astype(BF16)
    flat_ref[pieces * LANES :] = jnp.concatenate(tails, axis=1).astype(BF16)


def unpack_scratch(devices, count, feature):
    return [
        pltpu.VMEM((devices * count, feature // LANES * LANES), BF16),
        pltpu.VMEM((feature, devices * count), BF16),
    ]


def gather_kernel(table_ref, *refs, group, neg_cap):
    feature, rows_dev = table_ref.shape
    first = pl.program_id(0) * group
    req_ref, out_ref = refs[0], refs[-1]
    row = [req_ref[pl.ds(first + i, 1), :] for i in range(group)]
    if neg_cap:
        row += [refs[1][pl.ds(first + i, 1), :neg_cap] for i in range(group)]
    rows = dot(table_ref[...], one_hot(rows_dev, jnp.concatenate(row, axis=1)), NN)
    start = out_ref.shape[1] - feature
    for i in range(group):
        out_ref[i, start:] = rows[:, i * LANES : (i + 1) * LANES].astype(BF16)
    if neg_cap:
        neg = rows[:, group * LANES :]
        pack_all(out_ref, 0, neg_cap, neg.T, neg)


def gather(table, requests, neg_requests=None, neg_cap=0):
    feature, rows_dev = table.shape
    devices = requests.shape[0]
    group = 4
    height = feature + (packed_height(neg_cap, feature) if neg_cap else 0)
    slots = devices * (LANES + neg_cap)
    whole = pl.BlockSpec((devices, LANES), lambda i: (0, 0))
    return call(
        functools.partial(gather_kernel, group=group, neg_cap=neg_cap),
        "gather_rows",
        2 * feature * rows_dev * slots,
        2 * feature * (rows_dev + slots),
        grid=(devices // group,),
        in_specs=[pl.BlockSpec((feature, rows_dev), lambda i: (0, 0)), whole]
        + ([whole] if neg_cap else []),
        out_specs=pl.BlockSpec((group, height, LANES), lambda i: (i, 0, 0)),
        out_shape=jax.ShapeDtypeStruct((devices, height, LANES), BF16),
    )(table, requests, *([neg_requests] if neg_cap else []))


def quarter_ids(ids):
    group = lax.broadcasted_iota(jnp.int32, (1, LANES), 1) // SHARE
    rows = []
    for part in range(PARTS):
        pieces = []
        for first in range(0, len(ids), PARTS):
            piece = ids[first + part]
            for j in range(1, PARTS):
                piece = jnp.where(group == j, ids[first + (part ^ j)], piece)
            pieces.append(piece)
        rows.append(jnp.concatenate(pieces, axis=1))
    return rows


def gather_quarters_kernel(table_ref, req_ref, neg_req_ref, out_ref, *, neg_cap):
    feature, rows_dev = table_ref.shape
    group = out_ref.shape[0]
    share = rows_dev // PARTS
    first = pl.program_id(0) * group
    ids = [req_ref[pl.ds(first + i, 1), :] for i in range(group)]
    found = []
    for part, row in enumerate(quarter_ids(ids)):
        start = part * share
        found.append(dot(table_ref[:, start : start + share], one_hot(share, row, start), NN))
    start = out_ref.shape[1] - feature
    lanes = lax.broadcasted_iota(jnp.int32, (feature, LANES), 1) // SHARE
    for i in range(group):
        at = slice(i // PARTS * LANES, (i // PARTS + 1) * LANES)
        rows = found[i % PARTS][:, at]
        for j in range(1, PARTS):
            rows = jnp.where(lanes == j, found[j ^ (i % PARTS)][:, at], rows)
        out_ref[i, start:] = rows.astype(BF16)
    row = [neg_req_ref[pl.ds(first + i, 1), :neg_cap] for i in range(group)]
    neg = dot(table_ref[...], one_hot(rows_dev, jnp.concatenate(row, axis=1)), NN)
    pack_all(out_ref, 0, neg_cap, neg.T, neg)


def gather_quarters(table, requests, neg_requests, neg_cap):
    feature, rows_dev = table.shape
    devices = requests.shape[0]
    group = 16
    height = feature + packed_height(neg_cap, feature)
    whole = pl.BlockSpec((devices, LANES), lambda i: (0, 0))
    return call(
        functools.partial(gather_quarters_kernel, neg_cap=neg_cap),
        "gather_quarters",
        feature * rows_dev * devices * (LANES // 2 + 2 * neg_cap),
        2 * feature * (rows_dev + devices * (LANES + neg_cap)),
        grid=(devices // group,),
        in_specs=[pl.BlockSpec((feature, rows_dev), lambda i: (0, 0)), whole, whole],
        out_specs=pl.BlockSpec((group, height, LANES), lambda i: (i, 0, 0)),
        out_shape=jax.ShapeDtypeStruct((devices, height, LANES), BF16),
    )(table, requests, neg_requests)


def gather_pool_kernel(table_ref, req_ref, out_ref, *, group):
    rows_dev = table_ref.shape[1]
    row = req_ref[...].reshape(1, group * POOL)
    rows = dot(table_ref[...], one_hot(rows_dev, row), NN)
    pack_all(out_ref, 0, POOL, rows.T, rows)


def gather_pool(table, requests, devices):
    feature, rows_dev = table.shape
    group = 8
    steps = devices // group
    height = packed_height(POOL, feature)
    return call(
        functools.partial(gather_pool_kernel, group=group),
        "gather_pool",
        2 * feature * rows_dev * requests.size,
        2 * feature * (rows_dev + requests.size),
        grid=(steps,),
        in_specs=[
            pl.BlockSpec((feature, rows_dev), lambda i: (0, 0)),
            pl.BlockSpec((1, 1, group * POOL), lambda i: (i, 0, 0)),
        ],
        out_specs=pl.BlockSpec((group, height, LANES), lambda i: (i, 0, 0)),
        out_shape=jax.ShapeDtypeStruct((devices, height, LANES), BF16),
    )(table, requests.reshape(steps, 1, group * POOL))


def spread_neg_kernel(back_ref, slot_ref, out_ref, rows, flat, *, cap):
    unpack_all(back_ref, 0, cap, rows, flat)
    for part in range(slot_ref.shape[0]):
        hot = one_hot(flat.shape[1], slot_ref[part : part + 1, :])
        out_ref[part] = dot(flat[...], hot, NN).T.astype(BF16)


def spread_neg(back, slot, cap, feature):
    devices = back.shape[0]
    parts, width = slot.shape
    height = packed_height(cap, feature)
    return call(
        functools.partial(spread_neg_kernel, cap=cap),
        "spread_negatives",
        2 * devices * cap * feature * slot.size,
        2 * devices * cap * feature,
        grid=(1,),
        in_specs=[
            pl.BlockSpec((devices, height, LANES), lambda i: (0, 0, 0)),
            pl.BlockSpec(slot.shape, lambda i: (0, 0)),
        ],
        out_specs=pl.BlockSpec((parts, width, feature), lambda i: (0, 0, 0)),
        out_shape=jax.ShapeDtypeStruct((parts, width, feature), BF16),
        scratch_shapes=unpack_scratch(devices, cap, feature),
    )(back, slot)


def spread_kernel(*refs, first):
    back_ref, slot_ref = refs[:2]
    so_far_ref = None if first else refs[2]
    out_ref, flat = refs[2 + (not first)], refs[-1]
    devices = back_ref.shape[0]
    feature = flat.shape[0]

    @pl.when(pl.program_id(0) == 0)
    def _():
        start = back_ref.shape[1] - feature
        for d in range(devices):
            flat[:, d * LANES : (d + 1) * LANES] = back_ref[d, start:]

    row = slot_ref[...].reshape(1, slot_ref.shape[-1])
    rows = dot(flat[...], one_hot(flat.shape[1], row), NN)
    if not first:
        rows = rows + so_far_ref[...].astype(F32)
    out_ref[...] = rows.astype(BF16)


def spread(back, slot, so_far, feature):
    devices = back.shape[0]
    segments, width = slot.shape
    slots = devices * LANES
    tile = 512 if slots <= 4096 else 128
    steps = width // tile
    rows_spec = pl.BlockSpec((feature, tile), lambda i: (0, i))
    extra = [] if so_far is None else [so_far]
    return call(
        functools.partial(spread_kernel, first=so_far is None),
        "spread_rows",
        2 * feature * slots * slot.size,
        2 * feature * (slots + slot.size),
        grid=(segments * steps,),
        in_specs=[
            pl.BlockSpec(back.shape, lambda i: (0, 0, 0)),
            pl.BlockSpec((1, 1, tile), lambda i: (i // steps, 0, i % steps)),
        ]
        + [rows_spec] * len(extra),
        out_specs=rows_spec,
        out_shape=jax.ShapeDtypeStruct((feature, slot.size), BF16),
        scratch_shapes=[pltpu.VMEM((feature, slots), BF16)],
    )(back, slot.reshape(segments, 1, width), *extra)


def compact_places(shards):
    places = []
    for start, end, whose in ((0, SMALL, range(shards)), (SMALL, RELAYS * POOL, [None])):
        for shard in whose:
            place = start
            while place < end:
                relay, first = place // POOL, place % POOL
                count = min(POOL - first, end - place)
                to = (shards - 1 if shard is None else shard) * SMALL + place
                places.append((shard, relay, first, count, to))
                place += count
    return places


def compact_size(shards):
    return shards * SMALL + RELAYS * POOL - SMALL


def compact_pool(back_ref, busy, rows_ref, flat_ref):
    feature = flat_ref.shape[0]
    pieces = feature // LANES
    tails = []
    for shard, relay, first, count, to in compact_places(back_ref.shape[0] // RELAYS):
        at = (busy if shard is None else shard) * RELAYS + relay
        for piece in range(pieces):
            start = piece * POOL + first
            rows_ref[to : to + count, piece * LANES : (piece + 1) * LANES] = back_ref[
                at, start : start + count, :
            ]
        tail = back_ref[at, pieces * POOL :, :].astype(F32)
        tails.append(tail[:, first : first + count])
    flat_ref[: pieces * LANES] = rows_ref[...].astype(F32).T.astype(BF16)
    flat_ref[pieces * LANES :] = jnp.concatenate(tails, axis=1).astype(BF16)


def expand_pool(rows, busy, out_ref):
    feature = rows.shape[1]
    pieces = feature // LANES
    turned = rows.T
    out_ref[...] = jnp.zeros(out_ref.shape, out_ref.dtype)
    shards = out_ref.shape[0] // RELAYS
    for shard, relay, first, count, to in compact_places(shards):
        at = (busy if shard is None else shard) * RELAYS + relay
        for piece in range(pieces):
            start = piece * POOL + first
            out_ref[at, start : start + count, :] = rows[
                to : to + count, piece * LANES : (piece + 1) * LANES
            ].astype(BF16)
        if shard is not None:
            tail = turned[pieces * LANES :, to : to + count]
        else:
            tail = turned[pieces * LANES :, to : to + count]
            if first:
                kept = jnp.zeros((feature % LANES, first), F32)
                for other in range(shards):
                    start = other * SMALL + relay * POOL
                    part = turned[pieces * LANES :, start : start + first]
                    kept = jnp.where(busy == other, part, kept)
                tail = jnp.concatenate([kept, tail], axis=1)
        blank = jnp.zeros((tail.shape[0], LANES - tail.shape[1]), F32)
        out_ref[at, pieces * POOL :, :] = jnp.concatenate([tail, blank], axis=1).astype(BF16)


def edges_kernel(*refs, parts, pooled):
    refs = list(refs)
    src_ref, dst_ref, rel_ids_ref, rel_ref = refs[:4]
    neg_refs = refs[4 : 4 + parts]
    refs = refs[4 + parts :]
    if pooled:
        back_ref, src_slot_ref, dst_slot_ref, busy_ref = refs[:4]
        refs = refs[4:]
        pool_out_ref = refs.pop(2 + parts)
        pool_rows, pool_flat, pool_sums = refs[-3:]
    src_grad_ref, dst_grad_ref = refs[:2]
    neg_grad_refs = refs[2 : 2 + parts]
    negatives, rel_flat = refs[2 + parts : 4 + parts]
    block = pl.program_id(0)
    part = neg_refs[0].shape[1]

    @pl.when(block == 0)
    def _():
        table, pieces = rel_ref[...], []
        for _ in range(3):
            pieces.append(table.astype(BF16).astype(F32))
            table = table - pieces[-1]
        rel_flat[...] = jnp.concatenate(pieces, axis=0).T.astype(BF16)
        if pooled:
            compact_pool(back_ref, busy_ref[0, 0], pool_rows, pool_flat)
            pool_sums[...] = jnp.zeros(pool_sums.shape, F32)

    for k in range(parts):
        negatives[k * part : (k + 1) * part] = neg_refs[k][0]
    turned = negatives[...].astype(F32).T.astype(BF16)
    hot = one_hot(rel_ref.shape[0], rel_ids_ref[...].reshape(1, rel_ids_ref.shape[-1]))
    relation = dot(rel_flat[...], jnp.concatenate([hot] * 3, axis=0), NN)
    source = src_ref[...].astype(F32)
    target = dst_ref[...].astype(F32)
    if pooled:
        count = pool_flat.shape[1]
        src_hot = one_hot(count, src_slot_ref[...].reshape(1, src_slot_ref.shape[-1]))
        dst_hot = one_hot(count, dst_slot_ref[...].reshape(1, dst_slot_ref.shape[-1]))
        source = source + dot(pool_flat[...], src_hot, NN)
        target = target + dot(pool_flat[...], dst_hot, NN)
    product = source * relation
    positive = jnp.sum(product * target, axis=0, keepdims=True)
    pos_weight = -jax.nn.sigmoid(-positive)
    query = product.astype(BF16)
    weight = jax.nn.sigmoid(dot(negatives[...], query, NN)).astype(BF16)
    gathered = dot(turned, weight, NN)
    src_grad = (relation * (pos_weight * target + gathered)).astype(BF16)
    dst_grad = (pos_weight * product).astype(BF16)
    src_grad_ref[...] = src_grad
    dst_grad_ref[...] = dst_grad
    neg_grad = dot(weight, query, NT)
    if pooled:
        pool_sums[...] += dot(src_hot, src_grad, NT) + dot(dst_hot, dst_grad, NT)

    for k in range(parts):
        neg_grad_refs[k][0] = neg_grad[k * part : (k + 1) * part].astype(BF16)
    if pooled:

        @pl.when(block == pl.num_programs(0) - 1)
        def _():
            expand_pool(pool_sums[...], busy_ref[0, 0], pool_out_ref)


def edges(rows, rel_ids, relations, negatives, pool=None, pool_slot=None, busy=None):
    feature, endpoints = rows.shape
    parts = len(negatives)
    spans, part, _ = negatives[0].shape
    width = rel_ids.shape[1]
    edge_spec = pl.BlockSpec((feature, width), lambda b: (0, b))
    neg_spec = pl.BlockSpec((1, part, feature), lambda b: (b, 0, 0))
    operands = [rows, rows, rel_ids.reshape(spans, 1, width), relations, *negatives]
    specs = [
        edge_spec,
        pl.BlockSpec((feature, width), lambda b: (0, spans + b)),
        pl.BlockSpec((1, 1, width), lambda b: (b, 0, 0)),
        pl.BlockSpec(relations.shape, lambda b: (0, 0)),
    ] + [neg_spec] * parts
    out_specs = [edge_spec, edge_spec] + [neg_spec] * parts
    out_shape = [jax.ShapeDtypeStruct((feature, endpoints // 2), BF16)] * 2
    out_shape += [jax.ShapeDtypeStruct((spans, part, feature), BF16)] * parts
    scratch = [
        pltpu.VMEM((parts * part, feature), BF16),
        pltpu.VMEM((feature, 3 * relations.shape[0]), BF16),
    ]
    if pool is not None:
        slot = pool_slot.reshape(2 * spans, 1, width)
        pool_spec = pl.BlockSpec(pool.shape, lambda b: (0, 0, 0))
        operands += [pool, slot, slot, busy]
        specs += [
            pool_spec,
            pl.BlockSpec((1, 1, width), lambda b: (b, 0, 0)),
            pl.BlockSpec((1, 1, width), lambda b: (spans + b, 0, 0)),
            pl.BlockSpec(memory_space=pltpu.SMEM),
        ]
        out_specs.append(pool_spec)
        out_shape.append(jax.ShapeDtypeStruct(pool.shape, BF16))
        count = compact_size(pool.shape[0] // RELAYS)
        scratch += [
            pltpu.VMEM((count, feature // LANES * LANES), BF16),
            pltpu.VMEM((feature, count), BF16),
            pltpu.VMEM((count, feature), F32),
        ]
    src_grad, dst_grad, *rest = call(
        functools.partial(edges_kernel, parts=parts, pooled=pool is not None),
        "edges",
        6 * feature * parts * part * spans * width,
        4 * (rows.size + parts * negatives[0].size),
        grid=(spans,),
        in_specs=specs,
        out_specs=out_specs,
        out_shape=out_shape,
        scratch_shapes=scratch,
    )(*operands)
    return src_grad, dst_grad, rest


def collect_kernel(src_ref, dst_ref, slot_ref, out_ref, *, group):
    segments, width = slot_ref.shape
    feature = src_ref.shape[0]
    step = pl.program_id(0)
    total = jnp.zeros((feature, group * LANES), F32)
    for segment in range(segments):
        grads = src_ref if segment < segments // 2 else dst_ref
        start = segment % (segments // 2) * width
        hot = one_hot(group * LANES, slot_ref[segment : segment + 1, :], step * group * LANES)
        total = total + dot(grads[:, start : start + width], hot, NT)
    total = total.astype(BF16)
    first = out_ref.shape[1] - feature
    for i in range(group):
        out_ref[i, first:] = total[:, i * LANES : (i + 1) * LANES]


def collect(src_grad, dst_grad, slot, devices, neg_cap=0):
    feature = src_grad.shape[0]
    group = 4
    slots = devices * LANES
    height = feature + (packed_height(neg_cap, feature) if neg_cap else 0)
    whole = pl.BlockSpec(src_grad.shape, lambda i: (0, 0))
    return call(
        functools.partial(collect_kernel, group=group),
        "collect_grads",
        2 * feature * slots * slot.size,
        2 * feature * (slots + slot.size),
        grid=(devices // group,),
        in_specs=[whole, whole, pl.BlockSpec(slot.shape, lambda i: (0, 0))],
        out_specs=pl.BlockSpec((group, height, LANES), lambda i: (i, 0, 0)),
        out_shape=jax.ShapeDtypeStruct((devices, height, LANES), BF16),
    )(src_grad, dst_grad, slot)


def collect_neg_kernel(sent_ref, slot_ref, *refs, group, cap):
    grad_refs, out_ref, sums = refs[:-2], refs[-2], refs[-1]
    step = pl.program_id(0)

    @pl.when(step == 0)
    def _():
        total = grad_refs[0][...].astype(F32)
        for grad_ref in grad_refs[1:]:
            total = total + grad_ref[...].astype(F32)
        sums[...] = total.astype(BF16)

    rows = jnp.zeros((group * cap, sums.shape[-1]), F32)
    for part in range(slot_ref.shape[0]):
        hot = one_hot(group * cap, slot_ref[part : part + 1, :], step * group * cap)
        rows = rows + dot(hot, sums[part], NN)
    pack_all(out_ref, 0, cap, rows, rows.T)


def collect_neg(sent, slot, grads, cap):
    devices = sent.shape[0]
    feature = grads[0].shape[-1]
    group = 16
    height = packed_height(cap, feature)
    return call(
        functools.partial(collect_neg_kernel, group=group, cap=cap),
        "collect_negatives",
        2 * devices * cap * feature * slot.size,
        4 * len(grads) * grads[0].size,
        grid=(devices // group,),
        in_specs=[
            pl.BlockSpec(memory_space=pl.ANY),
            pl.BlockSpec(slot.shape, lambda i: (0, 0)),
        ]
        + [pl.BlockSpec(grads[0].shape, lambda i: (0, 0, 0))] * len(grads),
        out_specs=pl.BlockSpec((group, height, LANES), lambda i: (i, 0, 0)),
        out_shape=jax.ShapeDtypeStruct(sent.shape, BF16),
        scratch_shapes=[pltpu.VMEM(grads[0].shape, BF16)],
        input_output_aliases={0: 0},
    )(sent, slot, *grads)


def add_kernel(*refs, rows, neg_cap, first):
    refs = list(refs)
    recv_ref, req_ref = refs[:2]
    refs = refs[2:]
    if neg_cap:
        neg_req_ref = refs.pop(0)
        neg_rows, neg_flat = refs[-2:]
    if not first:
        so_far_ref = refs.pop(0)
    out_ref, flat = refs[:2]
    devices = recv_ref.shape[0]
    feature = flat.shape[0]
    step = pl.program_id(0)

    @pl.when(step == 0)
    def _():
        start = recv_ref.shape[1] - feature
        for d in range(devices):
            flat[:, d * LANES : (d + 1) * LANES] = recv_ref[d, start:]
        if neg_cap:
            unpack_all(recv_ref, 0, neg_cap, neg_rows, neg_flat)

    base = step * rows
    row = jnp.concatenate([req_ref[d : d + 1, :] for d in range(devices)], axis=1)
    total = dot(flat[...], one_hot(rows, row, base), NT)
    if neg_cap:
        row = jnp.concatenate([neg_req_ref[d : d + 1, :neg_cap] for d in range(devices)], axis=1)
        total = total + dot(neg_flat[...], one_hot(rows, row, base), NT)
    if not first:
        total = total + so_far_ref[...]
    out_ref[...] = total


def add_rows(recv, requests, so_far, feature, rows_dev, neg_requests=None, neg_cap=0):
    devices = recv.shape[0]
    rows = 512 if devices * LANES <= 4096 else 128
    slots = devices * LANES
    whole_req = pl.BlockSpec((devices, LANES), lambda i: (0, 0))
    rows_spec = pl.BlockSpec((feature, rows), lambda i: (0, i))
    operands = [recv, requests]
    specs = [pl.BlockSpec(recv.shape, lambda i: (0, 0, 0)), whole_req]
    scratch = [pltpu.VMEM((feature, slots), BF16)]
    if neg_cap:
        operands.append(neg_requests)
        specs.append(whole_req)
        scratch += unpack_scratch(devices, neg_cap, feature)
    if so_far is not None:
        operands.append(so_far)
        specs.append(rows_spec)
    return call(
        functools.partial(add_kernel, rows=rows, neg_cap=neg_cap, first=so_far is None),
        "add_grads",
        2 * feature * slots * rows_dev,
        2 * feature * slots + 8 * feature * rows_dev,
        grid=(rows_dev // rows,),
        in_specs=specs,
        out_specs=rows_spec,
        out_shape=jax.ShapeDtypeStruct((feature, rows_dev), F32),
        scratch_shapes=scratch,
    )(*operands)


def add_quarters_kernel(
    recv_ref, req_ref, neg_req_ref, so_far_ref, out_ref, flat, neg_rows, neg_flat, *, neg_cap
):
    devices = recv_ref.shape[0]
    feature, rows = out_ref.shape
    step = pl.program_id(0)

    @pl.when(step == 0)
    def _():
        start = recv_ref.shape[1] - feature
        for first in range(0, devices, PARTS):
            for part in range(PARTS):
                for j in range(PARTS):
                    to = first // PARTS * LANES + j * SHARE
                    flat[part, :, to : to + SHARE] = recv_ref[
                        first + (part ^ j), start:, j * SHARE : (j + 1) * SHARE
                    ]
        unpack_all(recv_ref, 0, neg_cap, neg_rows, neg_flat)

    base = step * rows
    asked = quarter_ids([req_ref[d : d + 1, :] for d in range(devices)])
    row = asked[0]
    for part in range(1, PARTS):
        row = jnp.where(step == part, asked[part], row)
    total = dot(flat[step], one_hot(rows, row, base), NT)
    row = jnp.concatenate([neg_req_ref[d : d + 1, :neg_cap] for d in range(devices)], axis=1)
    out_ref[...] = total + dot(neg_flat[...], one_hot(rows, row, base), NT) + so_far_ref[...]


def add_quarters(recv, requests, neg_requests, so_far, neg_cap):
    feature, rows_dev = so_far.shape
    devices = recv.shape[0]
    slots = devices * LANES
    whole_req = pl.BlockSpec((devices, LANES), lambda i: (0, 0))
    rows_spec = pl.BlockSpec((feature, rows_dev // PARTS), lambda i: (0, i))
    return call(
        functools.partial(add_quarters_kernel, neg_cap=neg_cap),
        "add_quarters",
        feature * (slots // 2 + 2 * devices * neg_cap) * rows_dev,
        2 * feature * slots + 8 * feature * rows_dev,
        grid=(PARTS,),
        in_specs=[pl.BlockSpec(recv.shape, lambda i: (0, 0, 0)), whole_req, whole_req, rows_spec],
        out_specs=rows_spec,
        out_shape=jax.ShapeDtypeStruct((feature, rows_dev), F32),
        scratch_shapes=[pltpu.VMEM((PARTS, feature, slots // PARTS), BF16)]
        + unpack_scratch(devices, neg_cap, feature),
    )(recv, requests, neg_requests, so_far)


def add_pool_kernel(*refs, rows, first):
    one_ref, two_ref, one_req_ref, two_req_ref = refs[:4]
    out_ref, packed, *flats = refs[4 + (not first) :]
    step = pl.program_id(0)

    @pl.when(step == 0)
    def _():
        for recv_ref, flat in zip((one_ref, two_ref), flats):
            unpack_all(recv_ref, 0, POOL, packed, flat)

    total = dot(flats[0][...], one_hot(rows, one_req_ref[...], step * rows), NT)
    total = total + dot(flats[1][...], one_hot(rows, two_req_ref[...], step * rows), NT)
    if not first:
        total = total + refs[4][...]
    out_ref[...] = total


def add_pool(one, two, requests, so_far, feature, rows_dev):
    rows = 512
    devices = one.shape[0]
    slots = devices * POOL
    recv_spec = pl.BlockSpec(one.shape, lambda i: (0, 0, 0))
    req_spec = pl.BlockSpec((1, slots), lambda i: (0, 0))
    rows_spec = pl.BlockSpec((feature, rows), lambda i: (0, i))
    packed, flat = unpack_scratch(devices, POOL, feature)
    extra = [] if so_far is None else [so_far]
    return call(
        functools.partial(add_pool_kernel, rows=rows, first=so_far is None),
        "add_pool",
        4 * feature * slots * rows_dev,
        4 * feature * slots + 4 * feature * rows_dev,
        grid=(rows_dev // rows,),
        in_specs=[recv_spec, recv_spec, req_spec, req_spec] + [rows_spec] * len(extra),
        out_specs=rows_spec,
        out_shape=jax.ShapeDtypeStruct((feature, rows_dev), F32),
        scratch_shapes=[packed, flat, flat],
    )(one, two, requests[0][None], requests[1][None], *extra)


def after(value, other):
    anywhere = pl.BlockSpec(memory_space=pl.ANY)
    return call(
        lambda value_ref, other_ref, out_ref: None,
        "after",
        0,
        0,
        in_specs=[anywhere, anywhere],
        out_specs=anywhere,
        out_shape=jax.ShapeDtypeStruct(value.shape, value.dtype),
        input_output_aliases={0: 0},
    )(value, other)


def exchange(value):
    return lax.all_to_all(value, ("shard", "grp"), split_axis=0, concat_axis=0, tiled=True)


def swap(value, bit):
    sharers = lax.axis_size("grp")
    return lax.ppermute(value, "grp", [(i, i ^ bit) for i in range(sharers)])


def share_out(value, wait=lambda block: block):
    sharers = lax.axis_size("grp")
    blocks = {0: value}
    bit = sharers // 2
    while bit:
        for k in list(blocks):
            blocks[k ^ bit] = swap(wait(blocks[k]) if k else blocks[k], bit)
        bit //= 2
    return [blocks[k] for k in range(sharers)]


def trade(blocks):
    sharers = len(blocks)
    terms = [[block] for block in blocks]
    bit = 1
    while bit < sharers:
        for k in range(0, sharers, 2 * bit):
            total = terms[k ^ bit][0].astype(F32)
            for term in terms[k ^ bit][1:]:
                total = total + term.astype(F32)
            terms[k].append(swap(total.astype(BF16), bit))
        bit *= 2
    return terms[0]


def pad_lanes(value, width, fill):
    return jnp.pad(value, ((0, 0), (0, width - value.shape[1])), constant_values=fill)


def body(entity_table, rel_diag, src_ids, dst_ids, rel_ids, neg_ids):
    rows_dev, feature = entity_table.shape
    sharers = lax.axis_size("grp")
    devices = lax.axis_size("shard") * sharers
    spans, neg_count = neg_ids.shape
    edge_count = src_ids.shape[0]
    block_len = edge_count // spans
    edge_cap = 4 * edge_count // devices
    chunks = round_up(edge_cap, LANES) // LANES
    part_width = neg_count // sharers
    neg_cap = round_up(2 * spans * part_width // devices, 16)
    width = round_up(block_len, 512)
    part = round_up(part_width, LANES)
    me = lax.axis_index("grp")

    table = entity_table.T.astype(BF16)
    own_ids = lax.dynamic_slice_in_dim(neg_ids, me * part_width, part_width, 1)
    rel_rows = pad_lanes(rel_ids.reshape(spans, block_len), width, -1)

    def ask(zero, chunks):
        message, *slots = make_slots(
            lax.axis_index(("shard", "grp")),
            src_ids + zero,
            dst_ids + zero,
            own_ids,
            rows_dev,
            devices,
            chunks,
            neg_cap,
            width,
            part,
        )
        asked = exchange(message)
        return asked, asked[:, -LANES:], slots, slots[-1]

    def chunked(zero):
        asked, neg_asked, slots, neg_slot = ask(zero, chunks)
        direct = [asked[:, c * LANES : (c + 1) * LANES] for c in range(chunks)]
        back = [exchange(gather(table, direct[0], neg_asked, neg_cap))]
        back += [exchange(gather(table, direct[c])) for c in range(1, chunks)]
        negatives = share_out(spread_neg(back[0], neg_slot, neg_cap, feature))
        rows = None
        for c in range(chunks):
            rows = spread(back[c], slots[c], rows, feature)
        src_grad, dst_grad, neg_grads = edges(rows, rel_rows, rel_diag, negatives)
        grad = None
        for c in range(1, chunks):
            sent = exchange(collect(src_grad, dst_grad, slots[c], devices))
            grad = add_rows(sent, direct[c], grad, feature, rows_dev)
        sent = collect(src_grad, dst_grad, slots[0], devices, neg_cap)
        sent = exchange(collect_neg(sent, neg_slot, trade(neg_grads), neg_cap))
        return add_rows(sent, direct[0], grad, feature, rows_dev, neg_asked, neg_cap)

    def pooled():
        asked, neg_asked, (slot, pool_slot, busy, _), neg_slot = ask(0, 0)
        direct = asked[:, :LANES]
        listed = asked[:, LANES : LANES + RELAYS * POOL].reshape(devices, RELAYS, POOL)
        listed = listed.transpose(1, 0, 2).reshape(RELAYS, devices * POOL) - me * rows_dev
        listed = listed[me ^ jnp.arange(RELAYS, dtype=jnp.int32)]
        back = exchange(gather_quarters(table, direct, neg_asked, neg_cap))
        far = swap(gather_pool(table, listed[3], devices), 1)
        far = swap(gather_pool(table, listed[2], devices) + far, 2)
        near = swap(gather_pool(table, listed[1], devices), 1)
        near = gather_pool(table, listed[0], devices) + near
        rows = spread(back, slot, None, feature)
        negatives = share_out(
            spread_neg(back, neg_slot, neg_cap, feature), lambda block: after(block, rows)
        )
        src_grad, dst_grad, rest = edges(
            rows, rel_rows, rel_diag, negatives, exchange(near + far), pool_slot, busy
        )
        neg_grads, pool = rest[:-1], rest[-1]
        near = exchange(pool)
        far = swap(near, 2)
        sent = collect(src_grad, dst_grad, slot, devices, neg_cap)
        sent = exchange(collect_neg(sent, neg_slot, trade(neg_grads), neg_cap))
        grad = add_pool(near, swap(near, 1), listed[:2], None, feature, rows_dev)
        far = after(far, grad)
        grad = add_pool(far, swap(far, 1), listed[2:], grad, feature, rows_dev)
        return add_quarters(sent, direct, neg_asked, grad, neg_cap), jnp.max(neg_asked[:, -1])

    if chunks == 1 or sharers != RELAYS:
        return chunked(0).T
    return lax.while_loop(
        lambda state: state[1] > 0,
        lambda state: (chunked(jnp.minimum(state[1], 0)), -state[1]),
        pooled(),
    )[0].T


def solution(mesh):
    placed = (
        P(("shard", "grp"), None),
        P(),
        P(("shard", "grp")),
        P(("shard", "grp")),
        P(("shard", "grp")),
        P("shard", None),
    )
    return jax.shard_map(
        body, mesh=mesh, in_specs=placed, out_specs=P(("shard", "grp"), None), check_vma=False
    )
```

```python
import functools

import jax
import jax.numpy as jnp
from jax import lax
from jax.experimental import pallas as pl
from jax.experimental.pallas import tpu as pltpu
from jax.sharding import PartitionSpec as P

LANES = 128
POOL = 48
RELAYS = 4
SMALL = 80
PARTS = 4
SHARE = LANES // PARTS
VMEM_BYTES = 56 << 20
F32 = jnp.float32
BF16 = jnp.bfloat16
NN = (((1,), (0,)), ((), ()))
NT = (((1,), (1,)), ((), ()))
TN = (((0,), (0,)), ((), ()))


def round_up(value, unit):
    return -(-value // unit) * unit


def dot(left, right, dims):
    return lax.dot_general(left, right, dims, preferred_element_type=F32)


def one_hot(rows, row, base=0):
    places = lax.broadcasted_iota(jnp.int32, (rows, row.shape[1]), 0) + base
    return jnp.where(places == row, 1.0, 0.0).astype(BF16)


def call(kernel, name, flops, nbytes, **kwargs):
    return pl.pallas_call(
        kernel,
        name=name,
        compiler_params=pltpu.CompilerParams(vmem_limit_bytes=VMEM_BYTES),
        cost_estimate=pl.CostEstimate(flops=flops, bytes_accessed=nbytes, transcendentals=0),
        **kwargs,
    )


def ranks(members, mixer):
    groups = members[0].shape[0]
    both = dot(jnp.concatenate(members, axis=0).astype(BF16), mixer, NN)
    taken = jnp.zeros((groups, LANES), F32)
    found = []
    for i, member in enumerate(members):
        chunk = both[i * groups : (i + 1) * groups]
        found.append(jnp.sum((chunk[:, :LANES] + taken) * member, axis=0, keepdims=True))
        taken = taken + chunk[:, LANES:]
    return [rank.astype(jnp.int32) for rank in found], taken


def fill(members, codes, places, count):
    groups = members[0].shape[0]
    high = [m * (c // LANES).astype(F32) for m, c in zip(members, codes)]
    low = [m * (c % LANES).astype(F32) for m, c in zip(members, codes)]
    left = jnp.concatenate(
        [jnp.concatenate(high, axis=1), jnp.concatenate(low, axis=1)], axis=0
    ).astype(BF16)
    sums = dot(left, one_hot(count, jnp.concatenate(places, axis=1)), NT)
    return (LANES * sums[:groups] + sums[groups:]).astype(jnp.int32) - 1


def slots_kernel(
    me_ref, src_ref, dst_ref, own_ref, *refs, rows_dev, devices, chunks, neg_cap, spans, part
):
    pooled = chunks == 0
    msg_ref, neg_ref = refs[0], refs[-1]
    slot_refs = refs[1:-1]
    row = lax.broadcasted_iota(jnp.int32, (LANES, 2 * LANES), 0)
    lane = lax.broadcasted_iota(jnp.int32, (LANES, 2 * LANES), 1)
    mixer = jnp.where(row < lane, 1.0, 0.0).astype(BF16)
    owners = lax.broadcasted_iota(jnp.int32, (devices, LANES), 0)

    def prepare(rows, width):
        where, holder, codes, members = [], [], [], []
        for segment, ids_row in enumerate(rows):
            blank = jnp.full((1, width - ids_row.shape[1]), -1, jnp.int32)
            ids_row = jnp.concatenate([ids_row, blank], axis=1)
            for start in range(0, width, LANES):
                ids = ids_row[:, start : start + LANES]
                owner = jnp.where(ids >= 0, ids // rows_dev, -1)
                where.append((slice(segment, segment + 1), slice(start, start + LANES)))
                holder.append(owner)
                codes.append(jnp.where(ids >= 0, ids - owner * rows_dev + 1, 0))
                members.append(jnp.where(owners == owner, 1.0, 0.0))
        return where, holder, codes, members

    ends = []
    for ids_ref in (src_ref, dst_ref):
        ids = ids_ref[...].reshape(1, ids_ref.shape[0])
        length = ids.shape[1] // spans
        ends += [ids[:, b * length : (b + 1) * length] for b in range(spans)]
    where, holder, codes, members = prepare(ends, slot_refs[0].shape[1])
    flag = jnp.full((1, 1), -1, jnp.int32)
    if pooled:
        turn = me_ref[0, 0] % PARTS
        quarters = [jnp.maximum(code - 1, 0) // (rows_dev // PARTS) for code in codes]
        split = [
            jnp.concatenate([jnp.where(q == k, member, 0.0) for k in range(PARTS)], axis=0)
            for member, q in zip(members, quarters)
        ]
        found, _ = ranks(split, mixer)
        places = []
        for at, owner, rank, q in zip(where, holder, found, quarters):
            inside = (owner >= 0) & (rank < SHARE)
            place = (q ^ turn) * SHARE + rank
            slot_refs[0][at] = jnp.where(inside, owner * LANES + place, -1)
            places.append(jnp.where(inside, place, -1))
        msg_ref[:, 0, :LANES] = fill(members, codes, places, LANES)
        offset = LANES

        pool_ref, busy_ref = slot_refs[1:]
        shards = devices // RELAYS
        room = RELAYS * POOL
        shard_rows = lax.broadcasted_iota(jnp.int32, (shards, LANES), 0)
        spilled, spill_codes = [], []
        for owner, code, rank in zip(holder, codes, found):
            shard = jnp.where(rank >= SHARE, owner // RELAYS, -1)
            spilled.append(jnp.where(shard_rows == shard, 1.0, 0.0))
            spill_codes.append(code + (owner % RELAYS) * rows_dev)
        listed, taken = ranks(spilled, mixer)
        places = []
        for at, owner, rank, place in zip(where, holder, found, listed):
            inside = (owner >= 0) & (rank >= SHARE) & (place < room)
            compact = jnp.where(
                place < SMALL, owner // RELAYS * SMALL + place, (shards - 1) * SMALL + place
            )
            pool_ref[at] = jnp.where(inside, compact, -1)
            places.append(jnp.where(inside, place, -1))
        listed = fill(spilled, spill_codes, places, 2 * LANES)
        for shard in range(shards):
            msg_ref[shard * RELAYS : (shard + 1) * RELAYS, 0, offset : offset + 2 * LANES] = (
                jnp.broadcast_to(listed[shard : shard + 1], (RELAYS, 2 * LANES))
            )
        offset += 2 * LANES
        most = jnp.max(taken, axis=0, keepdims=True)
        busy = jnp.where(taken > SMALL, 1.0, 0.0)
        crowded = jnp.sum(busy, axis=0, keepdims=True) > 1.0
        flag = jnp.where((most > room) | crowded, 1, -1)[:, :1]
        place = jnp.sum(busy * shard_rows.astype(F32), axis=0, keepdims=True).astype(jnp.int32)
        busy_ref[...] = jnp.minimum(place, shards - 1)[:, :1]
    else:
        found, _ = ranks(members, mixer)
        for chunk in range(chunks):
            places = []
            for at, owner, rank in zip(where, holder, found):
                place = rank - chunk * LANES
                place = jnp.where((owner >= 0) & (place >= 0) & (place < LANES), place, -1)
                slot_refs[chunk][at] = jnp.where(place >= 0, owner * LANES + place, -1)
                places.append(place)
            listed = fill(members, codes, places, LANES)
            msg_ref[:, 0, chunk * LANES : (chunk + 1) * LANES] = listed
        offset = chunks * LANES

    where, holder, codes, members = prepare([own_ref[b : b + 1, :] for b in range(spans)], part)
    found, _ = ranks(members, mixer)
    for at, owner, rank in zip(where, holder, found):
        neg_ref[at] = jnp.where(owner >= 0, owner * neg_cap + rank, -1)
    places = [jnp.where(owner >= 0, rank, -1) for owner, rank in zip(holder, found)]
    listed = fill(members, codes, places, LANES)
    lanes = lax.broadcasted_iota(jnp.int32, listed.shape, 1)
    msg_ref[:, 0, offset:] = jnp.where(lanes == LANES - 1, flag, listed)


def make_slots(me, src_ids, dst_ids, own, rows_dev, devices, chunks, neg_cap, width, part):
    lanes = (chunks + 1 if chunks else 4) * LANES
    spans = own.shape[0]
    ends_shape = jax.ShapeDtypeStruct((2 * spans, width), jnp.int32)
    if chunks:
        slots = [ends_shape] * chunks
    else:
        slots = [ends_shape, ends_shape, jax.ShapeDtypeStruct((1, 1), jnp.int32)]
    return call(
        functools.partial(
            slots_kernel,
            rows_dev=rows_dev,
            devices=devices,
            chunks=chunks,
            neg_cap=neg_cap,
            spans=spans,
            part=part,
        ),
        "slots",
        32 * devices * LANES * spans * width,
        16 * spans * width,
        in_specs=[
            pl.BlockSpec(memory_space=pltpu.SMEM),
            pl.BlockSpec(src_ids.shape, lambda: (0,)),
            pl.BlockSpec(dst_ids.shape, lambda: (0,)),
            pl.BlockSpec(own.shape, lambda: (0, 0)),
        ],
        out_shape=[jax.ShapeDtypeStruct((devices, 1, lanes), jnp.int32)]
        + slots
        + [jax.ShapeDtypeStruct((spans, part), jnp.int32)],
    )(me.reshape(1, 1), src_ids, dst_ids, own)


def packed_height(count, feature):
    return feature // LANES * count + feature % LANES


def pack(out_ref, at, start, rows, tail):
    count, feature = rows.shape
    for piece in range(feature // LANES):
        out_ref[at, start + piece * count : start + (piece + 1) * count, :] = rows[
            :, piece * LANES : (piece + 1) * LANES
        ].astype(out_ref.dtype)
    tail = jnp.concatenate([tail, jnp.zeros((tail.shape[0], LANES - count), tail.dtype)], axis=1)
    end = start + packed_height(count, feature)
    out_ref[at, end - tail.shape[0] : end, :] = tail.astype(out_ref.dtype)


def pack_all(out_ref, start, count, rows, turned):
    feature = rows.shape[1]
    first = feature // LANES * LANES
    for i in range(out_ref.shape[0]):
        at = slice(i * count, (i + 1) * count)
        pack(out_ref, i, start, rows[at], turned[first:, at])


def unpack_all(in_ref, start, count, rows_ref, flat_ref):
    feature = flat_ref.shape[0]
    pieces = feature // LANES
    end = start + packed_height(count, feature)
    devices = in_ref.shape[0]
    for d in range(devices):
        for piece in range(pieces):
            rows_ref[d * count : (d + 1) * count, piece * LANES : (piece + 1) * LANES] = in_ref[
                d, start + piece * count : start + (piece + 1) * count, :
            ]
    tails = [
        in_ref[d, end - feature % LANES : end, :].astype(F32)[:, :count] for d in range(devices)
    ]
    flat_ref[: pieces * LANES] = rows_ref[...].astype(F32).T.astype(BF16)
    flat_ref[pieces * LANES :] = jnp.concatenate(tails, axis=1).astype(BF16)


def unpack_scratch(devices, count, feature):
    return [
        pltpu.VMEM((devices * count, feature // LANES * LANES), BF16),
        pltpu.VMEM((feature, devices * count), BF16),
    ]


def gather_kernel(table_ref, *refs, group, neg_cap):
    feature, rows_dev = table_ref.shape
    first = pl.program_id(0) * group
    req_ref, out_ref = refs[0], refs[-1]
    row = [req_ref[pl.ds(first + i, 1), :] for i in range(group)]
    if neg_cap:
        row += [refs[1][pl.ds(first + i, 1), :neg_cap] for i in range(group)]
    rows = dot(table_ref[...], one_hot(rows_dev, jnp.concatenate(row, axis=1)), NN)
    start = out_ref.shape[1] - feature
    for i in range(group):
        out_ref[i, start:] = rows[:, i * LANES : (i + 1) * LANES].astype(BF16)
    if neg_cap:
        neg = rows[:, group * LANES :]
        pack_all(out_ref, 0, neg_cap, neg.T, neg)


def gather(table, requests, neg_requests=None, neg_cap=0):
    feature, rows_dev = table.shape
    devices = requests.shape[0]
    group = 4
    height = feature + (packed_height(neg_cap, feature) if neg_cap else 0)
    slots = devices * (LANES + neg_cap)
    whole = pl.BlockSpec((devices, LANES), lambda i: (0, 0))
    return call(
        functools.partial(gather_kernel, group=group, neg_cap=neg_cap),
        "gather_rows",
        2 * feature * rows_dev * slots,
        2 * feature * (rows_dev + slots),
        grid=(devices // group,),
        in_specs=[pl.BlockSpec((feature, rows_dev), lambda i: (0, 0)), whole]
        + ([whole] if neg_cap else []),
        out_specs=pl.BlockSpec((group, height, LANES), lambda i: (i, 0, 0)),
        out_shape=jax.ShapeDtypeStruct((devices, height, LANES), BF16),
    )(table, requests, *([neg_requests] if neg_cap else []))


def quarter_ids(ids):
    group = lax.broadcasted_iota(jnp.int32, (1, LANES), 1) // SHARE
    rows = []
    for part in range(PARTS):
        pieces = []
        for first in range(0, len(ids), PARTS):
            piece = ids[first + part]
            for j in range(1, PARTS):
                piece = jnp.where(group == j, ids[first + (part ^ j)], piece)
            pieces.append(piece)
        rows.append(jnp.concatenate(pieces, axis=1))
    return rows


def gather_quarters_kernel(table_ref, asked_ref, out_ref, *, neg_cap):
    feature, rows_dev = table_ref.shape
    group = out_ref.shape[0]
    share = rows_dev // PARTS
    ids = [asked_ref[i : i + 1, :LANES] for i in range(group)]
    found = []
    for part, row in enumerate(quarter_ids(ids)):
        start = part * share
        found.append(dot(table_ref[:, start : start + share], one_hot(share, row, start), NN))
    start = out_ref.shape[1] - feature
    lanes = lax.broadcasted_iota(jnp.int32, (feature, LANES), 1) // SHARE
    for i in range(group):
        at = slice(i // PARTS * LANES, (i // PARTS + 1) * LANES)
        rows = found[i % PARTS][:, at]
        for j in range(1, PARTS):
            rows = jnp.where(lanes == j, found[j ^ (i % PARTS)][:, at], rows)
        out_ref[i, start:] = rows.astype(BF16)
    negs = slice(asked_ref.shape[1] - LANES, asked_ref.shape[1] - LANES + neg_cap)
    row = [asked_ref[i : i + 1, negs] for i in range(group)]
    neg = dot(table_ref[...], one_hot(rows_dev, jnp.concatenate(row, axis=1)), NN)
    pack_all(out_ref, 0, neg_cap, neg.T, neg)


def gather_quarters(table, asked, neg_cap):
    feature, rows_dev = table.shape
    devices = asked.shape[0]
    group = 16
    height = feature + packed_height(neg_cap, feature)
    return call(
        functools.partial(gather_quarters_kernel, neg_cap=neg_cap),
        "gather_quarters",
        feature * rows_dev * devices * (LANES // 2 + 2 * neg_cap),
        2 * feature * (rows_dev + devices * (LANES + neg_cap)),
        grid=(devices // group,),
        in_specs=[pl.BlockSpec((feature, rows_dev), lambda i: (0, 0)), pl.BlockSpec((group, asked.shape[1]), lambda i: (i, 0))],
        out_specs=pl.BlockSpec((group, height, LANES), lambda i: (i, 0, 0)),
        out_shape=jax.ShapeDtypeStruct((devices, height, LANES), BF16),
    )(table, asked)


def gather_pool_kernel(table_ref, req_ref, out_ref, *, group):
    rows_dev = table_ref.shape[1]
    row = req_ref[...].reshape(1, group * POOL)
    rows = dot(table_ref[...], one_hot(rows_dev, row), NN)
    pack_all(out_ref, 0, POOL, rows.T, rows)


def gather_pool(table, requests, devices):
    feature, rows_dev = table.shape
    group = 8
    steps = devices // group
    height = packed_height(POOL, feature)
    return call(
        functools.partial(gather_pool_kernel, group=group),
        "gather_pool",
        2 * feature * rows_dev * requests.size,
        2 * feature * (rows_dev + requests.size),
        grid=(steps,),
        in_specs=[
            pl.BlockSpec((feature, rows_dev), lambda i: (0, 0)),
            pl.BlockSpec((1, 1, group * POOL), lambda i: (i, 0, 0)),
        ],
        out_specs=pl.BlockSpec((group, height, LANES), lambda i: (i, 0, 0)),
        out_shape=jax.ShapeDtypeStruct((devices, height, LANES), BF16),
    )(table, requests.reshape(steps, 1, group * POOL))


def spread_neg_kernel(back_ref, slot_ref, out_ref, rows, flat, *, cap):
    unpack_all(back_ref, 0, cap, rows, flat)
    for part in range(slot_ref.shape[0]):
        hot = one_hot(flat.shape[1], slot_ref[part : part + 1, :])
        out_ref[part] = dot(flat[...], hot, NN).T.astype(BF16)


def spread_neg(back, slot, cap, feature):
    devices = back.shape[0]
    parts, width = slot.shape
    height = packed_height(cap, feature)
    return call(
        functools.partial(spread_neg_kernel, cap=cap),
        "spread_negatives",
        2 * devices * cap * feature * slot.size,
        2 * devices * cap * feature,
        grid=(1,),
        in_specs=[
            pl.BlockSpec((devices, height, LANES), lambda i: (0, 0, 0)),
            pl.BlockSpec(slot.shape, lambda i: (0, 0)),
        ],
        out_specs=pl.BlockSpec((parts, width, feature), lambda i: (0, 0, 0)),
        out_shape=jax.ShapeDtypeStruct((parts, width, feature), BF16),
        scratch_shapes=unpack_scratch(devices, cap, feature),
    )(back, slot)


def spread_kernel(*refs, first):
    back_ref, slot_ref = refs[:2]
    so_far_ref = None if first else refs[2]
    out_ref, flat = refs[2 + (not first)], refs[-1]
    devices = back_ref.shape[0]
    feature = flat.shape[0]

    @pl.when(pl.program_id(0) == 0)
    def _():
        start = back_ref.shape[1] - feature
        for d in range(devices):
            flat[:, d * LANES : (d + 1) * LANES] = back_ref[d, start:]

    row = slot_ref[...].reshape(1, slot_ref.shape[-1])
    rows = dot(flat[...], one_hot(flat.shape[1], row), NN)
    if not first:
        rows = rows + so_far_ref[...].astype(F32)
    out_ref[...] = rows.astype(BF16)


def spread(back, slot, so_far, feature):
    devices = back.shape[0]
    segments, width = slot.shape
    slots = devices * LANES
    tile = 512 if slots <= 4096 else 128
    steps = width // tile
    rows_spec = pl.BlockSpec((feature, tile), lambda i: (0, i))
    extra = [] if so_far is None else [so_far]
    return call(
        functools.partial(spread_kernel, first=so_far is None),
        "spread_rows",
        2 * feature * slots * slot.size,
        2 * feature * (slots + slot.size),
        grid=(segments * steps,),
        in_specs=[
            pl.BlockSpec(back.shape, lambda i: (0, 0, 0)),
            pl.BlockSpec((1, 1, tile), lambda i: (i // steps, 0, i % steps)),
        ]
        + [rows_spec] * len(extra),
        out_specs=rows_spec,
        out_shape=jax.ShapeDtypeStruct((feature, slot.size), BF16),
        scratch_shapes=[pltpu.VMEM((feature, slots), BF16)],
    )(back, slot.reshape(segments, 1, width), *extra)


def compact_places(shards):
    places = []
    for start, end, whose in ((0, SMALL, range(shards)), (SMALL, RELAYS * POOL, [None])):
        for shard in whose:
            place = start
            while place < end:
                relay, first = place // POOL, place % POOL
                count = min(POOL - first, end - place)
                to = (shards - 1 if shard is None else shard) * SMALL + place
                places.append((shard, relay, first, count, to))
                place += count
    return places


def compact_size(shards):
    return shards * SMALL + RELAYS * POOL - SMALL


def compact_pool(back_ref, busy, rows_ref, flat_ref):
    feature = flat_ref.shape[0]
    pieces = feature // LANES
    tails = []
    for shard, relay, first, count, to in compact_places(back_ref.shape[0] // RELAYS):
        at = (busy if shard is None else shard) * RELAYS + relay
        for piece in range(pieces):
            start = piece * POOL + first
            rows_ref[to : to + count, piece * LANES : (piece + 1) * LANES] = back_ref[
                at, start : start + count, :
            ]
        tail = back_ref[at, pieces * POOL :, :].astype(F32)
        tails.append(tail[:, first : first + count])
    flat_ref[: pieces * LANES] = rows_ref[...].astype(F32).T.astype(BF16)
    flat_ref[pieces * LANES :] = jnp.concatenate(tails, axis=1).astype(BF16)


def expand_pool(turned, busy, out_ref):
    feature = turned.shape[0]
    pieces = feature // LANES
    rows = turned.T
    out_ref[...] = jnp.zeros(out_ref.shape, out_ref.dtype)
    shards = out_ref.shape[0] // RELAYS
    for shard, relay, first, count, to in compact_places(shards):
        at = (busy if shard is None else shard) * RELAYS + relay
        for piece in range(pieces):
            start = piece * POOL + first
            out_ref[at, start : start + count, :] = rows[
                to : to + count, piece * LANES : (piece + 1) * LANES
            ].astype(BF16)
        if shard is not None:
            tail = turned[pieces * LANES :, to : to + count]
        else:
            tail = turned[pieces * LANES :, to : to + count]
            if first:
                kept = jnp.zeros((feature % LANES, first), F32)
                for other in range(shards):
                    start = other * SMALL + relay * POOL
                    part = turned[pieces * LANES :, start : start + first]
                    kept = jnp.where(busy == other, part, kept)
                tail = jnp.concatenate([kept, tail], axis=1)
        blank = jnp.zeros((tail.shape[0], LANES - tail.shape[1]), F32)
        out_ref[at, pieces * POOL :, :] = jnp.concatenate([tail, blank], axis=1).astype(BF16)


def edges_kernel(*refs, parts, pooled):
    refs = list(refs)
    src_ref, dst_ref, rel_ids_ref, rel_ref = refs[:4]
    neg_refs = refs[4 : 4 + parts]
    refs = refs[4 + parts :]
    if pooled:
        back_ref, src_slot_ref, dst_slot_ref, busy_ref = refs[:4]
        refs = refs[4:]
        pool_out_ref = refs.pop(2 + parts)
        pool_rows, pool_flat, pool_sums = refs[-3:]
    src_grad_ref, dst_grad_ref = refs[:2]
    neg_grad_refs = refs[2 : 2 + parts]
    negatives, rel_flat = refs[2 + parts : 4 + parts]
    block = pl.program_id(0)
    part = neg_refs[0].shape[1]

    @pl.when(block == 0)
    def _():
        table, pieces = rel_ref[...], []
        for _ in range(3):
            pieces.append(table.astype(BF16).astype(F32))
            table = table - pieces[-1]
        rel_flat[...] = jnp.concatenate(pieces, axis=0).T.astype(BF16)
        if pooled:
            compact_pool(back_ref, busy_ref[0, 0], pool_rows, pool_flat)
            pool_sums[...] = jnp.zeros(pool_sums.shape, F32)

    for k in range(parts):
        negatives[k * part : (k + 1) * part] = neg_refs[k][0]
    turned = negatives[...].astype(F32).T.astype(BF16)
    hot = one_hot(rel_ref.shape[0], rel_ids_ref[...].reshape(1, rel_ids_ref.shape[-1]))
    relation = dot(rel_flat[...], jnp.concatenate([hot] * 3, axis=0), NN)
    source = src_ref[...].astype(F32)
    target = dst_ref[...].astype(F32)
    if pooled:
        count = pool_flat.shape[1]
        src_hot = one_hot(count, src_slot_ref[...].reshape(1, src_slot_ref.shape[-1]))
        dst_hot = one_hot(count, dst_slot_ref[...].reshape(1, dst_slot_ref.shape[-1]))
        source = source + dot(pool_flat[...], src_hot, NN)
        target = target + dot(pool_flat[...], dst_hot, NN)
    product = source * relation
    positive = jnp.sum(product * target, axis=0, keepdims=True)
    pos_weight = -jax.nn.sigmoid(-positive)
    query = product.astype(BF16)
    weight = jax.nn.sigmoid(dot(negatives[...], query, NN)).astype(BF16)
    gathered = dot(turned, weight, NN)
    src_grad = (relation * (pos_weight * target + gathered)).astype(BF16)
    dst_grad = (pos_weight * product).astype(BF16)
    src_grad_ref[...] = src_grad
    dst_grad_ref[...] = dst_grad
    neg_grad = dot(query, weight, NT).T
    if pooled:
        pool_sums[...] += dot(src_grad, src_hot, NT) + dot(dst_grad, dst_hot, NT)

    for k in range(parts):
        neg_grad_refs[k][0] = neg_grad[k * part : (k + 1) * part].astype(BF16)
    if pooled:

        @pl.when(block == pl.num_programs(0) - 1)
        def _():
            expand_pool(pool_sums[...], busy_ref[0, 0], pool_out_ref)


def edges(rows, rel_ids, relations, negatives, pool=None, pool_slot=None, busy=None):
    feature, endpoints = rows.shape
    parts = len(negatives)
    spans, part, _ = negatives[0].shape
    width = rel_ids.shape[1]
    edge_spec = pl.BlockSpec((feature, width), lambda b: (0, b))
    neg_spec = pl.BlockSpec((1, part, feature), lambda b: (b, 0, 0))
    operands = [rows, rows, rel_ids.reshape(spans, 1, width), relations, *negatives]
    specs = [
        edge_spec,
        pl.BlockSpec((feature, width), lambda b: (0, spans + b)),
        pl.BlockSpec((1, 1, width), lambda b: (b, 0, 0)),
        pl.BlockSpec(relations.shape, lambda b: (0, 0)),
    ] + [neg_spec] * parts
    out_specs = [edge_spec, edge_spec] + [neg_spec] * parts
    out_shape = [jax.ShapeDtypeStruct((feature, endpoints // 2), BF16)] * 2
    out_shape += [jax.ShapeDtypeStruct((spans, part, feature), BF16)] * parts
    scratch = [
        pltpu.VMEM((parts * part, feature), BF16),
        pltpu.VMEM((feature, 3 * relations.shape[0]), BF16),
    ]
    if pool is not None:
        slot = pool_slot.reshape(2 * spans, 1, width)
        pool_spec = pl.BlockSpec(pool.shape, lambda b: (0, 0, 0))
        operands += [pool, slot, slot, busy]
        specs += [
            pool_spec,
            pl.BlockSpec((1, 1, width), lambda b: (b, 0, 0)),
            pl.BlockSpec((1, 1, width), lambda b: (spans + b, 0, 0)),
            pl.BlockSpec(memory_space=pltpu.SMEM),
        ]
        out_specs.append(pool_spec)
        out_shape.append(jax.ShapeDtypeStruct(pool.shape, BF16))
        count = compact_size(pool.shape[0] // RELAYS)
        scratch += [
            pltpu.VMEM((count, feature // LANES * LANES), BF16),
            pltpu.VMEM((feature, count), BF16),
            pltpu.VMEM((feature, count), F32),
        ]
    src_grad, dst_grad, *rest = call(
        functools.partial(edges_kernel, parts=parts, pooled=pool is not None),
        "edges",
        6 * feature * parts * part * spans * width,
        4 * (rows.size + parts * negatives[0].size),
        grid=(spans,),
        in_specs=specs,
        out_specs=out_specs,
        out_shape=out_shape,
        scratch_shapes=scratch,
    )(*operands)
    return src_grad, dst_grad, rest


def collect_kernel(src_ref, dst_ref, slot_ref, out_ref, *, group):
    segments, width = slot_ref.shape
    feature = src_ref.shape[0]
    step = pl.program_id(0)
    total = jnp.zeros((feature, group * LANES), F32)
    for segment in range(segments):
        grads = src_ref if segment < segments // 2 else dst_ref
        start = segment % (segments // 2) * width
        hot = one_hot(group * LANES, slot_ref[segment : segment + 1, :], step * group * LANES)
        total = total + dot(grads[:, start : start + width], hot, NT)
    total = total.astype(BF16)
    first = out_ref.shape[1] - feature
    for i in range(group):
        out_ref[i, first:] = total[:, i * LANES : (i + 1) * LANES]


def collect(src_grad, dst_grad, slot, devices, neg_cap=0):
    feature = src_grad.shape[0]
    group = 4
    slots = devices * LANES
    height = feature + (packed_height(neg_cap, feature) if neg_cap else 0)
    whole = pl.BlockSpec(src_grad.shape, lambda i: (0, 0))
    return call(
        functools.partial(collect_kernel, group=group),
        "collect_grads",
        2 * feature * slots * slot.size,
        2 * feature * (slots + slot.size),
        grid=(devices // group,),
        in_specs=[whole, whole, pl.BlockSpec(slot.shape, lambda i: (0, 0))],
        out_specs=pl.BlockSpec((group, height, LANES), lambda i: (i, 0, 0)),
        out_shape=jax.ShapeDtypeStruct((devices, height, LANES), BF16),
    )(src_grad, dst_grad, slot)


def collect_neg_kernel(sent_ref, slot_ref, *refs, group, cap):
    grad_refs, out_ref, sums = refs[:-2], refs[-2], refs[-1]
    step = pl.program_id(0)

    @pl.when(step == 0)
    def _():
        total = grad_refs[0][...].astype(F32)
        for grad_ref in grad_refs[1:]:
            total = total + grad_ref[...].astype(F32)
        sums[...] = total.astype(BF16)

    rows = jnp.zeros((group * cap, sums.shape[-1]), F32)
    for part in range(slot_ref.shape[0]):
        hot = one_hot(group * cap, slot_ref[part : part + 1, :], step * group * cap)
        rows = rows + dot(hot, sums[part], NN)
    pack_all(out_ref, 0, cap, rows, rows.T)


def collect_neg(sent, slot, grads, cap):
    devices = sent.shape[0]
    feature = grads[0].shape[-1]
    group = 16
    height = packed_height(cap, feature)
    return call(
        functools.partial(collect_neg_kernel, group=group, cap=cap),
        "collect_negatives",
        2 * devices * cap * feature * slot.size,
        4 * len(grads) * grads[0].size,
        grid=(devices // group,),
        in_specs=[
            pl.BlockSpec(memory_space=pl.ANY),
            pl.BlockSpec(slot.shape, lambda i: (0, 0)),
        ]
        + [pl.BlockSpec(grads[0].shape, lambda i: (0, 0, 0))] * len(grads),
        out_specs=pl.BlockSpec((group, height, LANES), lambda i: (i, 0, 0)),
        out_shape=jax.ShapeDtypeStruct(sent.shape, BF16),
        scratch_shapes=[pltpu.VMEM(grads[0].shape, BF16)],
        input_output_aliases={0: 0},
    )(sent, slot, *grads)


def add_kernel(*refs, rows, neg_cap, first):
    refs = list(refs)
    recv_ref, req_ref = refs[:2]
    refs = refs[2:]
    if neg_cap:
        neg_req_ref = refs.pop(0)
        neg_rows, neg_flat = refs[-2:]
    if not first:
        so_far_ref = refs.pop(0)
    out_ref, flat = refs[:2]
    devices = recv_ref.shape[0]
    feature = flat.shape[0]
    step = pl.program_id(0)

    @pl.when(step == 0)
    def _():
        start = recv_ref.shape[1] - feature
        for d in range(devices):
            flat[:, d * LANES : (d + 1) * LANES] = recv_ref[d, start:]
        if neg_cap:
            unpack_all(recv_ref, 0, neg_cap, neg_rows, neg_flat)

    base = step * rows
    row = jnp.concatenate([req_ref[d : d + 1, :] for d in range(devices)], axis=1)
    total = dot(flat[...], one_hot(rows, row, base), NT)
    if neg_cap:
        row = jnp.concatenate([neg_req_ref[d : d + 1, :neg_cap] for d in range(devices)], axis=1)
        total = total + dot(neg_flat[...], one_hot(rows, row, base), NT)
    if not first:
        total = total + so_far_ref[...]
    out_ref[...] = total


def add_rows(recv, requests, so_far, feature, rows_dev, neg_requests=None, neg_cap=0):
    devices = recv.shape[0]
    rows = 512 if devices * LANES <= 4096 else 128
    slots = devices * LANES
    whole_req = pl.BlockSpec((devices, LANES), lambda i: (0, 0))
    rows_spec = pl.BlockSpec((feature, rows), lambda i: (0, i))
    operands = [recv, requests]
    specs = [pl.BlockSpec(recv.shape, lambda i: (0, 0, 0)), whole_req]
    scratch = [pltpu.VMEM((feature, slots), BF16)]
    if neg_cap:
        operands.append(neg_requests)
        specs.append(whole_req)
        scratch += unpack_scratch(devices, neg_cap, feature)
    if so_far is not None:
        operands.append(so_far)
        specs.append(rows_spec)
    return call(
        functools.partial(add_kernel, rows=rows, neg_cap=neg_cap, first=so_far is None),
        "add_grads",
        2 * feature * slots * rows_dev,
        2 * feature * slots + 8 * feature * rows_dev,
        grid=(rows_dev // rows,),
        in_specs=specs,
        out_specs=rows_spec,
        out_shape=jax.ShapeDtypeStruct((feature, rows_dev), F32),
        scratch_shapes=scratch,
    )(*operands)


def add_quarters_kernel(
    recv_ref, asked_ref, so_far_ref, out_ref, flat, neg_rows, neg_flat, *, neg_cap
):
    devices = recv_ref.shape[0]
    feature, rows = out_ref.shape
    step = pl.program_id(0)

    @pl.when(step == 0)
    def _():
        start = recv_ref.shape[1] - feature
        for first in range(0, devices, PARTS):
            for part in range(PARTS):
                for j in range(PARTS):
                    to = first // PARTS * LANES + j * SHARE
                    flat[part, :, to : to + SHARE] = recv_ref[
                        first + (part ^ j), start:, j * SHARE : (j + 1) * SHARE
                    ]
        unpack_all(recv_ref, 0, neg_cap, neg_rows, neg_flat)

    base = step * rows
    asked = quarter_ids([asked_ref[d : d + 1, :LANES] for d in range(devices)])
    row = asked[0]
    for part in range(1, PARTS):
        row = jnp.where(step == part, asked[part], row)
    total = dot(flat[step], one_hot(rows, row, base), NT)
    negs = slice(asked_ref.shape[1] - LANES, asked_ref.shape[1] - LANES + neg_cap)
    row = jnp.concatenate([asked_ref[d : d + 1, negs] for d in range(devices)], axis=1)
    out_ref[...] = total + dot(neg_flat[...], one_hot(rows, row, base), NT) + so_far_ref[...]


def add_quarters(recv, asked, so_far, neg_cap):
    feature, rows_dev = so_far.shape
    devices = recv.shape[0]
    slots = devices * LANES
    whole_asked = pl.BlockSpec(asked.shape, lambda i: (0, 0))
    rows_spec = pl.BlockSpec((feature, rows_dev // PARTS), lambda i: (0, i))
    return call(
        functools.partial(add_quarters_kernel, neg_cap=neg_cap),
        "add_quarters",
        feature * (slots // 2 + 2 * devices * neg_cap) * rows_dev,
        2 * feature * slots + 8 * feature * rows_dev,
        grid=(PARTS,),
        in_specs=[pl.BlockSpec(recv.shape, lambda i: (0, 0, 0)), whole_asked, rows_spec],
        out_specs=rows_spec,
        out_shape=jax.ShapeDtypeStruct((feature, rows_dev), F32),
        scratch_shapes=[pltpu.VMEM((PARTS, feature, slots // PARTS), BF16)]
        + unpack_scratch(devices, neg_cap, feature),
    )(recv, asked, so_far)


def add_pool_kernel(*refs, rows, first):
    one_ref, two_ref, one_req_ref, two_req_ref = refs[:4]
    out_ref, packed, *flats = refs[4 + (not first) :]
    step = pl.program_id(0)

    @pl.when(step == 0)
    def _():
        for recv_ref, flat in zip((one_ref, two_ref), flats):
            unpack_all(recv_ref, 0, POOL, packed, flat)

    total = dot(flats[0][...], one_hot(rows, one_req_ref[...], step * rows), NT)
    total = total + dot(flats[1][...], one_hot(rows, two_req_ref[...], step * rows), NT)
    if not first:
        total = total + refs[4][...]
    out_ref[...] = total


def add_pool(one, two, requests, so_far, feature, rows_dev):
    rows = 512
    devices = one.shape[0]
    slots = devices * POOL
    recv_spec = pl.BlockSpec(one.shape, lambda i: (0, 0, 0))
    req_spec = pl.BlockSpec((1, slots), lambda i: (0, 0))
    rows_spec = pl.BlockSpec((feature, rows), lambda i: (0, i))
    packed, flat = unpack_scratch(devices, POOL, feature)
    extra = [] if so_far is None else [so_far]
    return call(
        functools.partial(add_pool_kernel, rows=rows, first=so_far is None),
        "add_pool",
        4 * feature * slots * rows_dev,
        4 * feature * slots + 4 * feature * rows_dev,
        grid=(rows_dev // rows,),
        in_specs=[recv_spec, recv_spec, req_spec, req_spec] + [rows_spec] * len(extra),
        out_specs=rows_spec,
        out_shape=jax.ShapeDtypeStruct((feature, rows_dev), F32),
        scratch_shapes=[packed, flat, flat],
    )(one, two, requests[0][None], requests[1][None], *extra)


def after(value, other):
    anywhere = pl.BlockSpec(memory_space=pl.ANY)
    return call(
        lambda value_ref, other_ref, out_ref: None,
        "after",
        0,
        0,
        in_specs=[anywhere, anywhere],
        out_specs=anywhere,
        out_shape=jax.ShapeDtypeStruct(value.shape, value.dtype),
        input_output_aliases={0: 0},
    )(value, other)


def exchange(value):
    return lax.all_to_all(value, ("shard", "grp"), split_axis=0, concat_axis=0, tiled=True)


def swap(value, bit):
    sharers = lax.axis_size("grp")
    return lax.ppermute(value, "grp", [(i, i ^ bit) for i in range(sharers)])


def share_out(value, wait=lambda block: block):
    sharers = lax.axis_size("grp")
    blocks = {0: value}
    bit = sharers // 2
    while bit:
        for k in list(blocks):
            blocks[k ^ bit] = swap(wait(blocks[k]) if k else blocks[k], bit)
        bit //= 2
    return [blocks[k] for k in range(sharers)]


def trade(blocks):
    sharers = len(blocks)
    terms = [[block] for block in blocks]
    bit = 1
    while bit < sharers:
        for k in range(0, sharers, 2 * bit):
            total = terms[k ^ bit][0].astype(F32)
            for term in terms[k ^ bit][1:]:
                total = total + term.astype(F32)
            terms[k].append(swap(total.astype(BF16), bit))
        bit *= 2
    return terms[0]


def pad_lanes(value, width, fill):
    return jnp.pad(value, ((0, 0), (0, width - value.shape[1])), constant_values=fill)


def body(entity_table, rel_diag, src_ids, dst_ids, rel_ids, neg_ids):
    rows_dev, feature = entity_table.shape
    sharers = lax.axis_size("grp")
    devices = lax.axis_size("shard") * sharers
    spans, neg_count = neg_ids.shape
    edge_count = src_ids.shape[0]
    block_len = edge_count // spans
    edge_cap = 4 * edge_count // devices
    chunks = round_up(edge_cap, LANES) // LANES
    part_width = neg_count // sharers
    neg_cap = round_up(2 * spans * part_width // devices, 16)
    width = round_up(block_len, 512)
    part = round_up(part_width, LANES)
    me = lax.axis_index("grp")

    table = entity_table.T.astype(BF16)
    own_ids = lax.dynamic_slice_in_dim(neg_ids, me * part_width, part_width, 1)
    rel_rows = pad_lanes(rel_ids.reshape(spans, block_len), width, -1)

    def ask(zero, chunks):
        message, *slots = make_slots(
            lax.axis_index(("shard", "grp")),
            src_ids + zero,
            dst_ids + zero,
            own_ids,
            rows_dev,
            devices,
            chunks,
            neg_cap,
            width,
            part,
        )
        asked = exchange(message)[:, 0]
        return asked, asked[:, -LANES:], slots, slots[-1]

    def chunked(zero):
        asked, neg_asked, slots, neg_slot = ask(zero, chunks)
        direct = [asked[:, c * LANES : (c + 1) * LANES] for c in range(chunks)]
        back = [exchange(gather(table, direct[0], neg_asked, neg_cap))]
        back += [exchange(gather(table, direct[c])) for c in range(1, chunks)]
        negatives = share_out(spread_neg(back[0], neg_slot, neg_cap, feature))
        rows = None
        for c in range(chunks):
            rows = spread(back[c], slots[c], rows, feature)
        src_grad, dst_grad, neg_grads = edges(rows, rel_rows, rel_diag, negatives)
        grad = None
        for c in range(1, chunks):
            sent = exchange(collect(src_grad, dst_grad, slots[c], devices))
            grad = add_rows(sent, direct[c], grad, feature, rows_dev)
        sent = collect(src_grad, dst_grad, slots[0], devices, neg_cap)
        sent = exchange(collect_neg(sent, neg_slot, trade(neg_grads), neg_cap))
        return add_rows(sent, direct[0], grad, feature, rows_dev, neg_asked, neg_cap)

    def pooled():
        asked, neg_asked, (slot, pool_slot, busy, _), neg_slot = ask(0, 0)
        listed = asked[:, LANES : LANES + RELAYS * POOL].reshape(devices, RELAYS, POOL)
        listed = listed.transpose(1, 0, 2).reshape(RELAYS, devices * POOL) - me * rows_dev
        listed = listed[me ^ jnp.arange(RELAYS, dtype=jnp.int32)]
        back = exchange(gather_quarters(table, asked, neg_cap))
        far = swap(gather_pool(table, listed[3], devices), 1)
        far = swap(gather_pool(table, listed[2], devices) + far, 2)
        near = swap(gather_pool(table, listed[1], devices), 1)
        near = gather_pool(table, listed[0], devices) + near
        rows = spread(back, slot, None, feature)
        negatives = share_out(
            spread_neg(back, neg_slot, neg_cap, feature), lambda block: after(block, rows)
        )
        src_grad, dst_grad, rest = edges(
            rows, rel_rows, rel_diag, negatives, exchange(near + far), pool_slot, busy
        )
        neg_grads, pool = rest[:-1], rest[-1]
        near = exchange(pool)
        far = swap(near, 2)
        sent = collect(src_grad, dst_grad, slot, devices, neg_cap)
        sent = exchange(collect_neg(sent, neg_slot, trade(neg_grads), neg_cap))
        grad = add_pool(near, swap(near, 1), listed[:2], None, feature, rows_dev)
        far = after(far, grad)
        grad = add_pool(far, swap(far, 1), listed[2:], grad, feature, rows_dev)
        return add_quarters(sent, asked, grad, neg_cap), jnp.max(neg_asked[:, -1])

    if chunks == 1 or sharers != RELAYS:
        return chunked(0).T
    return lax.while_loop(
        lambda state: state[1] > 0,
        lambda state: (chunked(jnp.minimum(state[1], 0)), -state[1]),
        pooled(),
    )[0].T


def solution(mesh):
    placed = (
        P(("shard", "grp"), None),
        P(),
        P(("shard", "grp")),
        P(("shard", "grp")),
        P(("shard", "grp")),
        P("shard", None),
    )
    return jax.shard_map(
        body, mesh=mesh, in_specs=placed, out_specs=P(("shard", "grp"), None), check_vma=False
    )
```

```python
import functools

import jax
import jax.numpy as jnp
from jax import lax
from jax.experimental import pallas as pl
from jax.experimental.pallas import tpu as pltpu
from jax.sharding import PartitionSpec as P

LANES = 128
POOL = 48
RELAYS = 4
SMALL = 80
PARTS = 4
SHARE = LANES // PARTS
VMEM_BYTES = 56 << 20
F32 = jnp.float32
BF16 = jnp.bfloat16
NN = (((1,), (0,)), ((), ()))
NT = (((1,), (1,)), ((), ()))
TN = (((0,), (0,)), ((), ()))


def round_up(value, unit):
    return -(-value // unit) * unit


def dot(left, right, dims):
    return lax.dot_general(left, right, dims, preferred_element_type=F32)


def one_hot(rows, row, base=0):
    places = lax.broadcasted_iota(jnp.int32, (rows, row.shape[1]), 0) + base
    return jnp.where(places == row, 1.0, 0.0).astype(BF16)


def call(kernel, name, flops, nbytes, **kwargs):
    return pl.pallas_call(
        kernel,
        name=name,
        compiler_params=pltpu.CompilerParams(vmem_limit_bytes=VMEM_BYTES),
        cost_estimate=pl.CostEstimate(flops=flops, bytes_accessed=nbytes, transcendentals=0),
        **kwargs,
    )


def ranks(members, mixer):
    groups = members[0].shape[0]
    both = dot(jnp.concatenate(members, axis=0).astype(BF16), mixer, NN)
    taken = jnp.zeros((groups, LANES), F32)
    found = []
    for i, member in enumerate(members):
        chunk = both[i * groups : (i + 1) * groups]
        found.append(jnp.sum((chunk[:, :LANES] + taken) * member, axis=0, keepdims=True))
        taken = taken + chunk[:, LANES:]
    return [rank.astype(jnp.int32) for rank in found], taken


def fill(members, codes, places, count):
    groups = members[0].shape[0]
    high = [m * (c // LANES).astype(F32) for m, c in zip(members, codes)]
    low = [m * (c % LANES).astype(F32) for m, c in zip(members, codes)]
    left = jnp.concatenate(
        [jnp.concatenate(high, axis=1), jnp.concatenate(low, axis=1)], axis=0
    ).astype(BF16)
    sums = dot(left, one_hot(count, jnp.concatenate(places, axis=1)), NT)
    return (LANES * sums[:groups] + sums[groups:]).astype(jnp.int32) - 1


def slots_kernel(
    me_ref, src_ref, dst_ref, own_ref, *refs, rows_dev, devices, chunks, neg_cap, spans, part
):
    pooled = chunks == 0
    msg_ref, neg_ref = refs[0], refs[-1]
    slot_refs = refs[1:-1]
    row = lax.broadcasted_iota(jnp.int32, (LANES, 2 * LANES), 0)
    lane = lax.broadcasted_iota(jnp.int32, (LANES, 2 * LANES), 1)
    mixer = jnp.where(row < lane, 1.0, 0.0).astype(BF16)
    owners = lax.broadcasted_iota(jnp.int32, (devices, LANES), 0)

    def prepare(rows, width):
        where, holder, codes, members = [], [], [], []
        for segment, ids_row in enumerate(rows):
            blank = jnp.full((1, width - ids_row.shape[1]), -1, jnp.int32)
            ids_row = jnp.concatenate([ids_row, blank], axis=1)
            for start in range(0, width, LANES):
                ids = ids_row[:, start : start + LANES]
                owner = jnp.where(ids >= 0, ids // rows_dev, -1)
                where.append((slice(segment, segment + 1), slice(start, start + LANES)))
                holder.append(owner)
                codes.append(jnp.where(ids >= 0, ids - owner * rows_dev + 1, 0))
                members.append(jnp.where(owners == owner, 1.0, 0.0))
        return where, holder, codes, members

    ends = []
    for ids_ref in (src_ref, dst_ref):
        ids = ids_ref[...].reshape(1, ids_ref.shape[0])
        length = ids.shape[1] // spans
        ends += [ids[:, b * length : (b + 1) * length] for b in range(spans)]
    where, holder, codes, members = prepare(ends, slot_refs[0].shape[1])
    flag = jnp.full((1, 1), -1, jnp.int32)
    if pooled:
        turn = me_ref[0, 0] % PARTS
        quarters = [jnp.maximum(code - 1, 0) // (rows_dev // PARTS) for code in codes]
        split = [
            jnp.concatenate([jnp.where(q == k, member, 0.0) for k in range(PARTS)], axis=0)
            for member, q in zip(members, quarters)
        ]
        found, _ = ranks(split, mixer)
        places = []
        for at, owner, rank, q in zip(where, holder, found, quarters):
            inside = (owner >= 0) & (rank < SHARE)
            place = (q ^ turn) * SHARE + rank
            slot_refs[0][at] = jnp.where(inside, owner * LANES + place, -1)
            places.append(jnp.where(inside, place, -1))
        msg_ref[:, 0, :LANES] = fill(members, codes, places, LANES)
        offset = LANES

        pool_ref, busy_ref = slot_refs[1:]
        shards = devices // RELAYS
        room = RELAYS * POOL
        shard_rows = lax.broadcasted_iota(jnp.int32, (shards, LANES), 0)
        spilled, spill_codes = [], []
        for owner, code, rank in zip(holder, codes, found):
            shard = jnp.where(rank >= SHARE, owner // RELAYS, -1)
            spilled.append(jnp.where(shard_rows == shard, 1.0, 0.0))
            spill_codes.append(code + (owner % RELAYS) * rows_dev)
        listed, taken = ranks(spilled, mixer)
        places = []
        for at, owner, rank, place in zip(where, holder, found, listed):
            inside = (owner >= 0) & (rank >= SHARE) & (place < room)
            compact = jnp.where(
                place < SMALL, owner // RELAYS * SMALL + place, (shards - 1) * SMALL + place
            )
            pool_ref[at] = jnp.where(inside, compact, -1)
            places.append(jnp.where(inside, place, -1))
        listed = fill(spilled, spill_codes, places, 2 * LANES)
        for shard in range(shards):
            msg_ref[shard * RELAYS : (shard + 1) * RELAYS, 0, offset : offset + 2 * LANES] = (
                jnp.broadcast_to(listed[shard : shard + 1], (RELAYS, 2 * LANES))
            )
        offset += 2 * LANES
        most = jnp.max(taken, axis=0, keepdims=True)
        busy = jnp.where(taken > SMALL, 1.0, 0.0)
        crowded = jnp.sum(busy, axis=0, keepdims=True) > 1.0
        flag = jnp.where((most > room) | crowded, 1, -1)[:, :1]
        place = jnp.sum(busy * shard_rows.astype(F32), axis=0, keepdims=True).astype(jnp.int32)
        busy_ref[...] = jnp.minimum(place, shards - 1)[:, :1]
    else:
        found, _ = ranks(members, mixer)
        for chunk in range(chunks):
            places = []
            for at, owner, rank in zip(where, holder, found):
                place = rank - chunk * LANES
                place = jnp.where((owner >= 0) & (place >= 0) & (place < LANES), place, -1)
                slot_refs[chunk][at] = jnp.where(place >= 0, owner * LANES + place, -1)
                places.append(place)
            listed = fill(members, codes, places, LANES)
            msg_ref[:, 0, chunk * LANES : (chunk + 1) * LANES] = listed
        offset = chunks * LANES

    where, holder, codes, members = prepare([own_ref[b : b + 1, :] for b in range(spans)], part)
    found, _ = ranks(members, mixer)
    for at, owner, rank in zip(where, holder, found):
        neg_ref[at] = jnp.where(owner >= 0, owner * neg_cap + rank, -1)
    places = [jnp.where(owner >= 0, rank, -1) for owner, rank in zip(holder, found)]
    listed = fill(members, codes, places, LANES)
    lanes = lax.broadcasted_iota(jnp.int32, listed.shape, 1)
    msg_ref[:, 0, offset:] = jnp.where(lanes == LANES - 1, flag, listed)


def make_slots(me, src_ids, dst_ids, own, rows_dev, devices, chunks, neg_cap, width, part):
    lanes = (chunks + 1 if chunks else 4) * LANES
    spans = own.shape[0]
    ends_shape = jax.ShapeDtypeStruct((2 * spans, width), jnp.int32)
    if chunks:
        slots = [ends_shape] * chunks
    else:
        slots = [ends_shape, ends_shape, jax.ShapeDtypeStruct((1, 1), jnp.int32)]
    return call(
        functools.partial(
            slots_kernel,
            rows_dev=rows_dev,
            devices=devices,
            chunks=chunks,
            neg_cap=neg_cap,
            spans=spans,
            part=part,
        ),
        "slots",
        32 * devices * LANES * spans * width,
        16 * spans * width,
        in_specs=[
            pl.BlockSpec(memory_space=pltpu.SMEM),
            pl.BlockSpec(src_ids.shape, lambda: (0,)),
            pl.BlockSpec(dst_ids.shape, lambda: (0,)),
            pl.BlockSpec(own.shape, lambda: (0, 0)),
        ],
        out_shape=[jax.ShapeDtypeStruct((devices, 1, lanes), jnp.int32)]
        + slots
        + [jax.ShapeDtypeStruct((spans, part), jnp.int32)],
    )(me.reshape(1, 1), src_ids, dst_ids, own)


def packed_height(count, feature):
    return feature // LANES * count + feature % LANES


def pack(out_ref, at, start, rows, tail):
    count, feature = rows.shape
    for piece in range(feature // LANES):
        out_ref[at, start + piece * count : start + (piece + 1) * count, :] = rows[
            :, piece * LANES : (piece + 1) * LANES
        ].astype(out_ref.dtype)
    tail = jnp.concatenate([tail, jnp.zeros((tail.shape[0], LANES - count), tail.dtype)], axis=1)
    end = start + packed_height(count, feature)
    out_ref[at, end - tail.shape[0] : end, :] = tail.astype(out_ref.dtype)


def pack_all(out_ref, start, count, rows, turned):
    feature = rows.shape[1]
    first = feature // LANES * LANES
    for i in range(out_ref.shape[0]):
        at = slice(i * count, (i + 1) * count)
        pack(out_ref, i, start, rows[at], turned[first:, at])


def unpack_all(in_ref, start, count, rows_ref, flat_ref):
    feature = flat_ref.shape[0]
    pieces = feature // LANES
    end = start + packed_height(count, feature)
    devices = in_ref.shape[0]
    for d in range(devices):
        for piece in range(pieces):
            rows_ref[d * count : (d + 1) * count, piece * LANES : (piece + 1) * LANES] = in_ref[
                d, start + piece * count : start + (piece + 1) * count, :
            ]
    tails = [
        in_ref[d, end - feature % LANES : end, :].astype(F32)[:, :count] for d in range(devices)
    ]
    flat_ref[: pieces * LANES] = rows_ref[...].astype(F32).T.astype(BF16)
    flat_ref[pieces * LANES :] = jnp.concatenate(tails, axis=1).astype(BF16)


def unpack_scratch(devices, count, feature):
    return [
        pltpu.VMEM((devices * count, feature // LANES * LANES), BF16),
        pltpu.VMEM((feature, devices * count), BF16),
    ]


def gather_kernel(table_ref, *refs, group, neg_cap):
    feature, rows_dev = table_ref.shape
    first = pl.program_id(0) * group
    req_ref, out_ref = refs[0], refs[-1]
    row = [req_ref[pl.ds(first + i, 1), :] for i in range(group)]
    if neg_cap:
        row += [refs[1][pl.ds(first + i, 1), :neg_cap] for i in range(group)]
    rows = dot(table_ref[...], one_hot(rows_dev, jnp.concatenate(row, axis=1)), NN)
    start = out_ref.shape[1] - feature
    for i in range(group):
        out_ref[i, start:] = rows[:, i * LANES : (i + 1) * LANES].astype(BF16)
    if neg_cap:
        neg = rows[:, group * LANES :]
        pack_all(out_ref, 0, neg_cap, neg.T, neg)


def gather(table, requests, neg_requests=None, neg_cap=0):
    feature, rows_dev = table.shape
    devices = requests.shape[0]
    group = 4
    height = feature + (packed_height(neg_cap, feature) if neg_cap else 0)
    slots = devices * (LANES + neg_cap)
    whole = pl.BlockSpec((devices, LANES), lambda i: (0, 0))
    return call(
        functools.partial(gather_kernel, group=group, neg_cap=neg_cap),
        "gather_rows",
        2 * feature * rows_dev * slots,
        2 * feature * (rows_dev + slots),
        grid=(devices // group,),
        in_specs=[pl.BlockSpec((feature, rows_dev), lambda i: (0, 0)), whole]
        + ([whole] if neg_cap else []),
        out_specs=pl.BlockSpec((group, height, LANES), lambda i: (i, 0, 0)),
        out_shape=jax.ShapeDtypeStruct((devices, height, LANES), BF16),
    )(table, requests, *([neg_requests] if neg_cap else []))


def quarter_ids(ids):
    group = lax.broadcasted_iota(jnp.int32, (1, LANES), 1) // SHARE
    rows = []
    for part in range(PARTS):
        pieces = []
        for first in range(0, len(ids), PARTS):
            piece = ids[first + part]
            for j in range(1, PARTS):
                piece = jnp.where(group == j, ids[first + (part ^ j)], piece)
            pieces.append(piece)
        rows.append(jnp.concatenate(pieces, axis=1))
    return rows


def gather_quarters_kernel(table_ref, asked_ref, out_ref, *, neg_cap):
    feature, rows_dev = table_ref.shape
    group = out_ref.shape[0]
    share = rows_dev // PARTS
    ids = [asked_ref[i : i + 1, :LANES] for i in range(group)]
    found = []
    for part, row in enumerate(quarter_ids(ids)):
        start = part * share
        found.append(dot(table_ref[:, start : start + share], one_hot(share, row, start), NN))
    start = out_ref.shape[1] - feature
    lanes = lax.broadcasted_iota(jnp.int32, (feature, LANES), 1) // SHARE
    for i in range(group):
        at = slice(i // PARTS * LANES, (i // PARTS + 1) * LANES)
        rows = found[i % PARTS][:, at]
        for j in range(1, PARTS):
            rows = jnp.where(lanes == j, found[j ^ (i % PARTS)][:, at], rows)
        out_ref[i, start:] = rows.astype(BF16)
    negs = slice(asked_ref.shape[1] - LANES, asked_ref.shape[1] - LANES + neg_cap)
    row = [asked_ref[i : i + 1, negs] for i in range(group)]
    neg = dot(table_ref[...], one_hot(rows_dev, jnp.concatenate(row, axis=1)), NN)
    pack_all(out_ref, 0, neg_cap, neg.T, neg)


def gather_quarters(table, asked, neg_cap):
    feature, rows_dev = table.shape
    devices = asked.shape[0]
    group = 8
    height = feature + packed_height(neg_cap, feature)
    return call(
        functools.partial(gather_quarters_kernel, neg_cap=neg_cap),
        "gather_quarters",
        feature * rows_dev * devices * (LANES // 2 + 2 * neg_cap),
        2 * feature * (rows_dev + devices * (LANES + neg_cap)),
        grid=(devices // group,),
        in_specs=[pl.BlockSpec((feature, rows_dev), lambda i: (0, 0)), pl.BlockSpec((group, asked.shape[1]), lambda i: (i, 0))],
        out_specs=pl.BlockSpec((group, height, LANES), lambda i: (i, 0, 0)),
        out_shape=jax.ShapeDtypeStruct((devices, height, LANES), BF16),
    )(table, asked)


def gather_pool_kernel(table_ref, req_ref, out_ref, *, group):
    rows_dev = table_ref.shape[1]
    row = req_ref[...].reshape(1, group * POOL)
    rows = dot(table_ref[...], one_hot(rows_dev, row), NN)
    pack_all(out_ref, 0, POOL, rows.T, rows)


def gather_pool(table, requests, devices):
    feature, rows_dev = table.shape
    group = 8
    steps = devices // group
    height = packed_height(POOL, feature)
    return call(
        functools.partial(gather_pool_kernel, group=group),
        "gather_pool",
        2 * feature * rows_dev * requests.size,
        2 * feature * (rows_dev + requests.size),
        grid=(steps,),
        in_specs=[
            pl.BlockSpec((feature, rows_dev), lambda i: (0, 0)),
            pl.BlockSpec((1, 1, group * POOL), lambda i: (i, 0, 0)),
        ],
        out_specs=pl.BlockSpec((group, height, LANES), lambda i: (i, 0, 0)),
        out_shape=jax.ShapeDtypeStruct((devices, height, LANES), BF16),
    )(table, requests.reshape(steps, 1, group * POOL))


def spread_neg_kernel(back_ref, slot_ref, out_ref, rows, flat, *, cap):
    unpack_all(back_ref, 0, cap, rows, flat)
    for part in range(slot_ref.shape[0]):
        hot = one_hot(flat.shape[1], slot_ref[part : part + 1, :])
        out_ref[part] = dot(flat[...], hot, NN).T.astype(BF16)


def spread_neg(back, slot, cap, feature):
    devices = back.shape[0]
    parts, width = slot.shape
    height = packed_height(cap, feature)
    return call(
        functools.partial(spread_neg_kernel, cap=cap),
        "spread_negatives",
        2 * devices * cap * feature * slot.size,
        2 * devices * cap * feature,
        grid=(1,),
        in_specs=[
            pl.BlockSpec((devices, height, LANES), lambda i: (0, 0, 0)),
            pl.BlockSpec(slot.shape, lambda i: (0, 0)),
        ],
        out_specs=pl.BlockSpec((parts, width, feature), lambda i: (0, 0, 0)),
        out_shape=jax.ShapeDtypeStruct((parts, width, feature), BF16),
        scratch_shapes=unpack_scratch(devices, cap, feature),
    )(back, slot)


def spread_kernel(*refs, first):
    back_ref, slot_ref = refs[:2]
    so_far_ref = None if first else refs[2]
    out_ref, flat = refs[2 + (not first)], refs[-1]
    devices = back_ref.shape[0]
    feature = flat.shape[0]

    @pl.when(pl.program_id(0) == 0)
    def _():
        start = back_ref.shape[1] - feature
        for d in range(devices):
            flat[:, d * LANES : (d + 1) * LANES] = back_ref[d, start:]

    row = slot_ref[...].reshape(1, slot_ref.shape[-1])
    rows = dot(flat[...], one_hot(flat.shape[1], row), NN)
    if not first:
        rows = rows + so_far_ref[...].astype(F32)
    out_ref[...] = rows.astype(BF16)


def spread(back, slot, so_far, feature):
    devices = back.shape[0]
    segments, width = slot.shape
    slots = devices * LANES
    tile = 512 if slots <= 4096 else 128
    steps = width // tile
    rows_spec = pl.BlockSpec((feature, tile), lambda i: (0, i))
    extra = [] if so_far is None else [so_far]
    return call(
        functools.partial(spread_kernel, first=so_far is None),
        "spread_rows",
        2 * feature * slots * slot.size,
        2 * feature * (slots + slot.size),
        grid=(segments * steps,),
        in_specs=[
            pl.BlockSpec(back.shape, lambda i: (0, 0, 0)),
            pl.BlockSpec((1, 1, tile), lambda i: (i // steps, 0, i % steps)),
        ]
        + [rows_spec] * len(extra),
        out_specs=rows_spec,
        out_shape=jax.ShapeDtypeStruct((feature, slot.size), BF16),
        scratch_shapes=[pltpu.VMEM((feature, slots), BF16)],
    )(back, slot.reshape(segments, 1, width), *extra)


def compact_places(shards):
    places = []
    for start, end, whose in ((0, SMALL, range(shards)), (SMALL, RELAYS * POOL, [None])):
        for shard in whose:
            place = start
            while place < end:
                relay, first = place // POOL, place % POOL
                count = min(POOL - first, end - place)
                to = (shards - 1 if shard is None else shard) * SMALL + place
                places.append((shard, relay, first, count, to))
                place += count
    return places


def compact_size(shards):
    return shards * SMALL + RELAYS * POOL - SMALL


def compact_pool(back_ref, busy, rows_ref, flat_ref):
    feature = flat_ref.shape[0]
    pieces = feature // LANES
    tails = []
    for shard, relay, first, count, to in compact_places(back_ref.shape[0] // RELAYS):
        at = (busy if shard is None else shard) * RELAYS + relay
        for piece in range(pieces):
            start = piece * POOL + first
            rows_ref[to : to + count, piece * LANES : (piece + 1) * LANES] = back_ref[
                at, start : start + count, :
            ]
        tail = back_ref[at, pieces * POOL :, :].astype(F32)
        tails.append(tail[:, first : first + count])
    flat_ref[: pieces * LANES] = rows_ref[...].astype(F32).T.astype(BF16)
    flat_ref[pieces * LANES :] = jnp.concatenate(tails, axis=1).astype(BF16)


def expand_pool(turned, busy, out_ref):
    feature = turned.shape[0]
    pieces = feature // LANES
    rows = turned.T
    out_ref[...] = jnp.zeros(out_ref.shape, out_ref.dtype)
    shards = out_ref.shape[0] // RELAYS
    for shard, relay, first, count, to in compact_places(shards):
        at = (busy if shard is None else shard) * RELAYS + relay
        for piece in range(pieces):
            start = piece * POOL + first
            out_ref[at, start : start + count, :] = rows[
                to : to + count, piece * LANES : (piece + 1) * LANES
            ].astype(BF16)
        if shard is not None:
            tail = turned[pieces * LANES :, to : to + count]
        else:
            tail = turned[pieces * LANES :, to : to + count]
            if first:
                kept = jnp.zeros((feature % LANES, first), F32)
                for other in range(shards):
                    start = other * SMALL + relay * POOL
                    part = turned[pieces * LANES :, start : start + first]
                    kept = jnp.where(busy == other, part, kept)
                tail = jnp.concatenate([kept, tail], axis=1)
        blank = jnp.zeros((tail.shape[0], LANES - tail.shape[1]), F32)
        out_ref[at, pieces * POOL :, :] = jnp.concatenate([tail, blank], axis=1).astype(BF16)


def edges_kernel(*refs, parts, pooled):
    refs = list(refs)
    src_ref, dst_ref, rel_ids_ref, rel_ref = refs[:4]
    neg_refs = refs[4 : 4 + parts]
    refs = refs[4 + parts :]
    if pooled:
        back_ref, src_slot_ref, dst_slot_ref, busy_ref = refs[:4]
        refs = refs[4:]
        pool_out_ref = refs.pop(2 + parts)
        pool_rows, pool_flat, pool_sums = refs[-3:]
    src_grad_ref, dst_grad_ref = refs[:2]
    neg_grad_refs = refs[2 : 2 + parts]
    negatives, rel_flat = refs[2 + parts : 4 + parts]
    block = pl.program_id(0)
    part = neg_refs[0].shape[1]

    @pl.when(block == 0)
    def _():
        table, pieces = rel_ref[...], []
        for _ in range(3):
            pieces.append(table.astype(BF16).astype(F32))
            table = table - pieces[-1]
        rel_flat[...] = jnp.concatenate(pieces, axis=0).T.astype(BF16)
        if pooled:
            compact_pool(back_ref, busy_ref[0, 0], pool_rows, pool_flat)
            pool_sums[...] = jnp.zeros(pool_sums.shape, F32)

    for k in range(parts):
        negatives[k * part : (k + 1) * part] = neg_refs[k][0]
    turned = negatives[...].astype(F32).T.astype(BF16)
    hot = one_hot(rel_ref.shape[0], rel_ids_ref[...].reshape(1, rel_ids_ref.shape[-1]))
    relation = dot(rel_flat[...], jnp.concatenate([hot] * 3, axis=0), NN)
    source = src_ref[...].astype(F32)
    target = dst_ref[...].astype(F32)
    if pooled:
        count = pool_flat.shape[1]
        src_hot = one_hot(count, src_slot_ref[...].reshape(1, src_slot_ref.shape[-1]))
        dst_hot = one_hot(count, dst_slot_ref[...].reshape(1, dst_slot_ref.shape[-1]))
        source = source + dot(pool_flat[...], src_hot, NN)
        target = target + dot(pool_flat[...], dst_hot, NN)
    product = source * relation
    positive = jnp.sum(product * target, axis=0, keepdims=True)
    pos_weight = -jax.nn.sigmoid(-positive)
    query = product.astype(BF16)
    weight = jax.nn.sigmoid(dot(negatives[...], query, NN)).astype(BF16)
    gathered = dot(turned, weight, NN)
    src_grad = (relation * (pos_weight * target + gathered)).astype(BF16)
    dst_grad = (pos_weight * product).astype(BF16)
    src_grad_ref[...] = src_grad
    dst_grad_ref[...] = dst_grad
    neg_grad = dot(query, weight, NT).T
    if pooled:
        pool_sums[...] += dot(src_grad, src_hot, NT) + dot(dst_grad, dst_hot, NT)

    for k in range(parts):
        neg_grad_refs[k][0] = neg_grad[k * part : (k + 1) * part].astype(BF16)
    if pooled:

        @pl.when(block == pl.num_programs(0) - 1)
        def _():
            expand_pool(pool_sums[...], busy_ref[0, 0], pool_out_ref)


def edges(rows, rel_ids, relations, negatives, pool=None, pool_slot=None, busy=None):
    feature, endpoints = rows.shape
    parts = len(negatives)
    spans, part, _ = negatives[0].shape
    width = rel_ids.shape[1]
    edge_spec = pl.BlockSpec((feature, width), lambda b: (0, b))
    neg_spec = pl.BlockSpec((1, part, feature), lambda b: (b, 0, 0))
    operands = [rows, rows, rel_ids.reshape(spans, 1, width), relations, *negatives]
    specs = [
        edge_spec,
        pl.BlockSpec((feature, width), lambda b: (0, spans + b)),
        pl.BlockSpec((1, 1, width), lambda b: (b, 0, 0)),
        pl.BlockSpec(relations.shape, lambda b: (0, 0)),
    ] + [neg_spec] * parts
    out_specs = [edge_spec, edge_spec] + [neg_spec] * parts
    out_shape = [jax.ShapeDtypeStruct((feature, endpoints // 2), BF16)] * 2
    out_shape += [jax.ShapeDtypeStruct((spans, part, feature), BF16)] * parts
    scratch = [
        pltpu.VMEM((parts * part, feature), BF16),
        pltpu.VMEM((feature, 3 * relations.shape[0]), BF16),
    ]
    if pool is not None:
        slot = pool_slot.reshape(2 * spans, 1, width)
        pool_spec = pl.BlockSpec(pool.shape, lambda b: (0, 0, 0))
        operands += [pool, slot, slot, busy]
        specs += [
            pool_spec,
            pl.BlockSpec((1, 1, width), lambda b: (b, 0, 0)),
            pl.BlockSpec((1, 1, width), lambda b: (spans + b, 0, 0)),
            pl.BlockSpec(memory_space=pltpu.SMEM),
        ]
        out_specs.append(pool_spec)
        out_shape.append(jax.ShapeDtypeStruct(pool.shape, BF16))
        count = compact_size(pool.shape[0] // RELAYS)
        scratch += [
            pltpu.VMEM((count, feature // LANES * LANES), BF16),
            pltpu.VMEM((feature, count), BF16),
            pltpu.VMEM((feature, count), F32),
        ]
    src_grad, dst_grad, *rest = call(
        functools.partial(edges_kernel, parts=parts, pooled=pool is not None),
        "edges",
        6 * feature * parts * part * spans * width,
        4 * (rows.size + parts * negatives[0].size),
        grid=(spans,),
        in_specs=specs,
        out_specs=out_specs,
        out_shape=out_shape,
        scratch_shapes=scratch,
    )(*operands)
    return src_grad, dst_grad, rest


def collect_kernel(src_ref, dst_ref, slot_ref, out_ref, *, group):
    segments, width = slot_ref.shape
    feature = src_ref.shape[0]
    step = pl.program_id(0)
    total = jnp.zeros((feature, group * LANES), F32)
    for segment in range(segments):
        grads = src_ref if segment < segments // 2 else dst_ref
        start = segment % (segments // 2) * width
        hot = one_hot(group * LANES, slot_ref[segment : segment + 1, :], step * group * LANES)
        total = total + dot(grads[:, start : start + width], hot, NT)
    total = total.astype(BF16)
    first = out_ref.shape[1] - feature
    for i in range(group):
        out_ref[i, first:] = total[:, i * LANES : (i + 1) * LANES]


def collect(src_grad, dst_grad, slot, devices, neg_cap=0):
    feature = src_grad.shape[0]
    group = 4
    slots = devices * LANES
    height = feature + (packed_height(neg_cap, feature) if neg_cap else 0)
    whole = pl.BlockSpec(src_grad.shape, lambda i: (0, 0))
    return call(
        functools.partial(collect_kernel, group=group),
        "collect_grads",
        2 * feature * slots * slot.size,
        2 * feature * (slots + slot.size),
        grid=(devices // group,),
        in_specs=[whole, whole, pl.BlockSpec(slot.shape, lambda i: (0, 0))],
        out_specs=pl.BlockSpec((group, height, LANES), lambda i: (i, 0, 0)),
        out_shape=jax.ShapeDtypeStruct((devices, height, LANES), BF16),
    )(src_grad, dst_grad, slot)


def collect_neg_kernel(sent_ref, slot_ref, *refs, group, cap):
    grad_refs, out_ref, sums = refs[:-2], refs[-2], refs[-1]
    step = pl.program_id(0)

    @pl.when(step == 0)
    def _():
        total = grad_refs[0][...].astype(F32)
        for grad_ref in grad_refs[1:]:
            total = total + grad_ref[...].astype(F32)
        sums[...] = total.astype(BF16)

    rows = jnp.zeros((group * cap, sums.shape[-1]), F32)
    for part in range(slot_ref.shape[0]):
        hot = one_hot(group * cap, slot_ref[part : part + 1, :], step * group * cap)
        rows = rows + dot(hot, sums[part], NN)
    pack_all(out_ref, 0, cap, rows, rows.T)


def collect_neg(sent, slot, grads, cap):
    devices = sent.shape[0]
    feature = grads[0].shape[-1]
    group = 16
    height = packed_height(cap, feature)
    return call(
        functools.partial(collect_neg_kernel, group=group, cap=cap),
        "collect_negatives",
        2 * devices * cap * feature * slot.size,
        4 * len(grads) * grads[0].size,
        grid=(devices // group,),
        in_specs=[
            pl.BlockSpec(memory_space=pl.ANY),
            pl.BlockSpec(slot.shape, lambda i: (0, 0)),
        ]
        + [pl.BlockSpec(grads[0].shape, lambda i: (0, 0, 0))] * len(grads),
        out_specs=pl.BlockSpec((group, height, LANES), lambda i: (i, 0, 0)),
        out_shape=jax.ShapeDtypeStruct(sent.shape, BF16),
        scratch_shapes=[pltpu.VMEM(grads[0].shape, BF16)],
        input_output_aliases={0: 0},
    )(sent, slot, *grads)


def add_kernel(*refs, rows, neg_cap, first):
    refs = list(refs)
    recv_ref, req_ref = refs[:2]
    refs = refs[2:]
    if neg_cap:
        neg_req_ref = refs.pop(0)
        neg_rows, neg_flat = refs[-2:]
    if not first:
        so_far_ref = refs.pop(0)
    out_ref, flat = refs[:2]
    devices = recv_ref.shape[0]
    feature = flat.shape[0]
    step = pl.program_id(0)

    @pl.when(step == 0)
    def _():
        start = recv_ref.shape[1] - feature
        for d in range(devices):
            flat[:, d * LANES : (d + 1) * LANES] = recv_ref[d, start:]
        if neg_cap:
            unpack_all(recv_ref, 0, neg_cap, neg_rows, neg_flat)

    base = step * rows
    row = jnp.concatenate([req_ref[d : d + 1, :] for d in range(devices)], axis=1)
    total = dot(flat[...], one_hot(rows, row, base), NT)
    if neg_cap:
        row = jnp.concatenate([neg_req_ref[d : d + 1, :neg_cap] for d in range(devices)], axis=1)
        total = total + dot(neg_flat[...], one_hot(rows, row, base), NT)
    if not first:
        total = total + so_far_ref[...]
    out_ref[...] = total


def add_rows(recv, requests, so_far, feature, rows_dev, neg_requests=None, neg_cap=0):
    devices = recv.shape[0]
    rows = 512 if devices * LANES <= 4096 else 128
    slots = devices * LANES
    whole_req = pl.BlockSpec((devices, LANES), lambda i: (0, 0))
    rows_spec = pl.BlockSpec((feature, rows), lambda i: (0, i))
    operands = [recv, requests]
    specs = [pl.BlockSpec(recv.shape, lambda i: (0, 0, 0)), whole_req]
    scratch = [pltpu.VMEM((feature, slots), BF16)]
    if neg_cap:
        operands.append(neg_requests)
        specs.append(whole_req)
        scratch += unpack_scratch(devices, neg_cap, feature)
    if so_far is not None:
        operands.append(so_far)
        specs.append(rows_spec)
    return call(
        functools.partial(add_kernel, rows=rows, neg_cap=neg_cap, first=so_far is None),
        "add_grads",
        2 * feature * slots * rows_dev,
        2 * feature * slots + 8 * feature * rows_dev,
        grid=(rows_dev // rows,),
        in_specs=specs,
        out_specs=rows_spec,
        out_shape=jax.ShapeDtypeStruct((feature, rows_dev), F32),
        scratch_shapes=scratch,
    )(*operands)


def add_quarters_kernel(
    recv_ref, asked_ref, so_far_ref, out_ref, flat, neg_rows, neg_flat, *, neg_cap
):
    devices = recv_ref.shape[0]
    feature, rows = out_ref.shape
    step = pl.program_id(0)

    @pl.when(step == 0)
    def _():
        start = recv_ref.shape[1] - feature
        lanes = lax.broadcasted_iota(jnp.int32, (feature, LANES), 1) // SHARE
        for first in range(0, devices, PARTS):
            to = first // PARTS * LANES
            blocks = [recv_ref[first + i, start:, :].astype(F32) for i in range(PARTS)]
            for part in range(PARTS):
                piece = blocks[part]
                for j in range(1, PARTS):
                    piece = jnp.where(lanes == j, blocks[part ^ j], piece)
                flat[part, :, to : to + LANES] = piece.astype(BF16)
        unpack_all(recv_ref, 0, neg_cap, neg_rows, neg_flat)

    base = step * rows
    asked = quarter_ids([asked_ref[d : d + 1, :LANES] for d in range(devices)])
    row = asked[0]
    for part in range(1, PARTS):
        row = jnp.where(step == part, asked[part], row)
    total = dot(flat[step], one_hot(rows, row, base), NT)
    negs = slice(asked_ref.shape[1] - LANES, asked_ref.shape[1] - LANES + neg_cap)
    row = jnp.concatenate([asked_ref[d : d + 1, negs] for d in range(devices)], axis=1)
    out_ref[...] = total + dot(neg_flat[...], one_hot(rows, row, base), NT) + so_far_ref[...]


def add_quarters(recv, asked, so_far, neg_cap):
    feature, rows_dev = so_far.shape
    devices = recv.shape[0]
    slots = devices * LANES
    whole_asked = pl.BlockSpec(asked.shape, lambda i: (0, 0))
    rows_spec = pl.BlockSpec((feature, rows_dev // PARTS), lambda i: (0, i))
    return call(
        functools.partial(add_quarters_kernel, neg_cap=neg_cap),
        "add_quarters",
        feature * (slots // 2 + 2 * devices * neg_cap) * rows_dev,
        2 * feature * slots + 8 * feature * rows_dev,
        grid=(PARTS,),
        in_specs=[pl.BlockSpec(recv.shape, lambda i: (0, 0, 0)), whole_asked, rows_spec],
        out_specs=rows_spec,
        out_shape=jax.ShapeDtypeStruct((feature, rows_dev), F32),
        scratch_shapes=[pltpu.VMEM((PARTS, feature, slots // PARTS), BF16)]
        + unpack_scratch(devices, neg_cap, feature),
    )(recv, asked, so_far)


def add_pool_kernel(*refs, rows, first):
    one_ref, two_ref, one_req_ref, two_req_ref = refs[:4]
    out_ref, packed, *flats = refs[4 + (not first) :]
    step = pl.program_id(0)

    @pl.when(step == 0)
    def _():
        for recv_ref, flat in zip((one_ref, two_ref), flats):
            unpack_all(recv_ref, 0, POOL, packed, flat)

    total = dot(flats[0][...], one_hot(rows, one_req_ref[...], step * rows), NT)
    total = total + dot(flats[1][...], one_hot(rows, two_req_ref[...], step * rows), NT)
    if not first:
        total = total + refs[4][...]
    out_ref[...] = total


def add_pool(one, two, requests, so_far, feature, rows_dev):
    rows = 512
    devices = one.shape[0]
    slots = devices * POOL
    recv_spec = pl.BlockSpec(one.shape, lambda i: (0, 0, 0))
    req_spec = pl.BlockSpec((1, slots), lambda i: (0, 0))
    rows_spec = pl.BlockSpec((feature, rows), lambda i: (0, i))
    packed, flat = unpack_scratch(devices, POOL, feature)
    extra = [] if so_far is None else [so_far]
    return call(
        functools.partial(add_pool_kernel, rows=rows, first=so_far is None),
        "add_pool",
        4 * feature * slots * rows_dev,
        4 * feature * slots + 4 * feature * rows_dev,
        grid=(rows_dev // rows,),
        in_specs=[recv_spec, recv_spec, req_spec, req_spec] + [rows_spec] * len(extra),
        out_specs=rows_spec,
        out_shape=jax.ShapeDtypeStruct((feature, rows_dev), F32),
        scratch_shapes=[packed, flat, flat],
    )(one, two, requests[0][None], requests[1][None], *extra)


def after(value, other):
    anywhere = pl.BlockSpec(memory_space=pl.ANY)
    return call(
        lambda value_ref, other_ref, out_ref: None,
        "after",
        0,
        0,
        in_specs=[anywhere, anywhere],
        out_specs=anywhere,
        out_shape=jax.ShapeDtypeStruct(value.shape, value.dtype),
        input_output_aliases={0: 0},
    )(value, other)


def exchange(value):
    return lax.all_to_all(value, ("shard", "grp"), split_axis=0, concat_axis=0, tiled=True)


def swap(value, bit):
    sharers = lax.axis_size("grp")
    return lax.ppermute(value, "grp", [(i, i ^ bit) for i in range(sharers)])


def share_out(value, wait=lambda block: block):
    sharers = lax.axis_size("grp")
    blocks = {0: value}
    bit = sharers // 2
    while bit:
        for k in list(blocks):
            blocks[k ^ bit] = swap(wait(blocks[k]) if k else blocks[k], bit)
        bit //= 2
    return [blocks[k] for k in range(sharers)]


def trade(blocks):
    sharers = len(blocks)
    terms = [[block] for block in blocks]
    bit = 1
    while bit < sharers:
        for k in range(0, sharers, 2 * bit):
            total = terms[k ^ bit][0].astype(F32)
            for term in terms[k ^ bit][1:]:
                total = total + term.astype(F32)
            terms[k].append(swap(total.astype(BF16), bit))
        bit *= 2
    return terms[0]


def pad_lanes(value, width, fill):
    return jnp.pad(value, ((0, 0), (0, width - value.shape[1])), constant_values=fill)


def body(entity_table, rel_diag, src_ids, dst_ids, rel_ids, neg_ids):
    rows_dev, feature = entity_table.shape
    sharers = lax.axis_size("grp")
    devices = lax.axis_size("shard") * sharers
    spans, neg_count = neg_ids.shape
    edge_count = src_ids.shape[0]
    block_len = edge_count // spans
    edge_cap = 4 * edge_count // devices
    chunks = round_up(edge_cap, LANES) // LANES
    part_width = neg_count // sharers
    neg_cap = round_up(2 * spans * part_width // devices, 16)
    width = round_up(block_len, 512)
    part = round_up(part_width, LANES)
    me = lax.axis_index("grp")

    table = entity_table.T.astype(BF16)
    own_ids = lax.dynamic_slice_in_dim(neg_ids, me * part_width, part_width, 1)
    rel_rows = pad_lanes(rel_ids.reshape(spans, block_len), width, -1)

    def ask(zero, chunks):
        message, *slots = make_slots(
            lax.axis_index(("shard", "grp")),
            src_ids + zero,
            dst_ids + zero,
            own_ids,
            rows_dev,
            devices,
            chunks,
            neg_cap,
            width,
            part,
        )
        asked = exchange(message)[:, 0]
        return asked, asked[:, -LANES:], slots, slots[-1]

    def chunked(zero):
        asked, neg_asked, slots, neg_slot = ask(zero, chunks)
        direct = [asked[:, c * LANES : (c + 1) * LANES] for c in range(chunks)]
        back = [exchange(gather(table, direct[0], neg_asked, neg_cap))]
        back += [exchange(gather(table, direct[c])) for c in range(1, chunks)]
        negatives = share_out(spread_neg(back[0], neg_slot, neg_cap, feature))
        rows = None
        for c in range(chunks):
            rows = spread(back[c], slots[c], rows, feature)
        src_grad, dst_grad, neg_grads = edges(rows, rel_rows, rel_diag, negatives)
        grad = None
        for c in range(1, chunks):
            sent = exchange(collect(src_grad, dst_grad, slots[c], devices))
            grad = add_rows(sent, direct[c], grad, feature, rows_dev)
        sent = collect(src_grad, dst_grad, slots[0], devices, neg_cap)
        sent = exchange(collect_neg(sent, neg_slot, trade(neg_grads), neg_cap))
        return add_rows(sent, direct[0], grad, feature, rows_dev, neg_asked, neg_cap)

    def pooled():
        asked, neg_asked, (slot, pool_slot, busy, _), neg_slot = ask(0, 0)
        listed = asked[:, LANES : LANES + RELAYS * POOL].reshape(devices, RELAYS, POOL)
        listed = listed.transpose(1, 0, 2).reshape(RELAYS, devices * POOL) - me * rows_dev
        listed = listed[me ^ jnp.arange(RELAYS, dtype=jnp.int32)]
        back = exchange(gather_quarters(table, asked, neg_cap))
        far = swap(gather_pool(table, listed[3], devices), 1)
        far = swap(gather_pool(table, listed[2], devices) + far, 2)
        near = swap(gather_pool(table, listed[1], devices), 1)
        near = gather_pool(table, listed[0], devices) + near
        rows = spread(back, slot, None, feature)
        negatives = share_out(
            spread_neg(back, neg_slot, neg_cap, feature), lambda block: after(block, rows)
        )
        src_grad, dst_grad, rest = edges(
            rows, rel_rows, rel_diag, negatives, exchange(near + far), pool_slot, busy
        )
        neg_grads, pool = rest[:-1], rest[-1]
        near = exchange(pool)
        far = swap(near, 2)
        sent = collect(src_grad, dst_grad, slot, devices, neg_cap)
        sent = exchange(collect_neg(sent, neg_slot, trade(neg_grads), neg_cap))
        grad = add_pool(near, swap(near, 1), listed[:2], None, feature, rows_dev)
        far = after(far, grad)
        grad = add_pool(far, swap(far, 1), listed[2:], grad, feature, rows_dev)
        return add_quarters(sent, asked, grad, neg_cap), jnp.max(neg_asked[:, -1])

    if chunks == 1 or sharers != RELAYS:
        return chunked(0).T
    return lax.while_loop(
        lambda state: state[1] > 0,
        lambda state: (chunked(jnp.minimum(state[1], 0)), -state[1]),
        pooled(),
    )[0].T


def solution(mesh):
    placed = (
        P(("shard", "grp"), None),
        P(),
        P(("shard", "grp")),
        P(("shard", "grp")),
        P(("shard", "grp")),
        P("shard", None),
    )
    return jax.shard_map(
        body, mesh=mesh, in_specs=placed, out_specs=P(("shard", "grp"), None), check_vma=False
    )
```

```python
import functools

import jax
import jax.numpy as jnp
from jax import lax
from jax.experimental import pallas as pl
from jax.experimental.pallas import tpu as pltpu
from jax.sharding import PartitionSpec as P

LANES = 128
POOL = 48
RELAYS = 4
SMALL = 80
PARTS = 4
SHARE = LANES // PARTS
VMEM_BYTES = 56 << 20
F32 = jnp.float32
BF16 = jnp.bfloat16
NN = (((1,), (0,)), ((), ()))
NT = (((1,), (1,)), ((), ()))
TN = (((0,), (0,)), ((), ()))


def round_up(value, unit):
    return -(-value // unit) * unit


def dot(left, right, dims):
    return lax.dot_general(left, right, dims, preferred_element_type=F32)


def one_hot(rows, row, base=0):
    places = lax.broadcasted_iota(jnp.int32, (rows, row.shape[1]), 0) + base
    return jnp.where(places == row, 1.0, 0.0).astype(BF16)


def call(kernel, name, flops, nbytes, **kwargs):
    return pl.pallas_call(
        kernel,
        name=name,
        compiler_params=pltpu.CompilerParams(vmem_limit_bytes=VMEM_BYTES),
        cost_estimate=pl.CostEstimate(flops=flops, bytes_accessed=nbytes, transcendentals=0),
        **kwargs,
    )


def ranks(members, mixer):
    groups = members[0].shape[0]
    both = dot(jnp.concatenate(members, axis=0).astype(BF16), mixer, NN)
    taken = jnp.zeros((groups, LANES), F32)
    found = []
    for i, member in enumerate(members):
        chunk = both[i * groups : (i + 1) * groups]
        found.append(jnp.sum((chunk[:, :LANES] + taken) * member, axis=0, keepdims=True))
        taken = taken + chunk[:, LANES:]
    return [rank.astype(jnp.int32) for rank in found], taken


def fill(members, codes, places, count):
    groups = members[0].shape[0]
    high = [m * (c // LANES).astype(F32) for m, c in zip(members, codes)]
    low = [m * (c % LANES).astype(F32) for m, c in zip(members, codes)]
    left = jnp.concatenate(
        [jnp.concatenate(high, axis=1), jnp.concatenate(low, axis=1)], axis=0
    ).astype(BF16)
    sums = dot(left, one_hot(count, jnp.concatenate(places, axis=1)), NT)
    return (LANES * sums[:groups] + sums[groups:]).astype(jnp.int32) - 1


def slots_kernel(
    me_ref, src_ref, dst_ref, own_ref, *refs, rows_dev, devices, chunks, neg_cap, spans, part
):
    pooled = chunks == 0
    msg_ref, neg_ref = refs[0], refs[-1]
    slot_refs = refs[1:-1]
    row = lax.broadcasted_iota(jnp.int32, (LANES, 2 * LANES), 0)
    lane = lax.broadcasted_iota(jnp.int32, (LANES, 2 * LANES), 1)
    mixer = jnp.where(row < lane, 1.0, 0.0).astype(BF16)
    owners = lax.broadcasted_iota(jnp.int32, (devices, LANES), 0)

    def prepare(rows, width):
        where, holder, codes, members = [], [], [], []
        for segment, ids_row in enumerate(rows):
            blank = jnp.full((1, width - ids_row.shape[1]), -1, jnp.int32)
            ids_row = jnp.concatenate([ids_row, blank], axis=1)
            for start in range(0, width, LANES):
                ids = ids_row[:, start : start + LANES]
                owner = jnp.where(ids >= 0, ids // rows_dev, -1)
                where.append((slice(segment, segment + 1), slice(start, start + LANES)))
                holder.append(owner)
                codes.append(jnp.where(ids >= 0, ids - owner * rows_dev + 1, 0))
                members.append(jnp.where(owners == owner, 1.0, 0.0))
        return where, holder, codes, members

    ends = []
    for ids_ref in (src_ref, dst_ref):
        ids = ids_ref[...].reshape(1, ids_ref.shape[0])
        length = ids.shape[1] // spans
        ends += [ids[:, b * length : (b + 1) * length] for b in range(spans)]
    where, holder, codes, members = prepare(ends, slot_refs[0].shape[1])
    flag = jnp.full((1, 1), -1, jnp.int32)
    if pooled:
        turn = me_ref[0, 0] % PARTS
        quarters = [jnp.maximum(code - 1, 0) // (rows_dev // PARTS) for code in codes]
        split = [
            jnp.concatenate([jnp.where(q == k, member, 0.0) for k in range(PARTS)], axis=0)
            for member, q in zip(members, quarters)
        ]
        found, _ = ranks(split, mixer)
        places = []
        for at, owner, rank, q in zip(where, holder, found, quarters):
            inside = (owner >= 0) & (rank < SHARE)
            place = (q ^ turn) * SHARE + rank
            slot_refs[0][at] = jnp.where(inside, owner * LANES + place, -1)
            places.append(jnp.where(inside, place, -1))
        msg_ref[:, 0, :LANES] = fill(members, codes, places, LANES)
        offset = LANES

        pool_ref, busy_ref = slot_refs[1:]
        shards = devices // RELAYS
        room = RELAYS * POOL
        shard_rows = lax.broadcasted_iota(jnp.int32, (shards, LANES), 0)
        spilled, spill_codes = [], []
        for owner, code, rank in zip(holder, codes, found):
            shard = jnp.where(rank >= SHARE, owner // RELAYS, -1)
            spilled.append(jnp.where(shard_rows == shard, 1.0, 0.0))
            spill_codes.append(code + (owner % RELAYS) * rows_dev)
        listed, taken = ranks(spilled, mixer)
        places = []
        for at, owner, rank, place in zip(where, holder, found, listed):
            inside = (owner >= 0) & (rank >= SHARE) & (place < room)
            compact = jnp.where(
                place < SMALL, owner // RELAYS * SMALL + place, (shards - 1) * SMALL + place
            )
            pool_ref[at] = jnp.where(inside, compact, -1)
            places.append(jnp.where(inside, place, -1))
        listed = fill(spilled, spill_codes, places, 2 * LANES)
        for shard in range(shards):
            msg_ref[shard * RELAYS : (shard + 1) * RELAYS, 0, offset : offset + 2 * LANES] = (
                jnp.broadcast_to(listed[shard : shard + 1], (RELAYS, 2 * LANES))
            )
        offset += 2 * LANES
        most = jnp.max(taken, axis=0, keepdims=True)
        busy = jnp.where(taken > SMALL, 1.0, 0.0)
        crowded = jnp.sum(busy, axis=0, keepdims=True) > 1.0
        flag = jnp.where((most > room) | crowded, 1, -1)[:, :1]
        place = jnp.sum(busy * shard_rows.astype(F32), axis=0, keepdims=True).astype(jnp.int32)
        busy_ref[...] = jnp.minimum(place, shards - 1)[:, :1]
    else:
        found, _ = ranks(members, mixer)
        for chunk in range(chunks):
            places = []
            for at, owner, rank in zip(where, holder, found):
                place = rank - chunk * LANES
                place = jnp.where((owner >= 0) & (place >= 0) & (place < LANES), place, -1)
                slot_refs[chunk][at] = jnp.where(place >= 0, owner * LANES + place, -1)
                places.append(place)
            listed = fill(members, codes, places, LANES)
            msg_ref[:, 0, chunk * LANES : (chunk + 1) * LANES] = listed
        offset = chunks * LANES

    where, holder, codes, members = prepare([own_ref[b : b + 1, :] for b in range(spans)], part)
    found, _ = ranks(members, mixer)
    for at, owner, rank in zip(where, holder, found):
        neg_ref[at] = jnp.where(owner >= 0, owner * neg_cap + rank, -1)
    places = [jnp.where(owner >= 0, rank, -1) for owner, rank in zip(holder, found)]
    listed = fill(members, codes, places, LANES)
    lanes = lax.broadcasted_iota(jnp.int32, listed.shape, 1)
    msg_ref[:, 0, offset:] = jnp.where(lanes == LANES - 1, flag, listed)


def make_slots(me, src_ids, dst_ids, own, rows_dev, devices, chunks, neg_cap, width, part):
    lanes = (chunks + 1 if chunks else 4) * LANES
    spans = own.shape[0]
    ends_shape = jax.ShapeDtypeStruct((2 * spans, width), jnp.int32)
    if chunks:
        slots = [ends_shape] * chunks
    else:
        slots = [ends_shape, ends_shape, jax.ShapeDtypeStruct((1, 1), jnp.int32)]
    return call(
        functools.partial(
            slots_kernel,
            rows_dev=rows_dev,
            devices=devices,
            chunks=chunks,
            neg_cap=neg_cap,
            spans=spans,
            part=part,
        ),
        "slots",
        32 * devices * LANES * spans * width,
        16 * spans * width,
        in_specs=[
            pl.BlockSpec(memory_space=pltpu.SMEM),
            pl.BlockSpec(src_ids.shape, lambda: (0,)),
            pl.BlockSpec(dst_ids.shape, lambda: (0,)),
            pl.BlockSpec(own.shape, lambda: (0, 0)),
        ],
        out_shape=[jax.ShapeDtypeStruct((devices, 1, lanes), jnp.int32)]
        + slots
        + [jax.ShapeDtypeStruct((spans, part), jnp.int32)],
    )(me.reshape(1, 1), src_ids, dst_ids, own)


def packed_height(count, feature):
    return feature // LANES * count + feature % LANES


def pack(out_ref, at, start, rows, tail):
    count, feature = rows.shape
    for piece in range(feature // LANES):
        out_ref[at, start + piece * count : start + (piece + 1) * count, :] = rows[
            :, piece * LANES : (piece + 1) * LANES
        ].astype(out_ref.dtype)
    tail = jnp.concatenate([tail, jnp.zeros((tail.shape[0], LANES - count), tail.dtype)], axis=1)
    end = start + packed_height(count, feature)
    out_ref[at, end - tail.shape[0] : end, :] = tail.astype(out_ref.dtype)


def pack_all(out_ref, start, count, rows, turned):
    feature = rows.shape[1]
    first = feature // LANES * LANES
    for i in range(out_ref.shape[0]):
        at = slice(i * count, (i + 1) * count)
        pack(out_ref, i, start, rows[at], turned[first:, at])


def unpack_all(in_ref, start, count, rows_ref, flat_ref):
    feature = flat_ref.shape[0]
    pieces = feature // LANES
    end = start + packed_height(count, feature)
    devices = in_ref.shape[0]
    for d in range(devices):
        for piece in range(pieces):
            rows_ref[d * count : (d + 1) * count, piece * LANES : (piece + 1) * LANES] = in_ref[
                d, start + piece * count : start + (piece + 1) * count, :
            ]
    tails = [
        in_ref[d, end - feature % LANES : end, :].astype(F32)[:, :count] for d in range(devices)
    ]
    flat_ref[: pieces * LANES] = rows_ref[...].astype(F32).T.astype(BF16)
    flat_ref[pieces * LANES :] = jnp.concatenate(tails, axis=1).astype(BF16)


def unpack_scratch(devices, count, feature):
    return [
        pltpu.VMEM((devices * count, feature // LANES * LANES), BF16),
        pltpu.VMEM((feature, devices * count), BF16),
    ]


def gather_kernel(table_ref, *refs, group, neg_cap):
    feature, rows_dev = table_ref.shape
    first = pl.program_id(0) * group
    req_ref, out_ref = refs[0], refs[-1]
    row = [req_ref[pl.ds(first + i, 1), :] for i in range(group)]
    if neg_cap:
        row += [refs[1][pl.ds(first + i, 1), :neg_cap] for i in range(group)]
    rows = dot(table_ref[...], one_hot(rows_dev, jnp.concatenate(row, axis=1)), NN)
    start = out_ref.shape[1] - feature
    for i in range(group):
        out_ref[i, start:] = rows[:, i * LANES : (i + 1) * LANES].astype(BF16)
    if neg_cap:
        neg = rows[:, group * LANES :]
        pack_all(out_ref, 0, neg_cap, neg.T, neg)


def gather(table, requests, neg_requests=None, neg_cap=0):
    feature, rows_dev = table.shape
    devices = requests.shape[0]
    group = 4
    height = feature + (packed_height(neg_cap, feature) if neg_cap else 0)
    slots = devices * (LANES + neg_cap)
    whole = pl.BlockSpec((devices, LANES), lambda i: (0, 0))
    return call(
        functools.partial(gather_kernel, group=group, neg_cap=neg_cap),
        "gather_rows",
        2 * feature * rows_dev * slots,
        2 * feature * (rows_dev + slots),
        grid=(devices // group,),
        in_specs=[pl.BlockSpec((feature, rows_dev), lambda i: (0, 0)), whole]
        + ([whole] if neg_cap else []),
        out_specs=pl.BlockSpec((group, height, LANES), lambda i: (i, 0, 0)),
        out_shape=jax.ShapeDtypeStruct((devices, height, LANES), BF16),
    )(table, requests, *([neg_requests] if neg_cap else []))


def quarter_ids(ids):
    group = lax.broadcasted_iota(jnp.int32, (1, LANES), 1) // SHARE
    rows = []
    for part in range(PARTS):
        pieces = []
        for first in range(0, len(ids), PARTS):
            piece = ids[first + part]
            for j in range(1, PARTS):
                piece = jnp.where(group == j, ids[first + (part ^ j)], piece)
            pieces.append(piece)
        rows.append(jnp.concatenate(pieces, axis=1))
    return rows


def gather_quarters_kernel(table_ref, asked_ref, out_ref, *, neg_cap):
    feature, rows_dev = table_ref.shape
    group = out_ref.shape[0]
    share = rows_dev // PARTS
    ids = [asked_ref[i : i + 1, :LANES] for i in range(group)]
    found = []
    for part, row in enumerate(quarter_ids(ids)):
        start = part * share
        found.append(dot(table_ref[:, start : start + share], one_hot(share, row, start), NN))
    start = out_ref.shape[1] - feature
    lanes = lax.broadcasted_iota(jnp.int32, (feature, LANES), 1) // SHARE
    for i in range(group):
        at = slice(i // PARTS * LANES, (i // PARTS + 1) * LANES)
        rows = found[i % PARTS][:, at]
        for j in range(1, PARTS):
            rows = jnp.where(lanes == j, found[j ^ (i % PARTS)][:, at], rows)
        out_ref[i, start:] = rows.astype(BF16)
    negs = slice(asked_ref.shape[1] - LANES, asked_ref.shape[1] - LANES + neg_cap)
    row = [asked_ref[i : i + 1, negs] for i in range(group)]
    neg = dot(table_ref[...], one_hot(rows_dev, jnp.concatenate(row, axis=1)), NN)
    pack_all(out_ref, 0, neg_cap, neg.T, neg)


def gather_quarters(table, asked, neg_cap):
    feature, rows_dev = table.shape
    devices = asked.shape[0]
    group = 16
    height = feature + packed_height(neg_cap, feature)
    return call(
        functools.partial(gather_quarters_kernel, neg_cap=neg_cap),
        "gather_quarters",
        feature * rows_dev * devices * (LANES // 2 + 2 * neg_cap),
        2 * feature * (rows_dev + devices * (LANES + neg_cap)),
        grid=(devices // group,),
        in_specs=[pl.BlockSpec((feature, rows_dev), lambda i: (0, 0)), pl.BlockSpec((group, asked.shape[1]), lambda i: (i, 0))],
        out_specs=pl.BlockSpec((group, height, LANES), lambda i: (i, 0, 0)),
        out_shape=jax.ShapeDtypeStruct((devices, height, LANES), BF16),
    )(table, asked)


def gather_pool_kernel(table_ref, req_ref, out_ref, *, group):
    rows_dev = table_ref.shape[1]
    row = req_ref[...].reshape(1, group * POOL)
    rows = dot(table_ref[...], one_hot(rows_dev, row), NN)
    pack_all(out_ref, 0, POOL, rows.T, rows)


def gather_pool(table, requests, devices):
    feature, rows_dev = table.shape
    group = 8
    steps = devices // group
    height = packed_height(POOL, feature)
    return call(
        functools.partial(gather_pool_kernel, group=group),
        "gather_pool",
        2 * feature * rows_dev * requests.size,
        2 * feature * (rows_dev + requests.size),
        grid=(steps,),
        in_specs=[
            pl.BlockSpec((feature, rows_dev), lambda i: (0, 0)),
            pl.BlockSpec((1, 1, group * POOL), lambda i: (i, 0, 0)),
        ],
        out_specs=pl.BlockSpec((group, height, LANES), lambda i: (i, 0, 0)),
        out_shape=jax.ShapeDtypeStruct((devices, height, LANES), BF16),
    )(table, requests.reshape(steps, 1, group * POOL))


def spread_neg_kernel(back_ref, slot_ref, out_ref, rows, flat, *, cap):
    unpack_all(back_ref, 0, cap, rows, flat)
    for part in range(slot_ref.shape[0]):
        hot = one_hot(flat.shape[1], slot_ref[part : part + 1, :])
        out_ref[part] = dot(flat[...], hot, NN).T.astype(BF16)


def spread_neg(back, slot, cap, feature):
    devices = back.shape[0]
    parts, width = slot.shape
    height = packed_height(cap, feature)
    return call(
        functools.partial(spread_neg_kernel, cap=cap),
        "spread_negatives",
        2 * devices * cap * feature * slot.size,
        2 * devices * cap * feature,
        grid=(1,),
        in_specs=[
            pl.BlockSpec((devices, height, LANES), lambda i: (0, 0, 0)),
            pl.BlockSpec(slot.shape, lambda i: (0, 0)),
        ],
        out_specs=pl.BlockSpec((parts, width, feature), lambda i: (0, 0, 0)),
        out_shape=jax.ShapeDtypeStruct((parts, width, feature), BF16),
        scratch_shapes=unpack_scratch(devices, cap, feature),
    )(back, slot)


def spread_kernel(*refs, first):
    back_ref, slot_ref = refs[:2]
    so_far_ref = None if first else refs[2]
    out_ref, flat = refs[2 + (not first)], refs[-1]
    devices = back_ref.shape[0]
    feature = flat.shape[0]

    @pl.when(pl.program_id(0) == 0)
    def _():
        start = back_ref.shape[1] - feature
        for d in range(devices):
            flat[:, d * LANES : (d + 1) * LANES] = back_ref[d, start:]

    row = slot_ref[...].reshape(1, slot_ref.shape[-1])
    rows = dot(flat[...], one_hot(flat.shape[1], row), NN)
    if not first:
        rows = rows + so_far_ref[...].astype(F32)
    out_ref[...] = rows.astype(BF16)


def spread(back, slot, so_far, feature):
    devices = back.shape[0]
    segments, width = slot.shape
    slots = devices * LANES
    tile = 512 if slots <= 4096 else 128
    steps = width // tile
    rows_spec = pl.BlockSpec((feature, tile), lambda i: (0, i))
    extra = [] if so_far is None else [so_far]
    return call(
        functools.partial(spread_kernel, first=so_far is None),
        "spread_rows",
        2 * feature * slots * slot.size,
        2 * feature * (slots + slot.size),
        grid=(segments * steps,),
        in_specs=[
            pl.BlockSpec(back.shape, lambda i: (0, 0, 0)),
            pl.BlockSpec((1, 1, tile), lambda i: (i // steps, 0, i % steps)),
        ]
        + [rows_spec] * len(extra),
        out_specs=rows_spec,
        out_shape=jax.ShapeDtypeStruct((feature, slot.size), BF16),
        scratch_shapes=[pltpu.VMEM((feature, slots), BF16)],
    )(back, slot.reshape(segments, 1, width), *extra)


def compact_places(shards):
    places = []
    for start, end, whose in ((0, SMALL, range(shards)), (SMALL, RELAYS * POOL, [None])):
        for shard in whose:
            place = start
            while place < end:
                relay, first = place // POOL, place % POOL
                count = min(POOL - first, end - place)
                to = (shards - 1 if shard is None else shard) * SMALL + place
                places.append((shard, relay, first, count, to))
                place += count
    return places


def compact_size(shards):
    return shards * SMALL + RELAYS * POOL - SMALL


def compact_pool(back_ref, busy, rows_ref, flat_ref):
    feature = flat_ref.shape[0]
    pieces = feature // LANES
    tails = []
    for shard, relay, first, count, to in compact_places(back_ref.shape[0] // RELAYS):
        at = (busy if shard is None else shard) * RELAYS + relay
        for piece in range(pieces):
            start = piece * POOL + first
            rows_ref[to : to + count, piece * LANES : (piece + 1) * LANES] = back_ref[
                at, start : start + count, :
            ]
        tail = back_ref[at, pieces * POOL :, :].astype(F32)
        tails.append(tail[:, first : first + count])
    flat_ref[: pieces * LANES] = rows_ref[...].astype(F32).T.astype(BF16)
    flat_ref[pieces * LANES :] = jnp.concatenate(tails, axis=1).astype(BF16)


def expand_pool(turned, busy, out_ref):
    feature = turned.shape[0]
    pieces = feature // LANES
    rows = turned.T
    out_ref[...] = jnp.zeros(out_ref.shape, out_ref.dtype)
    shards = out_ref.shape[0] // RELAYS
    for shard, relay, first, count, to in compact_places(shards):
        at = (busy if shard is None else shard) * RELAYS + relay
        for piece in range(pieces):
            start = piece * POOL + first
            out_ref[at, start : start + count, :] = rows[
                to : to + count, piece * LANES : (piece + 1) * LANES
            ].astype(BF16)
        if shard is not None:
            tail = turned[pieces * LANES :, to : to + count]
        else:
            tail = turned[pieces * LANES :, to : to + count]
            if first:
                kept = jnp.zeros((feature % LANES, first), F32)
                for other in range(shards):
                    start = other * SMALL + relay * POOL
                    part = turned[pieces * LANES :, start : start + first]
                    kept = jnp.where(busy == other, part, kept)
                tail = jnp.concatenate([kept, tail], axis=1)
        blank = jnp.zeros((tail.shape[0], LANES - tail.shape[1]), F32)
        out_ref[at, pieces * POOL :, :] = jnp.concatenate([tail, blank], axis=1).astype(BF16)


def edges_kernel(*refs, parts, pooled):
    refs = list(refs)
    src_ref, dst_ref, rel_ids_ref, rel_ref = refs[:4]
    neg_refs = refs[4 : 4 + parts]
    refs = refs[4 + parts :]
    if pooled:
        back_ref, src_slot_ref, dst_slot_ref, busy_ref = refs[:4]
        refs = refs[4:]
        pool_out_ref = refs.pop(2 + parts)
        pool_rows, pool_flat, pool_sums = refs[-3:]
    src_grad_ref, dst_grad_ref = refs[:2]
    neg_grad_refs = refs[2 : 2 + parts]
    negatives, rel_flat = refs[2 + parts : 4 + parts]
    block = pl.program_id(0)
    part = neg_refs[0].shape[1]

    @pl.when(block == 0)
    def _():
        table, pieces = rel_ref[...], []
        for _ in range(3):
            pieces.append(table.astype(BF16).astype(F32))
            table = table - pieces[-1]
        rel_flat[...] = jnp.concatenate(pieces, axis=0).T.astype(BF16)
        if pooled:
            compact_pool(back_ref, busy_ref[0, 0], pool_rows, pool_flat)
            pool_sums[...] = jnp.zeros(pool_sums.shape, F32)

    for k in range(parts):
        negatives[k * part : (k + 1) * part] = neg_refs[k][0]
    turned = negatives[...].astype(F32).T.astype(BF16)
    hot = one_hot(rel_ref.shape[0], rel_ids_ref[...].reshape(1, rel_ids_ref.shape[-1]))
    relation = dot(rel_flat[...], jnp.concatenate([hot] * 3, axis=0), NN)
    source = src_ref[...].astype(F32)
    target = dst_ref[...].astype(F32)
    if pooled:
        count = pool_flat.shape[1]
        src_hot = one_hot(count, src_slot_ref[...].reshape(1, src_slot_ref.shape[-1]))
        dst_hot = one_hot(count, dst_slot_ref[...].reshape(1, dst_slot_ref.shape[-1]))
        source = source + dot(pool_flat[...], src_hot, NN)
        target = target + dot(pool_flat[...], dst_hot, NN)
    product = source * relation
    positive = jnp.sum(product * target, axis=0, keepdims=True)
    pos_weight = -jax.nn.sigmoid(-positive)
    query = product.astype(BF16)
    weight = jax.nn.sigmoid(dot(negatives[...], query, NN)).astype(BF16)
    gathered = dot(turned, weight, NN)
    src_grad = (relation * (pos_weight * target + gathered)).astype(BF16)
    dst_grad = (pos_weight * product).astype(BF16)
    src_grad_ref[...] = src_grad
    dst_grad_ref[...] = dst_grad
    neg_grad = dot(query, weight, NT).T
    if pooled:
        pool_sums[...] += dot(src_grad, src_hot, NT) + dot(dst_grad, dst_hot, NT)

    for k in range(parts):
        neg_grad_refs[k][0] = neg_grad[k * part : (k + 1) * part].astype(BF16)
    if pooled:

        @pl.when(block == pl.num_programs(0) - 1)
        def _():
            expand_pool(pool_sums[...], busy_ref[0, 0], pool_out_ref)


def edges(rows, rel_ids, relations, negatives, pool=None, pool_slot=None, busy=None):
    feature, endpoints = rows.shape
    parts = len(negatives)
    spans, part, _ = negatives[0].shape
    width = rel_ids.shape[1]
    edge_spec = pl.BlockSpec((feature, width), lambda b: (0, b))
    neg_spec = pl.BlockSpec((1, part, feature), lambda b: (b, 0, 0))
    operands = [rows, rows, rel_ids.reshape(spans, 1, width), relations, *negatives]
    specs = [
        edge_spec,
        pl.BlockSpec((feature, width), lambda b: (0, spans + b)),
        pl.BlockSpec((1, 1, width), lambda b: (b, 0, 0)),
        pl.BlockSpec(relations.shape, lambda b: (0, 0)),
    ] + [neg_spec] * parts
    out_specs = [edge_spec, edge_spec] + [neg_spec] * parts
    out_shape = [jax.ShapeDtypeStruct((feature, endpoints // 2), BF16)] * 2
    out_shape += [jax.ShapeDtypeStruct((spans, part, feature), BF16)] * parts
    scratch = [
        pltpu.VMEM((parts * part, feature), BF16),
        pltpu.VMEM((feature, 3 * relations.shape[0]), BF16),
    ]
    if pool is not None:
        slot = pool_slot.reshape(2 * spans, 1, width)
        pool_spec = pl.BlockSpec(pool.shape, lambda b: (0, 0, 0))
        operands += [pool, slot, slot, busy]
        specs += [
            pool_spec,
            pl.BlockSpec((1, 1, width), lambda b: (b, 0, 0)),
            pl.BlockSpec((1, 1, width), lambda b: (spans + b, 0, 0)),
            pl.BlockSpec(memory_space=pltpu.SMEM),
        ]
        out_specs.append(pool_spec)
        out_shape.append(jax.ShapeDtypeStruct(pool.shape, BF16))
        count = compact_size(pool.shape[0] // RELAYS)
        scratch += [
            pltpu.VMEM((count, feature // LANES * LANES), BF16),
            pltpu.VMEM((feature, count), BF16),
            pltpu.VMEM((feature, count), F32),
        ]
    src_grad, dst_grad, *rest = call(
        functools.partial(edges_kernel, parts=parts, pooled=pool is not None),
        "edges",
        6 * feature * parts * part * spans * width,
        4 * (rows.size + parts * negatives[0].size),
        grid=(spans,),
        in_specs=specs,
        out_specs=out_specs,
        out_shape=out_shape,
        scratch_shapes=scratch,
    )(*operands)
    return src_grad, dst_grad, rest


def collect_kernel(src_ref, dst_ref, slot_ref, out_ref, *, group):
    segments, width = slot_ref.shape
    feature = src_ref.shape[0]
    step = pl.program_id(0)
    total = jnp.zeros((feature, group * LANES), F32)
    for segment in range(segments):
        grads = src_ref if segment < segments // 2 else dst_ref
        start = segment % (segments // 2) * width
        hot = one_hot(group * LANES, slot_ref[segment : segment + 1, :], step * group * LANES)
        total = total + dot(grads[:, start : start + width], hot, NT)
    total = total.astype(BF16)
    first = out_ref.shape[1] - feature
    for i in range(group):
        out_ref[i, first:] = total[:, i * LANES : (i + 1) * LANES]


def collect(src_grad, dst_grad, slot, devices, neg_cap=0):
    feature = src_grad.shape[0]
    group = 4
    slots = devices * LANES
    height = feature + (packed_height(neg_cap, feature) if neg_cap else 0)
    whole = pl.BlockSpec(src_grad.shape, lambda i: (0, 0))
    return call(
        functools.partial(collect_kernel, group=group),
        "collect_grads",
        2 * feature * slots * slot.size,
        2 * feature * (slots + slot.size),
        grid=(devices // group,),
        in_specs=[whole, whole, pl.BlockSpec(slot.shape, lambda i: (0, 0))],
        out_specs=pl.BlockSpec((group, height, LANES), lambda i: (i, 0, 0)),
        out_shape=jax.ShapeDtypeStruct((devices, height, LANES), BF16),
    )(src_grad, dst_grad, slot)


def collect_neg_kernel(sent_ref, slot_ref, *refs, group, cap):
    grad_refs, out_ref, sums = refs[:-2], refs[-2], refs[-1]
    step = pl.program_id(0)

    @pl.when(step == 0)
    def _():
        total = grad_refs[0][...].astype(F32)
        for grad_ref in grad_refs[1:]:
            total = total + grad_ref[...].astype(F32)
        sums[...] = total.astype(BF16)

    rows = jnp.zeros((group * cap, sums.shape[-1]), F32)
    for part in range(slot_ref.shape[0]):
        hot = one_hot(group * cap, slot_ref[part : part + 1, :], step * group * cap)
        rows = rows + dot(hot, sums[part], NN)
    pack_all(out_ref, 0, cap, rows, rows.T)


def collect_neg(sent, slot, grads, cap):
    devices = sent.shape[0]
    feature = grads[0].shape[-1]
    group = 16
    height = packed_height(cap, feature)
    return call(
        functools.partial(collect_neg_kernel, group=group, cap=cap),
        "collect_negatives",
        2 * devices * cap * feature * slot.size,
        4 * len(grads) * grads[0].size,
        grid=(devices // group,),
        in_specs=[
            pl.BlockSpec(memory_space=pl.ANY),
            pl.BlockSpec(slot.shape, lambda i: (0, 0)),
        ]
        + [pl.BlockSpec(grads[0].shape, lambda i: (0, 0, 0))] * len(grads),
        out_specs=pl.BlockSpec((group, height, LANES), lambda i: (i, 0, 0)),
        out_shape=jax.ShapeDtypeStruct(sent.shape, BF16),
        scratch_shapes=[pltpu.VMEM(grads[0].shape, BF16)],
        input_output_aliases={0: 0},
    )(sent, slot, *grads)


def add_kernel(*refs, rows, neg_cap, first):
    refs = list(refs)
    recv_ref, req_ref = refs[:2]
    refs = refs[2:]
    if neg_cap:
        neg_req_ref = refs.pop(0)
        neg_rows, neg_flat = refs[-2:]
    if not first:
        so_far_ref = refs.pop(0)
    out_ref, flat = refs[:2]
    devices = recv_ref.shape[0]
    feature = flat.shape[0]
    step = pl.program_id(0)

    @pl.when(step == 0)
    def _():
        start = recv_ref.shape[1] - feature
        for d in range(devices):
            flat[:, d * LANES : (d + 1) * LANES] = recv_ref[d, start:]
        if neg_cap:
            unpack_all(recv_ref, 0, neg_cap, neg_rows, neg_flat)

    base = step * rows
    row = jnp.concatenate([req_ref[d : d + 1, :] for d in range(devices)], axis=1)
    total = dot(flat[...], one_hot(rows, row, base), NT)
    if neg_cap:
        row = jnp.concatenate([neg_req_ref[d : d + 1, :neg_cap] for d in range(devices)], axis=1)
        total = total + dot(neg_flat[...], one_hot(rows, row, base), NT)
    if not first:
        total = total + so_far_ref[...]
    out_ref[...] = total


def add_rows(recv, requests, so_far, feature, rows_dev, neg_requests=None, neg_cap=0):
    devices = recv.shape[0]
    rows = 512 if devices * LANES <= 4096 else 128
    slots = devices * LANES
    whole_req = pl.BlockSpec((devices, LANES), lambda i: (0, 0))
    rows_spec = pl.BlockSpec((feature, rows), lambda i: (0, i))
    operands = [recv, requests]
    specs = [pl.BlockSpec(recv.shape, lambda i: (0, 0, 0)), whole_req]
    scratch = [pltpu.VMEM((feature, slots), BF16)]
    if neg_cap:
        operands.append(neg_requests)
        specs.append(whole_req)
        scratch += unpack_scratch(devices, neg_cap, feature)
    if so_far is not None:
        operands.append(so_far)
        specs.append(rows_spec)
    return call(
        functools.partial(add_kernel, rows=rows, neg_cap=neg_cap, first=so_far is None),
        "add_grads",
        2 * feature * slots * rows_dev,
        2 * feature * slots + 8 * feature * rows_dev,
        grid=(rows_dev // rows,),
        in_specs=specs,
        out_specs=rows_spec,
        out_shape=jax.ShapeDtypeStruct((feature, rows_dev), F32),
        scratch_shapes=scratch,
    )(*operands)


def add_quarters_kernel(
    recv_ref, asked_ref, so_far_ref, out_ref, flat, neg_rows, neg_flat, *, neg_cap
):
    devices = recv_ref.shape[0]
    feature, rows = out_ref.shape
    step = pl.program_id(0)

    @pl.when(step == 0)
    def _():
        start = recv_ref.shape[1] - feature
        lanes = lax.broadcasted_iota(jnp.int32, (feature, LANES), 1) // SHARE
        for first in range(0, devices, PARTS):
            to = first // PARTS * LANES
            blocks = [recv_ref[first + i, start:, :].astype(F32) for i in range(PARTS)]
            for part in range(PARTS):
                piece = blocks[part]
                for j in range(1, PARTS):
                    piece = jnp.where(lanes == j, blocks[part ^ j], piece)
                flat[part, :, to : to + LANES] = piece.astype(BF16)
        unpack_all(recv_ref, 0, neg_cap, neg_rows, neg_flat)

    base = step * rows
    asked = quarter_ids([asked_ref[d : d + 1, :LANES] for d in range(devices)])
    row = asked[0]
    for part in range(1, PARTS):
        row = jnp.where(step == part, asked[part], row)
    total = dot(flat[step], one_hot(rows, row, base), NT)
    negs = slice(asked_ref.shape[1] - LANES, asked_ref.shape[1] - LANES + neg_cap)
    row = jnp.concatenate([asked_ref[d : d + 1, negs] for d in range(devices)], axis=1)
    out_ref[...] = total + dot(neg_flat[...], one_hot(rows, row, base), NT) + so_far_ref[...]


def add_quarters(recv, asked, so_far, neg_cap):
    feature, rows_dev = so_far.shape
    devices = recv.shape[0]
    slots = devices * LANES
    whole_asked = pl.BlockSpec(asked.shape, lambda i: (0, 0))
    rows_spec = pl.BlockSpec((feature, rows_dev // PARTS), lambda i: (0, i))
    return call(
        functools.partial(add_quarters_kernel, neg_cap=neg_cap),
        "add_quarters",
        feature * (slots // 2 + 2 * devices * neg_cap) * rows_dev,
        2 * feature * slots + 8 * feature * rows_dev,
        grid=(PARTS,),
        in_specs=[pl.BlockSpec(recv.shape, lambda i: (0, 0, 0)), whole_asked, rows_spec],
        out_specs=rows_spec,
        out_shape=jax.ShapeDtypeStruct((feature, rows_dev), F32),
        scratch_shapes=[pltpu.VMEM((PARTS, feature, slots // PARTS), BF16)]
        + unpack_scratch(devices, neg_cap, feature),
    )(recv, asked, so_far)


def add_pool_kernel(*refs, rows, first):
    one_ref, two_ref, one_req_ref, two_req_ref = refs[:4]
    out_ref, packed, *flats = refs[4 + (not first) :]
    step = pl.program_id(0)

    @pl.when(step == 0)
    def _():
        for recv_ref, flat in zip((one_ref, two_ref), flats):
            unpack_all(recv_ref, 0, POOL, packed, flat)

    total = dot(flats[0][...], one_hot(rows, one_req_ref[...], step * rows), NT)
    total = total + dot(flats[1][...], one_hot(rows, two_req_ref[...], step * rows), NT)
    if not first:
        total = total + refs[4][...]
    out_ref[...] = total


def add_pool(one, two, requests, so_far, feature, rows_dev):
    rows = 512
    devices = one.shape[0]
    slots = devices * POOL
    recv_spec = pl.BlockSpec(one.shape, lambda i: (0, 0, 0))
    req_spec = pl.BlockSpec((1, slots), lambda i: (0, 0))
    rows_spec = pl.BlockSpec((feature, rows), lambda i: (0, i))
    packed, flat = unpack_scratch(devices, POOL, feature)
    extra = [] if so_far is None else [so_far]
    return call(
        functools.partial(add_pool_kernel, rows=rows, first=so_far is None),
        "add_pool",
        4 * feature * slots * rows_dev,
        4 * feature * slots + 4 * feature * rows_dev,
        grid=(rows_dev // rows,),
        in_specs=[recv_spec, recv_spec, req_spec, req_spec] + [rows_spec] * len(extra),
        out_specs=rows_spec,
        out_shape=jax.ShapeDtypeStruct((feature, rows_dev), F32),
        scratch_shapes=[packed, flat, flat],
    )(one, two, requests[0][None], requests[1][None], *extra)


def after(value, other):
    anywhere = pl.BlockSpec(memory_space=pl.ANY)
    return call(
        lambda value_ref, other_ref, out_ref: None,
        "after",
        0,
        0,
        in_specs=[anywhere, anywhere],
        out_specs=anywhere,
        out_shape=jax.ShapeDtypeStruct(value.shape, value.dtype),
        input_output_aliases={0: 0},
    )(value, other)


def exchange(value):
    return lax.all_to_all(value, ("shard", "grp"), split_axis=0, concat_axis=0, tiled=True)


def swap(value, bit):
    sharers = lax.axis_size("grp")
    return lax.ppermute(value, "grp", [(i, i ^ bit) for i in range(sharers)])


def share_out(value, wait=lambda block: block):
    sharers = lax.axis_size("grp")
    blocks = {0: value}
    bit = sharers // 2
    while bit:
        for k in list(blocks):
            blocks[k ^ bit] = swap(wait(blocks[k]) if k else blocks[k], bit)
        bit //= 2
    return [blocks[k] for k in range(sharers)]


def trade(blocks):
    sharers = len(blocks)
    terms = [[block] for block in blocks]
    bit = 1
    while bit < sharers:
        for k in range(0, sharers, 2 * bit):
            total = terms[k ^ bit][0].astype(F32)
            for term in terms[k ^ bit][1:]:
                total = total + term.astype(F32)
            terms[k].append(swap(total.astype(BF16), bit))
        bit *= 2
    return terms[0]


def pad_lanes(value, width, fill):
    return jnp.pad(value, ((0, 0), (0, width - value.shape[1])), constant_values=fill)


def body(entity_table, rel_diag, src_ids, dst_ids, rel_ids, neg_ids):
    rows_dev, feature = entity_table.shape
    sharers = lax.axis_size("grp")
    devices = lax.axis_size("shard") * sharers
    spans, neg_count = neg_ids.shape
    edge_count = src_ids.shape[0]
    block_len = edge_count // spans
    edge_cap = 4 * edge_count // devices
    chunks = round_up(edge_cap, LANES) // LANES
    part_width = neg_count // sharers
    neg_cap = round_up(2 * spans * part_width // devices, 16)
    width = round_up(block_len, 512)
    part = round_up(part_width, LANES)
    me = lax.axis_index("grp")

    table = entity_table.T.astype(BF16)
    own_ids = lax.dynamic_slice_in_dim(neg_ids, me * part_width, part_width, 1)
    rel_rows = pad_lanes(rel_ids.reshape(spans, block_len), width, -1)

    def ask(zero, chunks):
        message, *slots = make_slots(
            lax.axis_index(("shard", "grp")),
            src_ids + zero,
            dst_ids + zero,
            own_ids,
            rows_dev,
            devices,
            chunks,
            neg_cap,
            width,
            part,
        )
        asked = exchange(message)[:, 0]
        return asked, asked[:, -LANES:], slots, slots[-1]

    def chunked(zero):
        asked, neg_asked, slots, neg_slot = ask(zero, chunks)
        direct = [asked[:, c * LANES : (c + 1) * LANES] for c in range(chunks)]
        back = [exchange(gather(table, direct[0], neg_asked, neg_cap))]
        back += [exchange(gather(table, direct[c])) for c in range(1, chunks)]
        negatives = share_out(spread_neg(back[0], neg_slot, neg_cap, feature))
        rows = None
        for c in range(chunks):
            rows = spread(back[c], slots[c], rows, feature)
        src_grad, dst_grad, neg_grads = edges(rows, rel_rows, rel_diag, negatives)
        grad = None
        for c in range(1, chunks):
            sent = exchange(collect(src_grad, dst_grad, slots[c], devices))
            grad = add_rows(sent, direct[c], grad, feature, rows_dev)
        sent = collect(src_grad, dst_grad, slots[0], devices, neg_cap)
        sent = exchange(collect_neg(sent, neg_slot, trade(neg_grads), neg_cap))
        return add_rows(sent, direct[0], grad, feature, rows_dev, neg_asked, neg_cap)

    def pooled():
        asked, neg_asked, (slot, pool_slot, busy, _), neg_slot = ask(0, 0)
        listed = asked[:, LANES : LANES + RELAYS * POOL].reshape(devices, RELAYS, POOL)
        listed = listed.transpose(1, 0, 2).reshape(RELAYS, devices * POOL) - me * rows_dev
        listed = listed[me ^ jnp.arange(RELAYS, dtype=jnp.int32)]
        back = exchange(gather_quarters(table, asked, neg_cap))
        far = swap(gather_pool(table, listed[3], devices), 1)
        far = swap(gather_pool(table, listed[2], devices) + far, 2)
        near = swap(gather_pool(table, listed[1], devices), 1)
        near = gather_pool(table, listed[0], devices) + near
        rows = spread(back, slot, None, feature)
        negatives = share_out(
            spread_neg(back, neg_slot, neg_cap, feature), lambda block: after(block, rows)
        )
        src_grad, dst_grad, rest = edges(
            rows, rel_rows, rel_diag, negatives, exchange(near + far), pool_slot, busy
        )
        neg_grads, pool = rest[:-1], rest[-1]
        near = exchange(pool)
        far = swap(near, 2)
        sent = collect(src_grad, dst_grad, slot, devices, neg_cap)
        sent = exchange(collect_neg(sent, neg_slot, trade(neg_grads), neg_cap))
        grad = add_pool(near, swap(near, 1), listed[:2], None, feature, rows_dev)
        far = after(far, grad)
        grad = add_pool(far, swap(far, 1), listed[2:], grad, feature, rows_dev)
        return add_quarters(sent, asked, grad, neg_cap), jnp.max(neg_asked[:, -1])

    if chunks == 1 or sharers != RELAYS:
        return chunked(0).T
    return lax.while_loop(
        lambda state: state[1] > 0,
        lambda state: (chunked(jnp.minimum(state[1], 0)), -state[1]),
        pooled(),
    )[0].T


def solution(mesh):
    placed = (
        P(("shard", "grp"), None),
        P(),
        P(("shard", "grp")),
        P(("shard", "grp")),
        P(("shard", "grp")),
        P("shard", None),
    )
    return jax.shard_map(
        body, mesh=mesh, in_specs=placed, out_specs=P(("shard", "grp"), None), check_vma=False
    )
```

```python
import functools

import jax
import jax.numpy as jnp
from jax import lax
from jax.experimental import pallas as pl
from jax.experimental.pallas import tpu as pltpu
from jax.sharding import PartitionSpec as P

LANES = 128
POOL = 48
RELAYS = 4
SMALL = 80
PARTS = 4
SHARE = LANES // PARTS
VMEM_BYTES = 56 << 20
F32 = jnp.float32
BF16 = jnp.bfloat16
NN = (((1,), (0,)), ((), ()))
NT = (((1,), (1,)), ((), ()))
TN = (((0,), (0,)), ((), ()))


def round_up(value, unit):
    return -(-value // unit) * unit


def dot(left, right, dims):
    return lax.dot_general(left, right, dims, preferred_element_type=F32)


def one_hot(rows, row, base=0):
    places = lax.broadcasted_iota(jnp.int32, (rows, row.shape[1]), 0) + base
    return jnp.where(places == row, 1.0, 0.0).astype(BF16)


def call(kernel, name, flops, nbytes, **kwargs):
    return pl.pallas_call(
        kernel,
        name=name,
        compiler_params=pltpu.CompilerParams(vmem_limit_bytes=VMEM_BYTES),
        cost_estimate=pl.CostEstimate(flops=flops, bytes_accessed=nbytes, transcendentals=0),
        **kwargs,
    )


def ranks(members, mixer):
    groups = members[0].shape[0]
    both = dot(jnp.concatenate(members, axis=0).astype(BF16), mixer, NN)
    taken = jnp.zeros((groups, LANES), F32)
    found = []
    for i, member in enumerate(members):
        chunk = both[i * groups : (i + 1) * groups]
        found.append(jnp.sum((chunk[:, :LANES] + taken) * member, axis=0, keepdims=True))
        taken = taken + chunk[:, LANES:]
    return [rank.astype(jnp.int32) for rank in found], taken


def fill(members, codes, places, count):
    groups = members[0].shape[0]
    high = [m * (c // LANES).astype(F32) for m, c in zip(members, codes)]
    low = [m * (c % LANES).astype(F32) for m, c in zip(members, codes)]
    left = jnp.concatenate(
        [jnp.concatenate(high, axis=1), jnp.concatenate(low, axis=1)], axis=0
    ).astype(BF16)
    sums = dot(left, one_hot(count, jnp.concatenate(places, axis=1)), NT)
    return (LANES * sums[:groups] + sums[groups:]).astype(jnp.int32) - 1


def slots_kernel(
    me_ref, src_ref, dst_ref, own_ref, *refs, rows_dev, devices, chunks, neg_cap, spans, part
):
    pooled = chunks == 0
    msg_ref, neg_ref = refs[0], refs[-1]
    slot_refs = refs[1:-1]
    row = lax.broadcasted_iota(jnp.int32, (LANES, 2 * LANES), 0)
    lane = lax.broadcasted_iota(jnp.int32, (LANES, 2 * LANES), 1)
    mixer = jnp.where(row < lane, 1.0, 0.0).astype(BF16)
    owners = lax.broadcasted_iota(jnp.int32, (devices, LANES), 0)

    def prepare(rows, width):
        where, holder, codes, members = [], [], [], []
        for segment, ids_row in enumerate(rows):
            blank = jnp.full((1, width - ids_row.shape[1]), -1, jnp.int32)
            ids_row = jnp.concatenate([ids_row, blank], axis=1)
            for start in range(0, width, LANES):
                ids = ids_row[:, start : start + LANES]
                owner = jnp.where(ids >= 0, ids // rows_dev, -1)
                where.append((slice(segment, segment + 1), slice(start, start + LANES)))
                holder.append(owner)
                codes.append(jnp.where(ids >= 0, ids - owner * rows_dev + 1, 0))
                members.append(jnp.where(owners == owner, 1.0, 0.0))
        return where, holder, codes, members

    ends = []
    for ids_ref in (src_ref, dst_ref):
        ids = ids_ref[...].reshape(1, ids_ref.shape[0])
        length = ids.shape[1] // spans
        ends += [ids[:, b * length : (b + 1) * length] for b in range(spans)]
    where, holder, codes, members = prepare(ends, slot_refs[0].shape[1])
    flag = jnp.full((1, 1), -1, jnp.int32)
    if pooled:
        turn = me_ref[0, 0] % PARTS
        quarters = [jnp.maximum(code - 1, 0) // (rows_dev // PARTS) for code in codes]
        split = [
            jnp.concatenate([jnp.where(q == k, member, 0.0) for k in range(PARTS)], axis=0)
            for member, q in zip(members, quarters)
        ]
        found, _ = ranks(split, mixer)
        places = []
        for at, owner, rank, q in zip(where, holder, found, quarters):
            inside = (owner >= 0) & (rank < SHARE)
            place = (q ^ turn) * SHARE + rank
            slot_refs[0][at] = jnp.where(inside, owner * LANES + place, -1)
            places.append(jnp.where(inside, place, -1))
        msg_ref[:, 0, :LANES] = fill(members, codes, places, LANES)
        offset = LANES

        pool_ref, busy_ref = slot_refs[1:]
        shards = devices // RELAYS
        room = RELAYS * POOL
        shard_rows = lax.broadcasted_iota(jnp.int32, (shards, LANES), 0)
        spilled, spill_codes = [], []
        for owner, code, rank in zip(holder, codes, found):
            shard = jnp.where(rank >= SHARE, owner // RELAYS, -1)
            spilled.append(jnp.where(shard_rows == shard, 1.0, 0.0))
            spill_codes.append(code + (owner % RELAYS) * rows_dev)
        listed, taken = ranks(spilled, mixer)
        places = []
        for at, owner, rank, place in zip(where, holder, found, listed):
            inside = (owner >= 0) & (rank >= SHARE) & (place < room)
            compact = jnp.where(
                place < SMALL, owner // RELAYS * SMALL + place, (shards - 1) * SMALL + place
            )
            pool_ref[at] = jnp.where(inside, compact, -1)
            places.append(jnp.where(inside, place, -1))
        listed = fill(spilled, spill_codes, places, room)
        for shard in range(shards):
            msg_ref[shard * RELAYS : (shard + 1) * RELAYS, 0, offset : offset + room] = (
                jnp.broadcast_to(listed[shard : shard + 1], (RELAYS, room))
            )
        offset += 2 * LANES
        most = jnp.max(taken, axis=0, keepdims=True)
        busy = jnp.where(taken > SMALL, 1.0, 0.0)
        crowded = jnp.sum(busy, axis=0, keepdims=True) > 1.0
        flag = jnp.where((most > room) | crowded, 1, -1)[:, :1]
        place = jnp.sum(busy * shard_rows.astype(F32), axis=0, keepdims=True).astype(jnp.int32)
        busy_ref[...] = jnp.minimum(place, shards - 1)[:, :1]
    else:
        found, _ = ranks(members, mixer)
        for chunk in range(chunks):
            places = []
            for at, owner, rank in zip(where, holder, found):
                place = rank - chunk * LANES
                place = jnp.where((owner >= 0) & (place >= 0) & (place < LANES), place, -1)
                slot_refs[chunk][at] = jnp.where(place >= 0, owner * LANES + place, -1)
                places.append(place)
            listed = fill(members, codes, places, LANES)
            msg_ref[:, 0, chunk * LANES : (chunk + 1) * LANES] = listed
        offset = chunks * LANES

    where, holder, codes, members = prepare([own_ref[b : b + 1, :] for b in range(spans)], part)
    found, _ = ranks(members, mixer)
    for at, owner, rank in zip(where, holder, found):
        neg_ref[at] = jnp.where(owner >= 0, owner * neg_cap + rank, -1)
    places = [jnp.where(owner >= 0, rank, -1) for owner, rank in zip(holder, found)]
    listed = fill(members, codes, places, LANES)
    lanes = lax.broadcasted_iota(jnp.int32, listed.shape, 1)
    msg_ref[:, 0, offset:] = jnp.where(lanes == LANES - 1, flag, listed)


def make_slots(me, src_ids, dst_ids, own, rows_dev, devices, chunks, neg_cap, width, part):
    lanes = (chunks + 1 if chunks else 4) * LANES
    spans = own.shape[0]
    ends_shape = jax.ShapeDtypeStruct((2 * spans, width), jnp.int32)
    if chunks:
        slots = [ends_shape] * chunks
    else:
        slots = [ends_shape, ends_shape, jax.ShapeDtypeStruct((1, 1), jnp.int32)]
    return call(
        functools.partial(
            slots_kernel,
            rows_dev=rows_dev,
            devices=devices,
            chunks=chunks,
            neg_cap=neg_cap,
            spans=spans,
            part=part,
        ),
        "slots",
        32 * devices * LANES * spans * width,
        16 * spans * width,
        in_specs=[
            pl.BlockSpec(memory_space=pltpu.SMEM),
            pl.BlockSpec(src_ids.shape, lambda: (0,)),
            pl.BlockSpec(dst_ids.shape, lambda: (0,)),
            pl.BlockSpec(own.shape, lambda: (0, 0)),
        ],
        out_shape=[jax.ShapeDtypeStruct((devices, 1, lanes), jnp.int32)]
        + slots
        + [jax.ShapeDtypeStruct((spans, part), jnp.int32)],
    )(me.reshape(1, 1), src_ids, dst_ids, own)


def packed_height(count, feature):
    return feature // LANES * count + feature % LANES


def pack(out_ref, at, start, rows, tail):
    count, feature = rows.shape
    for piece in range(feature // LANES):
        out_ref[at, start + piece * count : start + (piece + 1) * count, :] = rows[
            :, piece * LANES : (piece + 1) * LANES
        ].astype(out_ref.dtype)
    tail = jnp.concatenate([tail, jnp.zeros((tail.shape[0], LANES - count), tail.dtype)], axis=1)
    end = start + packed_height(count, feature)
    out_ref[at, end - tail.shape[0] : end, :] = tail.astype(out_ref.dtype)


def pack_all(out_ref, start, count, rows, turned):
    feature = rows.shape[1]
    first = feature // LANES * LANES
    for i in range(out_ref.shape[0]):
        at = slice(i * count, (i + 1) * count)
        pack(out_ref, i, start, rows[at], turned[first:, at])


def unpack_all(in_ref, start, count, rows_ref, flat_ref):
    feature = flat_ref.shape[0]
    pieces = feature // LANES
    end = start + packed_height(count, feature)
    devices = in_ref.shape[0]
    for d in range(devices):
        for piece in range(pieces):
            rows_ref[d * count : (d + 1) * count, piece * LANES : (piece + 1) * LANES] = in_ref[
                d, start + piece * count : start + (piece + 1) * count, :
            ]
    tails = [
        in_ref[d, end - feature % LANES : end, :].astype(F32)[:, :count] for d in range(devices)
    ]
    flat_ref[: pieces * LANES] = rows_ref[...].astype(F32).T.astype(BF16)
    flat_ref[pieces * LANES :] = jnp.concatenate(tails, axis=1).astype(BF16)


def unpack_scratch(devices, count, feature):
    return [
        pltpu.VMEM((devices * count, feature // LANES * LANES), BF16),
        pltpu.VMEM((feature, devices * count), BF16),
    ]


def gather_kernel(table_ref, *refs, group, neg_cap):
    feature, rows_dev = table_ref.shape
    first = pl.program_id(0) * group
    req_ref, out_ref = refs[0], refs[-1]
    row = [req_ref[pl.ds(first + i, 1), :] for i in range(group)]
    if neg_cap:
        row += [refs[1][pl.ds(first + i, 1), :neg_cap] for i in range(group)]
    rows = dot(table_ref[...], one_hot(rows_dev, jnp.concatenate(row, axis=1)), NN)
    start = out_ref.shape[1] - feature
    for i in range(group):
        out_ref[i, start:] = rows[:, i * LANES : (i + 1) * LANES].astype(BF16)
    if neg_cap:
        neg = rows[:, group * LANES :]
        pack_all(out_ref, 0, neg_cap, neg.T, neg)


def gather(table, requests, neg_requests=None, neg_cap=0):
    feature, rows_dev = table.shape
    devices = requests.shape[0]
    group = 4
    height = feature + (packed_height(neg_cap, feature) if neg_cap else 0)
    slots = devices * (LANES + neg_cap)
    whole = pl.BlockSpec((devices, LANES), lambda i: (0, 0))
    return call(
        functools.partial(gather_kernel, group=group, neg_cap=neg_cap),
        "gather_rows",
        2 * feature * rows_dev * slots,
        2 * feature * (rows_dev + slots),
        grid=(devices // group,),
        in_specs=[pl.BlockSpec((feature, rows_dev), lambda i: (0, 0)), whole]
        + ([whole] if neg_cap else []),
        out_specs=pl.BlockSpec((group, height, LANES), lambda i: (i, 0, 0)),
        out_shape=jax.ShapeDtypeStruct((devices, height, LANES), BF16),
    )(table, requests, *([neg_requests] if neg_cap else []))


def quarter_ids(ids):
    group = lax.broadcasted_iota(jnp.int32, (1, LANES), 1) // SHARE
    rows = []
    for part in range(PARTS):
        pieces = []
        for first in range(0, len(ids), PARTS):
            piece = ids[first + part]
            for j in range(1, PARTS):
                piece = jnp.where(group == j, ids[first + (part ^ j)], piece)
            pieces.append(piece)
        rows.append(jnp.concatenate(pieces, axis=1))
    return rows


def gather_quarters_kernel(table_ref, asked_ref, out_ref, *, neg_cap):
    feature, rows_dev = table_ref.shape
    group = out_ref.shape[0]
    share = rows_dev // PARTS
    ids = [asked_ref[i : i + 1, :LANES] for i in range(group)]
    found = []
    for part, row in enumerate(quarter_ids(ids)):
        start = part * share
        found.append(dot(table_ref[:, start : start + share], one_hot(share, row, start), NN))
    start = out_ref.shape[1] - feature
    lanes = lax.broadcasted_iota(jnp.int32, (feature, LANES), 1) // SHARE
    for i in range(group):
        at = slice(i // PARTS * LANES, (i // PARTS + 1) * LANES)
        rows = found[i % PARTS][:, at]
        for j in range(1, PARTS):
            rows = jnp.where(lanes == j, found[j ^ (i % PARTS)][:, at], rows)
        out_ref[i, start:] = rows.astype(BF16)
    negs = slice(asked_ref.shape[1] - LANES, asked_ref.shape[1] - LANES + neg_cap)
    row = [asked_ref[i : i + 1, negs] for i in range(group)]
    neg = dot(table_ref[...], one_hot(rows_dev, jnp.concatenate(row, axis=1)), NN)
    pack_all(out_ref, 0, neg_cap, neg.T, neg)


def gather_quarters(table, asked, neg_cap):
    feature, rows_dev = table.shape
    devices = asked.shape[0]
    group = 16
    height = feature + packed_height(neg_cap, feature)
    return call(
        functools.partial(gather_quarters_kernel, neg_cap=neg_cap),
        "gather_quarters",
        feature * rows_dev * devices * (LANES // 2 + 2 * neg_cap),
        2 * feature * (rows_dev + devices * (LANES + neg_cap)),
        grid=(devices // group,),
        in_specs=[pl.BlockSpec((feature, rows_dev), lambda i: (0, 0)), pl.BlockSpec((group, asked.shape[1]), lambda i: (i, 0))],
        out_specs=pl.BlockSpec((group, height, LANES), lambda i: (i, 0, 0)),
        out_shape=jax.ShapeDtypeStruct((devices, height, LANES), BF16),
    )(table, asked)


def gather_pool_kernel(table_ref, req_ref, out_ref, *, group):
    rows_dev = table_ref.shape[1]
    row = req_ref[...].reshape(1, group * POOL)
    rows = dot(table_ref[...], one_hot(rows_dev, row), NN)
    pack_all(out_ref, 0, POOL, rows.T, rows)


def gather_pool(table, requests, devices):
    feature, rows_dev = table.shape
    group = 8
    steps = devices // group
    height = packed_height(POOL, feature)
    return call(
        functools.partial(gather_pool_kernel, group=group),
        "gather_pool",
        2 * feature * rows_dev * requests.size,
        2 * feature * (rows_dev + requests.size),
        grid=(steps,),
        in_specs=[
            pl.BlockSpec((feature, rows_dev), lambda i: (0, 0)),
            pl.BlockSpec((1, 1, group * POOL), lambda i: (i, 0, 0)),
        ],
        out_specs=pl.BlockSpec((group, height, LANES), lambda i: (i, 0, 0)),
        out_shape=jax.ShapeDtypeStruct((devices, height, LANES), BF16),
    )(table, requests.reshape(steps, 1, group * POOL))


def spread_neg_kernel(back_ref, slot_ref, out_ref, rows, flat, *, cap):
    unpack_all(back_ref, 0, cap, rows, flat)
    for part in range(slot_ref.shape[0]):
        hot = one_hot(flat.shape[1], slot_ref[part : part + 1, :])
        out_ref[part] = dot(flat[...], hot, NN).T.astype(BF16)


def spread_neg(back, slot, cap, feature):
    devices = back.shape[0]
    parts, width = slot.shape
    height = packed_height(cap, feature)
    return call(
        functools.partial(spread_neg_kernel, cap=cap),
        "spread_negatives",
        2 * devices * cap * feature * slot.size,
        2 * devices * cap * feature,
        grid=(1,),
        in_specs=[
            pl.BlockSpec((devices, height, LANES), lambda i: (0, 0, 0)),
            pl.BlockSpec(slot.shape, lambda i: (0, 0)),
        ],
        out_specs=pl.BlockSpec((parts, width, feature), lambda i: (0, 0, 0)),
        out_shape=jax.ShapeDtypeStruct((parts, width, feature), BF16),
        scratch_shapes=unpack_scratch(devices, cap, feature),
    )(back, slot)


def spread_kernel(*refs, first):
    back_ref, slot_ref = refs[:2]
    so_far_ref = None if first else refs[2]
    out_ref, flat = refs[2 + (not first)], refs[-1]
    devices = back_ref.shape[0]
    feature = flat.shape[0]

    @pl.when(pl.program_id(0) == 0)
    def _():
        start = back_ref.shape[1] - feature
        for d in range(devices):
            flat[:, d * LANES : (d + 1) * LANES] = back_ref[d, start:]

    row = slot_ref[...].reshape(1, slot_ref.shape[-1])
    rows = dot(flat[...], one_hot(flat.shape[1], row), NN)
    if not first:
        rows = rows + so_far_ref[...].astype(F32)
    out_ref[...] = rows.astype(BF16)


def spread(back, slot, so_far, feature):
    devices = back.shape[0]
    segments, width = slot.shape
    slots = devices * LANES
    tile = 512 if slots <= 4096 else 128
    steps = width // tile
    rows_spec = pl.BlockSpec((feature, tile), lambda i: (0, i))
    extra = [] if so_far is None else [so_far]
    return call(
        functools.partial(spread_kernel, first=so_far is None),
        "spread_rows",
        2 * feature * slots * slot.size,
        2 * feature * (slots + slot.size),
        grid=(segments * steps,),
        in_specs=[
            pl.BlockSpec(back.shape, lambda i: (0, 0, 0)),
            pl.BlockSpec((1, 1, tile), lambda i: (i // steps, 0, i % steps)),
        ]
        + [rows_spec] * len(extra),
        out_specs=rows_spec,
        out_shape=jax.ShapeDtypeStruct((feature, slot.size), BF16),
        scratch_shapes=[pltpu.VMEM((feature, slots), BF16)],
    )(back, slot.reshape(segments, 1, width), *extra)


def compact_places(shards):
    places = []
    for start, end, whose in ((0, SMALL, range(shards)), (SMALL, RELAYS * POOL, [None])):
        for shard in whose:
            place = start
            while place < end:
                relay, first = place // POOL, place % POOL
                count = min(POOL - first, end - place)
                to = (shards - 1 if shard is None else shard) * SMALL + place
                places.append((shard, relay, first, count, to))
                place += count
    return places


def compact_size(shards):
    return shards * SMALL + RELAYS * POOL - SMALL


def compact_pool(back_ref, busy, rows_ref, flat_ref):
    feature = flat_ref.shape[0]
    pieces = feature // LANES
    tails = []
    for shard, relay, first, count, to in compact_places(back_ref.shape[0] // RELAYS):
        at = (busy if shard is None else shard) * RELAYS + relay
        for piece in range(pieces):
            start = piece * POOL + first
            rows_ref[to : to + count, piece * LANES : (piece + 1) * LANES] = back_ref[
                at, start : start + count, :
            ]
        tail = back_ref[at, pieces * POOL :, :].astype(F32)
        tails.append(tail[:, first : first + count])
    flat_ref[: pieces * LANES] = rows_ref[...].astype(F32).T.astype(BF16)
    flat_ref[pieces * LANES :] = jnp.concatenate(tails, axis=1).astype(BF16)


def expand_pool(turned, busy, out_ref):
    feature = turned.shape[0]
    pieces = feature // LANES
    rows = turned.T
    out_ref[...] = jnp.zeros(out_ref.shape, out_ref.dtype)
    shards = out_ref.shape[0] // RELAYS
    for shard, relay, first, count, to in compact_places(shards):
        at = (busy if shard is None else shard) * RELAYS + relay
        for piece in range(pieces):
            start = piece * POOL + first
            out_ref[at, start : start + count, :] = rows[
                to : to + count, piece * LANES : (piece + 1) * LANES
            ].astype(BF16)
        if shard is not None:
            tail = turned[pieces * LANES :, to : to + count]
        else:
            tail = turned[pieces * LANES :, to : to + count]
            if first:
                kept = jnp.zeros((feature % LANES, first), F32)
                for other in range(shards):
                    start = other * SMALL + relay * POOL
                    part = turned[pieces * LANES :, start : start + first]
                    kept = jnp.where(busy == other, part, kept)
                tail = jnp.concatenate([kept, tail], axis=1)
        blank = jnp.zeros((tail.shape[0], LANES - tail.shape[1]), F32)
        out_ref[at, pieces * POOL :, :] = jnp.concatenate([tail, blank], axis=1).astype(BF16)


def edges_kernel(*refs, parts, pooled):
    refs = list(refs)
    src_ref, dst_ref, rel_ids_ref, rel_ref = refs[:4]
    neg_refs = refs[4 : 4 + parts]
    refs = refs[4 + parts :]
    if pooled:
        back_ref, src_slot_ref, dst_slot_ref, busy_ref = refs[:4]
        refs = refs[4:]
        pool_out_ref = refs.pop(2 + parts)
        pool_rows, pool_flat, pool_sums = refs[-3:]
    src_grad_ref, dst_grad_ref = refs[:2]
    neg_grad_refs = refs[2 : 2 + parts]
    negatives, rel_flat = refs[2 + parts : 4 + parts]
    block = pl.program_id(0)
    part = neg_refs[0].shape[1]

    @pl.when(block == 0)
    def _():
        table, pieces = rel_ref[...], []
        for _ in range(3):
            pieces.append(table.astype(BF16).astype(F32))
            table = table - pieces[-1]
        rel_flat[...] = jnp.concatenate(pieces, axis=0).T.astype(BF16)
        if pooled:
            compact_pool(back_ref, busy_ref[0, 0], pool_rows, pool_flat)
            pool_sums[...] = jnp.zeros(pool_sums.shape, F32)

    for k in range(parts):
        negatives[k * part : (k + 1) * part] = neg_refs[k][0]
    turned = negatives[...].astype(F32).T.astype(BF16)
    hot = one_hot(rel_ref.shape[0], rel_ids_ref[...].reshape(1, rel_ids_ref.shape[-1]))
    relation = dot(rel_flat[...], jnp.concatenate([hot] * 3, axis=0), NN)
    source = src_ref[...].astype(F32)
    target = dst_ref[...].astype(F32)
    if pooled:
        count = pool_flat.shape[1]
        src_hot = one_hot(count, src_slot_ref[...].reshape(1, src_slot_ref.shape[-1]))
        dst_hot = one_hot(count, dst_slot_ref[...].reshape(1, dst_slot_ref.shape[-1]))
        hots = jnp.concatenate([src_hot, dst_hot], axis=1)
        pool = dot(pool_flat[...], hots, NN)
        source = source + pool[:, : source.shape[1]]
        target = target + pool[:, source.shape[1] :]
    product = source * relation
    positive = jnp.sum(product * target, axis=0, keepdims=True)
    pos_weight = -jax.nn.sigmoid(-positive)
    query = product.astype(BF16)
    weight = jax.nn.sigmoid(dot(negatives[...], query, NN)).astype(BF16)
    gathered = dot(turned, weight, NN)
    src_grad = (relation * (pos_weight * target + gathered)).astype(BF16)
    dst_grad = (pos_weight * product).astype(BF16)
    src_grad_ref[...] = src_grad
    dst_grad_ref[...] = dst_grad
    neg_grad = dot(query, weight, NT).T
    if pooled:
        pool_sums[...] += dot(jnp.concatenate([src_grad, dst_grad], axis=1), hots, NT)

    for k in range(parts):
        neg_grad_refs[k][0] = neg_grad[k * part : (k + 1) * part].astype(BF16)
    if pooled:

        @pl.when(block == pl.num_programs(0) - 1)
        def _():
            expand_pool(pool_sums[...], busy_ref[0, 0], pool_out_ref)


def edges(rows, rel_ids, relations, negatives, pool=None, pool_slot=None, busy=None):
    feature, endpoints = rows.shape
    parts = len(negatives)
    spans, part, _ = negatives[0].shape
    width = rel_ids.shape[1]
    edge_spec = pl.BlockSpec((feature, width), lambda b: (0, b))
    neg_spec = pl.BlockSpec((1, part, feature), lambda b: (b, 0, 0))
    operands = [rows, rows, rel_ids.reshape(spans, 1, width), relations, *negatives]
    specs = [
        edge_spec,
        pl.BlockSpec((feature, width), lambda b: (0, spans + b)),
        pl.BlockSpec((1, 1, width), lambda b: (b, 0, 0)),
        pl.BlockSpec(relations.shape, lambda b: (0, 0)),
    ] + [neg_spec] * parts
    out_specs = [edge_spec, edge_spec] + [neg_spec] * parts
    out_shape = [jax.ShapeDtypeStruct((feature, endpoints // 2), BF16)] * 2
    out_shape += [jax.ShapeDtypeStruct((spans, part, feature), BF16)] * parts
    scratch = [
        pltpu.VMEM((parts * part, feature), BF16),
        pltpu.VMEM((feature, 3 * relations.shape[0]), BF16),
    ]
    if pool is not None:
        slot = pool_slot.reshape(2 * spans, 1, width)
        pool_spec = pl.BlockSpec(pool.shape, lambda b: (0, 0, 0))
        operands += [pool, slot, slot, busy]
        specs += [
            pool_spec,
            pl.BlockSpec((1, 1, width), lambda b: (b, 0, 0)),
            pl.BlockSpec((1, 1, width), lambda b: (spans + b, 0, 0)),
            pl.BlockSpec(memory_space=pltpu.SMEM),
        ]
        out_specs.append(pool_spec)
        out_shape.append(jax.ShapeDtypeStruct(pool.shape, BF16))
        count = compact_size(pool.shape[0] // RELAYS)
        scratch += [
            pltpu.VMEM((count, feature // LANES * LANES), BF16),
            pltpu.VMEM((feature, count), BF16),
            pltpu.VMEM((feature, count), F32),
        ]
    src_grad, dst_grad, *rest = call(
        functools.partial(edges_kernel, parts=parts, pooled=pool is not None),
        "edges",
        6 * feature * parts * part * spans * width,
        4 * (rows.size + parts * negatives[0].size),
        grid=(spans,),
        in_specs=specs,
        out_specs=out_specs,
        out_shape=out_shape,
        scratch_shapes=scratch,
    )(*operands)
    return src_grad, dst_grad, rest


def collect_kernel(src_ref, dst_ref, slot_ref, out_ref, *, group):
    segments, width = slot_ref.shape
    feature = src_ref.shape[0]
    step = pl.program_id(0)
    total = jnp.zeros((feature, group * LANES), F32)
    for segment in range(segments):
        grads = src_ref if segment < segments // 2 else dst_ref
        start = segment % (segments // 2) * width
        hot = one_hot(group * LANES, slot_ref[segment : segment + 1, :], step * group * LANES)
        total = total + dot(grads[:, start : start + width], hot, NT)
    total = total.astype(BF16)
    first = out_ref.shape[1] - feature
    for i in range(group):
        out_ref[i, first:] = total[:, i * LANES : (i + 1) * LANES]


def collect(src_grad, dst_grad, slot, devices, neg_cap=0):
    feature = src_grad.shape[0]
    group = 4
    slots = devices * LANES
    height = feature + (packed_height(neg_cap, feature) if neg_cap else 0)
    whole = pl.BlockSpec(src_grad.shape, lambda i: (0, 0))
    return call(
        functools.partial(collect_kernel, group=group),
        "collect_grads",
        2 * feature * slots * slot.size,
        2 * feature * (slots + slot.size),
        grid=(devices // group,),
        in_specs=[whole, whole, pl.BlockSpec(slot.shape, lambda i: (0, 0))],
        out_specs=pl.BlockSpec((group, height, LANES), lambda i: (i, 0, 0)),
        out_shape=jax.ShapeDtypeStruct((devices, height, LANES), BF16),
    )(src_grad, dst_grad, slot)


def collect_neg_kernel(sent_ref, slot_ref, *refs, group, cap):
    grad_refs, out_ref, sums = refs[:-2], refs[-2], refs[-1]
    step = pl.program_id(0)

    @pl.when(step == 0)
    def _():
        total = grad_refs[0][...].astype(F32)
        for grad_ref in grad_refs[1:]:
            total = total + grad_ref[...].astype(F32)
        sums[...] = total.astype(BF16)

    rows = jnp.zeros((group * cap, sums.shape[-1]), F32)
    for part in range(slot_ref.shape[0]):
        hot = one_hot(group * cap, slot_ref[part : part + 1, :], step * group * cap)
        rows = rows + dot(hot, sums[part], NN)
    pack_all(out_ref, 0, cap, rows, rows.T)


def collect_neg(sent, slot, grads, cap):
    devices = sent.shape[0]
    feature = grads[0].shape[-1]
    group = 16
    height = packed_height(cap, feature)
    return call(
        functools.partial(collect_neg_kernel, group=group, cap=cap),
        "collect_negatives",
        2 * devices * cap * feature * slot.size,
        4 * len(grads) * grads[0].size,
        grid=(devices // group,),
        in_specs=[
            pl.BlockSpec(memory_space=pl.ANY),
            pl.BlockSpec(slot.shape, lambda i: (0, 0)),
        ]
        + [pl.BlockSpec(grads[0].shape, lambda i: (0, 0, 0))] * len(grads),
        out_specs=pl.BlockSpec((group, height, LANES), lambda i: (i, 0, 0)),
        out_shape=jax.ShapeDtypeStruct(sent.shape, BF16),
        scratch_shapes=[pltpu.VMEM(grads[0].shape, BF16)],
        input_output_aliases={0: 0},
    )(sent, slot, *grads)


def add_kernel(*refs, rows, neg_cap, first):
    refs = list(refs)
    recv_ref, req_ref = refs[:2]
    refs = refs[2:]
    if neg_cap:
        neg_req_ref = refs.pop(0)
        neg_rows, neg_flat = refs[-2:]
    if not first:
        so_far_ref = refs.pop(0)
    out_ref, flat = refs[:2]
    devices = recv_ref.shape[0]
    feature = flat.shape[0]
    step = pl.program_id(0)

    @pl.when(step == 0)
    def _():
        start = recv_ref.shape[1] - feature
        for d in range(devices):
            flat[:, d * LANES : (d + 1) * LANES] = recv_ref[d, start:]
        if neg_cap:
            unpack_all(recv_ref, 0, neg_cap, neg_rows, neg_flat)

    base = step * rows
    row = jnp.concatenate([req_ref[d : d + 1, :] for d in range(devices)], axis=1)
    total = dot(flat[...], one_hot(rows, row, base), NT)
    if neg_cap:
        row = jnp.concatenate([neg_req_ref[d : d + 1, :neg_cap] for d in range(devices)], axis=1)
        total = total + dot(neg_flat[...], one_hot(rows, row, base), NT)
    if not first:
        total = total + so_far_ref[...]
    out_ref[...] = total


def add_rows(recv, requests, so_far, feature, rows_dev, neg_requests=None, neg_cap=0):
    devices = recv.shape[0]
    rows = 512 if devices * LANES <= 4096 else 128
    slots = devices * LANES
    whole_req = pl.BlockSpec((devices, LANES), lambda i: (0, 0))
    rows_spec = pl.BlockSpec((feature, rows), lambda i: (0, i))
    operands = [recv, requests]
    specs = [pl.BlockSpec(recv.shape, lambda i: (0, 0, 0)), whole_req]
    scratch = [pltpu.VMEM((feature, slots), BF16)]
    if neg_cap:
        operands.append(neg_requests)
        specs.append(whole_req)
        scratch += unpack_scratch(devices, neg_cap, feature)
    if so_far is not None:
        operands.append(so_far)
        specs.append(rows_spec)
    return call(
        functools.partial(add_kernel, rows=rows, neg_cap=neg_cap, first=so_far is None),
        "add_grads",
        2 * feature * slots * rows_dev,
        2 * feature * slots + 8 * feature * rows_dev,
        grid=(rows_dev // rows,),
        in_specs=specs,
        out_specs=rows_spec,
        out_shape=jax.ShapeDtypeStruct((feature, rows_dev), F32),
        scratch_shapes=scratch,
    )(*operands)


def add_quarters_kernel(
    recv_ref, asked_ref, so_far_ref, out_ref, flat, neg_rows, neg_flat, *, neg_cap
):
    devices = recv_ref.shape[0]
    feature, rows = out_ref.shape
    step = pl.program_id(0)

    @pl.when(step == 0)
    def _():
        start = recv_ref.shape[1] - feature
        lanes = lax.broadcasted_iota(jnp.int32, (feature, LANES), 1) // SHARE
        for first in range(0, devices, PARTS):
            to = first // PARTS * LANES
            blocks = [recv_ref[first + i, start:, :].astype(F32) for i in range(PARTS)]
            for part in range(PARTS):
                piece = blocks[part]
                for j in range(1, PARTS):
                    piece = jnp.where(lanes == j, blocks[part ^ j], piece)
                flat[part, :, to : to + LANES] = piece.astype(BF16)
        unpack_all(recv_ref, 0, neg_cap, neg_rows, neg_flat)

    base = step * rows
    asked = quarter_ids([asked_ref[d : d + 1, :LANES] for d in range(devices)])
    row = asked[0]
    for part in range(1, PARTS):
        row = jnp.where(step == part, asked[part], row)
    total = dot(flat[step], one_hot(rows, row, base), NT)
    negs = slice(asked_ref.shape[1] - LANES, asked_ref.shape[1] - LANES + neg_cap)
    row = jnp.concatenate([asked_ref[d : d + 1, negs] for d in range(devices)], axis=1)
    out_ref[...] = total + dot(neg_flat[...], one_hot(rows, row, base), NT) + so_far_ref[...]


def add_quarters(recv, asked, so_far, neg_cap):
    feature, rows_dev = so_far.shape
    devices = recv.shape[0]
    slots = devices * LANES
    whole_asked = pl.BlockSpec(asked.shape, lambda i: (0, 0))
    rows_spec = pl.BlockSpec((feature, rows_dev // PARTS), lambda i: (0, i))
    return call(
        functools.partial(add_quarters_kernel, neg_cap=neg_cap),
        "add_quarters",
        feature * (slots // 2 + 2 * devices * neg_cap) * rows_dev,
        2 * feature * slots + 8 * feature * rows_dev,
        grid=(PARTS,),
        in_specs=[pl.BlockSpec(recv.shape, lambda i: (0, 0, 0)), whole_asked, rows_spec],
        out_specs=rows_spec,
        out_shape=jax.ShapeDtypeStruct((feature, rows_dev), F32),
        scratch_shapes=[pltpu.VMEM((PARTS, feature, slots // PARTS), BF16)]
        + unpack_scratch(devices, neg_cap, feature),
    )(recv, asked, so_far)


def add_pool_kernel(*refs, rows, first):
    one_ref, two_ref, one_req_ref, two_req_ref = refs[:4]
    out_ref, packed, *flats = refs[4 + (not first) :]
    step = pl.program_id(0)

    @pl.when(step == 0)
    def _():
        for recv_ref, flat in zip((one_ref, two_ref), flats):
            unpack_all(recv_ref, 0, POOL, packed, flat)

    total = dot(flats[0][...], one_hot(rows, one_req_ref[...], step * rows), NT)
    total = total + dot(flats[1][...], one_hot(rows, two_req_ref[...], step * rows), NT)
    if not first:
        total = total + refs[4][...]
    out_ref[...] = total


def add_pool(one, two, requests, so_far, feature, rows_dev):
    rows = 512
    devices = one.shape[0]
    slots = devices * POOL
    recv_spec = pl.BlockSpec(one.shape, lambda i: (0, 0, 0))
    req_spec = pl.BlockSpec((1, slots), lambda i: (0, 0))
    rows_spec = pl.BlockSpec((feature, rows), lambda i: (0, i))
    packed, flat = unpack_scratch(devices, POOL, feature)
    extra = [] if so_far is None else [so_far]
    return call(
        functools.partial(add_pool_kernel, rows=rows, first=so_far is None),
        "add_pool",
        4 * feature * slots * rows_dev,
        4 * feature * slots + 4 * feature * rows_dev,
        grid=(rows_dev // rows,),
        in_specs=[recv_spec, recv_spec, req_spec, req_spec] + [rows_spec] * len(extra),
        out_specs=rows_spec,
        out_shape=jax.ShapeDtypeStruct((feature, rows_dev), F32),
        scratch_shapes=[packed, flat, flat],
    )(one, two, requests[0][None], requests[1][None], *extra)


def after(value, other):
    anywhere = pl.BlockSpec(memory_space=pl.ANY)
    return call(
        lambda value_ref, other_ref, out_ref: None,
        "after",
        0,
        0,
        in_specs=[anywhere, anywhere],
        out_specs=anywhere,
        out_shape=jax.ShapeDtypeStruct(value.shape, value.dtype),
        input_output_aliases={0: 0},
    )(value, other)


def exchange(value):
    return lax.all_to_all(value, ("shard", "grp"), split_axis=0, concat_axis=0, tiled=True)


def swap(value, bit):
    sharers = lax.axis_size("grp")
    return lax.ppermute(value, "grp", [(i, i ^ bit) for i in range(sharers)])


def share_out(value, wait=lambda block: block):
    sharers = lax.axis_size("grp")
    blocks = {0: value}
    bit = sharers // 2
    while bit:
        for k in list(blocks):
            blocks[k ^ bit] = swap(wait(blocks[k]) if k else blocks[k], bit)
        bit //= 2
    return [blocks[k] for k in range(sharers)]


def trade(blocks):
    sharers = len(blocks)
    terms = [[block] for block in blocks]
    bit = 1
    while bit < sharers:
        for k in range(0, sharers, 2 * bit):
            total = terms[k ^ bit][0].astype(F32)
            for term in terms[k ^ bit][1:]:
                total = total + term.astype(F32)
            terms[k].append(swap(total.astype(BF16), bit))
        bit *= 2
    return terms[0]


def pad_lanes(value, width, fill):
    return jnp.pad(value, ((0, 0), (0, width - value.shape[1])), constant_values=fill)


def body(entity_table, rel_diag, src_ids, dst_ids, rel_ids, neg_ids):
    rows_dev, feature = entity_table.shape
    sharers = lax.axis_size("grp")
    devices = lax.axis_size("shard") * sharers
    spans, neg_count = neg_ids.shape
    edge_count = src_ids.shape[0]
    block_len = edge_count // spans
    edge_cap = 4 * edge_count // devices
    chunks = round_up(edge_cap, LANES) // LANES
    part_width = neg_count // sharers
    neg_cap = round_up(2 * spans * part_width // devices, 16)
    width = round_up(block_len, 512)
    part = round_up(part_width, LANES)
    me = lax.axis_index("grp")

    table = entity_table.T.astype(BF16)
    own_ids = lax.dynamic_slice_in_dim(neg_ids, me * part_width, part_width, 1)
    rel_rows = pad_lanes(rel_ids.reshape(spans, block_len), width, -1)

    def ask(zero, chunks):
        message, *slots = make_slots(
            lax.axis_index(("shard", "grp")),
            src_ids + zero,
            dst_ids + zero,
            own_ids,
            rows_dev,
            devices,
            chunks,
            neg_cap,
            width,
            part,
        )
        asked = exchange(message)[:, 0]
        return asked, asked[:, -LANES:], slots, slots[-1]

    def chunked(zero):
        asked, neg_asked, slots, neg_slot = ask(zero, chunks)
        direct = [asked[:, c * LANES : (c + 1) * LANES] for c in range(chunks)]
        back = [exchange(gather(table, direct[0], neg_asked, neg_cap))]
        back += [exchange(gather(table, direct[c])) for c in range(1, chunks)]
        negatives = share_out(spread_neg(back[0], neg_slot, neg_cap, feature))
        rows = None
        for c in range(chunks):
            rows = spread(back[c], slots[c], rows, feature)
        src_grad, dst_grad, neg_grads = edges(rows, rel_rows, rel_diag, negatives)
        grad = None
        for c in range(1, chunks):
            sent = exchange(collect(src_grad, dst_grad, slots[c], devices))
            grad = add_rows(sent, direct[c], grad, feature, rows_dev)
        sent = collect(src_grad, dst_grad, slots[0], devices, neg_cap)
        sent = exchange(collect_neg(sent, neg_slot, trade(neg_grads), neg_cap))
        return add_rows(sent, direct[0], grad, feature, rows_dev, neg_asked, neg_cap)

    def pooled():
        asked, neg_asked, (slot, pool_slot, busy, _), neg_slot = ask(0, 0)
        listed = asked[:, LANES : LANES + RELAYS * POOL].reshape(devices, RELAYS, POOL)
        listed = listed.transpose(1, 0, 2).reshape(RELAYS, devices * POOL) - me * rows_dev
        listed = listed[me ^ jnp.arange(RELAYS, dtype=jnp.int32)]
        back = exchange(gather_quarters(table, asked, neg_cap))
        far = swap(gather_pool(table, listed[3], devices), 1)
        far = swap(gather_pool(table, listed[2], devices) + far, 2)
        near = swap(gather_pool(table, listed[1], devices), 1)
        near = gather_pool(table, listed[0], devices) + near
        rows = spread(back, slot, None, feature)
        negatives = share_out(
            spread_neg(back, neg_slot, neg_cap, feature), lambda block: after(block, rows)
        )
        src_grad, dst_grad, rest = edges(
            rows, rel_rows, rel_diag, negatives, exchange(near + far), pool_slot, busy
        )
        neg_grads, pool = rest[:-1], rest[-1]
        near = exchange(pool)
        far = swap(near, 2)
        sent = collect(src_grad, dst_grad, slot, devices, neg_cap)
        sent = exchange(collect_neg(sent, neg_slot, trade(neg_grads), neg_cap))
        grad = add_pool(near, swap(near, 1), listed[:2], None, feature, rows_dev)
        far = after(far, grad)
        grad = add_pool(far, swap(far, 1), listed[2:], grad, feature, rows_dev)
        return add_quarters(sent, asked, grad, neg_cap), jnp.max(neg_asked[:, -1])

    if chunks == 1 or sharers != RELAYS:
        return chunked(0).T
    return lax.while_loop(
        lambda state: state[1] > 0,
        lambda state: (chunked(jnp.minimum(state[1], 0)), -state[1]),
        pooled(),
    )[0].T


def solution(mesh):
    placed = (
        P(("shard", "grp"), None),
        P(),
        P(("shard", "grp")),
        P(("shard", "grp")),
        P(("shard", "grp")),
        P("shard", None),
    )
    return jax.shard_map(
        body, mesh=mesh, in_specs=placed, out_specs=P(("shard", "grp"), None), check_vma=False
    )
```
